32 devices in a mesh: dp: 4 (over x, core), tensor: 8 (over z, y).
Axes of the slice: x: 2, y: 2, z: 4, core: 2. Of those that a mesh axis runs over, the one named last changes fastest.
Arguments:
- tokens: bfloat16 [16384, 2048], P('dp'), may hold values from -6 to 6
- lengths: int32 [8], P('dp'), may hold values from 64 to 2048, as said below
- norm_gain: float32 [2048], replicated, may hold values from 0.5 to 1.5
- norm_shift: float32 [2048], replicated, may hold values from -1 to 1
- qkv_weight: bfloat16 [2048, 6144], P(None, 'tensor'), may hold values from -0.125 to 0.125
- qkv_bias: bfloat16 [6144], P('tensor'), may hold values from -1 to 1
- out_weight: bfloat16 [2048, 2048], P('tensor'), may hold values from -1 to 1
- gate_weight: bfloat16 [2048, 5632], P(None, 'tensor'), may hold values from -0.125 to 0.125
- up_weight: bfloat16 [2048, 5632], P(None, 'tensor'), may hold values from -0.125 to 0.125
- down_weight: bfloat16 [5632, 2048], P('tensor'), may hold values from -0.078125 to 0.078125
- cotangent: bfloat16 [16384, 2048], P('dp'), may hold values from -6 to 6
Outputs:
- layer_out: bfloat16 [16384, 2048], P('dp')
- grad_tokens: bfloat16 [16384, 2048], P('dp')
- grad_gain: float32 [2048], replicated
- grad_shift: float32 [2048], replicated
- grad_qkv: float32 [2048, 6144], P(None, 'tensor')
- grad_bias: float32 [6144], P('tensor')
- grad_out: float32 [2048, 2048], P('tensor')
- grad_gate: float32 [2048, 5632], P(None, 'tensor')
- grad_up: float32 [2048, 5632], P(None, 'tensor')
- grad_down: float32 [5632, 2048], P('tensor')
The draws below stay inside these ranges and needn't reach their ends.
Inputs may be any that keep to these rules, and one draw needn't show every extreme that they name: Each bucket (the 2 sequences on one index of dp) holds one sequence of exactly 2048 tokens; the others have lengths from 64 to 2048. A sequence's tokens fill the first slots of its 2048.
All inputs are finite; a program needn't handle non-finite values.
Results may differ from the reference program's by a relative error of at most 0.012.
Values may be sent and summed in bfloat16 or wider, within the bound.
A program may use at most 384 MiB of HBM per device.

```python
import jax
import jax.numpy as jnp
from jax import lax

D = 2048
HEADS = 32
HEAD = 64
ROT = 16
FF = 5632
SEQS = 2
LEN = 2048
MIN_LEN = 64
SEQ_ALL = 8
TOKENS = 16384


def draw_lengths(key, part):
    key = jax.random.fold_in(key, 11)
    first_key, second_key, third_key = jax.random.split(key, 3)
    buckets = SEQ_ALL // SEQS
    first_draw = jax.random.randint(first_key, (buckets, SEQS), 0, 1025)
    second_draw = jax.random.randint(second_key, (buckets, SEQS), 0, 1025)
    span_len = LEN - MIN_LEN
    shorter = MIN_LEN + span_len * first_draw // 1024 * second_draw // 1024
    chosen = jax.random.randint(third_key, (buckets, 1), 0, SEQS)
    longest = jnp.arange(SEQS)[None, :] == chosen
    return jnp.where(longest, LEN, shorter).reshape(-1).astype(jnp.int32)


def shard_levels(rng, extent, cuts, smallest, top_value):
    gain = 1.0
    for position, shards_of in cuts:
        draws = jax.random.uniform(jax.random.fold_in(jax.random.fold_in(rng, 6), position), (shards_of,), jnp.float32, smallest / len(cuts), top_value / len(cuts))
        gain = gain * jnp.repeat(jnp.exp(draws), extent[position] // shards_of).reshape((-1,) + (1,) * (len(extent) - 1 - position))
    return gain


def gaussian(stream_key, extent, spread, limit, cuts=(), kind=jnp.bfloat16):
    values = spread * jax.random.normal(stream_key, extent, jnp.float32)
    if cuts:
        values = values * shard_levels(stream_key, extent, cuts, -0.22, 0.18)
    return jnp.clip(values, -limit, limit).astype(kind)


def setup_inputs(seed: int = 0) -> dict:
    keys = jax.random.split(jax.random.key(seed), 12)
    return {
        "tokens": gaussian(keys[0], (TOKENS, D), 1.0, 6.0, ((0, 4),)),
        "lengths": draw_lengths(jax.random.fold_in(keys[11], 71), 0),
        "norm_gain": jnp.clip(1.0 + 0.1 * jax.random.normal(keys[2], (D,), jnp.float32), 0.5, 1.5),
        "norm_shift": gaussian(keys[3], (D,), 0.2, 1.0, (), jnp.float32),
        "qkv_weight": gaussian(keys[4], (D, 3 * HEADS * HEAD), D ** -0.5, 0.125, ((1, 8),)),
        "qkv_bias": gaussian(keys[5], (3 * HEADS * HEAD,), 0.2, 1.0, ((0, 8),)),
        "out_weight": gaussian(keys[6], (HEADS * HEAD, D), (D // 64) ** -0.5, 1.0, ((0, 8),)),
        "gate_weight": gaussian(keys[7], (D, FF), D ** -0.5, 0.125, ((1, 8),)),
        "up_weight": gaussian(keys[8], (D, FF), D ** -0.5, 0.125, ((1, 8),)),
        "down_weight": gaussian(keys[9], (FF, D), FF ** -0.5, 0.078125, ((0, 8),)),
        "cotangent": gaussian(keys[10], (TOKENS, D), 1.0, 6.0, ((0, 4),)),
    }


@jax.custom_vjp
def low(v):
    return lax.optimization_barrier(v.astype(jnp.bfloat16)).astype(jnp.float32)

@jax.custom_vjp
def low_back(v):
    return v

def low_keep(v):
    return (low(v), None)

def low_pass(kept, grad):
    return (grad,)

def back_keep(v):
    return (v, None)

def back_low(kept, grad):
    return (low(grad),)
low.defvjp(low_keep, low_pass)
low_back.defvjp(back_keep, back_low)
EPSILON = 1e-05
NEGATIVE = -1e+30
PRECISE = lax.Precision.HIGHEST

def rotary_tables():
    frequency = 10000.0 ** (-jnp.arange(0, ROT, 2).astype(jnp.float32) / ROT)
    angles = jnp.arange(LEN).astype(jnp.float32)[:, None] * frequency[None, :]
    return (jnp.cos(angles)[:, None, :], jnp.sin(angles)[:, None, :])

def rotate(vectors, cosine, sine_table):
    half_size = cosine.shape[-1]
    front_half = vectors[..., :half_size]
    back_half = vectors[..., half_size:2 * half_size]
    return jnp.concatenate([front_half * cosine - back_half * sine_table, back_half * cosine + front_half * sine_table, vectors[..., 2 * half_size:]], axis=-1)

def attend(pieces):
    queries, key_rows, values, length = pieces
    scores = jnp.einsum('qhd,khd->hqk', queries, key_rows, precision=PRECISE) * HEAD ** (-0.5)
    scores = low_back(scores)
    places = jnp.arange(LEN)
    allowed = (places[None, :] <= places[:, None]) & (places[None, :] < length)
    scores = jnp.where(allowed[None], scores, NEGATIVE)
    weights_low = low(jax.nn.softmax(scores, axis=-1))
    return jnp.einsum('hqk,khd->qhd', weights_low, values, precision=PRECISE)

def forward(tokens_wide, norm_gain, norm_shift, qkv_weight, qkv_bias, out_weight, gate_weight, up_weight, down_weight, lengths):
    row_mean = lax.optimization_barrier(jnp.mean(tokens_wide, axis=-1, keepdims=True))
    centred = tokens_wide - row_mean
    row_var = lax.optimization_barrier(jnp.mean(centred * centred, axis=-1, keepdims=True))
    unit_rows = centred * lax.rsqrt(row_var + EPSILON)
    normed = low(unit_rows * norm_gain + norm_shift)
    qkv_full = low_back(jnp.dot(normed, qkv_weight, precision=PRECISE) + qkv_bias)
    qkv_full = qkv_full.reshape(SEQ_ALL, LEN, HEADS, 3, HEAD)
    cosine, sine_table = rotary_tables()
    queries = low(rotate(qkv_full[..., 0, :], cosine, sine_table))
    key_rows = low(rotate(qkv_full[..., 1, :], cosine, sine_table))
    values = low(qkv_full[..., 2, :])
    mixture = lax.map(jax.checkpoint(attend), (queries, key_rows, values, lengths))
    valid_rows = (jnp.arange(LEN)[None, :] < lengths[:, None]).astype(tokens_wide.dtype)
    mixture = mixture * valid_rows[:, :, None, None]
    attended = low_back(low(mixture.reshape(TOKENS, HEADS * HEAD)))
    gate_values = low_back(jnp.dot(normed, gate_weight, precision=PRECISE))
    up_values = low_back(jnp.dot(normed, up_weight, precision=PRECISE))
    hidden = low(jax.nn.silu(gate_values) * up_values)
    return tokens_wide + jnp.dot(attended, out_weight, precision=PRECISE) + jnp.dot(hidden, down_weight, precision=PRECISE)

def reference(tokens, lengths, norm_gain, norm_shift, qkv_weight, qkv_bias, out_weight, gate_weight, up_weight, down_weight, cotangent):

    def whole_layer(tokens_wide, gain_wide, shift_wide, qkv_wide, bias_wide, out_wide, gate_wide, up_wide, down_wide):
        return forward(tokens_wide, gain_wide, shift_wide, qkv_wide, bias_wide, out_wide, gate_wide, up_wide, down_wide, lengths)
    result, pullback = jax.vjp(whole_layer, tokens.astype(jnp.float32), norm_gain.astype(jnp.float32), norm_shift.astype(jnp.float32), qkv_weight.astype(jnp.float32), qkv_bias.astype(jnp.float32), out_weight.astype(jnp.float32), gate_weight.astype(jnp.float32), up_weight.astype(jnp.float32), down_weight.astype(jnp.float32))
    gradients = pullback(cotangent.astype(jnp.float32))
    return (result.astype(jnp.bfloat16), gradients[0].astype(jnp.bfloat16), gradients[1], gradients[2], gradients[3], gradients[4], gradients[5], gradients[6], gradients[7], gradients[8])
```

```python
import functools

import jax
import jax.numpy as jnp
from jax import lax
from jax.experimental import pallas as pl
from jax.experimental.pallas import tpu as pltpu
from jax.sharding import PartitionSpec as P

HEAD = 64
ROT = 16
PAIR = 2 * HEAD
TRIPLE = 6 * HEAD

EPSILON = 1e-05
NEGATIVE = -1e30
F32 = jnp.float32
BF16 = jnp.bfloat16


def rows_product(former, latter):
    return lax.dot_general(
        former, latter, (((0,), (0,)), ((), ())), preferred_element_type=F32
    )


def cols_product(former, latter):
    return lax.dot_general(
        former, latter, (((1,), (1,)), ((), ())), preferred_element_type=F32
    )


def product(former, latter):
    return jnp.dot(former, latter, preferred_element_type=F32)


def rotary_tables(seq_len):
    frequency = 10000.0 ** (-jnp.arange(0, ROT, 2).astype(F32) / ROT)
    angles = jnp.arange(seq_len).astype(F32)[:, None] * frequency[None, :]
    cosine, sine = jnp.cos(angles), jnp.sin(angles)
    still = HEAD - ROT
    cos_head = jnp.concatenate([cosine, cosine, jnp.ones((seq_len, still), F32)], axis=1)
    sin_head = jnp.concatenate([-sine, sine, jnp.zeros((seq_len, still), F32)], axis=1)
    return jnp.tile(cos_head, (1, 2)), jnp.tile(sin_head, (1, 2))


def attention_kernel(
    len_ref, qkv_ref, grad_ref, cos_ref, sin_ref, att_ref, back_ref,
    score, expo, query, key_value, query_t, grad_query, grad_kv_t,
):
    seq_len = qkv_ref.shape[0]
    block = score.shape[1]
    steps = seq_len // block
    length = len_ref[0]
    lane = lax.broadcasted_iota(jnp.int32, (block, PAIR), 1)
    left = lane < HEAD
    near = lax.rem(lane, HEAD) < ROT // 2

    def turn(tile, cosine, sine):
        swapped = jnp.where(
            near, pltpu.roll(tile, PAIR - ROT // 2, 1), pltpu.roll(tile, ROT // 2, 1)
        )
        return tile * cosine + swapped * sine

    def tables(rows):
        cosine, sine = cos_ref[rows, :], sin_ref[rows, :]
        return (
            (cosine, sine),
            (jnp.where(left, 1.0, cosine), jnp.where(left, 0.0, sine)),
            (jnp.where(left, cosine, 1.0), jnp.where(left, sine, 0.0)),
        )

    def prepare(i, carry):
        rows = pl.ds(pl.multiple_of(i * block, block), block)
        tabs = tables(rows)
        first = turn(qkv_ref[rows, 0:PAIR], *tabs[0])
        second = turn(qkv_ref[rows, PAIR : 2 * PAIR], *tabs[1])
        third = turn(qkv_ref[rows, 2 * PAIR : 3 * PAIR], *tabs[2])
        scale = HEAD**-0.5
        first_q = first.astype(BF16).astype(F32) * scale
        second_q = second.astype(BF16).astype(F32) * scale
        query[0, rows, :] = jnp.where(left, 0.0, pltpu.roll(first_q, HEAD, 1)).astype(BF16)
        query[1, rows, :] = jnp.where(left, pltpu.roll(second_q, HEAD, 1), 0.0).astype(BF16)
        key_value[0, rows, :] = jnp.where(left, second, first).astype(BF16)
        key_value[1, rows, :] = third.astype(BF16)
        query_t[0, :, rows] = first_q.T[0:HEAD, :].astype(BF16)
        query_t[1, :, rows] = second_q.T[HEAD:PAIR, :].astype(BF16)
        zero = jnp.zeros((block, PAIR), F32)
        grad_query[rows, :] = zero
        att_ref[rows, :] = zero.astype(BF16)
        for h in range(2):
            grad_kv_t[h, :, rows] = jnp.zeros((PAIR, block), F32)
        return carry

    lax.fori_loop(0, steps, prepare, 0)

    def block_rows(i, carry):
        rows = pl.ds(pl.multiple_of(i * block, block), block)
        q_block = [query[h, rows, :] for h in range(2)]

        def fold(tile, op):
            out = tile[:, 0:PAIR]
            for c in range(1, block // PAIR):
                out = op(out, tile[:, c * PAIR : (c + 1) * PAIR])
            return out

        def scores(j, tops):
            cols = pl.ds(pl.multiple_of(j * block, block), block)
            out = []
            for h in range(2):
                tile = cols_product(q_block[h], key_value[h, cols, :])
                score[h, :, cols] = tile
                out.append(jnp.maximum(tops[h], fold(tile, jnp.maximum)))
            return tuple(out)

        lowest = jnp.full((block, PAIR), NEGATIVE, F32)
        tops = lax.fori_loop(0, i, scores, (lowest, lowest))
        below = lax.broadcasted_iota(jnp.int32, (block, block), 1) <= lax.broadcasted_iota(
            jnp.int32, (block, block), 0
        )
        maxima = []
        for h in range(2):
            tile = jnp.where(below, cols_product(q_block[h], key_value[h, rows, :]), NEGATIVE)
            score[h, :, rows] = tile
            maxima.append(
                jnp.max(jnp.maximum(tops[h], fold(tile, jnp.maximum)), axis=1, keepdims=True)
            )

        def mix(j, sums):
            cols = pl.ds(pl.multiple_of(j * block, block), block)
            out = []
            for h in range(2):
                tile = jnp.exp(score[h, :, cols] - maxima[h])
                low = tile.astype(BF16)
                expo[h, :, cols] = low
                out.append(sums[2 * h] + product(low, key_value[h, cols, :]))
                out.append(sums[2 * h + 1] + fold(tile, jnp.add))
            return tuple(out)

        zero = jnp.zeros((block, PAIR), F32)
        sums = lax.fori_loop(0, i + 1, mix, (zero,) * 4)
        place = i * block + lax.broadcasted_iota(jnp.int32, (block, 1), 0)
        valid = (place < length).astype(F32)
        inverse = [1.0 / jnp.sum(sums[2 * h + 1], axis=1, keepdims=True) for h in range(2)]
        mixture = jnp.where(left, sums[0] * inverse[0], sums[2] * inverse[1]) * valid
        att_ref[rows, :] = mixture.astype(BF16)
        upstream = grad_ref[rows, :].astype(F32) * valid
        inner = upstream * mixture
        scaled, inner_sum, scaled_t = [], [], []
        for h in range(2):
            own = left if h == 0 else jnp.logical_not(left)
            inner_sum.append(
                jnp.sum(jnp.where(own, inner, 0.0), axis=1, keepdims=True) * inverse[h]
            )
            mine = jnp.where(own, upstream * inverse[h], 0.0)
            scaled.append(mine.astype(BF16))
            half = slice(0, HEAD) if h == 0 else slice(HEAD, PAIR)
            scaled_t.append(mine.T[half, :].astype(BF16))

        def grads(j, sums):
            cols = pl.ds(pl.multiple_of(j * block, block), block)
            out = []
            for h in range(2):
                low = expo[h, :, cols]
                kv = key_value[h, cols, :]
                grad_weight = cols_product(scaled[h], kv)
                grad_score = (low.astype(F32) * (grad_weight - inner_sum[h])).astype(BF16)
                out.append(sums[h] + product(grad_score, kv))
                key_part = product(query_t[h, :, rows], grad_score)
                value_part = product(scaled_t[h], low)
                key_at, value_at = (HEAD, 0) if h == 0 else (0, HEAD)
                grad_kv_t[h, key_at : key_at + HEAD, cols] += key_part
                grad_kv_t[h, value_at : value_at + HEAD, cols] += value_part
            return tuple(out)

        gq = lax.fori_loop(0, i + 1, grads, (zero, zero))
        scale = HEAD**-0.5
        grad_query[rows, :] = (
            jnp.where(left, pltpu.roll(gq[0], HEAD, 1), pltpu.roll(gq[1], HEAD, 1)) * scale
        )
        return carry

    lax.fori_loop(0, lax.div(length + block - 1, block), block_rows, 0)

    def finish(i, carry):
        rows = pl.ds(pl.multiple_of(i * block, block), block)
        tabs = tables(rows)
        gq = grad_query[rows, :]
        low_kv = grad_kv_t[0, :, rows].T
        high_kv = grad_kv_t[1, :, rows].T
        tiles = (jnp.where(left, gq, low_kv), jnp.where(left, low_kv, gq), high_kv)
        for c in range(3):
            back_ref[rows, c * PAIR : (c + 1) * PAIR] = turn(
                tiles[c], tabs[c][0], -tabs[c][1]
            ).astype(BF16)
        return carry

    lax.fori_loop(0, steps, finish, 0)


def attention(length, qkv, grad_mixture, cosine, sine):
    seq_len, width = qkv.shape
    pairs = width // TRIPLE
    block = min(512, seq_len)
    flops = 6 * 2 * (2 * pairs) * seq_len * seq_len * PAIR
    return pl.pallas_call(
        attention_kernel,
        grid=(pairs,),
        in_specs=[
            pl.BlockSpec(memory_space=pltpu.SMEM),
            pl.BlockSpec((seq_len, TRIPLE), lambda g: (0, g)),
            pl.BlockSpec((seq_len, PAIR), lambda g: (0, g)),
            pl.BlockSpec((seq_len, PAIR), lambda g: (0, 0)),
            pl.BlockSpec((seq_len, PAIR), lambda g: (0, 0)),
        ],
        out_specs=[
            pl.BlockSpec((seq_len, PAIR), lambda g: (0, g)),
            pl.BlockSpec((seq_len, TRIPLE), lambda g: (0, g)),
        ],
        out_shape=[
            jax.ShapeDtypeStruct((seq_len, pairs * PAIR), BF16),
            jax.ShapeDtypeStruct((seq_len, width), BF16),
        ],
        scratch_shapes=[
            pltpu.VMEM((2, block, seq_len), F32),
            pltpu.VMEM((2, block, seq_len), BF16),
            pltpu.VMEM((2, seq_len, PAIR), BF16),
            pltpu.VMEM((2, seq_len, PAIR), BF16),
            pltpu.VMEM((2, HEAD, seq_len), BF16),
            pltpu.VMEM((seq_len, PAIR), F32),
            pltpu.VMEM((2, PAIR, seq_len), F32),
        ],
        compiler_params=pltpu.CompilerParams(vmem_limit_bytes=48 * 2**20),
        cost_estimate=pl.CostEstimate(
            flops=flops,
            bytes_accessed=seq_len * width * 8,
            transcendentals=2 * pairs * seq_len * seq_len // 2,
        ),
        name="attention",
    )(length, qkv, grad_mixture, cosine, sine)


def norm_parts(tokens_wide):
    row_mean = jnp.mean(tokens_wide, axis=-1, keepdims=True)
    centred = tokens_wide - row_mean
    row_var = jnp.mean(centred * centred, axis=-1, keepdims=True)
    inv_scale = lax.rsqrt(row_var + EPSILON)
    return centred * inv_scale, inv_scale


def norm_backward(grad_normed, unit_rows, inv_scale, upstream, norm_gain):
    scaled = grad_normed * norm_gain
    mean_scaled = jnp.mean(scaled, axis=-1, keepdims=True)
    mean_cross = jnp.mean(scaled * unit_rows, axis=-1, keepdims=True)
    gradient = upstream.astype(F32) + inv_scale * (
        scaled - mean_scaled - unit_rows * mean_cross
    )
    return (
        gradient.astype(BF16),
        jnp.sum(grad_normed * unit_rows, axis=0),
        jnp.sum(grad_normed, axis=0),
    )


def line_reduce(terms, place, count):
    blocks = terms.reshape(count, terms.shape[0] // count, terms.shape[1])

    def block(index):
        return lax.dynamic_index_in_dim(
            blocks, jnp.clip(index, 0, count - 1), axis=0, keepdims=False
        )

    total = block(place).astype(F32)
    if count == 1:
        return total
    up, down = block(count - 1 + place), block(place - count + 1)
    for step in range(1, count):
        up_pairs, down_pairs = [], []
        for z in range(count):
            for y in range(2):
                if z <= step - 1 and z + 1 < count:
                    up_pairs.append((2 * z + y, 2 * z + 2 + y))
                if z >= count - step and z >= 1:
                    down_pairs.append((2 * z + y, 2 * z - 2 + y))
        up = lax.ppermute(up, "tensor", up_pairs)
        down = lax.ppermute(down, "tensor", down_pairs)
        if step < count - 1:
            up = (block(count - step - 1 + place).astype(F32) + up.astype(F32)).astype(BF16)
            down = (block(place + step + 1 - count).astype(F32) + down.astype(F32)).astype(BF16)
    return total + up.astype(F32) + down.astype(F32)


def line_gather(own, place, count):
    rows, cols = own.shape
    held = jnp.zeros((count * rows, cols), own.dtype)
    up = down = own
    for step in range(1, count):
        up_pairs, down_pairs = [], []
        for z in range(count):
            for y in range(2):
                if z >= step - 1 and z + 1 < count:
                    up_pairs.append((2 * z + y, 2 * z + 2 + y))
                if z <= count - step and z >= 1:
                    down_pairs.append((2 * z + y, 2 * z - 2 + y))
        up = lax.ppermute(up, "tensor", up_pairs)
        down = lax.ppermute(down, "tensor", down_pairs)
        from_up = jnp.where(place >= step, place - step, place)
        from_down = jnp.where(place + step < count, place + step, place)
        held = lax.dynamic_update_slice(held, up, (from_up * rows, 0))
        held = lax.dynamic_update_slice(held, down, (from_down * rows, 0))
    return lax.dynamic_update_slice(held, own, (place * rows, 0))


def body(
    tokens,
    lengths,
    norm_gain,
    norm_shift,
    qkv_weight,
    qkv_bias,
    out_weight,
    gate_weight,
    up_weight,
    down_weight,
    cotangent,
):
    tensor_size = lax.axis_size("tensor")
    dp_size = lax.axis_size("dp")
    count = tensor_size // 2
    where = lax.axis_index("tensor")
    dp_place = lax.axis_index("dp")
    place, side = where // 2, where % 2
    across = [(i, i ^ 1) for i in range(tensor_size)]
    row_count, width = tokens.shape
    rows = row_count // 2
    chunk_count = 4
    chunk = rows // chunk_count
    share = chunk // count

    def partner(weight):
        part = weight.shape[0] // dp_size
        mine = lax.dynamic_slice_in_dim(weight, dp_place * part, part, 0)
        return lax.all_gather(lax.ppermute(mine, "tensor", across), "dp", axis=0, tiled=True)

    qkv_both = jnp.concatenate([qkv_weight, partner(qkv_weight)], axis=1)
    bias_both = jnp.concatenate([qkv_bias, lax.ppermute(qkv_bias, "tensor", across)])
    out_both = jnp.concatenate([out_weight, partner(out_weight)], axis=0)
    gate_both = jnp.concatenate([gate_weight, partner(gate_weight)], axis=1)
    up_both = jnp.concatenate([up_weight, partner(up_weight)], axis=1)
    down_both = jnp.concatenate([down_weight, partner(down_weight)], axis=0)

    own_tokens = lax.dynamic_slice_in_dim(tokens, side * rows, rows, 0)
    own_cot = lax.dynamic_slice_in_dim(cotangent, side * rows, rows, 0)
    length = lax.dynamic_slice_in_dim(lengths, side, 1, 0)
    unit_rows, _ = norm_parts(own_tokens.astype(F32))
    normed = (unit_rows * norm_gain + norm_shift).astype(BF16)

    qkv = product(normed, qkv_both) + bias_both.astype(F32)
    grad_mixture = cols_product(own_cot, out_both).astype(BF16)
    attended, qkv_back = attention(length, qkv, grad_mixture, *rotary_tables(rows))

    layer_out = jnp.zeros(tokens.shape, BF16)
    grad_tokens = jnp.zeros(tokens.shape, BF16)
    gain_part = jnp.zeros((width,), F32)
    shift_part = jnp.zeros((width,), F32)

    def spread(whole, own, begin):
        held = line_gather(own, place, count)
        other = lax.ppermute(held, "tensor", across)
        whole = lax.dynamic_update_slice(whole, held, (side * rows + begin, 0))
        return lax.dynamic_update_slice(whole, other, ((1 - side) * rows + begin, 0))

    hidden_rows, gate_rows, up_rows = [], [], []
    for c in range(chunk_count):
        begin = c * chunk
        end = begin + chunk
        rows_in = normed[begin:end]
        cot = own_cot[begin:end]
        gate = product(rows_in, gate_both)
        up = product(rows_in, up_both)
        gate_sig = jax.nn.sigmoid(gate)
        gate_silu = gate * gate_sig
        hidden = (gate_silu * up).astype(BF16)
        grad_hidden = cols_product(cot, down_both)
        gate_back = (grad_hidden * up * gate_sig * (1.0 + gate * (1.0 - gate_sig))).astype(BF16)
        up_back = (grad_hidden * gate_silu).astype(BF16)
        hidden_rows.append(hidden)
        gate_rows.append(gate_back)
        up_rows.append(up_back)
        first_row = begin + place * share
        share_tokens = lax.dynamic_slice_in_dim(own_tokens, first_row, share, 0).astype(F32)
        share_cot = lax.dynamic_slice_in_dim(own_cot, first_row, share, 0)

        terms = (product(attended[begin:end], out_both) + product(hidden, down_both)).astype(BF16)
        own = share_tokens + line_reduce(terms, place, count)
        layer_out = spread(layer_out, own.astype(BF16), begin)

        terms = (
            cols_product(qkv_back[begin:end], qkv_both)
            + cols_product(gate_back, gate_both)
            + cols_product(up_back, up_both)
        ).astype(BF16)
        share_unit, share_scale = norm_parts(share_tokens)
        own, gain_term, shift_term = norm_backward(
            line_reduce(terms, place, count), share_unit, share_scale, share_cot, norm_gain
        )
        gain_part += gain_term
        shift_part += shift_term
        grad_tokens = spread(grad_tokens, own, begin)

    def settle(grad, axis):
        half = grad.shape[axis] // 2
        mine = lax.slice_in_dim(grad, 0, half, axis=axis)
        theirs = lax.slice_in_dim(grad, half, 2 * half, axis=axis)
        stacked = jnp.concatenate(
            [
                mine.reshape(dp_size, mine.shape[0] // dp_size, mine.shape[1]),
                theirs.reshape(dp_size, theirs.shape[0] // dp_size, theirs.shape[1]),
            ],
            axis=1,
        ).astype(BF16)
        part = lax.psum_scatter(stacked, "dp", scatter_dimension=0, tiled=False)
        cut = part.shape[0] // 2
        total = part[:cut].astype(F32) + lax.ppermute(part[cut:], "tensor", across).astype(F32)
        return lax.all_gather(total.astype(BF16), "dp", axis=0, tiled=True).astype(F32)

    grad_qkv = settle(rows_product(normed, qkv_back), 1)
    grad_out = settle(rows_product(attended, own_cot), 0)
    hidden = jnp.concatenate(hidden_rows, axis=0)
    gate_back = jnp.concatenate(gate_rows, axis=0)
    up_back = jnp.concatenate(up_rows, axis=0)
    grad_gate = settle(rows_product(normed, gate_back), 1)
    grad_up = settle(rows_product(normed, up_back), 1)
    grad_down = settle(rows_product(hidden, own_cot), 0)
    bias_part = jnp.sum(qkv_back.astype(F32), axis=0)
    half = qkv_bias.shape[0]
    bias_part = bias_part[:half] + lax.ppermute(bias_part[half:], "tensor", across)
    grad_bias = lax.psum(bias_part, "dp")
    gain_part, shift_part = lax.psum((gain_part, shift_part), ("dp", "tensor"))
    return (
        layer_out,
        grad_tokens,
        gain_part,
        shift_part,
        grad_qkv,
        grad_bias,
        grad_out,
        grad_gate,
        grad_up,
        grad_down,
    )


def solution(mesh):
    placed = (
        P("dp", None),
        P("dp"),
        P(),
        P(),
        P(None, "tensor"),
        P("tensor"),
        P("tensor", None),
        P(None, "tensor"),
        P(None, "tensor"),
        P("tensor", None),
        P("dp", None),
    )
    return jax.shard_map(
        body,
        mesh=mesh,
        in_specs=placed,
        out_specs=(
            P("dp", None),
            P("dp", None),
            P(),
            P(),
            P(None, "tensor"),
            P("tensor"),
            P("tensor", None),
            P(None, "tensor"),
            P(None, "tensor"),
            P("tensor", None),
        ),
        check_vma=False,
    )
```

```python
import functools

import jax
import jax.numpy as jnp
from jax import lax
from jax.experimental import pallas as pl
from jax.experimental.pallas import tpu as pltpu
from jax.sharding import PartitionSpec as P

HEAD = 64
ROT = 16
PAIR = 2 * HEAD
TRIPLE = 6 * HEAD

EPSILON = 1e-05
NEGATIVE = -1e30
F32 = jnp.float32
BF16 = jnp.bfloat16


def rows_product(former, latter):
    return lax.dot_general(
        former, latter, (((0,), (0,)), ((), ())), preferred_element_type=F32
    )


def cols_product(former, latter):
    return lax.dot_general(
        former, latter, (((1,), (1,)), ((), ())), preferred_element_type=F32
    )


def product(former, latter):
    return jnp.dot(former, latter, preferred_element_type=F32)


def rotary_tables(seq_len):
    frequency = 10000.0 ** (-jnp.arange(0, ROT, 2).astype(F32) / ROT)
    angles = jnp.arange(seq_len).astype(F32)[:, None] * frequency[None, :]
    cosine, sine = jnp.cos(angles), jnp.sin(angles)
    still = HEAD - ROT
    cos_head = jnp.concatenate([cosine, cosine, jnp.ones((seq_len, still), F32)], axis=1)
    sin_head = jnp.concatenate([-sine, sine, jnp.zeros((seq_len, still), F32)], axis=1)
    return jnp.tile(cos_head, (1, 2)), jnp.tile(sin_head, (1, 2))


def attention_kernel(
    len_ref, qkv_ref, grad_ref, cos_ref, sin_ref, att_ref, back_ref,
    score, expo, query, key_value, query_t, grad_query, grad_kv_t,
):
    seq_len = qkv_ref.shape[0]
    block = score.shape[1]
    steps = seq_len // block
    length = len_ref[0]
    lane = lax.broadcasted_iota(jnp.int32, (block, PAIR), 1)
    left = lane < HEAD
    near = lax.rem(lane, HEAD) < ROT // 2

    def turn(tile, cosine, sine):
        swapped = jnp.where(
            near, pltpu.roll(tile, PAIR - ROT // 2, 1), pltpu.roll(tile, ROT // 2, 1)
        )
        return tile * cosine + swapped * sine

    def tables(rows):
        cosine, sine = cos_ref[rows, :], sin_ref[rows, :]
        return (
            (cosine, sine),
            (jnp.where(left, 1.0, cosine), jnp.where(left, 0.0, sine)),
            (jnp.where(left, cosine, 1.0), jnp.where(left, sine, 0.0)),
        )

    def prepare(i, carry):
        rows = pl.ds(pl.multiple_of(i * block, block), block)
        tabs = tables(rows)
        first = turn(qkv_ref[rows, 0:PAIR], *tabs[0])
        second = turn(qkv_ref[rows, PAIR : 2 * PAIR], *tabs[1])
        third = turn(qkv_ref[rows, 2 * PAIR : 3 * PAIR], *tabs[2])
        scale = HEAD**-0.5
        first_q = first.astype(BF16).astype(F32) * scale
        second_q = second.astype(BF16).astype(F32) * scale
        query[0, rows, :] = jnp.where(left, 0.0, pltpu.roll(first_q, HEAD, 1)).astype(BF16)
        query[1, rows, :] = jnp.where(left, pltpu.roll(second_q, HEAD, 1), 0.0).astype(BF16)
        key_value[0, rows, :] = jnp.where(left, second, first).astype(BF16)
        key_value[1, rows, :] = third.astype(BF16)
        query_t[0, :, rows] = first_q.T[0:HEAD, :].astype(BF16)
        query_t[1, :, rows] = second_q.T[HEAD:PAIR, :].astype(BF16)
        zero = jnp.zeros((block, PAIR), F32)
        grad_query[rows, :] = zero
        att_ref[rows, :] = zero.astype(BF16)
        for h in range(2):
            grad_kv_t[h, :, rows] = jnp.zeros((PAIR, block), F32)
        return carry

    lax.fori_loop(0, steps, prepare, 0)

    def block_rows(i, carry):
        rows = pl.ds(pl.multiple_of(i * block, block), block)
        q_block = [query[h, rows, :] for h in range(2)]

        def fold(tile, op):
            out = tile[:, 0:PAIR]
            for c in range(1, block // PAIR):
                out = op(out, tile[:, c * PAIR : (c + 1) * PAIR])
            return out

        def scores(j, tops):
            cols = pl.ds(pl.multiple_of(j * block, block), block)
            out = []
            for h in range(2):
                tile = cols_product(q_block[h], key_value[h, cols, :])
                score[h, :, cols] = tile
                out.append(jnp.maximum(tops[h], fold(tile, jnp.maximum)))
            return tuple(out)

        lowest = jnp.full((block, PAIR), NEGATIVE, F32)
        tops = lax.fori_loop(0, i, scores, (lowest, lowest))
        below = lax.broadcasted_iota(jnp.int32, (block, block), 1) <= lax.broadcasted_iota(
            jnp.int32, (block, block), 0
        )
        maxima = []
        for h in range(2):
            tile = jnp.where(below, cols_product(q_block[h], key_value[h, rows, :]), NEGATIVE)
            score[h, :, rows] = tile
            maxima.append(
                jnp.max(jnp.maximum(tops[h], fold(tile, jnp.maximum)), axis=1, keepdims=True)
            )

        def mix(j, sums):
            cols = pl.ds(pl.multiple_of(j * block, block), block)
            out = []
            for h in range(2):
                tile = jnp.exp(score[h, :, cols] - maxima[h])
                low = tile.astype(BF16)
                expo[h, :, cols] = low
                out.append(sums[2 * h] + product(low, key_value[h, cols, :]))
                out.append(sums[2 * h + 1] + fold(tile, jnp.add))
            return tuple(out)

        zero = jnp.zeros((block, PAIR), F32)
        sums = lax.fori_loop(0, i + 1, mix, (zero,) * 4)
        place = i * block + lax.broadcasted_iota(jnp.int32, (block, 1), 0)
        valid = (place < length).astype(F32)
        inverse = [1.0 / jnp.sum(sums[2 * h + 1], axis=1, keepdims=True) for h in range(2)]
        mixture = jnp.where(left, sums[0] * inverse[0], sums[2] * inverse[1]) * valid
        att_ref[rows, :] = mixture.astype(BF16)
        upstream = grad_ref[rows, :].astype(F32) * valid
        inner = upstream * mixture
        scaled, inner_sum, scaled_t = [], [], []
        for h in range(2):
            own = left if h == 0 else jnp.logical_not(left)
            inner_sum.append(
                jnp.sum(jnp.where(own, inner, 0.0), axis=1, keepdims=True) * inverse[h]
            )
            mine = jnp.where(own, upstream * inverse[h], 0.0)
            scaled.append(mine.astype(BF16))
            half = slice(0, HEAD) if h == 0 else slice(HEAD, PAIR)
            scaled_t.append(mine.T[half, :].astype(BF16))

        def grads(j, sums):
            cols = pl.ds(pl.multiple_of(j * block, block), block)
            out = []
            for h in range(2):
                low = expo[h, :, cols]
                kv = key_value[h, cols, :]
                grad_weight = cols_product(scaled[h], kv)
                grad_score = (low.astype(F32) * (grad_weight - inner_sum[h])).astype(BF16)
                out.append(sums[h] + product(grad_score, kv))
                key_part = product(query_t[h, :, rows], grad_score)
                value_part = product(scaled_t[h], low)
                key_at, value_at = (HEAD, 0) if h == 0 else (0, HEAD)
                grad_kv_t[h, key_at : key_at + HEAD, cols] += key_part
                grad_kv_t[h, value_at : value_at + HEAD, cols] += value_part
            return tuple(out)

        gq = lax.fori_loop(0, i + 1, grads, (zero, zero))
        scale = HEAD**-0.5
        grad_query[rows, :] = (
            jnp.where(left, pltpu.roll(gq[0], HEAD, 1), pltpu.roll(gq[1], HEAD, 1)) * scale
        )
        return carry

    lax.fori_loop(0, lax.div(length + block - 1, block), block_rows, 0)

    def finish(i, carry):
        rows = pl.ds(pl.multiple_of(i * block, block), block)
        tabs = tables(rows)
        gq = grad_query[rows, :]
        low_kv = grad_kv_t[0, :, rows].T
        high_kv = grad_kv_t[1, :, rows].T
        tiles = (jnp.where(left, gq, low_kv), jnp.where(left, low_kv, gq), high_kv)
        for c in range(3):
            back_ref[rows, c * PAIR : (c + 1) * PAIR] = turn(
                tiles[c], tabs[c][0], -tabs[c][1]
            ).astype(BF16)
        return carry

    lax.fori_loop(0, steps, finish, 0)


def attention(length, qkv, grad_mixture, cosine, sine):
    seq_len, width = qkv.shape
    pairs = width // TRIPLE
    block = min(512, seq_len)
    flops = 6 * 2 * (2 * pairs) * seq_len * seq_len * PAIR
    return pl.pallas_call(
        attention_kernel,
        grid=(pairs,),
        in_specs=[
            pl.BlockSpec(memory_space=pltpu.SMEM),
            pl.BlockSpec((seq_len, TRIPLE), lambda g: (0, g)),
            pl.BlockSpec((seq_len, PAIR), lambda g: (0, g)),
            pl.BlockSpec((seq_len, PAIR), lambda g: (0, 0)),
            pl.BlockSpec((seq_len, PAIR), lambda g: (0, 0)),
        ],
        out_specs=[
            pl.BlockSpec((seq_len, PAIR), lambda g: (0, g)),
            pl.BlockSpec((seq_len, TRIPLE), lambda g: (0, g)),
        ],
        out_shape=[
            jax.ShapeDtypeStruct((seq_len, pairs * PAIR), BF16),
            jax.ShapeDtypeStruct((seq_len, width), BF16),
        ],
        scratch_shapes=[
            pltpu.VMEM((2, block, seq_len), F32),
            pltpu.VMEM((2, block, seq_len), BF16),
            pltpu.VMEM((2, seq_len, PAIR), BF16),
            pltpu.VMEM((2, seq_len, PAIR), BF16),
            pltpu.VMEM((2, HEAD, seq_len), BF16),
            pltpu.VMEM((seq_len, PAIR), F32),
            pltpu.VMEM((2, PAIR, seq_len), F32),
        ],
        compiler_params=pltpu.CompilerParams(vmem_limit_bytes=48 * 2**20),
        cost_estimate=pl.CostEstimate(
            flops=flops,
            bytes_accessed=seq_len * width * 8,
            transcendentals=2 * pairs * seq_len * seq_len // 2,
        ),
        name="attention",
    )(length, qkv, grad_mixture, cosine, sine)


def norm_parts(tokens_wide):
    row_mean = jnp.mean(tokens_wide, axis=-1, keepdims=True)
    centred = tokens_wide - row_mean
    row_var = jnp.mean(centred * centred, axis=-1, keepdims=True)
    inv_scale = lax.rsqrt(row_var + EPSILON)
    return centred * inv_scale, inv_scale


def exchange_kernel(
    chunks, f_ref, g_ref, tok_ref, cot_ref, gain_ref,
    out_ref, grad_ref, part_ref,
    terms, landed, ready, tok_buf, cot_buf,
    term_sem, tok_sem, cot_sem, sum_send, sum_recv,
    line_send, line_recv, side_send, side_recv, keep_sem,
):
    count = landed.shape[3]
    share, width = landed.shape[4:]
    rows = chunks * count * share
    where = lax.axis_index("tensor")
    group = lax.axis_index("dp")
    place, side = where // 2, where % 2
    whole_refs = (out_ref, grad_ref)

    def device(index):
        return (group, index)

    above, below, across = device(where + 2), device(where - 2), device(where + 1 - 2 * side)
    has_above, has_below = place < count - 1, place > 0

    barrier = pltpu.get_barrier_semaphore()

    def greet(target):
        pl.semaphore_signal(barrier, inc=1, device_id=target, device_id_type=pl.DeviceIdType.MESH)

    pl.when(has_above)(lambda: greet(above))
    pl.when(has_below)(lambda: greet(below))
    greet(across)

    def load(c, k):
        source = (f_ref, g_ref)[k].at[pl.ds(c * (count * share), count * share), :]
        return pltpu.make_async_copy(source, terms.at[c, k], term_sem.at[c, k])

    def load_share(c, k):
        begin = pl.ds(side * rows + c * (count * share) + place * share, share)
        source, target, done = ((tok_ref, tok_buf, tok_sem), (cot_ref, cot_buf, cot_sem))[k]
        return pltpu.make_async_copy(source.at[begin, :], target.at[c], done.at[c])

    for c in range(chunks):
        load(c, 0).start()
        load(c, 1).start()
        load_share(c, 0).start()
        load_share(c, 1).start()
    pl.semaphore_wait(
        barrier, 1 + has_above.astype(jnp.int32) + has_below.astype(jnp.int32)
    )

    def remote(source, target, send, recv, device_id):
        return pltpu.make_async_remote_copy(
            src_ref=source, dst_ref=target, send_sem=send, recv_sem=recv,
            device_id=device_id, device_id_type=pl.DeviceIdType.MESH,
        )

    def block_of(b):
        return pl.ds(pl.multiple_of(b * share, share), share)

    def sum_copy(c, k, way, b, first):
        target = landed.at[c, k, way, b]
        source = terms.at[c, k, block_of(b), :] if first else target
        return remote(
            source, target, sum_send.at[c, k, way, b], sum_recv.at[c, k, way, b],
            (above, below)[way],
        )

    def place_of(c, b, on_side):
        return pl.ds(
            pl.multiple_of(on_side * rows + c * (count * share) + b * share, share), share
        )

    def line_copy(c, k, b, way, first):
        target = whole_refs[k].at[place_of(c, b, side), :]
        source = ready.at[c, k] if first else target
        return remote(
            source, target, line_send.at[c, k, way, b], line_recv.at[c, k, b],
            (above, below)[way],
        )

    def side_copy(c, k, b, first):
        target = whole_refs[k].at[place_of(c, b, side), :]
        source = ready.at[c, k] if first else target
        return remote(
            source, target, side_send.at[c, k, b], side_recv.at[c, k, b], across
        )

    def keep_copy(c, k):
        return pltpu.make_async_copy(
            ready.at[c, k], whole_refs[k].at[place_of(c, place, side), :], keep_sem.at[c, k]
        )

    def send_ends(c, k):
        load(c, k).wait()

        @pl.when(jnp.logical_not(has_below))
        def _():
            for b in range(count - 1, 0, -1):
                sum_copy(c, k, 0, b, True).start()

        @pl.when(jnp.logical_not(has_above))
        def _():
            for b in range(count - 1):
                sum_copy(c, k, 1, b, True).start()

    step = min(16, share)

    def add_on(c, k, way, b):
        def body(i, carry):
            at = pl.ds(pl.multiple_of(i * step, step), step)
            from_block = pl.ds(pl.multiple_of(b * share + i * step, step), step)
            mine = terms[c, k, from_block, :].astype(F32)
            landed[c, k, way, b, at, :] = (
                mine + landed[c, k, way, b, at, :].astype(F32)
            ).astype(BF16)
            return carry

        lax.fori_loop(0, share // step, body, 0)

    def sums(c, k):
        for i in range(count - 1):
            b = count - 1 - i

            @pl.when(has_below & (place <= b))
            def _(b=b):
                sum_copy(c, k, 0, b, False).wait_recv()

            @pl.when(has_below & (place < b))
            def _(b=b):
                add_on(c, k, 0, b)
                sum_copy(c, k, 0, b, False).start()

            b = i

            @pl.when(has_above & (place >= b))
            def _(b=b):
                sum_copy(c, k, 1, b, False).wait_recv()

            @pl.when(has_above & (place > b))
            def _(b=b):
                add_on(c, k, 1, b)
                sum_copy(c, k, 1, b, False).start()

    def finish(c, k):
        load_share(c, k).wait()

        def body(i, carry):
            at = pl.ds(pl.multiple_of(i * step, step), step)
            mine = pl.ds(pl.multiple_of(place * share + i * step, step), step)
            up = landed[c, k, 0, place, at, :].astype(F32)
            down = landed[c, k, 1, place, at, :].astype(F32)
            total = (
                terms[c, k, mine, :].astype(F32)
                + jnp.where(has_below, up, 0.0)
                + jnp.where(has_above, down, 0.0)
            )
            wide = tok_buf[c, at, :].astype(F32)
            if k == 0:
                ready[c, k, at, :] = (wide + total).astype(BF16)
                return carry
            scale = 1.0 / width
            centred = wide - jnp.sum(wide, axis=1, keepdims=True) * scale
            variance = jnp.sum(centred * centred, axis=1, keepdims=True) * scale
            inverse = lax.rsqrt(variance + EPSILON)
            unit = centred * inverse
            scaled = total * gain_ref[0:1, :]
            mean_scaled = jnp.sum(scaled, axis=1, keepdims=True) * scale
            mean_cross = jnp.sum(scaled * unit, axis=1, keepdims=True) * scale
            ready[c, k, at, :] = (
                cot_buf[c, at, :].astype(F32)
                + inverse * (scaled - mean_scaled - unit * mean_cross)
            ).astype(BF16)
            gain_term = total * unit
            for r in range(0, step, 8):
                part_ref[0:8, :] += gain_term[r : r + 8, :]
                part_ref[8:16, :] += total[r : r + 8, :]
            return carry

        lax.fori_loop(0, share // step, body, 0)
        pl.when(has_above)(lambda: line_copy(c, k, place, 0, True).start())
        pl.when(has_below)(lambda: line_copy(c, k, place, 1, True).start())
        side_copy(c, k, place, True).start()
        keep_copy(c, k).start()

    def pass_on(c, k):
        for s in range(1, count):
            b = place - s

            @pl.when(b >= 0)
            def _(b=b):
                line_copy(c, k, b, 0, False).wait_recv()
                pl.when(has_above)(lambda: line_copy(c, k, b, 0, False).start())
                side_copy(c, k, b, False).start()

            b = place + s

            @pl.when(b < count)
            def _(b=b):
                line_copy(c, k, b, 1, False).wait_recv()
                pl.when(has_below)(lambda: line_copy(c, k, b, 1, False).start())
                side_copy(c, k, b, False).start()

    part_ref[...] = jnp.zeros_like(part_ref)

    def ends(c, carry):
        send_ends(c, 0)
        send_ends(c, 1)
        return carry

    lax.fori_loop(0, chunks, ends, 0)

    def chunk(c, carry):
        sums(c, 0)
        finish(c, 0)
        pl.when(c > 0)(lambda: pass_on(c - 1, 1))
        sums(c, 1)
        finish(c, 1)
        pass_on(c, 0)
        return carry

    lax.fori_loop(0, chunks, chunk, 0)
    pass_on(chunks - 1, 1)

    def drain(c, carry):
        for k in range(2):
            keep_copy(c, k).wait()
            for b in range(count):
                pl.when(place < b)(lambda: sum_copy(c, k, 0, b, False).wait_send())
                pl.when(place > b)(lambda: sum_copy(c, k, 1, b, False).wait_send())
                pl.when((place >= b) & has_above)(
                    lambda: line_copy(c, k, b, 0, False).wait_send()
                )
                pl.when((place <= b) & has_below)(
                    lambda: line_copy(c, k, b, 1, False).wait_send()
                )
                side_copy(c, k, b, False).wait_send()
                side_copy(c, k, b, False).wait_recv()
        return carry

    lax.fori_loop(0, chunks, drain, 0)


def exchange(f_terms, g_terms, tokens, cotangent, gain, count, chunks):
    row_count, width = tokens.shape
    share = row_count // 2 // chunks // count
    sem = pltpu.SemaphoreType.DMA
    out, grad, part = pl.pallas_call(
        functools.partial(exchange_kernel, chunks),
        in_specs=[pl.BlockSpec(memory_space=pl.ANY)] * 4
        + [pl.BlockSpec(memory_space=pltpu.VMEM)],
        out_specs=[
            pl.BlockSpec(memory_space=pl.ANY),
            pl.BlockSpec(memory_space=pl.ANY),
            pl.BlockSpec(memory_space=pltpu.VMEM),
        ],
        out_shape=[
            jax.ShapeDtypeStruct(tokens.shape, BF16),
            jax.ShapeDtypeStruct(tokens.shape, BF16),
            jax.ShapeDtypeStruct((16, width), F32),
        ],
        scratch_shapes=[
            pltpu.VMEM((chunks, 2, count * share, width), BF16),
            pltpu.VMEM((chunks, 2, 2, count, share, width), BF16),
            pltpu.VMEM((chunks, 2, share, width), BF16),
            pltpu.VMEM((chunks, share, width), BF16),
            pltpu.VMEM((chunks, share, width), BF16),
            sem((chunks, 2)),
            sem((chunks,)),
            sem((chunks,)),
            sem((chunks, 2, 2, count)),
            sem((chunks, 2, 2, count)),
            sem((chunks, 2, 2, count)),
            sem((chunks, 2, count)),
            sem((chunks, 2, count)),
            sem((chunks, 2, count)),
            sem((chunks, 2)),
        ],
        compiler_params=pltpu.CompilerParams(
            collective_id=0, has_side_effects=True, vmem_limit_bytes=62 * 2**20
        ),
        cost_estimate=pl.CostEstimate(
            flops=10 * row_count * width, bytes_accessed=800 * 2**20, transcendentals=0
        ),
        name="exchange",
    )(f_terms, g_terms, tokens, cotangent, gain)
    return out, grad, part[0:8].sum(axis=0), part[8:16].sum(axis=0)


def body(
    tokens,
    lengths,
    norm_gain,
    norm_shift,
    qkv_weight,
    qkv_bias,
    out_weight,
    gate_weight,
    up_weight,
    down_weight,
    cotangent,
):
    tensor_size = lax.axis_size("tensor")
    dp_size = lax.axis_size("dp")
    count = tensor_size // 2
    where = lax.axis_index("tensor")
    dp_place = lax.axis_index("dp")
    side = where % 2
    across = [(i, i ^ 1) for i in range(tensor_size)]
    row_count, width = tokens.shape
    rows = row_count // 2
    chunk_count = 4
    chunk = rows // chunk_count

    def partner(weight):
        part = weight.shape[0] // dp_size
        mine = lax.dynamic_slice_in_dim(weight, dp_place * part, part, 0)
        return lax.all_gather(lax.ppermute(mine, "tensor", across), "dp", axis=0, tiled=True)

    qkv_both = jnp.concatenate([qkv_weight, partner(qkv_weight)], axis=1)
    bias_both = jnp.concatenate([qkv_bias, lax.ppermute(qkv_bias, "tensor", across)])
    out_both = jnp.concatenate([out_weight, partner(out_weight)], axis=0)
    gate_both = jnp.concatenate([gate_weight, partner(gate_weight)], axis=1)
    up_both = jnp.concatenate([up_weight, partner(up_weight)], axis=1)
    down_both = jnp.concatenate([down_weight, partner(down_weight)], axis=0)

    own_tokens = lax.dynamic_slice_in_dim(tokens, side * rows, rows, 0)
    own_cot = lax.dynamic_slice_in_dim(cotangent, side * rows, rows, 0)
    length = lax.dynamic_slice_in_dim(lengths, side, 1, 0)
    unit_rows, _ = norm_parts(own_tokens.astype(F32))
    normed = (unit_rows * norm_gain + norm_shift).astype(BF16)

    qkv = product(normed, qkv_both) + bias_both.astype(F32)
    grad_mixture = cols_product(own_cot, out_both).astype(BF16)
    attended, qkv_back = attention(length, qkv, grad_mixture, *rotary_tables(rows))

    hidden_rows, gate_rows, up_rows, f_rows, g_rows = [], [], [], [], []
    for c in range(chunk_count):
        begin = c * chunk
        end = begin + chunk
        rows_in = normed[begin:end]
        cot = own_cot[begin:end]
        gate = product(rows_in, gate_both)
        up = product(rows_in, up_both)
        gate_sig = jax.nn.sigmoid(gate)
        gate_silu = gate * gate_sig
        hidden = (gate_silu * up).astype(BF16)
        grad_hidden = cols_product(cot, down_both)
        gate_back = (grad_hidden * up * gate_sig * (1.0 + gate * (1.0 - gate_sig))).astype(BF16)
        up_back = (grad_hidden * gate_silu).astype(BF16)
        hidden_rows.append(hidden)
        gate_rows.append(gate_back)
        up_rows.append(up_back)
        f_rows.append(
            (product(attended[begin:end], out_both) + product(hidden, down_both)).astype(BF16)
        )
        g_rows.append(
            (
                cols_product(qkv_back[begin:end], qkv_both)
                + cols_product(gate_back, gate_both)
                + cols_product(up_back, up_both)
            ).astype(BF16)
        )
    layer_out, grad_tokens, gain_part, shift_part = exchange(
        jnp.concatenate(f_rows, axis=0), jnp.concatenate(g_rows, axis=0), tokens, cotangent,
        norm_gain[None, :], count, chunk_count,
    )

    def settle(grad, axis):
        half = grad.shape[axis] // 2
        mine = lax.slice_in_dim(grad, 0, half, axis=axis)
        theirs = lax.slice_in_dim(grad, half, 2 * half, axis=axis)
        stacked = jnp.concatenate(
            [
                mine.reshape(dp_size, mine.shape[0] // dp_size, mine.shape[1]),
                theirs.reshape(dp_size, theirs.shape[0] // dp_size, theirs.shape[1]),
            ],
            axis=1,
        ).astype(BF16)
        part = lax.psum_scatter(stacked, "dp", scatter_dimension=0, tiled=False)
        cut = part.shape[0] // 2
        total = part[:cut].astype(F32) + lax.ppermute(part[cut:], "tensor", across).astype(F32)
        return lax.all_gather(total.astype(BF16), "dp", axis=0, tiled=True).astype(F32)

    grad_qkv = settle(rows_product(normed, qkv_back), 1)
    grad_out = settle(rows_product(attended, own_cot), 0)
    hidden = jnp.concatenate(hidden_rows, axis=0)
    gate_back = jnp.concatenate(gate_rows, axis=0)
    up_back = jnp.concatenate(up_rows, axis=0)
    grad_gate = settle(rows_product(normed, gate_back), 1)
    grad_up = settle(rows_product(normed, up_back), 1)
    grad_down = settle(rows_product(hidden, own_cot), 0)
    bias_part = jnp.sum(qkv_back.astype(F32), axis=0)
    half = qkv_bias.shape[0]
    bias_part = bias_part[:half] + lax.ppermute(bias_part[half:], "tensor", across)
    grad_bias = lax.psum(bias_part, "dp")
    gain_part, shift_part = lax.psum((gain_part, shift_part), ("dp", "tensor"))
    return (
        layer_out,
        grad_tokens,
        gain_part,
        shift_part,
        grad_qkv,
        grad_bias,
        grad_out,
        grad_gate,
        grad_up,
        grad_down,
    )


def solution(mesh):
    placed = (
        P("dp", None),
        P("dp"),
        P(),
        P(),
        P(None, "tensor"),
        P("tensor"),
        P("tensor", None),
        P(None, "tensor"),
        P(None, "tensor"),
        P("tensor", None),
        P("dp", None),
    )
    return jax.shard_map(
        body,
        mesh=mesh,
        in_specs=placed,
        out_specs=(
            P("dp", None),
            P("dp", None),
            P(),
            P(),
            P(None, "tensor"),
            P("tensor"),
            P("tensor", None),
            P(None, "tensor"),
            P(None, "tensor"),
            P("tensor", None),
        ),
        check_vma=False,
    )
```

```python
import functools

import jax
import jax.numpy as jnp
from jax import lax
from jax.experimental import pallas as pl
from jax.experimental.pallas import tpu as pltpu
from jax.sharding import PartitionSpec as P

HEAD = 64
ROT = 16
PAIR = 2 * HEAD
TRIPLE = 6 * HEAD

EPSILON = 1e-05
NEGATIVE = -1e30
F32 = jnp.float32
BF16 = jnp.bfloat16


def rows_product(former, latter):
    return lax.dot_general(
        former, latter, (((0,), (0,)), ((), ())), preferred_element_type=F32
    )


def cols_product(former, latter):
    return lax.dot_general(
        former, latter, (((1,), (1,)), ((), ())), preferred_element_type=F32
    )


def product(former, latter):
    return jnp.dot(former, latter, preferred_element_type=F32)


def rotary_tables(seq_len):
    frequency = 10000.0 ** (-jnp.arange(0, ROT, 2).astype(F32) / ROT)
    angles = jnp.arange(seq_len).astype(F32)[:, None] * frequency[None, :]
    cosine, sine = jnp.cos(angles), jnp.sin(angles)
    still = HEAD - ROT
    cos_head = jnp.concatenate([cosine, cosine, jnp.ones((seq_len, still), F32)], axis=1)
    sin_head = jnp.concatenate([-sine, sine, jnp.zeros((seq_len, still), F32)], axis=1)
    return jnp.tile(cos_head, (1, 2)), jnp.tile(sin_head, (1, 2))


def attention_kernel(
    len_ref, qkv_ref, grad_ref, cos_ref, sin_ref, att_ref, back_ref,
    score, expo, query, key_value, query_t, grad_query, grad_kv_t,
):
    seq_len = qkv_ref.shape[0]
    block = score.shape[1]
    steps = seq_len // block
    length = len_ref[0]
    lane = lax.broadcasted_iota(jnp.int32, (block, PAIR), 1)
    left = lane < HEAD
    near = lax.rem(lane, HEAD) < ROT // 2

    def turn(tile, cosine, sine):
        swapped = jnp.where(
            near, pltpu.roll(tile, PAIR - ROT // 2, 1), pltpu.roll(tile, ROT // 2, 1)
        )
        return tile * cosine + swapped * sine

    def tables(rows):
        cosine, sine = cos_ref[rows, :], sin_ref[rows, :]
        return (
            (cosine, sine),
            (jnp.where(left, 1.0, cosine), jnp.where(left, 0.0, sine)),
            (jnp.where(left, cosine, 1.0), jnp.where(left, sine, 0.0)),
        )

    def prepare(i, carry):
        rows = pl.ds(pl.multiple_of(i * block, block), block)
        tabs = tables(rows)
        first = turn(qkv_ref[rows, 0:PAIR], *tabs[0])
        second = turn(qkv_ref[rows, PAIR : 2 * PAIR], *tabs[1])
        third = turn(qkv_ref[rows, 2 * PAIR : 3 * PAIR], *tabs[2])
        scale = HEAD**-0.5
        first_q = first.astype(BF16).astype(F32) * scale
        second_q = second.astype(BF16).astype(F32) * scale
        query[0, rows, :] = jnp.where(left, 0.0, pltpu.roll(first_q, HEAD, 1)).astype(BF16)
        query[1, rows, :] = jnp.where(left, pltpu.roll(second_q, HEAD, 1), 0.0).astype(BF16)
        key_value[0, rows, :] = jnp.where(left, second, first).astype(BF16)
        key_value[1, rows, :] = third.astype(BF16)
        query_t[0, :, rows] = first_q.T[0:HEAD, :].astype(BF16)
        query_t[1, :, rows] = second_q.T[HEAD:PAIR, :].astype(BF16)
        zero = jnp.zeros((block, PAIR), F32)
        grad_query[rows, :] = zero
        att_ref[rows, :] = zero.astype(BF16)
        for h in range(2):
            grad_kv_t[h, :, rows] = jnp.zeros((PAIR, block), F32)
        return carry

    lax.fori_loop(0, steps, prepare, 0)

    def block_rows(i, carry):
        rows = pl.ds(pl.multiple_of(i * block, block), block)
        q_block = [query[h, rows, :] for h in range(2)]

        def fold(tile, op):
            out = tile[:, 0:PAIR]
            for c in range(1, block // PAIR):
                out = op(out, tile[:, c * PAIR : (c + 1) * PAIR])
            return out

        def scores(j, tops):
            cols = pl.ds(pl.multiple_of(j * block, block), block)
            out = []
            for h in range(2):
                tile = cols_product(q_block[h], key_value[h, cols, :])
                score[h, :, cols] = tile
                out.append(jnp.maximum(tops[h], fold(tile, jnp.maximum)))
            return tuple(out)

        lowest = jnp.full((block, PAIR), NEGATIVE, F32)
        tops = lax.fori_loop(0, i, scores, (lowest, lowest))
        below = lax.broadcasted_iota(jnp.int32, (block, block), 1) <= lax.broadcasted_iota(
            jnp.int32, (block, block), 0
        )
        maxima = []
        for h in range(2):
            tile = jnp.where(below, cols_product(q_block[h], key_value[h, rows, :]), NEGATIVE)
            score[h, :, rows] = tile
            maxima.append(
                jnp.max(jnp.maximum(tops[h], fold(tile, jnp.maximum)), axis=1, keepdims=True)
            )

        def mix(j, sums):
            cols = pl.ds(pl.multiple_of(j * block, block), block)
            out = []
            for h in range(2):
                tile = jnp.exp(score[h, :, cols] - maxima[h])
                low = tile.astype(BF16)
                expo[h, :, cols] = low
                out.append(sums[2 * h] + product(low, key_value[h, cols, :]))
                out.append(sums[2 * h + 1] + fold(tile, jnp.add))
            return tuple(out)

        zero = jnp.zeros((block, PAIR), F32)
        sums = lax.fori_loop(0, i + 1, mix, (zero,) * 4)
        place = i * block + lax.broadcasted_iota(jnp.int32, (block, 1), 0)
        valid = (place < length).astype(F32)
        inverse = [1.0 / jnp.sum(sums[2 * h + 1], axis=1, keepdims=True) for h in range(2)]
        mixture = jnp.where(left, sums[0] * inverse[0], sums[2] * inverse[1]) * valid
        att_ref[rows, :] = mixture.astype(BF16)
        upstream = grad_ref[rows, :].astype(F32) * valid
        inner = upstream * mixture
        scaled, inner_sum, scaled_t = [], [], []
        for h in range(2):
            own = left if h == 0 else jnp.logical_not(left)
            inner_sum.append(
                jnp.sum(jnp.where(own, inner, 0.0), axis=1, keepdims=True) * inverse[h]
            )
            mine = jnp.where(own, upstream * inverse[h], 0.0)
            scaled.append(mine.astype(BF16))
            half = slice(0, HEAD) if h == 0 else slice(HEAD, PAIR)
            scaled_t.append(mine.T[half, :].astype(BF16))

        def grads(j, sums):
            cols = pl.ds(pl.multiple_of(j * block, block), block)
            out = []
            for h in range(2):
                low = expo[h, :, cols]
                kv = key_value[h, cols, :]
                grad_weight = cols_product(scaled[h], kv)
                grad_score = (low.astype(F32) * (grad_weight - inner_sum[h])).astype(BF16)
                out.append(sums[h] + product(grad_score, kv))
                key_part = product(query_t[h, :, rows], grad_score)
                value_part = product(scaled_t[h], low)
                key_at, value_at = (HEAD, 0) if h == 0 else (0, HEAD)
                grad_kv_t[h, key_at : key_at + HEAD, cols] += key_part
                grad_kv_t[h, value_at : value_at + HEAD, cols] += value_part
            return tuple(out)

        gq = lax.fori_loop(0, i + 1, grads, (zero, zero))
        scale = HEAD**-0.5
        grad_query[rows, :] = (
            jnp.where(left, pltpu.roll(gq[0], HEAD, 1), pltpu.roll(gq[1], HEAD, 1)) * scale
        )
        return carry

    lax.fori_loop(0, lax.div(length + block - 1, block), block_rows, 0)

    def finish(i, carry):
        rows = pl.ds(pl.multiple_of(i * block, block), block)
        tabs = tables(rows)
        gq = grad_query[rows, :]
        low_kv = grad_kv_t[0, :, rows].T
        high_kv = grad_kv_t[1, :, rows].T
        tiles = (jnp.where(left, gq, low_kv), jnp.where(left, low_kv, gq), high_kv)
        for c in range(3):
            back_ref[rows, c * PAIR : (c + 1) * PAIR] = turn(
                tiles[c], tabs[c][0], -tabs[c][1]
            ).astype(BF16)
        return carry

    lax.fori_loop(0, steps, finish, 0)


def attention(length, qkv, grad_mixture, cosine, sine):
    seq_len, width = qkv.shape
    pairs = width // TRIPLE
    block = min(512, seq_len)
    flops = 6 * 2 * (2 * pairs) * seq_len * seq_len * PAIR
    return pl.pallas_call(
        attention_kernel,
        grid=(pairs,),
        in_specs=[
            pl.BlockSpec(memory_space=pltpu.SMEM),
            pl.BlockSpec((seq_len, TRIPLE), lambda g: (0, g)),
            pl.BlockSpec((seq_len, PAIR), lambda g: (0, g)),
            pl.BlockSpec((seq_len, PAIR), lambda g: (0, 0)),
            pl.BlockSpec((seq_len, PAIR), lambda g: (0, 0)),
        ],
        out_specs=[
            pl.BlockSpec((seq_len, PAIR), lambda g: (0, g)),
            pl.BlockSpec((seq_len, TRIPLE), lambda g: (0, g)),
        ],
        out_shape=[
            jax.ShapeDtypeStruct((seq_len, pairs * PAIR), BF16),
            jax.ShapeDtypeStruct((seq_len, width), BF16),
        ],
        scratch_shapes=[
            pltpu.VMEM((2, block, seq_len), F32),
            pltpu.VMEM((2, block, seq_len), BF16),
            pltpu.VMEM((2, seq_len, PAIR), BF16),
            pltpu.VMEM((2, seq_len, PAIR), BF16),
            pltpu.VMEM((2, HEAD, seq_len), BF16),
            pltpu.VMEM((seq_len, PAIR), F32),
            pltpu.VMEM((2, PAIR, seq_len), F32),
        ],
        compiler_params=pltpu.CompilerParams(vmem_limit_bytes=48 * 2**20),
        cost_estimate=pl.CostEstimate(
            flops=flops,
            bytes_accessed=seq_len * width * 8,
            transcendentals=2 * pairs * seq_len * seq_len // 2,
        ),
        name="attention",
    )(length, qkv, grad_mixture, cosine, sine)


def norm_parts(tokens_wide):
    row_mean = jnp.mean(tokens_wide, axis=-1, keepdims=True)
    centred = tokens_wide - row_mean
    row_var = jnp.mean(centred * centred, axis=-1, keepdims=True)
    inv_scale = lax.rsqrt(row_var + EPSILON)
    return centred * inv_scale, inv_scale


def exchange_kernel(
    chunks, f_ref, g_ref, tok_ref, cot_ref, gain_ref,
    out_ref, grad_ref, part_ref,
    terms, landed, ready, tok_buf, cot_buf,
    term_sem, tok_sem, cot_sem, sum_send, sum_recv,
    line_send, line_recv, side_send, side_recv, keep_sem,
):
    count = landed.shape[3]
    share, width = landed.shape[4:]
    rows = chunks * count * share
    where = lax.axis_index("tensor")
    group = lax.axis_index("dp")
    place, side = where // 2, where % 2
    whole_refs = (out_ref, grad_ref)

    def device(index):
        return (group, index)

    above, below, across = device(where + 2), device(where - 2), device(where + 1 - 2 * side)
    has_above, has_below = place < count - 1, place > 0

    barrier = pltpu.get_barrier_semaphore()

    def greet(target):
        pl.semaphore_signal(barrier, inc=1, device_id=target, device_id_type=pl.DeviceIdType.MESH)

    pl.when(has_above)(lambda: greet(above))
    pl.when(has_below)(lambda: greet(below))
    greet(across)

    def load(c, k):
        source = (f_ref, g_ref)[k].at[pl.ds(c * (count * share), count * share), :]
        return pltpu.make_async_copy(source, terms.at[c, k], term_sem.at[c, k])

    def load_share(c, k):
        begin = pl.ds(side * rows + c * (count * share) + place * share, share)
        source, target, done = ((tok_ref, tok_buf, tok_sem), (cot_ref, cot_buf, cot_sem))[k]
        return pltpu.make_async_copy(source.at[begin, :], target.at[c], done.at[c])

    for c in range(chunks):
        load(c, 0).start()
        load(c, 1).start()
        load_share(c, 0).start()
        load_share(c, 1).start()
    pl.semaphore_wait(
        barrier, 1 + has_above.astype(jnp.int32) + has_below.astype(jnp.int32)
    )

    def remote(source, target, send, recv, device_id):
        return pltpu.make_async_remote_copy(
            src_ref=source, dst_ref=target, send_sem=send, recv_sem=recv,
            device_id=device_id, device_id_type=pl.DeviceIdType.MESH,
        )

    def block_of(b):
        return pl.ds(pl.multiple_of(b * share, share), share)

    def sum_copy(c, k, way, b, first):
        target = landed.at[c, k, way, b]
        source = terms.at[c, k, block_of(b), :] if first else target
        return remote(
            source, target, sum_send.at[c, k, way, b], sum_recv.at[c, k, way, b],
            (above, below)[way],
        )

    def place_of(c, b, on_side):
        return pl.ds(
            pl.multiple_of(on_side * rows + c * (count * share) + b * share, share), share
        )

    def line_copy(c, k, b, way, first):
        target = whole_refs[k].at[place_of(c, b, side), :]
        source = ready.at[c, k] if first else target
        return remote(
            source, target, line_send.at[c, k, way, b], line_recv.at[c, k, b],
            (above, below)[way],
        )

    def side_copy(c, k, b, first):
        target = whole_refs[k].at[place_of(c, b, side), :]
        source = ready.at[c, k] if first else target
        return remote(
            source, target, side_send.at[c, k, b], side_recv.at[c, k, b], across
        )

    def keep_copy(c, k):
        return pltpu.make_async_copy(
            ready.at[c, k], whole_refs[k].at[place_of(c, place, side), :], keep_sem.at[c, k]
        )

    def send_ends(c, k):
        load(c, k).wait()

        @pl.when(jnp.logical_not(has_below))
        def _():
            for b in range(count - 1, 0, -1):
                sum_copy(c, k, 0, b, True).start()

        @pl.when(jnp.logical_not(has_above))
        def _():
            for b in range(count - 1):
                sum_copy(c, k, 1, b, True).start()

    step = min(16, share)

    def add_on(c, k, way, b):
        def body(i, carry):
            at = pl.ds(pl.multiple_of(i * step, step), step)
            from_block = pl.ds(pl.multiple_of(b * share + i * step, step), step)
            mine = terms[c, k, from_block, :].astype(F32)
            landed[c, k, way, b, at, :] = (
                mine + landed[c, k, way, b, at, :].astype(F32)
            ).astype(BF16)
            return carry

        lax.fori_loop(0, share // step, body, 0)

    def sums(c, k, wave):
        ahead = count - 2 - wave
        for way, b, here in (
            (0, place + ahead, has_below & (place + ahead < count)),
            (1, place - ahead, has_above & (place >= ahead)),
        ):

            @pl.when(here)
            def _(way=way, b=b):
                sum_copy(c, k, way, b, False).wait_recv()
                if ahead:
                    add_on(c, k, way, b)
                    sum_copy(c, k, way, b, False).start()

    def finish(c, k):
        load_share(c, k).wait()

        def body(i, carry):
            at = pl.ds(pl.multiple_of(i * step, step), step)
            mine = pl.ds(pl.multiple_of(place * share + i * step, step), step)
            up = landed[c, k, 0, place, at, :].astype(F32)
            down = landed[c, k, 1, place, at, :].astype(F32)
            total = (
                terms[c, k, mine, :].astype(F32)
                + jnp.where(has_below, up, 0.0)
                + jnp.where(has_above, down, 0.0)
            )
            wide = tok_buf[c, at, :].astype(F32)
            if k == 0:
                ready[c, k, at, :] = (wide + total).astype(BF16)
                return carry
            scale = 1.0 / width
            centred = wide - jnp.sum(wide, axis=1, keepdims=True) * scale
            variance = jnp.sum(centred * centred, axis=1, keepdims=True) * scale
            inverse = lax.rsqrt(variance + EPSILON)
            unit = centred * inverse
            scaled = total * gain_ref[0:1, :]
            mean_scaled = jnp.sum(scaled, axis=1, keepdims=True) * scale
            mean_cross = jnp.sum(scaled * unit, axis=1, keepdims=True) * scale
            ready[c, k, at, :] = (
                cot_buf[c, at, :].astype(F32)
                + inverse * (scaled - mean_scaled - unit * mean_cross)
            ).astype(BF16)
            gain_term = total * unit
            for r in range(0, step, 8):
                part_ref[0:8, :] += gain_term[r : r + 8, :]
                part_ref[8:16, :] += total[r : r + 8, :]
            return carry

        lax.fori_loop(0, share // step, body, 0)
        pl.when(has_above)(lambda: line_copy(c, k, place, 0, True).start())
        pl.when(has_below)(lambda: line_copy(c, k, place, 1, True).start())
        side_copy(c, k, place, True).start()
        keep_copy(c, k).start()

    def pass_on(c, k, distance):
        for way, b, here in (
            (0, place - distance, place >= distance),
            (1, place + distance, place + distance < count),
        ):

            @pl.when(here)
            def _(way=way, b=b):
                line_copy(c, k, b, way, False).wait_recv()
                pl.when((has_above, has_below)[way])(
                    lambda: line_copy(c, k, b, way, False).start()
                )
                side_copy(c, k, b, False).start()

    part_ref[...] = jnp.zeros_like(part_ref)
    send_ends(0, 0)
    send_ends(0, 1)

    def chunk(c, carry):
        for k in range(2):
            for wave in range(count - 1):
                sums(c, k, wave)
                pl.when(c > 0)(lambda: pass_on(c - 1, k, wave + 1))
            finish(c, k)
            pl.when(c + 1 < chunks)(lambda: send_ends(c + 1, k))
        return carry

    lax.fori_loop(0, chunks, chunk, 0)
    for distance in range(1, count):
        pass_on(chunks - 1, 0, distance)
        pass_on(chunks - 1, 1, distance)

    def drain(c, carry):
        for k in range(2):
            keep_copy(c, k).wait()
            for b in range(count):
                pl.when(place < b)(lambda: sum_copy(c, k, 0, b, False).wait_send())
                pl.when(place > b)(lambda: sum_copy(c, k, 1, b, False).wait_send())
                pl.when((place >= b) & has_above)(
                    lambda: line_copy(c, k, b, 0, False).wait_send()
                )
                pl.when((place <= b) & has_below)(
                    lambda: line_copy(c, k, b, 1, False).wait_send()
                )
                side_copy(c, k, b, False).wait_send()
                side_copy(c, k, b, False).wait_recv()
        return carry

    lax.fori_loop(0, chunks, drain, 0)


def exchange(f_terms, g_terms, tokens, cotangent, gain, count, chunks):
    row_count, width = tokens.shape
    share = row_count // 2 // chunks // count
    sem = pltpu.SemaphoreType.DMA
    out, grad, part = pl.pallas_call(
        functools.partial(exchange_kernel, chunks),
        in_specs=[pl.BlockSpec(memory_space=pl.ANY)] * 4
        + [pl.BlockSpec(memory_space=pltpu.VMEM)],
        out_specs=[
            pl.BlockSpec(memory_space=pl.ANY),
            pl.BlockSpec(memory_space=pl.ANY),
            pl.BlockSpec(memory_space=pltpu.VMEM),
        ],
        out_shape=[
            jax.ShapeDtypeStruct(tokens.shape, BF16),
            jax.ShapeDtypeStruct(tokens.shape, BF16),
            jax.ShapeDtypeStruct((16, width), F32),
        ],
        scratch_shapes=[
            pltpu.VMEM((chunks, 2, count * share, width), BF16),
            pltpu.VMEM((chunks, 2, 2, count, share, width), BF16),
            pltpu.VMEM((chunks, 2, share, width), BF16),
            pltpu.VMEM((chunks, share, width), BF16),
            pltpu.VMEM((chunks, share, width), BF16),
            sem((chunks, 2)),
            sem((chunks,)),
            sem((chunks,)),
            sem((chunks, 2, 2, count)),
            sem((chunks, 2, 2, count)),
            sem((chunks, 2, 2, count)),
            sem((chunks, 2, count)),
            sem((chunks, 2, count)),
            sem((chunks, 2, count)),
            sem((chunks, 2)),
        ],
        compiler_params=pltpu.CompilerParams(
            collective_id=0, has_side_effects=True, vmem_limit_bytes=62 * 2**20
        ),
        cost_estimate=pl.CostEstimate(
            flops=10 * row_count * width, bytes_accessed=800 * 2**20, transcendentals=0
        ),
        name="exchange",
    )(f_terms, g_terms, tokens, cotangent, gain)
    return out, grad, part[0:8].sum(axis=0), part[8:16].sum(axis=0)


def branch_kernel(sides, widths, *refs):
    normed_ref, cot_ref = refs[:2]
    heads = refs[2 : 2 + 2 * len(widths)]
    refs = refs[2 + 2 * len(widths) :]
    weights, outs = refs[: 5 * sides], refs[5 * sides :]
    f_ref, g_ref = outs[:2]
    normed, cot = normed_ref[...], cot_ref[...]
    forward = backward = None

    def add(total, term):
        return term if total is None else total + term

    for s in range(sides):
        qkv_w, out_w, gate_w, up_w, down_w = weights[5 * s : 5 * s + 5]
        hidden_ref, gate_ref, up_ref = outs[2 + 3 * s : 5 + 3 * s]
        gate = product(normed, gate_w[...])
        up = product(normed, up_w[...])
        sig = 1.0 / (1.0 + jnp.exp(-gate))
        silu = gate * sig
        hidden = (silu * up).astype(BF16)
        grad_hidden = cols_product(cot, down_w[...])
        gate_back = (grad_hidden * up * sig * (1.0 + gate * (1.0 - sig))).astype(BF16)
        up_back = (grad_hidden * silu).astype(BF16)
        hidden_ref[...] = hidden
        gate_ref[...] = gate_back
        up_ref[...] = up_back
        forward = add(forward, product(hidden, down_w[...]))
        backward = add(backward, cols_product(gate_back, gate_w[...]))
        backward += cols_product(up_back, up_w[...])
        if len(widths) == sides:
            forward += product(heads[2 * s][...], out_w[...])
            backward += cols_product(heads[2 * s + 1][...], qkv_w[...])
        else:
            cut, wide = out_w.shape[0], qkv_w.shape[1]
            forward += product(heads[0][:, s * cut : (s + 1) * cut], out_w[...])
            backward += cols_product(heads[1][:, s * wide : (s + 1) * wide], qkv_w[...])
    f_ref[...] = forward.astype(BF16)
    g_ref[...] = backward.astype(BF16)


def branches(normed, cot, heads, weights):
    rows, width = normed.shape
    tile = min(256, rows)
    sides = len(weights)
    hidden = weights[0][3].shape[1]
    flat_heads = [array for group in heads for array in group]
    flat_weights = [array for side in weights for array in side]

    def rowed(columns):
        return pl.BlockSpec((tile, columns), lambda i: (i, 0))

    def held(array):
        return pl.BlockSpec(array.shape, lambda i: (0, 0), pipeline_mode=pl.Buffered(1))

    outs = pl.pallas_call(
        functools.partial(branch_kernel, sides, [group[0].shape[1] for group in heads]),
        grid=(rows // tile,),
        in_specs=[rowed(width), rowed(width)]
        + [rowed(array.shape[1]) for array in flat_heads]
        + [held(array) for array in flat_weights],
        out_specs=[rowed(width)] * 2 + [rowed(hidden)] * (3 * sides),
        out_shape=[jax.ShapeDtypeStruct((rows, width), BF16)] * 2
        + [jax.ShapeDtypeStruct((rows, hidden), BF16)] * (3 * sides),
        compiler_params=pltpu.CompilerParams(vmem_limit_bytes=62 * 2**20),
        cost_estimate=pl.CostEstimate(
            flops=2 * rows * sum(array.size for array in flat_weights) * 2,
            bytes_accessed=2 * rows * width * 8,
            transcendentals=rows * hidden * sides,
        ),
        name="branches",
    )(normed, cot, *flat_heads, *flat_weights)
    return outs[0], outs[1], [outs[2 + 3 * s : 5 + 3 * s] for s in range(sides)]


def body(
    tokens,
    lengths,
    norm_gain,
    norm_shift,
    qkv_weight,
    qkv_bias,
    out_weight,
    gate_weight,
    up_weight,
    down_weight,
    cotangent,
):
    tensor_size = lax.axis_size("tensor")
    dp_size = lax.axis_size("dp")
    count = tensor_size // 2
    where = lax.axis_index("tensor")
    dp_place = lax.axis_index("dp")
    side = where % 2
    across = [(i, i ^ 1) for i in range(tensor_size)]
    row_count, width = tokens.shape
    rows = row_count // 2
    chunk_count = 4

    def partner(weight):
        part = weight.shape[0] // dp_size
        mine = lax.dynamic_slice_in_dim(weight, dp_place * part, part, 0)
        return lax.all_gather(lax.ppermute(mine, "tensor", across), "dp", axis=0, tiled=True)

    own_weights = (qkv_weight, out_weight, gate_weight, up_weight, down_weight)
    weights = (own_weights, tuple(partner(weight) for weight in own_weights))
    biases = (qkv_bias, lax.ppermute(qkv_bias, "tensor", across))

    own_tokens = lax.dynamic_slice_in_dim(tokens, side * rows, rows, 0)
    own_cot = lax.dynamic_slice_in_dim(cotangent, side * rows, rows, 0)
    length = lax.dynamic_slice_in_dim(lengths, side, 1, 0)
    unit_rows, _ = norm_parts(own_tokens.astype(F32))
    normed = (unit_rows * norm_gain + norm_shift).astype(BF16)

    tables = rotary_tables(rows)
    even = (out_weight.shape[0] // HEAD) % 2 == 0
    groups = [
        (
            product(normed, weights[s][0]) + biases[s].astype(F32),
            cols_product(own_cot, weights[s][1]).astype(BF16),
        )
        for s in range(2)
    ]
    if not even:
        groups = [tuple(jnp.concatenate(pair, axis=1) for pair in zip(*groups))]
    heads = [attention(length, qkv, grad, *tables) for qkv, grad in groups]
    f_terms, g_terms, backs = branches(normed, own_cot, heads, weights)
    layer_out, grad_tokens, gain_part, shift_part = exchange(
        f_terms, g_terms, tokens, cotangent, norm_gain[None, :], count, chunk_count
    )
    if not even:
        attended, qkv_back = heads[0]
        cut, wide = out_weight.shape[0], qkv_weight.shape[1]
        heads = [
            (attended[:, s * cut : (s + 1) * cut], qkv_back[:, s * wide : (s + 1) * wide])
            for s in range(2)
        ]

    def settle(grads):
        mine, theirs = [
            grad.astype(BF16).reshape(dp_size, grad.shape[0] // dp_size, grad.shape[1])
            for grad in grads
        ]
        part = lax.psum_scatter(
            jnp.concatenate([mine, theirs], axis=1), "dp", scatter_dimension=0, tiled=False
        )
        cut = part.shape[0] // 2
        total = part[:cut].astype(F32) + lax.ppermute(part[cut:], "tensor", across).astype(F32)
        return lax.all_gather(total.astype(BF16), "dp", axis=0, tiled=True).astype(F32)

    grad_qkv = settle([rows_product(normed, heads[s][1]) for s in range(2)])
    grad_out = settle([rows_product(heads[s][0], own_cot) for s in range(2)])
    grad_gate = settle([rows_product(normed, backs[s][1]) for s in range(2)])
    grad_up = settle([rows_product(normed, backs[s][2]) for s in range(2)])
    grad_down = settle([rows_product(backs[s][0], own_cot) for s in range(2)])
    bias_mine, bias_theirs = [jnp.sum(heads[s][1].astype(F32), axis=0) for s in range(2)]
    grad_bias = lax.psum(bias_mine + lax.ppermute(bias_theirs, "tensor", across), "dp")
    gain_part, shift_part = lax.psum((gain_part, shift_part), ("dp", "tensor"))
    return (
        layer_out,
        grad_tokens,
        gain_part,
        shift_part,
        grad_qkv,
        grad_bias,
        grad_out,
        grad_gate,
        grad_up,
        grad_down,
    )


def solution(mesh):
    placed = (
        P("dp", None),
        P("dp"),
        P(),
        P(),
        P(None, "tensor"),
        P("tensor"),
        P("tensor", None),
        P(None, "tensor"),
        P(None, "tensor"),
        P("tensor", None),
        P("dp", None),
    )
    return jax.shard_map(
        body,
        mesh=mesh,
        in_specs=placed,
        out_specs=(
            P("dp", None),
            P("dp", None),
            P(),
            P(),
            P(None, "tensor"),
            P("tensor"),
            P("tensor", None),
            P(None, "tensor"),
            P(None, "tensor"),
            P("tensor", None),
        ),
        check_vma=False,
    )
```

```python
import functools

import jax
import jax.numpy as jnp
from jax import lax
from jax.experimental import pallas as pl
from jax.experimental.pallas import tpu as pltpu
from jax.sharding import PartitionSpec as P

HEAD = 64
ROT = 16
PAIR = 2 * HEAD
TRIPLE = 6 * HEAD

EPSILON = 1e-05
NEGATIVE = -1e30
F32 = jnp.float32
BF16 = jnp.bfloat16


def rows_product(former, latter):
    return lax.dot_general(
        former, latter, (((0,), (0,)), ((), ())), preferred_element_type=F32
    )


def cols_product(former, latter):
    return lax.dot_general(
        former, latter, (((1,), (1,)), ((), ())), preferred_element_type=F32
    )


def product(former, latter):
    return jnp.dot(former, latter, preferred_element_type=F32)


def rotary_tables(seq_len):
    frequency = 10000.0 ** (-jnp.arange(0, ROT, 2).astype(F32) / ROT)
    angles = jnp.arange(seq_len).astype(F32)[:, None] * frequency[None, :]
    cosine, sine = jnp.cos(angles), jnp.sin(angles)
    still = HEAD - ROT
    cos_head = jnp.concatenate([cosine, cosine, jnp.ones((seq_len, still), F32)], axis=1)
    sin_head = jnp.concatenate([-sine, sine, jnp.zeros((seq_len, still), F32)], axis=1)
    return jnp.tile(cos_head, (1, 2)), jnp.tile(sin_head, (1, 2))


def attention_kernel(
    len_ref, qkv_ref, grad_ref, cos_ref, sin_ref, att_ref, back_ref,
    score, expo, query, key_value, query_t, grad_query, grad_kv_t,
):
    seq_len = qkv_ref.shape[0]
    block = score.shape[1]
    steps = seq_len // block
    length = len_ref[0]
    lane = lax.broadcasted_iota(jnp.int32, (block, PAIR), 1)
    left = lane < HEAD
    near = lax.rem(lane, HEAD) < ROT // 2

    def turn(tile, cosine, sine):
        swapped = jnp.where(
            near, pltpu.roll(tile, PAIR - ROT // 2, 1), pltpu.roll(tile, ROT // 2, 1)
        )
        return tile * cosine + swapped * sine

    def tables(rows):
        cosine, sine = cos_ref[rows, :], sin_ref[rows, :]
        return (
            (cosine, sine),
            (jnp.where(left, 1.0, cosine), jnp.where(left, 0.0, sine)),
            (jnp.where(left, cosine, 1.0), jnp.where(left, sine, 0.0)),
        )

    def prepare(i, carry):
        rows = pl.ds(pl.multiple_of(i * block, block), block)
        tabs = tables(rows)
        first = turn(qkv_ref[rows, 0:PAIR], *tabs[0])
        second = turn(qkv_ref[rows, PAIR : 2 * PAIR], *tabs[1])
        third = turn(qkv_ref[rows, 2 * PAIR : 3 * PAIR], *tabs[2])
        scale = HEAD**-0.5
        first_q = first.astype(BF16).astype(F32) * scale
        second_q = second.astype(BF16).astype(F32) * scale
        query[0, rows, :] = jnp.where(left, 0.0, pltpu.roll(first_q, HEAD, 1)).astype(BF16)
        query[1, rows, :] = jnp.where(left, pltpu.roll(second_q, HEAD, 1), 0.0).astype(BF16)
        key_value[0, rows, :] = jnp.where(left, second, first).astype(BF16)
        key_value[1, rows, :] = third.astype(BF16)
        query_t[0, :, rows] = first_q.T[0:HEAD, :].astype(BF16)
        query_t[1, :, rows] = second_q.T[HEAD:PAIR, :].astype(BF16)
        zero = jnp.zeros((block, PAIR), F32)
        grad_query[rows, :] = zero
        att_ref[rows, :] = zero.astype(BF16)
        for h in range(2):
            grad_kv_t[h, :, rows] = jnp.zeros((PAIR, block), F32)
        return carry

    lax.fori_loop(0, steps, prepare, 0)

    def block_rows(i, carry):
        rows = pl.ds(pl.multiple_of(i * block, block), block)
        q_block = [query[h, rows, :] for h in range(2)]

        def fold(tile, op):
            out = tile[:, 0:PAIR]
            for c in range(1, block // PAIR):
                out = op(out, tile[:, c * PAIR : (c + 1) * PAIR])
            return out

        def scores(j, tops):
            cols = pl.ds(pl.multiple_of(j * block, block), block)
            out = []
            for h in range(2):
                tile = cols_product(q_block[h], key_value[h, cols, :])
                score[h, :, cols] = tile
                out.append(jnp.maximum(tops[h], fold(tile, jnp.maximum)))
            return tuple(out)

        lowest = jnp.full((block, PAIR), NEGATIVE, F32)
        tops = lax.fori_loop(0, i, scores, (lowest, lowest))
        below = lax.broadcasted_iota(jnp.int32, (block, block), 1) <= lax.broadcasted_iota(
            jnp.int32, (block, block), 0
        )
        maxima = []
        for h in range(2):
            tile = jnp.where(below, cols_product(q_block[h], key_value[h, rows, :]), NEGATIVE)
            score[h, :, rows] = tile
            maxima.append(
                jnp.max(jnp.maximum(tops[h], fold(tile, jnp.maximum)), axis=1, keepdims=True)
            )

        def mix(j, sums):
            cols = pl.ds(pl.multiple_of(j * block, block), block)
            out = []
            for h in range(2):
                tile = jnp.exp(score[h, :, cols] - maxima[h])
                low = tile.astype(BF16)
                expo[h, :, cols] = low
                out.append(sums[2 * h] + product(low, key_value[h, cols, :]))
                out.append(sums[2 * h + 1] + fold(tile, jnp.add))
            return tuple(out)

        zero = jnp.zeros((block, PAIR), F32)
        sums = lax.fori_loop(0, i + 1, mix, (zero,) * 4)
        place = i * block + lax.broadcasted_iota(jnp.int32, (block, 1), 0)
        valid = (place < length).astype(F32)
        inverse = [1.0 / jnp.sum(sums[2 * h + 1], axis=1, keepdims=True) for h in range(2)]
        mixture = jnp.where(left, sums[0] * inverse[0], sums[2] * inverse[1]) * valid
        att_ref[rows, :] = mixture.astype(BF16)
        upstream = grad_ref[rows, :].astype(F32) * valid
        inner = upstream * mixture
        scaled, inner_sum, scaled_t = [], [], []
        for h in range(2):
            own = left if h == 0 else jnp.logical_not(left)
            inner_sum.append(
                jnp.sum(jnp.where(own, inner, 0.0), axis=1, keepdims=True) * inverse[h]
            )
            mine = jnp.where(own, upstream * inverse[h], 0.0)
            scaled.append(mine.astype(BF16))
            half = slice(0, HEAD) if h == 0 else slice(HEAD, PAIR)
            scaled_t.append(mine.T[half, :].astype(BF16))

        def grads(j, sums):
            cols = pl.ds(pl.multiple_of(j * block, block), block)
            out = []
            for h in range(2):
                low = expo[h, :, cols]
                kv = key_value[h, cols, :]
                grad_weight = cols_product(scaled[h], kv)
                grad_score = (low.astype(F32) * (grad_weight - inner_sum[h])).astype(BF16)
                out.append(sums[h] + product(grad_score, kv))
                key_part = product(query_t[h, :, rows], grad_score)
                value_part = product(scaled_t[h], low)
                key_at, value_at = (HEAD, 0) if h == 0 else (0, HEAD)
                grad_kv_t[h, key_at : key_at + HEAD, cols] += key_part
                grad_kv_t[h, value_at : value_at + HEAD, cols] += value_part
            return tuple(out)

        gq = lax.fori_loop(0, i + 1, grads, (zero, zero))
        scale = HEAD**-0.5
        grad_query[rows, :] = (
            jnp.where(left, pltpu.roll(gq[0], HEAD, 1), pltpu.roll(gq[1], HEAD, 1)) * scale
        )
        return carry

    lax.fori_loop(0, lax.div(length + block - 1, block), block_rows, 0)

    def finish(i, carry):
        rows = pl.ds(pl.multiple_of(i * block, block), block)
        tabs = tables(rows)
        gq = grad_query[rows, :]
        low_kv = grad_kv_t[0, :, rows].T
        high_kv = grad_kv_t[1, :, rows].T
        tiles = (jnp.where(left, gq, low_kv), jnp.where(left, low_kv, gq), high_kv)
        for c in range(3):
            back_ref[rows, c * PAIR : (c + 1) * PAIR] = turn(
                tiles[c], tabs[c][0], -tabs[c][1]
            ).astype(BF16)
        return carry

    lax.fori_loop(0, steps, finish, 0)


def attention(length, qkv, grad_mixture, cosine, sine):
    seq_len, width = qkv.shape
    pairs = width // TRIPLE
    block = min(512, seq_len)
    flops = 6 * 2 * (2 * pairs) * seq_len * seq_len * PAIR
    return pl.pallas_call(
        attention_kernel,
        grid=(pairs,),
        in_specs=[
            pl.BlockSpec(memory_space=pltpu.SMEM),
            pl.BlockSpec((seq_len, TRIPLE), lambda g: (0, g)),
            pl.BlockSpec((seq_len, PAIR), lambda g: (0, g)),
            pl.BlockSpec((seq_len, PAIR), lambda g: (0, 0)),
            pl.BlockSpec((seq_len, PAIR), lambda g: (0, 0)),
        ],
        out_specs=[
            pl.BlockSpec((seq_len, PAIR), lambda g: (0, g)),
            pl.BlockSpec((seq_len, TRIPLE), lambda g: (0, g)),
        ],
        out_shape=[
            jax.ShapeDtypeStruct((seq_len, pairs * PAIR), BF16),
            jax.ShapeDtypeStruct((seq_len, width), BF16),
        ],
        scratch_shapes=[
            pltpu.VMEM((2, block, seq_len), F32),
            pltpu.VMEM((2, block, seq_len), BF16),
            pltpu.VMEM((2, seq_len, PAIR), BF16),
            pltpu.VMEM((2, seq_len, PAIR), BF16),
            pltpu.VMEM((2, HEAD, seq_len), BF16),
            pltpu.VMEM((seq_len, PAIR), F32),
            pltpu.VMEM((2, PAIR, seq_len), F32),
        ],
        compiler_params=pltpu.CompilerParams(vmem_limit_bytes=48 * 2**20),
        cost_estimate=pl.CostEstimate(
            flops=flops,
            bytes_accessed=seq_len * width * 8,
            transcendentals=2 * pairs * seq_len * seq_len // 2,
        ),
        name="attention",
    )(length, qkv, grad_mixture, cosine, sine)


def norm_parts(tokens_wide):
    row_mean = jnp.mean(tokens_wide, axis=-1, keepdims=True)
    centred = tokens_wide - row_mean
    row_var = jnp.mean(centred * centred, axis=-1, keepdims=True)
    inv_scale = lax.rsqrt(row_var + EPSILON)
    return centred * inv_scale, inv_scale


def exchange_kernel(
    chunks, by_rows, f_ref, g_ref, tok_ref, cot_ref, gain_ref, *refs
):
    arrays = len(by_rows)
    grad_ins = refs[: 2 * arrays]
    out_ref, grad_ref, part_ref = refs[2 * arrays : 2 * arrays + 3]
    refs = refs[2 * arrays + 3 :]
    grad_outs, core_land = refs[:arrays], refs[arrays : 3 * arrays]
    far_land, side_land = refs[3 * arrays : 5 * arrays], refs[5 * arrays : 6 * arrays]
    refs = refs[6 * arrays :]
    held, extra = refs[: 2 * arrays], refs[2 * arrays : 4 * arrays]
    (
        terms, landed, ready, tok_buf, cot_buf,
        term_sem, share_sem, sum_send, sum_recv,
        line_send, line_recv, side_send, side_recv, keep_sem,
        core_send, core_recv, far_send, far_recv, over_send, over_recv,
        back_send, back_recv, load_sem, save_sem,
    ) = refs[4 * arrays :]
    count = landed.shape[3]
    share, width = landed.shape[4:]
    rows = chunks * count * share
    where = lax.axis_index("tensor")
    group = lax.axis_index("dp")
    place, side = where // 2, where % 2
    half, core = group // 2, group % 2
    whole_refs = (out_ref, grad_ref)

    above, below = (group, where + 2), (group, where - 2)
    across = (group, where + 1 - 2 * side)
    other_core = (half * 2 + 1 - core, where)
    other_half = ((1 - half) * 2 + core, where)
    has_above, has_below = place < count - 1, place > 0

    barrier = pltpu.get_barrier_semaphore()

    def greet(target):
        pl.semaphore_signal(barrier, inc=1, device_id=target, device_id_type=pl.DeviceIdType.MESH)

    pl.when(has_above)(lambda: greet(above))
    pl.when(has_below)(lambda: greet(below))
    for target in (across, other_core, other_half):
        greet(target)

    def load(c, k):
        source = (f_ref, g_ref)[k].at[pl.ds(c * (count * share), count * share), :]
        return pltpu.make_async_copy(
            source, terms.at[lax.rem(c, 2), k], term_sem.at[lax.rem(c, 2), k]
        )

    def load_share(c, k):
        begin = pl.ds(
            pl.multiple_of(side * rows + c * (count * share) + place * share, share), share
        )
        source, target = ((tok_ref, tok_buf), (cot_ref, cot_buf))[k]
        return pltpu.make_async_copy(
            source.at[begin, :], target.at[lax.rem(c, 2)], share_sem.at[lax.rem(c, 2), k]
        )

    for k in range(2):
        load(0, k).start()
        load_share(0, k).start()
    pl.semaphore_wait(
        barrier, 3 + has_above.astype(jnp.int32) + has_below.astype(jnp.int32)
    )

    def remote(source, target, send, recv, device_id):
        return pltpu.make_async_remote_copy(
            src_ref=source, dst_ref=target, send_sem=send, recv_sem=recv,
            device_id=device_id, device_id_type=pl.DeviceIdType.MESH,
        )


    pieces = core_send.shape[2]
    each = pieces // lax.axis_size("dp")

    def piece(ref, a, j):
        size = grad_ins[2 * a].shape[0 if by_rows[a] else 1] // pieces
        at = pl.ds(pl.multiple_of(j * size, size), size)
        return ref.at[at, :] if by_rows[a] else ref.at[:, at]

    def to_core(a, s, j):
        return remote(
            piece(grad_ins[2 * a + s], a, j), piece(core_land[2 * a + s], a, j),
            core_send.at[a, s, j], core_recv.at[a, s, j], other_core,
        )

    def to_far(a, s, i, j):
        return remote(
            held[2 * a + s].at[i], piece(far_land[2 * a + s], a, j),
            far_send.at[a, s, j], far_recv.at[a, s, j], other_half,
        )

    def to_over(a, i, j):
        return remote(
            held[2 * a + 1].at[each + i], piece(side_land[a], a, j),
            over_send.at[a, j], over_recv.at[a, j], across,
        )

    def back_copy(a, i, j, way, first):
        target = piece(grad_outs[a], a, j)
        source = held[2 * a].at[each + i] if first else target
        return remote(
            source, target, back_send.at[a, way, j], back_recv.at[a, j],
            (other_core, other_half)[way],
        )

    def save_copy(a, i, j):
        return pltpu.make_async_copy(
            held[2 * a].at[each + i], piece(grad_outs[a], a, j), save_sem.at[a, i]
        )

    def their_piece(i):
        return ((1 - half) * 2 + core) * each + i

    def my_piece(i):
        return (half * 2 + core) * each + i

    def add_into(target, slot, source):
        size = target.shape[1]

        def body(i, carry):
            at = pl.ds(pl.multiple_of(i * 16, 16), 16)
            target[slot, at, :] = (
                target[slot, at, :].astype(F32) + source[at, :].astype(F32)
            ).astype(BF16)
            return carry

        lax.fori_loop(0, size // 16, body, 0)

    def gather_terms(slot, j):
        loads = []
        for a in range(arrays):
            for s in range(2):
                x = 2 * a + s
                to_core(a, s, j).wait_recv()
                loads.append(
                    pltpu.make_async_copy(
                        piece(grad_ins[x], a, j), held[x].at[slot], load_sem.at[0, x]
                    )
                )
                loads.append(
                    pltpu.make_async_copy(
                        piece(core_land[x], a, j), extra[x], load_sem.at[1, x]
                    )
                )
        for copy in loads:
            copy.start()
        for copy in loads:
            copy.wait()
        for x in range(2 * arrays):
            add_into(held[x], slot, extra[x])

    def start_grads():
        for j in range(pieces):

            @pl.when(core != (j // each) % 2)
            def _(j=j):
                for a in range(arrays):
                    for s in range(2):
                        to_core(a, s, j).start()

    def grads_far(i):
        j = their_piece(i)
        gather_terms(i, j)
        for a in range(arrays):
            for s in range(2):
                to_far(a, s, i, j).start()

    def grads_over(i):
        j = my_piece(i)
        gather_terms(each + i, j)
        loads = []
        for a in range(arrays):
            for s in range(2):
                x = 2 * a + s
                to_far(a, s, i, j).wait_recv()
                loads.append(
                    pltpu.make_async_copy(
                        piece(far_land[x], a, j), extra[x], load_sem.at[0, x]
                    )
                )
        for copy in loads:
            copy.start()
        for copy in loads:
            copy.wait()
        for a in range(arrays):
            add_into(held[2 * a + 1], each + i, extra[2 * a + 1])
            to_over(a, i, j).start()
        for a in range(arrays):
            add_into(held[2 * a], each + i, extra[2 * a])

    def grads_back(i):
        j = my_piece(i)
        loads = []
        for a in range(arrays):
            to_over(a, i, j).wait_recv()
            loads.append(
                pltpu.make_async_copy(
                    piece(side_land[a], a, j), extra[2 * a], load_sem.at[0, 2 * a]
                )
            )
        for copy in loads:
            copy.start()
        for copy in loads:
            copy.wait()
        for a in range(arrays):
            add_into(held[2 * a], each + i, extra[2 * a])
            back_copy(a, i, j, 1, True).start()
            back_copy(a, i, j, 0, True).start()
            save_copy(a, i, j).start()

    def grads_pass(i):
        j = their_piece(i)
        for a in range(arrays):
            back_copy(a, i, j, 1, False).wait_recv()
            back_copy(a, i, j, 0, False).start()

    def grads_drain():
        for i in range(each):
            mine, theirs = my_piece(i), their_piece(i)
            for a in range(arrays):
                for s in range(2):
                    to_far(a, s, i, theirs).wait_send()
                to_over(a, i, mine).wait_send()
                back_copy(a, i, mine, 1, True).wait_send()
                back_copy(a, i, mine, 0, True).wait_send()
                back_copy(a, i, theirs, 0, False).wait_send()
                save_copy(a, i, mine).wait()
        for j in range(pieces):

            @pl.when(core != (j // each) % 2)
            def _(j=j):
                for a in range(arrays):
                    for s in range(2):
                        to_core(a, s, j).wait_send()
                    back_copy(a, 0, j, 0, False).wait_recv()


    def block_of(b):
        return pl.ds(pl.multiple_of(b * share, share), share)

    def sum_copy(c, k, way, b, first):
        slot = lax.rem(c, 2)
        target = landed.at[slot, k, way, b]
        source = terms.at[slot, k, block_of(b), :] if first else target
        return remote(
            source, target, sum_send.at[slot, k, way, b], sum_recv.at[slot, k, way, b],
            (above, below)[way],
        )

    def place_of(c, b, on_side):
        return pl.ds(
            pl.multiple_of(on_side * rows + c * (count * share) + b * share, share), share
        )

    def line_copy(c, k, b, way, first):
        target = whole_refs[k].at[place_of(c, b, side), :]
        source = ready.at[lax.rem(c, 2), k] if first else target
        return remote(
            source, target, line_send.at[c, k, way, b], line_recv.at[c, k, b],
            (above, below)[way],
        )

    def side_copy(c, k, b, first):
        target = whole_refs[k].at[place_of(c, b, side), :]
        source = ready.at[lax.rem(c, 2), k] if first else target
        return remote(
            source, target, side_send.at[c, k, b], side_recv.at[c, k, b], across
        )

    def keep_copy(c, k):
        return pltpu.make_async_copy(
            ready.at[lax.rem(c, 2), k], whole_refs[k].at[place_of(c, place, side), :],
            keep_sem.at[c, k],
        )

    def each_first(c, k, act):
        @pl.when(jnp.logical_not(has_below))
        def _():
            for b in range(count - 1, 0, -1):
                act(sum_copy(c, k, 0, b, True))

        @pl.when(jnp.logical_not(has_above))
        def _():
            for b in range(count - 1):
                act(sum_copy(c, k, 1, b, True))

    def send_ends(c, k):
        load(c, k).wait()
        each_first(c, k, lambda copy: copy.start())

    def sums_left(c, k):
        for b in range(count):

            @pl.when(has_below & (place < b))
            def _(b=b):
                sum_copy(c, k, 0, b, False).wait_send()

            @pl.when(has_above & (place > b))
            def _(b=b):
                sum_copy(c, k, 1, b, False).wait_send()

    step = min(16, share)

    def add_on(c, k, way, b):
        slot = lax.rem(c, 2)

        def body(i, carry):
            at = pl.ds(pl.multiple_of(i * step, step), step)
            from_block = pl.ds(pl.multiple_of(b * share + i * step, step), step)
            mine = terms[slot, k, from_block, :].astype(F32)
            landed[slot, k, way, b, at, :] = (
                mine + landed[slot, k, way, b, at, :].astype(F32)
            ).astype(BF16)
            return carry

        lax.fori_loop(0, share // step, body, 0)

    def sums(c, k, wave):
        ahead = count - 2 - wave
        for way, b, here in (
            (0, place + ahead, has_below & (place + ahead < count)),
            (1, place - ahead, has_above & (place >= ahead)),
        ):

            @pl.when(here)
            def _(way=way, b=b):
                sum_copy(c, k, way, b, False).wait_recv()
                if ahead:
                    add_on(c, k, way, b)
                    sum_copy(c, k, way, b, False).start()

    def own_left(c, k):
        pl.when(has_above)(lambda: line_copy(c, k, place, 0, True).wait_send())
        pl.when(has_below)(lambda: line_copy(c, k, place, 1, True).wait_send())
        side_copy(c, k, place, True).wait_send()
        keep_copy(c, k).wait()

    def finish(c, k):
        load_share(c, k).wait()
        pl.when(c > 1)(lambda: own_left(c - 2, k))
        slot = lax.rem(c, 2)

        def body(i, carry):
            at = pl.ds(pl.multiple_of(i * step, step), step)
            mine = pl.ds(pl.multiple_of(place * share + i * step, step), step)
            up = landed[slot, k, 0, place, at, :].astype(F32)
            down = landed[slot, k, 1, place, at, :].astype(F32)
            total = (
                terms[slot, k, mine, :].astype(F32)
                + jnp.where(has_below, up, 0.0)
                + jnp.where(has_above, down, 0.0)
            )
            wide = tok_buf[slot, at, :].astype(F32)
            if k == 0:
                ready[slot, k, at, :] = (wide + total).astype(BF16)
                return carry
            scale = 1.0 / width
            centred = wide - jnp.sum(wide, axis=1, keepdims=True) * scale
            variance = jnp.sum(centred * centred, axis=1, keepdims=True) * scale
            inverse = lax.rsqrt(variance + EPSILON)
            unit = centred * inverse
            scaled = total * gain_ref[0:1, :]
            mean_scaled = jnp.sum(scaled, axis=1, keepdims=True) * scale
            mean_cross = jnp.sum(scaled * unit, axis=1, keepdims=True) * scale
            ready[slot, k, at, :] = (
                cot_buf[slot, at, :].astype(F32)
                + inverse * (scaled - mean_scaled - unit * mean_cross)
            ).astype(BF16)
            gain_term = total * unit
            for r in range(0, step, 8):
                part_ref[0:8, :] += gain_term[r : r + 8, :]
                part_ref[8:16, :] += total[r : r + 8, :]
            return carry

        lax.fori_loop(0, share // step, body, 0)
        pl.when(has_above)(lambda: line_copy(c, k, place, 0, True).start())
        pl.when(has_below)(lambda: line_copy(c, k, place, 1, True).start())
        side_copy(c, k, place, True).start()
        keep_copy(c, k).start()

    def pass_on(c, k, distance):
        for way, b, here in (
            (0, place - distance, place >= distance),
            (1, place + distance, place + distance < count),
        ):

            @pl.when(here)
            def _(way=way, b=b):
                line_copy(c, k, b, way, False).wait_recv()
                pl.when((has_above, has_below)[way])(
                    lambda: line_copy(c, k, b, way, False).start()
                )
                side_copy(c, k, b, False).start()

    part_ref[...] = jnp.zeros_like(part_ref)
    send_ends(0, 0)
    send_ends(0, 1)
    start_grads()

    def at_chunk(c, when, act, *args):
        pl.when(c == when)(lambda: act(*args))

    def chunk(c, carry):
        last = c + 1 == chunks

        for k in range(2):

            @pl.when(c > 0)
            def _(k=k):
                sums_left(c - 1, k)
                each_first(c - 1, k, lambda copy: copy.wait_send())

            @pl.when(jnp.logical_not(last))
            def _(k=k):
                load(c + 1, k).start()
                load_share(c + 1, k).start()

            for wave in range(count - 1):
                sums(c, k, wave)
                pl.when(c > 0)(lambda: pass_on(c - 1, k, wave + 1))
            finish(c, k)
            pl.when(jnp.logical_not(last))(lambda: send_ends(c + 1, k))
            if k == 0:
                at_chunk(c, 0, grads_far, 0)
                at_chunk(c, 2, grads_over, 0)
                at_chunk(c, 4, grads_back, 0)
                at_chunk(c, 5, grads_pass, 0)
            else:
                at_chunk(c, 0, grads_far, 1)
                at_chunk(c, 3, grads_over, 1)
                at_chunk(c, 4, grads_back, 1)
                at_chunk(c, 6, grads_pass, 1)
        return carry

    lax.fori_loop(0, chunks, chunk, 0)
    for distance in range(1, count):
        pass_on(chunks - 1, 0, distance)
        pass_on(chunks - 1, 1, distance)
    for k in range(2):
        sums_left(chunks - 1, k)
        each_first(chunks - 1, k, lambda copy: copy.wait_send())
        own_left(chunks - 2, k)
        own_left(chunks - 1, k)
    grads_drain()

    def drain(c, carry):
        for k in range(2):
            for b in range(count):
                pl.when((place > b) & has_above)(
                    lambda: line_copy(c, k, b, 0, False).wait_send()
                )
                pl.when((place < b) & has_below)(
                    lambda: line_copy(c, k, b, 1, False).wait_send()
                )
                pl.when(place != b)(lambda: side_copy(c, k, b, False).wait_send())
                side_copy(c, k, b, False).wait_recv()
        return carry

    lax.fori_loop(0, chunks, drain, 0)


def exchange(f_terms, g_terms, tokens, cotangent, gain, grads, by_rows, count, chunks, dp_size):
    row_count, width = tokens.shape
    share = row_count // 2 // chunks // count
    arrays = len(grads)
    pieces = 2 * dp_size
    each = pieces // dp_size
    sem = pltpu.SemaphoreType.DMA
    flat = [array for pair in grads for array in pair]
    shapes = [
        (array.shape[0] // pieces, array.shape[1])
        if by_rows[x // 2]
        else (array.shape[0], array.shape[1] // pieces)
        for x, array in enumerate(flat)
    ]
    held = [pltpu.VMEM((2 * each,) + shape, BF16) for shape in shapes]
    extra = [pltpu.VMEM(shape, BF16) for shape in shapes]
    whole = jax.ShapeDtypeStruct(tokens.shape, BF16)
    lands = [jax.ShapeDtypeStruct(array.shape, BF16) for array in flat]
    finals = [jax.ShapeDtypeStruct(pair[0].shape, BF16) for pair in grads]
    anywhere = pl.BlockSpec(memory_space=pl.ANY)
    vmem = pl.BlockSpec(memory_space=pltpu.VMEM)
    outs = pl.pallas_call(
        functools.partial(exchange_kernel, chunks, by_rows),
        in_specs=[anywhere] * 4 + [vmem] + [anywhere] * (2 * arrays),
        out_specs=[anywhere, anywhere, vmem] + [anywhere] * (6 * arrays),
        out_shape=[whole, whole, jax.ShapeDtypeStruct((16, width), F32)]
        + finals + lands + lands + finals,
        scratch_shapes=held + extra + [
            pltpu.VMEM((2, 2, count * share, width), BF16),
            pltpu.VMEM((2, 2, 2, count, share, width), BF16),
            pltpu.VMEM((2, 2, share, width), BF16),
            pltpu.VMEM((2, share, width), BF16),
            pltpu.VMEM((2, share, width), BF16),
            sem((2, 2)),
            sem((2, 2)),
            sem((2, 2, 2, count)),
            sem((2, 2, 2, count)),
            sem((chunks, 2, 2, count)),
            sem((chunks, 2, count)),
            sem((chunks, 2, count)),
            sem((chunks, 2, count)),
            sem((chunks, 2)),
            sem((arrays, 2, pieces)),
            sem((arrays, 2, pieces)),
            sem((arrays, 2, pieces)),
            sem((arrays, 2, pieces)),
            sem((arrays, pieces)),
            sem((arrays, pieces)),
            sem((arrays, 2, pieces)),
            sem((arrays, pieces)),
            sem((2, 2 * arrays)),
            sem((arrays, each)),
        ],
        compiler_params=pltpu.CompilerParams(
            collective_id=0, has_side_effects=True, vmem_limit_bytes=60 * 2**20
        ),
        cost_estimate=pl.CostEstimate(
            flops=10 * row_count * width, bytes_accessed=800 * 2**20, transcendentals=0
        ),
        name="exchange",
    )(f_terms, g_terms, tokens, cotangent, gain, *flat)
    out, grad, part = outs[:3]
    return (
        out, grad, part[0:8].sum(axis=0), part[8:16].sum(axis=0),
        [array.astype(F32) for array in outs[3 : 3 + arrays]],
    )


def branch_kernel(sides, widths, *refs):
    normed_ref, cot_ref = refs[:2]
    heads = refs[2 : 2 + 2 * len(widths)]
    refs = refs[2 + 2 * len(widths) :]
    weights, outs = refs[: 5 * sides], refs[5 * sides :]
    f_ref, g_ref = outs[:2]
    normed, cot = normed_ref[...], cot_ref[...]
    forward = backward = None

    def add(total, term):
        return term if total is None else total + term

    for s in range(sides):
        qkv_w, out_w, gate_w, up_w, down_w = weights[5 * s : 5 * s + 5]
        hidden_ref, gate_ref, up_ref = outs[2 + 3 * s : 5 + 3 * s]
        gate = product(normed, gate_w[...])
        up = product(normed, up_w[...])
        sig = 1.0 / (1.0 + jnp.exp(-gate))
        silu = gate * sig
        hidden = (silu * up).astype(BF16)
        grad_hidden = cols_product(cot, down_w[...])
        gate_back = (grad_hidden * up * sig * (1.0 + gate * (1.0 - sig))).astype(BF16)
        up_back = (grad_hidden * silu).astype(BF16)
        hidden_ref[...] = hidden
        gate_ref[...] = gate_back
        up_ref[...] = up_back
        forward = add(forward, product(hidden, down_w[...]))
        backward = add(backward, cols_product(gate_back, gate_w[...]))
        backward += cols_product(up_back, up_w[...])
        if len(widths) == sides:
            forward += product(heads[2 * s][...], out_w[...])
            backward += cols_product(heads[2 * s + 1][...], qkv_w[...])
        else:
            cut, wide = out_w.shape[0], qkv_w.shape[1]
            forward += product(heads[0][:, s * cut : (s + 1) * cut], out_w[...])
            backward += cols_product(heads[1][:, s * wide : (s + 1) * wide], qkv_w[...])
    f_ref[...] = forward.astype(BF16)
    g_ref[...] = backward.astype(BF16)


def branches(normed, cot, heads, weights):
    rows, width = normed.shape
    tile = min(256, rows)
    sides = len(weights)
    hidden = weights[0][3].shape[1]
    flat_heads = [array for group in heads for array in group]
    flat_weights = [array for side in weights for array in side]

    def rowed(columns):
        return pl.BlockSpec((tile, columns), lambda i: (i, 0))

    def held(array):
        return pl.BlockSpec(array.shape, lambda i: (0, 0), pipeline_mode=pl.Buffered(1))

    outs = pl.pallas_call(
        functools.partial(branch_kernel, sides, [group[0].shape[1] for group in heads]),
        grid=(rows // tile,),
        in_specs=[rowed(width), rowed(width)]
        + [rowed(array.shape[1]) for array in flat_heads]
        + [held(array) for array in flat_weights],
        out_specs=[rowed(width)] * 2 + [rowed(hidden)] * (3 * sides),
        out_shape=[jax.ShapeDtypeStruct((rows, width), BF16)] * 2
        + [jax.ShapeDtypeStruct((rows, hidden), BF16)] * (3 * sides),
        compiler_params=pltpu.CompilerParams(vmem_limit_bytes=62 * 2**20),
        cost_estimate=pl.CostEstimate(
            flops=2 * rows * sum(array.size for array in flat_weights) * 2,
            bytes_accessed=2 * rows * width * 8,
            transcendentals=rows * hidden * sides,
        ),
        name="branches",
    )(normed, cot, *flat_heads, *flat_weights)
    return outs[0], outs[1], [outs[2 + 3 * s : 5 + 3 * s] for s in range(sides)]


def body(
    tokens,
    lengths,
    norm_gain,
    norm_shift,
    qkv_weight,
    qkv_bias,
    out_weight,
    gate_weight,
    up_weight,
    down_weight,
    cotangent,
):
    tensor_size = lax.axis_size("tensor")
    dp_size = lax.axis_size("dp")
    count = tensor_size // 2
    where = lax.axis_index("tensor")
    dp_place = lax.axis_index("dp")
    side = where % 2
    across = [(i, i ^ 1) for i in range(tensor_size)]
    row_count, width = tokens.shape
    rows = row_count // 2
    chunk_count = 8

    def partner(weight):
        part = weight.shape[0] // dp_size
        mine = lax.dynamic_slice_in_dim(weight, dp_place * part, part, 0)
        return lax.all_gather(lax.ppermute(mine, "tensor", across), "dp", axis=0, tiled=True)

    own_weights = (qkv_weight, out_weight, gate_weight, up_weight, down_weight)
    weights = (own_weights, tuple(partner(weight) for weight in own_weights))
    biases = (qkv_bias, lax.ppermute(qkv_bias, "tensor", across))

    own_tokens = lax.dynamic_slice_in_dim(tokens, side * rows, rows, 0)
    own_cot = lax.dynamic_slice_in_dim(cotangent, side * rows, rows, 0)
    length = lax.dynamic_slice_in_dim(lengths, side, 1, 0)
    unit_rows, _ = norm_parts(own_tokens.astype(F32))
    normed = (unit_rows * norm_gain + norm_shift).astype(BF16)

    tables = rotary_tables(rows)
    even = (out_weight.shape[0] // HEAD) % 2 == 0
    groups = [
        (
            product(normed, weights[s][0]) + biases[s].astype(F32),
            cols_product(own_cot, weights[s][1]).astype(BF16),
        )
        for s in range(2)
    ]
    if not even:
        groups = [tuple(jnp.concatenate(pair, axis=1) for pair in zip(*groups))]
    heads = [attention(length, qkv, grad, *tables) for qkv, grad in groups]
    f_terms, g_terms, backs = branches(normed, own_cot, heads, weights)
    if not even:
        attended, qkv_back = heads[0]
        cut, wide = out_weight.shape[0], qkv_weight.shape[1]
        heads = [
            (attended[:, s * cut : (s + 1) * cut], qkv_back[:, s * wide : (s + 1) * wide])
            for s in range(2)
        ]

    both = range(2)
    grads = [
        [rows_product(normed, heads[s][1]).astype(BF16) for s in both],
        [rows_product(normed, backs[s][1]).astype(BF16) for s in both],
        [rows_product(normed, backs[s][2]).astype(BF16) for s in both],
        [rows_product(backs[s][0], own_cot).astype(BF16) for s in both],
        [rows_product(heads[s][0], own_cot).astype(BF16) for s in both],
    ]
    layer_out, grad_tokens, gain_part, shift_part, grads = exchange(
        f_terms, g_terms, tokens, cotangent, norm_gain[None, :], grads,
        (True, True, True, False, False), count, chunk_count, dp_size,
    )
    grad_qkv, grad_gate, grad_up, grad_down, grad_out = grads
    bias_mine, bias_theirs = [jnp.sum(heads[s][1].astype(F32), axis=0) for s in range(2)]
    grad_bias = lax.psum(bias_mine + lax.ppermute(bias_theirs, "tensor", across), "dp")
    gain_part, shift_part = lax.psum((gain_part, shift_part), ("dp", "tensor"))
    return (
        layer_out,
        grad_tokens,
        gain_part,
        shift_part,
        grad_qkv,
        grad_bias,
        grad_out,
        grad_gate,
        grad_up,
        grad_down,
    )


def solution(mesh):
    placed = (
        P("dp", None),
        P("dp"),
        P(),
        P(),
        P(None, "tensor"),
        P("tensor"),
        P("tensor", None),
        P(None, "tensor"),
        P(None, "tensor"),
        P("tensor", None),
        P("dp", None),
    )
    return jax.shard_map(
        body,
        mesh=mesh,
        in_specs=placed,
        out_specs=(
            P("dp", None),
            P("dp", None),
            P(),
            P(),
            P(None, "tensor"),
            P("tensor"),
            P("tensor", None),
            P(None, "tensor"),
            P(None, "tensor"),
            P("tensor", None),
        ),
        check_vma=False,
    )
```

```python
import functools

import jax
import jax.numpy as jnp
from jax import lax
from jax.experimental import pallas as pl
from jax.experimental.pallas import tpu as pltpu
from jax.sharding import PartitionSpec as P

HEAD = 64
ROT = 16
PAIR = 2 * HEAD
TRIPLE = 6 * HEAD

EPSILON = 1e-05
NEGATIVE = -1e30
F32 = jnp.float32
BF16 = jnp.bfloat16


def rows_product(former, latter):
    return lax.dot_general(
        former, latter, (((0,), (0,)), ((), ())), preferred_element_type=F32
    )


def cols_product(former, latter):
    return lax.dot_general(
        former, latter, (((1,), (1,)), ((), ())), preferred_element_type=F32
    )


def product(former, latter):
    return jnp.dot(former, latter, preferred_element_type=F32)


def rotary_tables(seq_len):
    frequency = 10000.0 ** (-jnp.arange(0, ROT, 2).astype(F32) / ROT)
    angles = jnp.arange(seq_len).astype(F32)[:, None] * frequency[None, :]
    cosine, sine = jnp.cos(angles), jnp.sin(angles)
    still = HEAD - ROT
    cos_head = jnp.concatenate([cosine, cosine, jnp.ones((seq_len, still), F32)], axis=1)
    sin_head = jnp.concatenate([-sine, sine, jnp.zeros((seq_len, still), F32)], axis=1)
    return jnp.tile(cos_head, (1, 2)), jnp.tile(sin_head, (1, 2))


def attention_kernel(
    len_ref, qkv_ref, grad_ref, cos_ref, sin_ref, att_ref, back_ref,
    score, expo, query, key_value, query_t, grad_query, grad_kv_t,
):
    seq_len = qkv_ref.shape[0]
    block = score.shape[1]
    steps = seq_len // block
    length = len_ref[0]
    lane = lax.broadcasted_iota(jnp.int32, (block, PAIR), 1)
    left = lane < HEAD
    near = lax.rem(lane, HEAD) < ROT // 2

    def turn(tile, cosine, sine):
        swapped = jnp.where(
            near, pltpu.roll(tile, PAIR - ROT // 2, 1), pltpu.roll(tile, ROT // 2, 1)
        )
        return tile * cosine + swapped * sine

    def tables(rows):
        cosine, sine = cos_ref[rows, :], sin_ref[rows, :]
        return (
            (cosine, sine),
            (jnp.where(left, 1.0, cosine), jnp.where(left, 0.0, sine)),
            (jnp.where(left, cosine, 1.0), jnp.where(left, sine, 0.0)),
        )

    def prepare(i, carry):
        rows = pl.ds(pl.multiple_of(i * block, block), block)
        tabs = tables(rows)
        first = turn(qkv_ref[rows, 0:PAIR], *tabs[0])
        second = turn(qkv_ref[rows, PAIR : 2 * PAIR], *tabs[1])
        third = turn(qkv_ref[rows, 2 * PAIR : 3 * PAIR], *tabs[2])
        scale = HEAD**-0.5
        first_q = first.astype(BF16).astype(F32) * scale
        second_q = second.astype(BF16).astype(F32) * scale
        query[0, rows, :] = jnp.where(left, 0.0, pltpu.roll(first_q, HEAD, 1)).astype(BF16)
        query[1, rows, :] = jnp.where(left, pltpu.roll(second_q, HEAD, 1), 0.0).astype(BF16)
        key_value[0, rows, :] = jnp.where(left, second, first).astype(BF16)
        key_value[1, rows, :] = third.astype(BF16)
        query_t[0, :, rows] = first_q.T[0:HEAD, :].astype(BF16)
        query_t[1, :, rows] = second_q.T[HEAD:PAIR, :].astype(BF16)
        zero = jnp.zeros((block, PAIR), F32)
        grad_query[rows, :] = zero
        att_ref[rows, :] = zero.astype(BF16)
        for h in range(2):
            grad_kv_t[h, :, rows] = jnp.zeros((PAIR, block), F32)
        return carry

    lax.fori_loop(0, steps, prepare, 0)

    def block_rows(i, carry):
        rows = pl.ds(pl.multiple_of(i * block, block), block)
        q_block = [query[h, rows, :] for h in range(2)]

        def fold(tile, op):
            out = tile[:, 0:PAIR]
            for c in range(1, block // PAIR):
                out = op(out, tile[:, c * PAIR : (c + 1) * PAIR])
            return out

        def scores(j, tops):
            cols = pl.ds(pl.multiple_of(j * block, block), block)
            out = []
            for h in range(2):
                tile = cols_product(q_block[h], key_value[h, cols, :])
                score[h, :, cols] = tile
                out.append(jnp.maximum(tops[h], fold(tile, jnp.maximum)))
            return tuple(out)

        lowest = jnp.full((block, PAIR), NEGATIVE, F32)
        tops = lax.fori_loop(0, i, scores, (lowest, lowest))
        below = lax.broadcasted_iota(jnp.int32, (block, block), 1) <= lax.broadcasted_iota(
            jnp.int32, (block, block), 0
        )
        maxima = []
        for h in range(2):
            tile = jnp.where(below, cols_product(q_block[h], key_value[h, rows, :]), NEGATIVE)
            score[h, :, rows] = tile
            maxima.append(
                jnp.max(jnp.maximum(tops[h], fold(tile, jnp.maximum)), axis=1, keepdims=True)
            )

        def mix(j, sums):
            cols = pl.ds(pl.multiple_of(j * block, block), block)
            out = []
            for h in range(2):
                tile = jnp.exp(score[h, :, cols] - maxima[h])
                low = tile.astype(BF16)
                expo[h, :, cols] = low
                out.append(sums[2 * h] + product(low, key_value[h, cols, :]))
                out.append(sums[2 * h + 1] + fold(tile, jnp.add))
            return tuple(out)

        zero = jnp.zeros((block, PAIR), F32)
        sums = lax.fori_loop(0, i + 1, mix, (zero,) * 4)
        place = i * block + lax.broadcasted_iota(jnp.int32, (block, 1), 0)
        valid = (place < length).astype(F32)
        inverse = [1.0 / jnp.sum(sums[2 * h + 1], axis=1, keepdims=True) for h in range(2)]
        mixture = jnp.where(left, sums[0] * inverse[0], sums[2] * inverse[1]) * valid
        att_ref[rows, :] = mixture.astype(BF16)
        upstream = grad_ref[rows, :].astype(F32) * valid
        inner = upstream * mixture
        scaled, inner_sum, scaled_t = [], [], []
        for h in range(2):
            own = left if h == 0 else jnp.logical_not(left)
            inner_sum.append(
                jnp.sum(jnp.where(own, inner, 0.0), axis=1, keepdims=True) * inverse[h]
            )
            mine = jnp.where(own, upstream * inverse[h], 0.0)
            scaled.append(mine.astype(BF16))
            half = slice(0, HEAD) if h == 0 else slice(HEAD, PAIR)
            scaled_t.append(mine.T[half, :].astype(BF16))

        def grads(j, sums):
            cols = pl.ds(pl.multiple_of(j * block, block), block)
            out = []
            for h in range(2):
                low = expo[h, :, cols]
                kv = key_value[h, cols, :]
                grad_weight = cols_product(scaled[h], kv)
                grad_score = (low.astype(F32) * (grad_weight - inner_sum[h])).astype(BF16)
                out.append(sums[h] + product(grad_score, kv))
                key_part = product(query_t[h, :, rows], grad_score)
                value_part = product(scaled_t[h], low)
                key_at, value_at = (HEAD, 0) if h == 0 else (0, HEAD)
                grad_kv_t[h, key_at : key_at + HEAD, cols] += key_part
                grad_kv_t[h, value_at : value_at + HEAD, cols] += value_part
            return tuple(out)

        gq = lax.fori_loop(0, i + 1, grads, (zero, zero))
        scale = HEAD**-0.5
        grad_query[rows, :] = (
            jnp.where(left, pltpu.roll(gq[0], HEAD, 1), pltpu.roll(gq[1], HEAD, 1)) * scale
        )
        return carry

    lax.fori_loop(0, lax.div(length + block - 1, block), block_rows, 0)

    def finish(i, carry):
        rows = pl.ds(pl.multiple_of(i * block, block), block)
        tabs = tables(rows)
        gq = grad_query[rows, :]
        low_kv = grad_kv_t[0, :, rows].T
        high_kv = grad_kv_t[1, :, rows].T
        tiles = (jnp.where(left, gq, low_kv), jnp.where(left, low_kv, gq), high_kv)
        for c in range(3):
            back_ref[rows, c * PAIR : (c + 1) * PAIR] = turn(
                tiles[c], tabs[c][0], -tabs[c][1]
            ).astype(BF16)
        return carry

    lax.fori_loop(0, steps, finish, 0)


def attention(length, qkv, grad_mixture, cosine, sine):
    seq_len, width = qkv.shape
    pairs = width // TRIPLE
    block = min(512, seq_len)
    flops = 6 * 2 * (2 * pairs) * seq_len * seq_len * PAIR
    return pl.pallas_call(
        attention_kernel,
        grid=(pairs,),
        in_specs=[
            pl.BlockSpec(memory_space=pltpu.SMEM),
            pl.BlockSpec((seq_len, TRIPLE), lambda g: (0, g)),
            pl.BlockSpec((seq_len, PAIR), lambda g: (0, g)),
            pl.BlockSpec((seq_len, PAIR), lambda g: (0, 0)),
            pl.BlockSpec((seq_len, PAIR), lambda g: (0, 0)),
        ],
        out_specs=[
            pl.BlockSpec((seq_len, PAIR), lambda g: (0, g)),
            pl.BlockSpec((seq_len, TRIPLE), lambda g: (0, g)),
        ],
        out_shape=[
            jax.ShapeDtypeStruct((seq_len, pairs * PAIR), BF16),
            jax.ShapeDtypeStruct((seq_len, width), BF16),
        ],
        scratch_shapes=[
            pltpu.VMEM((2, block, seq_len), F32),
            pltpu.VMEM((2, block, seq_len), BF16),
            pltpu.VMEM((2, seq_len, PAIR), BF16),
            pltpu.VMEM((2, seq_len, PAIR), BF16),
            pltpu.VMEM((2, HEAD, seq_len), BF16),
            pltpu.VMEM((seq_len, PAIR), F32),
            pltpu.VMEM((2, PAIR, seq_len), F32),
        ],
        compiler_params=pltpu.CompilerParams(vmem_limit_bytes=48 * 2**20),
        cost_estimate=pl.CostEstimate(
            flops=flops,
            bytes_accessed=seq_len * width * 8,
            transcendentals=2 * pairs * seq_len * seq_len // 2,
        ),
        name="attention",
    )(length, qkv, grad_mixture, cosine, sine)


def norm_parts(tokens_wide):
    row_mean = jnp.mean(tokens_wide, axis=-1, keepdims=True)
    centred = tokens_wide - row_mean
    row_var = jnp.mean(centred * centred, axis=-1, keepdims=True)
    inv_scale = lax.rsqrt(row_var + EPSILON)
    return centred * inv_scale, inv_scale


def layer_kernel(chunks, sides, *refs):
    normed_ref, tok_ref, cot_ref = refs[:3]
    head_refs, refs = refs[3 : 3 + 2 * sides], refs[3 + 2 * sides :]
    weight_refs, gain_ref = refs[: 5 * sides], refs[5 * sides]
    refs = refs[5 * sides + 1 :]
    out_ref, grad_ref, part_ref = refs[:3]
    refs = refs[3:]
    arrays = 5
    grad_outs, core_land = refs[:arrays], refs[arrays : 3 * arrays]
    far_land, side_land = refs[3 * arrays : 5 * arrays], refs[5 * arrays : 6 * arrays]
    refs = refs[6 * arrays :]
    f_ref, g_ref = refs[:2]
    mid_refs, refs = refs[2 : 2 + 3 * sides], refs[2 + 3 * sides :]
    (
        terms, landed, ready, tok_buf, cot_buf,
        term_sem, share_sem, sum_send, sum_recv,
        line_send, line_recv, side_send, side_recv, keep_sem,
        core_send, core_recv, far_send, far_recv, over_send, over_recv,
        back_send, back_recv, load_sem, save_sem,
    ) = refs
    share, width = landed.shape[4:]
    count = landed.shape[3] + 1
    chunk_rows = count * share
    rows = chunks * chunk_rows
    where = lax.axis_index("tensor")
    group = lax.axis_index("dp")
    place, side = where // 2, where % 2
    half, core = group // 2, group % 2
    whole_refs = (out_ref, grad_ref)
    factors = []
    for s in range(sides):
        hidden_ref, gate_ref, up_ref = mid_refs[3 * s : 3 * s + 3]
        factors.append(
            (head_refs[2 * s + 1], gate_ref, up_ref, hidden_ref, head_refs[2 * s])
        )
    factors = [factors[x % sides][x // sides] for x in range(arrays * sides)]

    above, below = (group, where + 2), (group, where - 2)
    across = (group, where + 1 - 2 * side)
    other_core = (half * 2 + 1 - core, where)
    other_half = ((1 - half) * 2 + core, where)
    has_above, has_below = place < count - 1, place > 0

    barrier = pltpu.get_barrier_semaphore()

    def greet(target):
        pl.semaphore_signal(barrier, inc=1, device_id=target, device_id_type=pl.DeviceIdType.MESH)

    pl.when(has_above)(lambda: greet(above))
    pl.when(has_below)(lambda: greet(below))
    for target in (across, other_core, other_half):
        greet(target)

    def span(begin, size):
        return pl.ds(pl.multiple_of(begin, size), size)

    def load(c, k):
        source = (f_ref, g_ref)[k].at[span(c * chunk_rows, chunk_rows), :]
        return pltpu.make_async_copy(
            source, terms.at[lax.rem(c, 2), k], term_sem.at[lax.rem(c, 2), k]
        )

    def load_share(c, k):
        begin = span(side * rows + c * chunk_rows + place * share, share)
        source, target = ((tok_ref, tok_buf), (cot_ref, cot_buf))[k]
        return pltpu.make_async_copy(
            source.at[begin, :], target.at[lax.rem(c, 2)], share_sem.at[lax.rem(c, 2), k]
        )

    def remote(source, target, send, recv, device_id):
        return pltpu.make_async_remote_copy(
            src_ref=source, dst_ref=target, send_sem=send, recv_sem=recv,
            device_id=device_id, device_id_type=pl.DeviceIdType.MESH,
        )


    def sum_copy(c, k, way, b, first):
        slot = lax.rem(c, 2)
        target = landed.at[slot, k, way, b - 1 + way]
        source = terms.at[slot, k, span(b * share, share), :] if first else target
        return remote(
            source, target, sum_send.at[slot, k, way, b], sum_recv.at[slot, k, way, b],
            (above, below)[way],
        )

    def place_of(c, b, on_side):
        return span(on_side * rows + c * chunk_rows + b * share, share)

    def line_copy(c, k, b, way, first):
        target = whole_refs[k].at[place_of(c, b, side), :]
        source = ready.at[lax.rem(c, 2), k] if first else target
        return remote(
            source, target, line_send.at[c, k, way, b], line_recv.at[c, k, b],
            (above, below)[way],
        )

    def side_copy(c, k, b, first):
        target = whole_refs[k].at[place_of(c, b, side), :]
        source = ready.at[lax.rem(c, 2), k] if first else target
        return remote(
            source, target, side_send.at[c, k, b], side_recv.at[c, k, b], across
        )

    def keep_copy(c, k):
        return pltpu.make_async_copy(
            ready.at[lax.rem(c, 2), k], whole_refs[k].at[place_of(c, place, side), :],
            keep_sem.at[c, k],
        )

    def each_first(c, k, act):
        @pl.when(jnp.logical_not(has_below))
        def _():
            for b in range(count - 1, 0, -1):
                act(sum_copy(c, k, 0, b, True))

        @pl.when(jnp.logical_not(has_above))
        def _():
            for b in range(count - 1):
                act(sum_copy(c, k, 1, b, True))

    def send_ends(c, k):
        load(c, k).wait()
        each_first(c, k, lambda copy: copy.start())

    def sums_left(c, k):
        for b in range(count):

            @pl.when(has_below & (place < b))
            def _(b=b):
                sum_copy(c, k, 0, b, False).wait_send()

            @pl.when(has_above & (place > b))
            def _(b=b):
                sum_copy(c, k, 1, b, False).wait_send()

    step = min(16, share)

    def add_on(c, k, way, b):
        slot = lax.rem(c, 2)

        def body(i, carry):
            at = span(i * step, step)
            mine = terms[slot, k, span(b * share + i * step, step), :].astype(F32)
            landed[slot, k, way, b - 1 + way, at, :] = (
                mine + landed[slot, k, way, b - 1 + way, at, :].astype(F32)
            ).astype(BF16)
            return carry

        lax.fori_loop(0, share // step, body, 0)

    def sums(c, k, wave):
        ahead = count - 2 - wave
        for way, b, here in (
            (0, place + ahead, has_below & (place + ahead < count)),
            (1, place - ahead, has_above & (place >= ahead)),
        ):

            @pl.when(here)
            def _(way=way, b=b):
                sum_copy(c, k, way, b, False).wait_recv()

                @pl.when(ahead > 0)
                def _():
                    add_on(c, k, way, b)
                    sum_copy(c, k, way, b, False).start()

    def own_left(c, k):
        pl.when(has_above)(lambda: line_copy(c, k, place, 0, True).wait_send())
        pl.when(has_below)(lambda: line_copy(c, k, place, 1, True).wait_send())
        side_copy(c, k, place, True).wait_send()
        keep_copy(c, k).wait()

    def finish(c, k):
        load_share(c, k).wait()
        pl.when(c > 1)(lambda: own_left(c - 2, k))
        slot = lax.rem(c, 2)

        def body(i, carry):
            at = span(i * step, step)
            up = landed[slot, k, 0, jnp.maximum(place - 1, 0), at, :].astype(F32)
            down = landed[slot, k, 1, jnp.minimum(place, count - 2), at, :].astype(F32)
            total = (
                terms[slot, k, span(place * share + i * step, step), :].astype(F32)
                + jnp.where(has_below, up, 0.0)
                + jnp.where(has_above, down, 0.0)
            )
            wide = tok_buf[slot, at, :].astype(F32)
            if k == 0:
                ready[slot, k, at, :] = (wide + total).astype(BF16)
                return carry
            scale = 1.0 / width
            centred = wide - jnp.sum(wide, axis=1, keepdims=True) * scale
            variance = jnp.sum(centred * centred, axis=1, keepdims=True) * scale
            inverse = lax.rsqrt(variance + EPSILON)
            unit = centred * inverse
            scaled = total * gain_ref[0:1, :]
            mean_scaled = jnp.sum(scaled, axis=1, keepdims=True) * scale
            mean_cross = jnp.sum(scaled * unit, axis=1, keepdims=True) * scale
            ready[slot, k, at, :] = (
                cot_buf[slot, at, :].astype(F32)
                + inverse * (scaled - mean_scaled - unit * mean_cross)
            ).astype(BF16)
            gain_term = total * unit
            for r in range(0, step, 8):
                part_ref[0:8, :] += gain_term[r : r + 8, :]
                part_ref[8:16, :] += total[r : r + 8, :]
            return carry

        lax.fori_loop(0, share // step, body, 0)
        pl.when(has_above)(lambda: line_copy(c, k, place, 0, True).start())
        pl.when(has_below)(lambda: line_copy(c, k, place, 1, True).start())
        side_copy(c, k, place, True).start()
        keep_copy(c, k).start()

    def pass_on(c, k, distance):
        for way, b, here in (
            (0, place - distance, place >= distance),
            (1, place + distance, place + distance < count),
        ):

            @pl.when(here)
            def _(way=way, b=b):
                line_copy(c, k, b, way, False).wait_recv()
                pl.when((has_above, has_below)[way])(
                    lambda: line_copy(c, k, b, way, False).start()
                )
                side_copy(c, k, b, False).start()

    waves = count - 1
    every = max(1, waves // 3)
    works = 2 * waves // every

    def chunk_steps(c, live, work):
        def one(s, carry):
            wave = lax.rem(s, waves)
            for k in range(2):

                @pl.when(live & (s // waves == k))
                def _(k=k):
                    @pl.when(wave == 0)
                    def _():
                        @pl.when(c > 0)
                        def _():
                            sums_left(c - 1, k)
                            each_first(c - 1, k, lambda copy: copy.wait_send())

                        pl.when(c + 1 < chunks)(lambda: load_share(c + 1, k).start())

                    sums(c, k, wave)
                    pl.when(c > 0)(lambda: pass_on(c - 1, k, wave + 1))

            pl.when(lax.rem(s, every) == 0)(lambda: work(s // every))
            for k in range(2):

                @pl.when(live & (s == (k + 1) * waves - 1))
                def _(k=k):
                    more = c + 1 < chunks
                    pl.when(more)(lambda: load(c + 1, k).start())
                    finish(c, k)
                    pl.when(more)(lambda: send_ends(c + 1, k))

            return carry

        lax.fori_loop(0, 2 * waves, one, 0)

    tile_works = works // 2
    tile_chunks = -(-(chunks - 1) // tile_works)

    def tiles_scope(*scratch):
        weights = scratch[: 5 * sides]
        scratch = scratch[5 * sides :]
        normed_buf, tile_cot = scratch[:2]
        head_bufs = scratch[2 : 2 + 2 * sides]
        scratch = scratch[2 + 2 * sides :]
        mids, f_buf, g_buf = scratch[: 3 * sides], scratch[3 * sides], scratch[3 * sides + 1]
        f_total, g_total, weight_sem, in_sem, out_sem = scratch[3 * sides + 2 :]

        def weight_copy(x):
            return pltpu.make_async_copy(weight_refs[x], weights[x], weight_sem.at[x])

        def tile_in(i):
            slot = lax.rem(i, 2)
            at = span(i * chunk_rows, chunk_rows)
            at_side = span(side * rows + i * chunk_rows, chunk_rows)
            pairs = [(normed_ref.at[at, :], normed_buf), (cot_ref.at[at_side, :], tile_cot)]
            pairs += [(ref.at[at, :], buf) for ref, buf in zip(head_refs, head_bufs)]
            return [
                pltpu.make_async_copy(ref, buf.at[slot], in_sem.at[slot, x])
                for x, (ref, buf) in enumerate(pairs)
            ]

        def tile_out(i):
            at = span(i * chunk_rows, chunk_rows)
            pairs = list(zip(mids, mid_refs)) + [(f_buf, f_ref), (g_buf, g_ref)]
            return [
                pltpu.make_async_copy(buf, ref.at[at, :], out_sem.at[x])
                for x, (buf, ref) in enumerate(pairs)
            ]

        def wait_out(i):
            for copy in tile_out(i):
                copy.wait()

        def tile(i, s):
            slot = lax.rem(i, 2)
            if s == 0:
                for copy in tile_in(i):
                    copy.wait()

                @pl.when(i + 1 < chunks)
                def _():
                    for copy in tile_in(i + 1):
                        copy.start()

                pl.when(i > 1)(lambda: wait_out(i - 1))

            @pl.when(i == 0)
            def _():
                for x in range(5 * s, 5 * s + 5):
                    weight_copy(x).wait()

            qkv_w, out_w, gate_w, up_w, down_w = weights[5 * s : 5 * s + 5]
            hidden_buf, gate_buf, up_buf = mids[3 * s : 3 * s + 3]
            normed, cot = normed_buf[slot], tile_cot[slot]
            gate = product(normed, gate_w[...])
            up = product(normed, up_w[...])
            sig = 1.0 / (1.0 + jnp.exp(-gate))
            silu = gate * sig
            hidden = (silu * up).astype(BF16)
            hidden_buf[...] = hidden
            grad_hidden = cols_product(cot, down_w[...])
            gate_back = (grad_hidden * up * sig * (1.0 + gate * (1.0 - sig))).astype(BF16)
            up_back = (grad_hidden * silu).astype(BF16)
            gate_buf[...] = gate_back
            up_buf[...] = up_back
            forward = product(hidden, down_w[...])
            forward += product(head_bufs[2 * s][slot], out_w[...])
            backward = cols_product(gate_back, gate_w[...])
            backward += cols_product(up_back, up_w[...])
            backward += cols_product(head_bufs[2 * s + 1][slot], qkv_w[...])
            if s > 0:
                forward += f_total[...]
                backward += g_total[...]
            if s < sides - 1:
                f_total[...] = forward
                g_total[...] = backward
                return
            f_buf[...] = forward.astype(BF16)
            g_buf[...] = backward.astype(BF16)
            for copy in tile_out(i):
                copy.start()

        def work(turn, n):
            first = turn == 0
            i = jnp.where(first, 0, tile_works * turn - tile_works + 1 + n // sides)
            here = jnp.where(first, n >= works - sides, i < chunks)
            for s in range(sides):
                pl.when((n % sides == s) & here)(lambda: tile(i, s))

        for x in range(5 * sides):
            weight_copy(x).start()
        for copy in tile_in(0):
            copy.start()
        for k in range(2):
            load_share(0, k).start()
        part_ref[...] = jnp.zeros_like(part_ref)
        pl.semaphore_wait(
            barrier, 3 + has_above.astype(jnp.int32) + has_below.astype(jnp.int32)
        )

        def chunk(turn, carry):
            chunk_steps(
                jnp.maximum(turn, 1) - 1, turn > 0, lambda n: work(turn, n)
            )

            @pl.when(turn == 0)
            def _():
                wait_out(0)
                for k in range(2):
                    load(0, k).start()
                for k in range(2):
                    send_ends(0, k)

            return carry

        lax.fori_loop(0, tile_chunks + 1, chunk, 0)
        wait_out(chunks - 1)

    tall = width
    hidden_cols = mid_refs[0].shape[1]
    pl.run_scoped(
        tiles_scope,
        *[pltpu.VMEM(ref.shape, BF16) for ref in weight_refs],
        pltpu.VMEM((2, chunk_rows, width), BF16),
        pltpu.VMEM((2, chunk_rows, width), BF16),
        *[pltpu.VMEM((2, chunk_rows, ref.shape[1]), BF16) for ref in head_refs],
        *[pltpu.VMEM((chunk_rows, hidden_cols), BF16) for _ in mid_refs],
        pltpu.VMEM((chunk_rows, width), BF16),
        pltpu.VMEM((chunk_rows, width), BF16),
        pltpu.VMEM((chunk_rows, width), F32),
        pltpu.VMEM((chunk_rows, width), F32),
        pltpu.SemaphoreType.DMA((5 * sides,)),
        pltpu.SemaphoreType.DMA((2, 2 + 2 * sides)),
        pltpu.SemaphoreType.DMA((3 * sides + 2,)),
    )


    pieces = core_send.shape[2]
    each = 2
    size = tall // pieces

    def grads_scope(*scratch):
        factor_bufs, scratch = scratch[: arrays * sides], scratch[arrays * sides :]
        held, scratch = scratch[: arrays * sides], scratch[arrays * sides :]
        extra, scratch = scratch[: arrays * sides], scratch[arrays * sides :]
        left_bufs, factor_sem, left_sem = scratch[:2], scratch[2], scratch[3]

        def factor_copy(x):
            return pltpu.make_async_copy(factors[x], factor_bufs[x], factor_sem.at[x])

        def piece(ref, j):
            return ref.at[span(j * size, size), :]

        def piece_of(u):
            owner_core = jnp.where(u < 2 * each, 1 - core, core)
            owner_half = jnp.where((u // each) % 2 == 0, 1 - half, half)
            return (owner_half * 2 + owner_core) * each + lax.rem(u, each)

        def slot_of(u):
            return jnp.where(u < 3 * each, lax.rem(u, each), each + lax.rem(u, each))

        def left_copy(u, which):
            at = span(piece_of(u) * size, size)
            source = (
                normed_ref.at[:, at] if which == 0 else cot_ref.at[span(side * rows, rows), at]
            )
            return pltpu.make_async_copy(
                source, left_bufs[which].at[lax.rem(u, 2)], left_sem.at[which, lax.rem(u, 2)]
            )

        def to_core(a, s, j, slot):
            x = 2 * a + s
            return remote(
                held[x].at[slot], piece(core_land[x], j),
                core_send.at[a, s, j], core_recv.at[a, s, j], other_core,
            )

        def to_far(a, s, i, j):
            x = 2 * a + s
            return remote(
                held[x].at[i], piece(far_land[x], j),
                far_send.at[a, s, j], far_recv.at[a, s, j], other_half,
            )

        def to_over(a, i, j):
            return remote(
                held[2 * a + 1].at[each + i], piece(side_land[a], j),
                over_send.at[a, j], over_recv.at[a, j], across,
            )

        def back_copy(a, i, j, way, first):
            target = piece(grad_outs[a], j)
            source = held[2 * a].at[each + i] if first else target
            return remote(
                source, target, back_send.at[a, way, j], back_recv.at[a, j],
                (other_core, other_half)[way],
            )

        def save_copy(a, i, j):
            return pltpu.make_async_copy(
                held[2 * a].at[each + i], piece(grad_outs[a], j), save_sem.at[a, i]
            )

        def their_piece(i):
            return ((1 - half) * 2 + core) * each + i

        def my_piece(i):
            return (half * 2 + core) * each + i

        def add_into(target, slot, source):
            def body(i, carry):
                at = span(i * 16, 16)
                target[slot, at, :] = (
                    target[slot, at, :].astype(F32) + source[at, :].astype(F32)
                ).astype(BF16)
                return carry

            lax.fori_loop(0, size // 16, body, 0)

        def fetch(lands, j, ids):
            copies = [
                pltpu.make_async_copy(piece(lands[n], j), extra[x], load_sem.at[x])
                for n, x in enumerate(ids)
            ]
            for copy in copies:
                copy.start()
            for copy in copies:
                copy.wait()

        everything = range(2 * arrays)

        def make(u, which):
            @pl.when(u == 0)
            def _():
                for x in everything:
                    if (x // 2 < 3) == (which == 0):
                        factor_copy(x).wait()

            left_copy(u, which).wait()
            pl.when(u + 1 < pieces)(lambda: left_copy(u + 1, which).start())
            slot = slot_of(u)
            left = left_bufs[which][lax.rem(u, 2)].T

            @pl.when((u >= each) & (u < 3 * each))
            def _():
                for x in everything:
                    if (x // 2 < 3) == (which == 0):
                        to_core(x // 2, x % 2, piece_of(u - each), slot).wait_send()

            for x in everything:
                if (x // 2 < 3) == (which == 0):
                    held[x][slot] = product(left, factor_bufs[x][...]).astype(BF16)

            @pl.when(u < 2 * each)
            def _():
                for x in everything:
                    if (x // 2 < 3) == (which == 0):
                        to_core(x // 2, x % 2, piece_of(u), slot).start()

        def gather_terms(slot, j):
            for x in everything:
                to_core(x // 2, x % 2, j, 0).wait_recv()
            fetch(core_land, j, everything)
            for x in everything:
                add_into(held[x], slot, extra[x])

        def grads_far(i):
            j = their_piece(i)
            gather_terms(i, j)
            for x in everything:
                to_far(x // 2, x % 2, i, j).start()

        def grads_over(i):
            j = my_piece(i)
            gather_terms(each + i, j)
            for x in everything:
                to_far(x // 2, x % 2, i, j).wait_recv()
            fetch(far_land, j, everything)
            for a in range(arrays):
                add_into(held[2 * a + 1], each + i, extra[2 * a + 1])
                to_over(a, i, j).start()
            for a in range(arrays):
                add_into(held[2 * a], each + i, extra[2 * a])

        def grads_back(i):
            j = my_piece(i)
            for a in range(arrays):
                to_over(a, i, j).wait_recv()
            fetch(side_land, j, range(0, 2 * arrays, 2))
            for a in range(arrays):
                add_into(held[2 * a], each + i, extra[2 * a])
                back_copy(a, i, j, 1, True).start()
                back_copy(a, i, j, 0, True).start()
                save_copy(a, i, j).start()

        def grads_pass(i):
            j = their_piece(i)
            for a in range(arrays):
                back_copy(a, i, j, 1, False).wait_recv()
                back_copy(a, i, j, 0, False).start()

        def grads_drain():
            for i in range(each):
                mine, theirs = my_piece(i), their_piece(i)
                for a in range(arrays):
                    for s in range(2):
                        to_far(a, s, i, theirs).wait_send()
                    to_over(a, i, mine).wait_send()
                    back_copy(a, i, mine, 1, True).wait_send()
                    back_copy(a, i, mine, 0, True).wait_send()
                    back_copy(a, i, theirs, 0, False).wait_send()
                    save_copy(a, i, mine).wait()
            for u in range(2 * each):
                for a in range(arrays):
                    back_copy(a, 0, piece_of(u), 0, False).wait_recv()

        events = {
            (4, works // 2): (grads_far, 0),
            (4, works - 1): (grads_far, 1),
            (6, works // 2 - 1): (grads_over, 0),
            (7, works // 2 - 1): (grads_over, 1),
            (7, works - 1): (grads_back, 0),
        }

        def work(c, n):
            v = works * (c - tile_chunks) + n
            for which in range(2):
                pl.when((v < 2 * pieces) & (n % 2 == which))(lambda: make(v // 2, which))
            for (at_chunk, at_work), (act, i) in events.items():
                pl.when((c == at_chunk) & (n == at_work))(lambda: act(i))

        for x in everything:
            factor_copy(x).start()
        for which in range(2):
            left_copy(0, which).start()

        def chunk(c, carry):
            chunk_steps(c, c >= 0, lambda n: work(c, n))
            return carry

        lax.fori_loop(tile_chunks, chunks, chunk, 0)
        for distance in range(1, count):
            pass_on(chunks - 1, 0, distance)
            pass_on(chunks - 1, 1, distance)
        grads_back(1)
        for i in range(each):
            grads_pass(i)
        grads_drain()

    factor_shapes = [ref.shape for ref in factors]
    pl.run_scoped(
        grads_scope,
        *[pltpu.VMEM(shape, BF16) for shape in factor_shapes],
        *[pltpu.VMEM((2 * each, size, shape[1]), BF16) for shape in factor_shapes],
        *[pltpu.VMEM((size, shape[1]), BF16) for shape in factor_shapes],
        pltpu.VMEM((2, rows, size), BF16),
        pltpu.VMEM((2, rows, size), BF16),
        pltpu.SemaphoreType.DMA((2 * arrays,)),
        pltpu.SemaphoreType.DMA((2, 2)),
    )

    for k in range(2):
        sums_left(chunks - 1, k)
        each_first(chunks - 1, k, lambda copy: copy.wait_send())
        own_left(chunks - 2, k)
        own_left(chunks - 1, k)

    def drain(c, carry):
        for k in range(2):
            for b in range(count):
                pl.when((place > b) & has_above)(
                    lambda: line_copy(c, k, b, 0, False).wait_send()
                )
                pl.when((place < b) & has_below)(
                    lambda: line_copy(c, k, b, 1, False).wait_send()
                )
                pl.when(place != b)(lambda: side_copy(c, k, b, False).wait_send())
                side_copy(c, k, b, False).wait_recv()
        return carry

    lax.fori_loop(0, chunks, drain, 0)


def layer(normed, tokens, cotangent, heads, weights, gain, count, chunks, dp_size):
    row_count, width = tokens.shape
    rows = row_count // 2
    share = rows // chunks // count
    sides, arrays = len(weights), 5
    pieces = 2 * dp_size
    sem = pltpu.SemaphoreType.DMA
    flat_heads = [array for group in heads for array in group]
    flat_weights = [array for side in weights for array in side]
    hidden = weights[0][2].shape[1]
    columns = [heads[0][1].shape[1], hidden, hidden, hidden, heads[0][0].shape[1]]
    whole = jax.ShapeDtypeStruct(tokens.shape, BF16)
    finals = [jax.ShapeDtypeStruct((width, n), BF16) for n in columns]
    lands = [shape for shape in finals for _ in range(sides)]
    anywhere = pl.BlockSpec(memory_space=pl.ANY)
    vmem = pl.BlockSpec(memory_space=pltpu.VMEM)
    own_rows = [jax.ShapeDtypeStruct((rows, width), BF16)] * 2
    own_rows += [jax.ShapeDtypeStruct((rows, hidden), BF16)] * (3 * sides)
    outs = pl.pallas_call(
        functools.partial(layer_kernel, chunks, sides),
        in_specs=[anywhere] * (3 + len(flat_heads) + len(flat_weights)) + [vmem],
        out_specs=[anywhere, anywhere, vmem] + [anywhere] * (6 * arrays + len(own_rows)),
        out_shape=[whole, whole, jax.ShapeDtypeStruct((16, width), F32)]
        + finals + lands + lands + finals + own_rows,
        scratch_shapes=[
            pltpu.VMEM((2, 2, count * share, width), BF16),
            pltpu.VMEM((2, 2, 2, count - 1, share, width), BF16),
            pltpu.VMEM((2, 2, share, width), BF16),
            pltpu.VMEM((2, share, width), BF16),
            pltpu.VMEM((2, share, width), BF16),
            sem((2, 2)),
            sem((2, 2)),
            sem((2, 2, 2, count)),
            sem((2, 2, 2, count)),
            sem((chunks, 2, 2, count)),
            sem((chunks, 2, count)),
            sem((chunks, 2, count)),
            sem((chunks, 2, count)),
            sem((chunks, 2)),
            sem((arrays, 2, pieces)),
            sem((arrays, 2, pieces)),
            sem((arrays, 2, pieces)),
            sem((arrays, 2, pieces)),
            sem((arrays, pieces)),
            sem((arrays, pieces)),
            sem((arrays, 2, pieces)),
            sem((arrays, pieces)),
            sem((2 * arrays,)),
            sem((arrays, 2)),
        ],
        compiler_params=pltpu.CompilerParams(
            collective_id=0, has_side_effects=True, vmem_limit_bytes=63 * 2**20
        ),
        cost_estimate=pl.CostEstimate(
            flops=6 * rows * sum(array.size for array in flat_weights),
            bytes_accessed=800 * 2**20,
            transcendentals=0,
        ),
        name="layer",
    )(normed, tokens, cotangent, *flat_heads, *flat_weights, gain)
    out, grad, part = outs[:3]
    return out, grad, part[0:8].sum(axis=0), part[8:16].sum(axis=0), outs[3 : 3 + arrays]


def body(
    tokens,
    lengths,
    norm_gain,
    norm_shift,
    qkv_weight,
    qkv_bias,
    out_weight,
    gate_weight,
    up_weight,
    down_weight,
    cotangent,
):
    tensor_size = lax.axis_size("tensor")
    dp_size = lax.axis_size("dp")
    count = tensor_size // 2
    where = lax.axis_index("tensor")
    dp_place = lax.axis_index("dp")
    side = where % 2
    across = [(i, i ^ 1) for i in range(tensor_size)]
    row_count, width = tokens.shape
    rows = row_count // 2
    chunk_count = 8

    def partner(weight):
        part = weight.shape[0] // dp_size
        mine = lax.dynamic_slice_in_dim(weight, dp_place * part, part, 0)
        return lax.all_gather(lax.ppermute(mine, "tensor", across), "dp", axis=0, tiled=True)

    own_weights = (qkv_weight, out_weight, gate_weight, up_weight, down_weight)
    weights = (own_weights, tuple(partner(weight) for weight in own_weights))
    biases = (qkv_bias, lax.ppermute(qkv_bias, "tensor", across))

    own_tokens = lax.dynamic_slice_in_dim(tokens, side * rows, rows, 0)
    own_cot = lax.dynamic_slice_in_dim(cotangent, side * rows, rows, 0)
    length = lax.dynamic_slice_in_dim(lengths, side, 1, 0)
    unit_rows, _ = norm_parts(own_tokens.astype(F32))
    normed = (unit_rows * norm_gain + norm_shift).astype(BF16)

    tables = rotary_tables(rows)
    even = (out_weight.shape[0] // HEAD) % 2 == 0
    groups = [
        (
            product(normed, weights[s][0]) + biases[s].astype(F32),
            cols_product(own_cot, weights[s][1]).astype(BF16),
        )
        for s in range(2)
    ]
    if not even:
        groups = [tuple(jnp.concatenate(pair, axis=1) for pair in zip(*groups))]
    heads = [attention(length, qkv, grad, *tables) for qkv, grad in groups]
    if not even:
        attended, qkv_back = heads[0]
        cut, wide = out_weight.shape[0], qkv_weight.shape[1]
        heads = [
            (attended[:, s * cut : (s + 1) * cut], qkv_back[:, s * wide : (s + 1) * wide])
            for s in range(2)
        ]

    layer_out, grad_tokens, gain_part, shift_part, grads = layer(
        normed, tokens, cotangent, heads, weights, norm_gain[None, :], count, chunk_count, dp_size
    )
    grad_qkv, grad_gate, grad_up = [grad.astype(F32) for grad in grads[:3]]
    grad_down, grad_out = [grad.T.astype(F32) for grad in grads[3:]]
    bias_mine, bias_theirs = [jnp.sum(heads[s][1].astype(F32), axis=0) for s in range(2)]
    grad_bias = lax.psum(bias_mine + lax.ppermute(bias_theirs, "tensor", across), "dp")
    gain_part, shift_part = lax.psum((gain_part, shift_part), ("dp", "tensor"))
    return (
        layer_out,
        grad_tokens,
        gain_part,
        shift_part,
        grad_qkv,
        grad_bias,
        grad_out,
        grad_gate,
        grad_up,
        grad_down,
    )


def solution(mesh):
    placed = (
        P("dp", None),
        P("dp"),
        P(),
        P(),
        P(None, "tensor"),
        P("tensor"),
        P("tensor", None),
        P(None, "tensor"),
        P(None, "tensor"),
        P("tensor", None),
        P("dp", None),
    )
    return jax.shard_map(
        body,
        mesh=mesh,
        in_specs=placed,
        out_specs=(
            P("dp", None),
            P("dp", None),
            P(),
            P(),
            P(None, "tensor"),
            P("tensor"),
            P("tensor", None),
            P(None, "tensor"),
            P(None, "tensor"),
            P("tensor", None),
        ),
        check_vma=False,
    )
```

```python
import functools

import jax
import jax.numpy as jnp
from jax import lax
from jax.experimental import pallas as pl
from jax.experimental.pallas import tpu as pltpu
from jax.sharding import PartitionSpec as P

HEAD = 64
ROT = 16
PAIR = 2 * HEAD
TRIPLE = 6 * HEAD

EPSILON = 1e-05
NEGATIVE = -1e30
F32 = jnp.float32
BF16 = jnp.bfloat16


def rows_product(former, latter):
    return lax.dot_general(
        former, latter, (((0,), (0,)), ((), ())), preferred_element_type=F32
    )


def cols_product(former, latter):
    return lax.dot_general(
        former, latter, (((1,), (1,)), ((), ())), preferred_element_type=F32
    )


def product(former, latter):
    return jnp.dot(former, latter, preferred_element_type=F32)


def rotary_tables(seq_len):
    frequency = 10000.0 ** (-jnp.arange(0, ROT, 2).astype(F32) / ROT)
    angles = jnp.arange(seq_len).astype(F32)[:, None] * frequency[None, :]
    cosine, sine = jnp.cos(angles), jnp.sin(angles)
    still = HEAD - ROT
    cos_head = jnp.concatenate([cosine, cosine, jnp.ones((seq_len, still), F32)], axis=1)
    sin_head = jnp.concatenate([-sine, sine, jnp.zeros((seq_len, still), F32)], axis=1)
    return jnp.tile(cos_head, (1, 2)), jnp.tile(sin_head, (1, 2))


def attention_kernel(
    len_ref, qkv_ref, grad_ref, cos_ref, sin_ref, att_ref, back_ref,
    score, expo, query, key_value, key_value_t, query_t, grad_query, grad_kv_t,
):
    seq_len = qkv_ref.shape[0]
    block = score.shape[1]
    steps = seq_len // block
    length = len_ref[0]
    lane = lax.broadcasted_iota(jnp.int32, (block, PAIR), 1)
    left = lane < HEAD
    near = lax.rem(lane, HEAD) < ROT // 2

    def turn(tile, cosine, sine):
        swapped = jnp.where(
            near, pltpu.roll(tile, PAIR - ROT // 2, 1), pltpu.roll(tile, ROT // 2, 1)
        )
        return tile * cosine + swapped * sine

    def tables(rows):
        cosine, sine = cos_ref[rows, :], sin_ref[rows, :]
        return (
            (cosine, sine),
            (jnp.where(left, 1.0, cosine), jnp.where(left, 0.0, sine)),
            (jnp.where(left, cosine, 1.0), jnp.where(left, sine, 0.0)),
        )

    def prepare(i, carry):
        rows = pl.ds(pl.multiple_of(i * block, block), block)
        tabs = tables(rows)
        first = turn(qkv_ref[rows, 0:PAIR], *tabs[0])
        second = turn(qkv_ref[rows, PAIR : 2 * PAIR], *tabs[1])
        third = turn(qkv_ref[rows, 2 * PAIR : 3 * PAIR], *tabs[2])
        scale = HEAD**-0.5
        first_q = first.astype(BF16).astype(F32) * scale
        second_q = second.astype(BF16).astype(F32) * scale
        query[0, rows, :] = jnp.where(left, 0.0, pltpu.roll(first_q, HEAD, 1)).astype(BF16)
        query[1, rows, :] = jnp.where(left, pltpu.roll(second_q, HEAD, 1), 0.0).astype(BF16)
        for h, tile in enumerate((jnp.where(left, second, first), third)):
            key_value[h, rows, :] = tile.astype(BF16)
            key_value_t[h, :, rows] = tile.T.astype(BF16)
        query_t[0, :, rows] = first_q.T[0:HEAD, :].astype(BF16)
        query_t[1, :, rows] = second_q.T[HEAD:PAIR, :].astype(BF16)
        zero = jnp.zeros((block, PAIR), F32)
        grad_query[rows, :] = zero
        att_ref[rows, :] = zero.astype(BF16)
        for h in range(2):
            grad_kv_t[h, :, rows] = jnp.zeros((PAIR, block), F32)
        return carry

    lax.fori_loop(0, steps, prepare, 0)

    def block_rows(i, carry):
        rows = pl.ds(pl.multiple_of(i * block, block), block)
        q_block = [query[h, rows, :] for h in range(2)]

        def fold(tile, op):
            out = tile[:, 0:PAIR]
            for c in range(1, block // PAIR):
                out = op(out, tile[:, c * PAIR : (c + 1) * PAIR])
            return out

        def scores(j, tops):
            cols = pl.ds(pl.multiple_of(j * block, block), block)
            out = []
            for h in range(2):
                tile = product(q_block[h], key_value_t[h, :, cols])
                score[h, :, cols] = tile
                out.append(jnp.maximum(tops[h], fold(tile, jnp.maximum)))
            return tuple(out)

        lowest = jnp.full((block, PAIR), NEGATIVE, F32)
        tops = lax.fori_loop(0, i, scores, (lowest, lowest))
        below = lax.broadcasted_iota(jnp.int32, (block, block), 1) <= lax.broadcasted_iota(
            jnp.int32, (block, block), 0
        )
        maxima = []
        for h in range(2):
            tile = jnp.where(below, product(q_block[h], key_value_t[h, :, rows]), NEGATIVE)
            score[h, :, rows] = tile
            maxima.append(
                jnp.max(jnp.maximum(tops[h], fold(tile, jnp.maximum)), axis=1, keepdims=True)
            )

        def mix(j, sums):
            cols = pl.ds(pl.multiple_of(j * block, block), block)
            out = []
            for h in range(2):
                tile = jnp.exp(score[h, :, cols] - maxima[h])
                low = tile.astype(BF16)
                expo[h, :, cols] = low
                out.append(sums[2 * h] + product(low, key_value[h, cols, :]))
                out.append(sums[2 * h + 1] + fold(tile, jnp.add))
            return tuple(out)

        zero = jnp.zeros((block, PAIR), F32)
        sums = lax.fori_loop(0, i + 1, mix, (zero,) * 4)
        place = i * block + lax.broadcasted_iota(jnp.int32, (block, 1), 0)
        valid = (place < length).astype(F32)
        inverse = [1.0 / jnp.sum(sums[2 * h + 1], axis=1, keepdims=True) for h in range(2)]
        mixture = jnp.where(left, sums[0] * inverse[0], sums[2] * inverse[1]) * valid
        att_ref[rows, :] = mixture.astype(BF16)
        upstream = grad_ref[rows, :].astype(F32) * valid
        inner = upstream * mixture
        scaled, inner_sum, scaled_t = [], [], []
        for h in range(2):
            own = left if h == 0 else jnp.logical_not(left)
            inner_sum.append(
                jnp.sum(jnp.where(own, inner, 0.0), axis=1, keepdims=True) * inverse[h]
            )
            mine = jnp.where(own, upstream * inverse[h], 0.0)
            scaled.append(mine.astype(BF16))
            half = slice(0, HEAD) if h == 0 else slice(HEAD, PAIR)
            scaled_t.append(mine.T[half, :].astype(BF16))

        def grads(j, sums):
            cols = pl.ds(pl.multiple_of(j * block, block), block)
            out = []
            for h in range(2):
                low = expo[h, :, cols]
                kv = key_value[h, cols, :]
                grad_weight = product(scaled[h], key_value_t[h, :, cols])
                grad_score = (low.astype(F32) * (grad_weight - inner_sum[h])).astype(BF16)
                out.append(sums[h] + product(grad_score, kv))
                key_part = product(query_t[h, :, rows], grad_score)
                value_part = product(scaled_t[h], low)
                key_at, value_at = (HEAD, 0) if h == 0 else (0, HEAD)
                grad_kv_t[h, key_at : key_at + HEAD, cols] += key_part
                grad_kv_t[h, value_at : value_at + HEAD, cols] += value_part
            return tuple(out)

        gq = lax.fori_loop(0, i + 1, grads, (zero, zero))
        scale = HEAD**-0.5
        grad_query[rows, :] = (
            jnp.where(left, pltpu.roll(gq[0], HEAD, 1), pltpu.roll(gq[1], HEAD, 1)) * scale
        )
        return carry

    lax.fori_loop(0, lax.div(length + block - 1, block), block_rows, 0)

    def finish(i, carry):
        rows = pl.ds(pl.multiple_of(i * block, block), block)
        tabs = tables(rows)
        gq = grad_query[rows, :]
        low_kv = grad_kv_t[0, :, rows].T
        high_kv = grad_kv_t[1, :, rows].T
        tiles = (jnp.where(left, gq, low_kv), jnp.where(left, low_kv, gq), high_kv)
        for c in range(3):
            back_ref[rows, c * PAIR : (c + 1) * PAIR] = turn(
                tiles[c], tabs[c][0], -tabs[c][1]
            ).astype(BF16)
        return carry

    lax.fori_loop(0, steps, finish, 0)


def attention(length, qkv, grad_mixture, cosine, sine):
    seq_len, width = qkv.shape
    pairs = width // TRIPLE
    block = min(512, seq_len)
    flops = 6 * 2 * (2 * pairs) * seq_len * seq_len * PAIR
    return pl.pallas_call(
        attention_kernel,
        grid=(pairs,),
        in_specs=[
            pl.BlockSpec(memory_space=pltpu.SMEM),
            pl.BlockSpec((seq_len, TRIPLE), lambda g: (0, g)),
            pl.BlockSpec((seq_len, PAIR), lambda g: (0, g)),
            pl.BlockSpec((seq_len, PAIR), lambda g: (0, 0)),
            pl.BlockSpec((seq_len, PAIR), lambda g: (0, 0)),
        ],
        out_specs=[
            pl.BlockSpec((seq_len, PAIR), lambda g: (0, g)),
            pl.BlockSpec((seq_len, TRIPLE), lambda g: (0, g)),
        ],
        out_shape=[
            jax.ShapeDtypeStruct((seq_len, pairs * PAIR), BF16),
            jax.ShapeDtypeStruct((seq_len, width), BF16),
        ],
        scratch_shapes=[
            pltpu.VMEM((2, block, seq_len), F32),
            pltpu.VMEM((2, block, seq_len), BF16),
            pltpu.VMEM((2, seq_len, PAIR), BF16),
            pltpu.VMEM((2, seq_len, PAIR), BF16),
            pltpu.VMEM((2, PAIR, seq_len), BF16),
            pltpu.VMEM((2, HEAD, seq_len), BF16),
            pltpu.VMEM((seq_len, PAIR), F32),
            pltpu.VMEM((2, PAIR, seq_len), F32),
        ],
        compiler_params=pltpu.CompilerParams(vmem_limit_bytes=48 * 2**20),
        cost_estimate=pl.CostEstimate(
            flops=flops,
            bytes_accessed=seq_len * width * 8,
            transcendentals=2 * pairs * seq_len * seq_len // 2,
        ),
        name="attention",
    )(length, qkv, grad_mixture, cosine, sine)


def norm_parts(tokens_wide):
    row_mean = jnp.mean(tokens_wide, axis=-1, keepdims=True)
    centred = tokens_wide - row_mean
    row_var = jnp.mean(centred * centred, axis=-1, keepdims=True)
    inv_scale = lax.rsqrt(row_var + EPSILON)
    return centred * inv_scale, inv_scale


def layer_kernel(chunks, sides, *refs):
    normed_ref, tok_ref, cot_ref = refs[:3]
    head_refs, refs = refs[3 : 3 + 2 * sides], refs[3 + 2 * sides :]
    weight_refs, gain_ref = refs[: 5 * sides], refs[5 * sides]
    refs = refs[5 * sides + 1 :]
    out_ref, grad_ref, small_ref = refs[:3]
    refs = refs[3:]
    arrays = 5
    grad_outs, core_land = refs[:arrays], refs[arrays : 3 * arrays]
    far_land, side_land = refs[3 * arrays : 5 * arrays], refs[5 * arrays : 6 * arrays]
    refs = refs[6 * arrays :]
    f_ref, g_ref = refs[:2]
    mid_refs, refs = refs[2 : 2 + 3 * sides], refs[2 + 3 * sides :]
    (
        terms, landed, ready, tok_buf, cot_buf,
        term_sem, share_sem, sum_send, sum_recv,
        line_send, line_recv, side_send, side_recv, keep_sem,
        core_send, core_recv, far_send, far_recv, over_send, over_recv,
        back_send, back_recv, load_sem, save_sem,
        part_ref, bias_part, stages, came, small_send, small_recv,
    ) = refs
    share, width = landed.shape[4:]
    count = landed.shape[3] + 1
    chunk_rows = count * share
    rows = chunks * chunk_rows
    where = lax.axis_index("tensor")
    group = lax.axis_index("dp")
    place, side = where // 2, where % 2
    half, core = group // 2, group % 2
    whole_refs = (out_ref, grad_ref)
    factors = []
    for s in range(sides):
        hidden_ref, gate_ref, up_ref = mid_refs[3 * s : 3 * s + 3]
        factors.append(
            (head_refs[2 * s + 1], gate_ref, up_ref, hidden_ref, head_refs[2 * s])
        )
    factors = [factors[x % sides][x // sides] for x in range(arrays * sides)]

    above, below = (group, where + 2), (group, where - 2)
    across = (group, where + 1 - 2 * side)
    other_core = (half * 2 + 1 - core, where)
    other_half = ((1 - half) * 2 + core, where)
    has_above, has_below = place < count - 1, place > 0

    barrier = pltpu.get_barrier_semaphore()

    def greet(target):
        pl.semaphore_signal(barrier, inc=1, device_id=target, device_id_type=pl.DeviceIdType.MESH)

    pl.when(has_above)(lambda: greet(above))
    pl.when(has_below)(lambda: greet(below))
    for target in (across, other_core, other_half):
        greet(target)

    def span(begin, size):
        return pl.ds(pl.multiple_of(begin, size), size)

    def load(c, k):
        source = (f_ref, g_ref)[k].at[span(c * chunk_rows, chunk_rows), :]
        return pltpu.make_async_copy(
            source, terms.at[lax.rem(c, 2), k], term_sem.at[lax.rem(c, 2), k]
        )

    def load_share(c, k):
        begin = span(side * rows + c * chunk_rows + place * share, share)
        source, target = ((tok_ref, tok_buf), (cot_ref, cot_buf))[k]
        return pltpu.make_async_copy(
            source.at[begin, :], target.at[lax.rem(c, 2)], share_sem.at[lax.rem(c, 2), k]
        )

    def remote(source, target, send, recv, device_id):
        return pltpu.make_async_remote_copy(
            src_ref=source, dst_ref=target, send_sem=send, recv_sem=recv,
            device_id=device_id, device_id_type=pl.DeviceIdType.MESH,
        )


    def sum_copy(c, k, way, b, first):
        slot = lax.rem(c, 2)
        target = landed.at[slot, k, way, b - 1 + way]
        source = terms.at[slot, k, span(b * share, share), :] if first else target
        return remote(
            source, target, sum_send.at[slot, k, way, b], sum_recv.at[slot, k, way, b],
            (above, below)[way],
        )

    def place_of(c, b, on_side):
        return span(on_side * rows + c * chunk_rows + b * share, share)

    def line_copy(c, k, b, way, first):
        target = whole_refs[k].at[place_of(c, b, side), :]
        source = ready.at[lax.rem(c, 2), k] if first else target
        return remote(
            source, target, line_send.at[c, k, way, b], line_recv.at[c, k, b],
            (above, below)[way],
        )

    def side_copy(c, k, b, first):
        target = whole_refs[k].at[place_of(c, b, side), :]
        source = ready.at[lax.rem(c, 2), k] if first else target
        return remote(
            source, target, side_send.at[c, k, b], side_recv.at[c, k, b], across
        )

    def keep_copy(c, k):
        return pltpu.make_async_copy(
            ready.at[lax.rem(c, 2), k], whole_refs[k].at[place_of(c, place, side), :],
            keep_sem.at[c, k],
        )

    def each_first(c, k, act):
        @pl.when(jnp.logical_not(has_below))
        def _():
            for b in range(count - 1, 0, -1):
                act(sum_copy(c, k, 0, b, True))

        @pl.when(jnp.logical_not(has_above))
        def _():
            for b in range(count - 1):
                act(sum_copy(c, k, 1, b, True))

    def send_ends(c, k):
        load(c, k).wait()
        each_first(c, k, lambda copy: copy.start())

    def sums_left(c, k):
        for b in range(count):

            @pl.when(has_below & (place < b))
            def _(b=b):
                sum_copy(c, k, 0, b, False).wait_send()

            @pl.when(has_above & (place > b))
            def _(b=b):
                sum_copy(c, k, 1, b, False).wait_send()

    step = min(16, share)

    def add_on(c, k, way, b):
        slot = lax.rem(c, 2)

        def body(i, carry):
            at = span(i * step, step)
            mine = terms[slot, k, span(b * share + i * step, step), :].astype(F32)
            landed[slot, k, way, b - 1 + way, at, :] = (
                mine + landed[slot, k, way, b - 1 + way, at, :].astype(F32)
            ).astype(BF16)
            return carry

        lax.fori_loop(0, share // step, body, 0)

    def sums(c, k, wave):
        ahead = count - 2 - wave
        for way, b, here in (
            (0, place + ahead, has_below & (place + ahead < count)),
            (1, place - ahead, has_above & (place >= ahead)),
        ):

            @pl.when(here)
            def _(way=way, b=b):
                sum_copy(c, k, way, b, False).wait_recv()

                @pl.when(ahead > 0)
                def _():
                    add_on(c, k, way, b)
                    sum_copy(c, k, way, b, False).start()

    def own_left(c, k):
        pl.when(has_above)(lambda: line_copy(c, k, place, 0, True).wait_send())
        pl.when(has_below)(lambda: line_copy(c, k, place, 1, True).wait_send())
        side_copy(c, k, place, True).wait_send()
        keep_copy(c, k).wait()

    def finish(c, k):
        load_share(c, k).wait()
        pl.when(c > 1)(lambda: own_left(c - 2, k))
        slot = lax.rem(c, 2)

        def body(i, carry):
            at = span(i * step, step)
            up = landed[slot, k, 0, jnp.maximum(place - 1, 0), at, :].astype(F32)
            down = landed[slot, k, 1, jnp.minimum(place, count - 2), at, :].astype(F32)
            total = (
                terms[slot, k, span(place * share + i * step, step), :].astype(F32)
                + jnp.where(has_below, up, 0.0)
                + jnp.where(has_above, down, 0.0)
            )
            wide = tok_buf[slot, at, :].astype(F32)
            if k == 0:
                ready[slot, k, at, :] = (wide + total).astype(BF16)
                return carry
            scale = 1.0 / width
            centred = wide - jnp.sum(wide, axis=1, keepdims=True) * scale
            variance = jnp.sum(centred * centred, axis=1, keepdims=True) * scale
            inverse = lax.rsqrt(variance + EPSILON)
            unit = centred * inverse
            scaled = total * gain_ref[0:1, :]
            mean_scaled = jnp.sum(scaled, axis=1, keepdims=True) * scale
            mean_cross = jnp.sum(scaled * unit, axis=1, keepdims=True) * scale
            ready[slot, k, at, :] = (
                cot_buf[slot, at, :].astype(F32)
                + inverse * (scaled - mean_scaled - unit * mean_cross)
            ).astype(BF16)
            gain_term = total * unit
            for r in range(0, step, 8):
                part_ref[0:8, :] += gain_term[r : r + 8, :]
                part_ref[8:16, :] += total[r : r + 8, :]
            return carry

        lax.fori_loop(0, share // step, body, 0)
        pl.when(has_above)(lambda: line_copy(c, k, place, 0, True).start())
        pl.when(has_below)(lambda: line_copy(c, k, place, 1, True).start())
        side_copy(c, k, place, True).start()
        keep_copy(c, k).start()

    def pass_on(c, k, distance):
        for way, b, here in (
            (0, place - distance, place >= distance),
            (1, place + distance, place + distance < count),
        ):

            @pl.when(here)
            def _(way=way, b=b):
                line_copy(c, k, b, way, False).wait_recv()
                pl.when((has_above, has_below)[way])(
                    lambda: line_copy(c, k, b, way, False).start()
                )
                side_copy(c, k, b, False).start()

    def small_copy(n, target):
        return remote(stages.at[n], came.at[n], small_send.at[n], small_recv.at[n], target)

    def small_sums():
        wide = bias_part.shape[2]
        stages[...] = jnp.zeros_like(stages)
        stages[0, 0:1, :] = jnp.sum(part_ref[0:8, :], axis=0, keepdims=True)
        stages[0, 1:2, :] = jnp.sum(part_ref[8:16, :], axis=0, keepdims=True)
        for s in range(sides):
            stages[0, 2 + s : 3 + s, 0:wide] = jnp.sum(bias_part[s], axis=0, keepdims=True)
        for n, target in enumerate((across, other_core, other_half)):
            copy = small_copy(n, target)
            copy.start()
            copy.wait_recv()
            if n == 0:
                stages[1, 0:2, :] = stages[0, 0:2, :] + came[0, 0:2, :]
                stages[1, 2:3, :] = stages[0, 2:3, :] + came[0, 3:4, :]
            else:
                stages[n + 1] = stages[n] + came[n]

        @pl.when(has_below)
        def _():
            small_copy(3, above).wait_recv()
            stages[3] = stages[3] + came[3]

        pl.when(has_above)(lambda: small_copy(3, above).start())
        stages[4] = stages[3]

        @pl.when(has_above)
        def _():
            small_copy(4, below).wait_recv()
            stages[4] = came[4]

        pl.when(has_below)(lambda: small_copy(4, below).start())
        small_ref[...] = stages[4]
        small_ref[2:3, :] = stages[2, 2:3, :] + came[2, 2:3, :]
        for n, target in enumerate((across, other_core, other_half)):
            small_copy(n, target).wait_send()
        pl.when(has_above)(lambda: small_copy(3, above).wait_send())
        pl.when(has_below)(lambda: small_copy(4, below).wait_send())

    waves = count - 1
    every = max(1, waves // 3)
    works = 2 * waves // every

    def chunk_steps(c, live, work):
        def one(s, carry):
            wave = lax.rem(s, waves)
            for k in range(2):

                @pl.when(live & (s // waves == k))
                def _(k=k):
                    @pl.when(wave == 0)
                    def _():
                        @pl.when(c > 0)
                        def _():
                            sums_left(c - 1, k)
                            each_first(c - 1, k, lambda copy: copy.wait_send())

                        pl.when(c + 1 < chunks)(lambda: load_share(c + 1, k).start())

                    sums(c, k, wave)
                    pl.when(c > 0)(lambda: pass_on(c - 1, k, wave + 1))

            pl.when(lax.rem(s, every) == 0)(lambda: work(s // every))
            for k in range(2):

                @pl.when(live & (s == (k + 1) * waves - 1))
                def _(k=k):
                    more = c + 1 < chunks
                    pl.when(more)(lambda: load(c + 1, k).start())
                    finish(c, k)
                    pl.when(more)(lambda: send_ends(c + 1, k))

            return carry

        lax.fori_loop(0, 2 * waves, one, 0)

    tile_works = works // 2
    tile_chunks = -(-(chunks - 1) // tile_works)

    def tiles_scope(*scratch):
        weights = scratch[: 5 * sides]
        scratch = scratch[5 * sides :]
        normed_buf, tile_cot = scratch[:2]
        head_bufs = scratch[2 : 2 + 2 * sides]
        scratch = scratch[2 + 2 * sides :]
        mids, f_buf, g_buf = scratch[: 3 * sides], scratch[3 * sides], scratch[3 * sides + 1]
        f_total, g_total, weight_sem, in_sem, out_sem = scratch[3 * sides + 2 :]

        def weight_copy(x):
            return pltpu.make_async_copy(weight_refs[x], weights[x], weight_sem.at[x])

        def tile_in(i):
            slot = lax.rem(i, 2)
            at = span(i * chunk_rows, chunk_rows)
            at_side = span(side * rows + i * chunk_rows, chunk_rows)
            pairs = [(normed_ref.at[at, :], normed_buf), (cot_ref.at[at_side, :], tile_cot)]
            pairs += [(ref.at[at, :], buf) for ref, buf in zip(head_refs, head_bufs)]
            return [
                pltpu.make_async_copy(ref, buf.at[slot], in_sem.at[slot, x])
                for x, (ref, buf) in enumerate(pairs)
            ]

        def tile_out(i):
            at = span(i * chunk_rows, chunk_rows)
            pairs = list(zip(mids, mid_refs)) + [(f_buf, f_ref), (g_buf, g_ref)]
            return [
                pltpu.make_async_copy(buf, ref.at[at, :], out_sem.at[x])
                for x, (buf, ref) in enumerate(pairs)
            ]

        def wait_out(i):
            for copy in tile_out(i):
                copy.wait()

        def tile(i, s):
            slot = lax.rem(i, 2)
            if s == 0:
                for copy in tile_in(i):
                    copy.wait()

                @pl.when(i + 1 < chunks)
                def _():
                    for copy in tile_in(i + 1):
                        copy.start()

                pl.when(i > 1)(lambda: wait_out(i - 1))

            @pl.when(i == 0)
            def _():
                for x in range(5 * s, 5 * s + 5):
                    weight_copy(x).wait()

            qkv_w, out_w, gate_w, up_w, down_w = weights[5 * s : 5 * s + 5]
            hidden_buf, gate_buf, up_buf = mids[3 * s : 3 * s + 3]
            normed, cot = normed_buf[slot], tile_cot[slot]
            gate = cols_product(normed, gate_w[...])
            up = cols_product(normed, up_w[...])
            sig = 1.0 / (1.0 + jnp.exp(-gate))
            silu = gate * sig
            hidden = (silu * up).astype(BF16)
            hidden_buf[...] = hidden
            grad_hidden = cols_product(cot, down_w[...])
            gate_back = (grad_hidden * up * sig * (1.0 + gate * (1.0 - sig))).astype(BF16)
            up_back = (grad_hidden * silu).astype(BF16)
            gate_buf[...] = gate_back
            up_buf[...] = up_back
            forward = product(hidden, down_w[...])
            forward += product(head_bufs[2 * s][slot], out_w[...])
            backward = product(gate_back, gate_w[...])
            backward += product(up_back, up_w[...])
            qkv_back = head_bufs[2 * s + 1][slot]
            backward += cols_product(qkv_back, qkv_w[...])
            bias_part[s] += (
                qkv_back.astype(F32).reshape(chunk_rows // 8, 8, qkv_back.shape[1]).sum(axis=0)
            )
            if s > 0:
                forward += f_total[...]
                backward += g_total[...]
            if s < sides - 1:
                f_total[...] = forward
                g_total[...] = backward
                return
            f_buf[...] = forward.astype(BF16)
            g_buf[...] = backward.astype(BF16)
            for copy in tile_out(i):
                copy.start()

        def work(turn, n):
            first = turn == 0
            i = jnp.where(first, 0, tile_works * turn - tile_works + 1 + n // sides)
            here = jnp.where(first, n >= works - sides, i < chunks)
            for s in range(sides):
                pl.when((n % sides == s) & here)(lambda: tile(i, s))

        for x in range(5 * sides):
            weight_copy(x).start()
        for copy in tile_in(0):
            copy.start()
        for k in range(2):
            load_share(0, k).start()
        part_ref[...] = jnp.zeros_like(part_ref)
        bias_part[...] = jnp.zeros_like(bias_part)
        pl.semaphore_wait(
            barrier, 3 + has_above.astype(jnp.int32) + has_below.astype(jnp.int32)
        )

        def chunk(turn, carry):
            chunk_steps(
                jnp.maximum(turn, 1) - 1, turn > 0, lambda n: work(turn, n)
            )

            @pl.when(turn == 0)
            def _():
                wait_out(0)
                for k in range(2):
                    load(0, k).start()
                for k in range(2):
                    send_ends(0, k)

            return carry

        lax.fori_loop(0, tile_chunks + 1, chunk, 0)
        wait_out(chunks - 1)

    tall = width
    hidden_cols = mid_refs[0].shape[1]
    pl.run_scoped(
        tiles_scope,
        *[pltpu.VMEM(ref.shape, BF16) for ref in weight_refs],
        pltpu.VMEM((2, chunk_rows, width), BF16),
        pltpu.VMEM((2, chunk_rows, width), BF16),
        *[pltpu.VMEM((2, chunk_rows, ref.shape[1]), BF16) for ref in head_refs],
        *[pltpu.VMEM((chunk_rows, hidden_cols), BF16) for _ in mid_refs],
        pltpu.VMEM((chunk_rows, width), BF16),
        pltpu.VMEM((chunk_rows, width), BF16),
        pltpu.VMEM((chunk_rows, width), F32),
        pltpu.VMEM((chunk_rows, width), F32),
        pltpu.SemaphoreType.DMA((5 * sides,)),
        pltpu.SemaphoreType.DMA((2, 2 + 2 * sides)),
        pltpu.SemaphoreType.DMA((3 * sides + 2,)),
    )


    pieces = core_send.shape[2]
    each = 2
    size = tall // pieces

    def grads_scope(*scratch):
        factor_bufs, scratch = scratch[: arrays * sides], scratch[arrays * sides :]
        held, scratch = scratch[: arrays * sides], scratch[arrays * sides :]
        extra, scratch = scratch[: arrays * sides], scratch[arrays * sides :]
        turned, scratch = scratch[: arrays - 1], scratch[arrays - 1 :]
        left_bufs, factor_sem, left_sem = scratch[:2], scratch[2], scratch[3]

        def factor_copy(x):
            return pltpu.make_async_copy(factors[x], factor_bufs[x], factor_sem.at[x])

        def piece(ref, j):
            return ref.at[span(j * size, size), :]

        def piece_of(u):
            owner_core = jnp.where(u < 2 * each, 1 - core, core)
            owner_half = jnp.where((u // each) % 2 == 0, 1 - half, half)
            return (owner_half * 2 + owner_core) * each + lax.rem(u, each)

        def slot_of(u):
            return jnp.where(u < 3 * each, lax.rem(u, each), each + lax.rem(u, each))

        def left_copy(u, which):
            at = span(piece_of(u) * size, size)
            source = (
                normed_ref.at[:, at] if which == 0 else cot_ref.at[span(side * rows, rows), at]
            )
            return pltpu.make_async_copy(
                source, left_bufs[which].at[lax.rem(u, 2)], left_sem.at[which, lax.rem(u, 2)]
            )

        def to_core(a, s, j, slot):
            x = 2 * a + s
            return remote(
                held[x].at[slot], piece(core_land[x], j),
                core_send.at[a, s, j], core_recv.at[a, s, j], other_core,
            )

        def to_far(a, s, i, j):
            x = 2 * a + s
            return remote(
                held[x].at[i], piece(far_land[x], j),
                far_send.at[a, s, j], far_recv.at[a, s, j], other_half,
            )

        def to_over(a, i, j):
            return remote(
                held[2 * a + 1].at[each + i], piece(side_land[a], j),
                over_send.at[a, j], over_recv.at[a, j], across,
            )

        def final_piece(a, j):
            at = span(j * size, size)
            return grad_outs[a].at[:, at] if a else grad_outs[a].at[at, :]

        def final_source(a, i):
            return turned[a - 1].at[i] if a else held[0].at[each + i]

        def back_copy(a, i, j, way, first):
            target = final_piece(a, j)
            source = final_source(a, i) if first else target
            return remote(
                source, target, back_send.at[a, way, j], back_recv.at[a, j],
                (other_core, other_half)[way],
            )

        def save_copy(a, i, j):
            return pltpu.make_async_copy(
                final_source(a, i), final_piece(a, j), save_sem.at[a, i]
            )

        def their_piece(i):
            return ((1 - half) * 2 + core) * each + i

        def my_piece(i):
            return (half * 2 + core) * each + i

        def add_into(target, slot, source):
            def body(i, carry):
                at = span(i * 16, 16)
                target[slot, at, :] = (
                    target[slot, at, :].astype(F32) + source[at, :].astype(F32)
                ).astype(BF16)
                return carry

            lax.fori_loop(0, size // 16, body, 0)

        def fetch(lands, j, ids):
            copies = [
                pltpu.make_async_copy(piece(lands[n], j), extra[x], load_sem.at[x])
                for n, x in enumerate(ids)
            ]
            for copy in copies:
                copy.start()
            for copy in copies:
                copy.wait()

        everything = range(2 * arrays)

        def make(u, which):
            @pl.when(u == 0)
            def _():
                for x in everything:
                    if (x // 2 < 3) == (which == 0):
                        factor_copy(x).wait()

            left_copy(u, which).wait()
            pl.when(u + 1 < pieces)(lambda: left_copy(u + 1, which).start())
            slot = slot_of(u)
            left = left_bufs[which][lax.rem(u, 2)].T

            @pl.when((u >= each) & (u < 3 * each))
            def _():
                for x in everything:
                    if (x // 2 < 3) == (which == 0):
                        to_core(x // 2, x % 2, piece_of(u - each), slot).wait_send()

            for x in everything:
                if (x // 2 < 3) == (which == 0):
                    held[x][slot] = product(left, factor_bufs[x][...]).astype(BF16)

            @pl.when(u < 2 * each)
            def _():
                for x in everything:
                    if (x // 2 < 3) == (which == 0):
                        to_core(x // 2, x % 2, piece_of(u), slot).start()

        def gather_terms(slot, j):
            for x in everything:
                to_core(x // 2, x % 2, j, 0).wait_recv()
            fetch(core_land, j, everything)
            for x in everything:
                add_into(held[x], slot, extra[x])

        def grads_far(i):
            j = their_piece(i)
            gather_terms(i, j)
            for x in everything:
                to_far(x // 2, x % 2, i, j).start()

        def grads_over(i):
            j = my_piece(i)
            gather_terms(each + i, j)
            for x in everything:
                to_far(x // 2, x % 2, i, j).wait_recv()
            fetch(far_land, j, everything)
            for a in range(arrays):
                add_into(held[2 * a + 1], each + i, extra[2 * a + 1])
                to_over(a, i, j).start()
            for a in range(arrays):
                add_into(held[2 * a], each + i, extra[2 * a])

        def grads_back(i):
            j = my_piece(i)
            for a in range(arrays):
                to_over(a, i, j).wait_recv()
            fetch(side_land, j, range(0, 2 * arrays, 2))
            for a in range(arrays):
                if a:
                    total = held[2 * a][each + i].astype(F32) + extra[2 * a][...].astype(F32)
                    turned[a - 1][i] = total.T.astype(BF16)
                else:
                    add_into(held[0], each + i, extra[0])
                back_copy(a, i, j, 1, True).start()
                back_copy(a, i, j, 0, True).start()
                save_copy(a, i, j).start()

        def grads_pass(i):
            j = their_piece(i)
            for a in range(arrays):
                back_copy(a, i, j, 1, False).wait_recv()
                back_copy(a, i, j, 0, False).start()

        def grads_drain():
            for i in range(each):
                mine, theirs = my_piece(i), their_piece(i)
                for a in range(arrays):
                    for s in range(2):
                        to_far(a, s, i, theirs).wait_send()
                    to_over(a, i, mine).wait_send()
                    back_copy(a, i, mine, 1, True).wait_send()
                    back_copy(a, i, mine, 0, True).wait_send()
                    back_copy(a, i, theirs, 0, False).wait_send()
                    save_copy(a, i, mine).wait()
            for u in range(2 * each):
                for a in range(arrays):
                    back_copy(a, 0, piece_of(u), 0, False).wait_recv()

        events = {
            (4, works // 2): (grads_far, 0),
            (4, works - 1): (grads_far, 1),
            (6, works // 2 - 1): (grads_over, 0),
            (7, works // 2 - 1): (grads_over, 1),
            (7, works - 1): (grads_back, 0),
        }

        def work(c, n):
            v = works * (c - tile_chunks) + n
            for which in range(2):
                pl.when((v < 2 * pieces) & (n % 2 == which))(lambda: make(v // 2, which))
            for (at_chunk, at_work), (act, i) in events.items():
                pl.when((c == at_chunk) & (n == at_work))(lambda: act(i))

        for x in everything:
            factor_copy(x).start()
        for which in range(2):
            left_copy(0, which).start()

        def chunk(c, carry):
            chunk_steps(c, c >= 0, lambda n: work(c, n))
            return carry

        lax.fori_loop(tile_chunks, chunks, chunk, 0)
        for distance in range(1, count):
            pass_on(chunks - 1, 0, distance)
            pass_on(chunks - 1, 1, distance)
        small_sums()
        grads_back(1)
        for i in range(each):
            grads_pass(i)
        grads_drain()

    factor_shapes = [ref.shape for ref in factors]
    pl.run_scoped(
        grads_scope,
        *[pltpu.VMEM(shape, BF16) for shape in factor_shapes],
        *[pltpu.VMEM((2 * each, size, shape[1]), BF16) for shape in factor_shapes],
        *[pltpu.VMEM((size, shape[1]), BF16) for shape in factor_shapes],
        *[pltpu.VMEM((each, shape[1], size), BF16) for shape in factor_shapes[2::2]],
        pltpu.VMEM((2, rows, size), BF16),
        pltpu.VMEM((2, rows, size), BF16),
        pltpu.SemaphoreType.DMA((2 * arrays,)),
        pltpu.SemaphoreType.DMA((2, 2)),
    )

    for k in range(2):
        sums_left(chunks - 1, k)
        each_first(chunks - 1, k, lambda copy: copy.wait_send())
        own_left(chunks - 2, k)
        own_left(chunks - 1, k)

    def drain(c, carry):
        for k in range(2):
            for b in range(count):
                pl.when((place > b) & has_above)(
                    lambda: line_copy(c, k, b, 0, False).wait_send()
                )
                pl.when((place < b) & has_below)(
                    lambda: line_copy(c, k, b, 1, False).wait_send()
                )
                pl.when(place != b)(lambda: side_copy(c, k, b, False).wait_send())
                side_copy(c, k, b, False).wait_recv()
        return carry

    lax.fori_loop(0, chunks, drain, 0)


def layer(normed, tokens, cotangent, heads, weights, gain, count, chunks, dp_size):
    row_count, width = tokens.shape
    rows = row_count // 2
    share = rows // chunks // count
    sides, arrays = len(weights), 5
    pieces = 2 * dp_size
    sem = pltpu.SemaphoreType.DMA
    flat_heads = [array for group in heads for array in group]
    flat_weights = [array for side in weights for array in side]
    hidden = weights[0][2].shape[0]
    columns = [heads[0][1].shape[1], hidden, hidden, hidden, heads[0][0].shape[1]]
    whole = jax.ShapeDtypeStruct(tokens.shape, BF16)
    half_sums = [jax.ShapeDtypeStruct((width, n), BF16) for n in columns]
    finals = half_sums[:1] + [jax.ShapeDtypeStruct((n, width), BF16) for n in columns[1:]]
    lands = [shape for shape in half_sums for _ in range(sides)]
    anywhere = pl.BlockSpec(memory_space=pl.ANY)
    vmem = pl.BlockSpec(memory_space=pltpu.VMEM)
    own_rows = [jax.ShapeDtypeStruct((rows, width), BF16)] * 2
    own_rows += [jax.ShapeDtypeStruct((rows, hidden), BF16)] * (3 * sides)
    outs = pl.pallas_call(
        functools.partial(layer_kernel, chunks, sides),
        in_specs=[anywhere] * (3 + len(flat_heads) + len(flat_weights)) + [vmem],
        out_specs=[anywhere, anywhere, vmem] + [anywhere] * (6 * arrays + len(own_rows)),
        out_shape=[whole, whole, jax.ShapeDtypeStruct((8, width), F32)]
        + finals + lands + lands + half_sums + own_rows,
        scratch_shapes=[
            pltpu.VMEM((2, 2, count * share, width), BF16),
            pltpu.VMEM((2, 2, 2, count - 1, share, width), BF16),
            pltpu.VMEM((2, 2, share, width), BF16),
            pltpu.VMEM((2, share, width), BF16),
            pltpu.VMEM((2, share, width), BF16),
            sem((2, 2)),
            sem((2, 2)),
            sem((2, 2, 2, count)),
            sem((2, 2, 2, count)),
            sem((chunks, 2, 2, count)),
            sem((chunks, 2, count)),
            sem((chunks, 2, count)),
            sem((chunks, 2, count)),
            sem((chunks, 2)),
            sem((arrays, 2, pieces)),
            sem((arrays, 2, pieces)),
            sem((arrays, 2, pieces)),
            sem((arrays, 2, pieces)),
            sem((arrays, pieces)),
            sem((arrays, pieces)),
            sem((arrays, 2, pieces)),
            sem((arrays, pieces)),
            sem((2 * arrays,)),
            sem((arrays, 2)),
            pltpu.VMEM((16, width), F32),
            pltpu.VMEM((sides, 8, columns[0]), F32),
            pltpu.VMEM((5, 8, width), F32),
            pltpu.VMEM((5, 8, width), F32),
            sem((5,)),
            sem((5,)),
        ],
        compiler_params=pltpu.CompilerParams(
            collective_id=0, has_side_effects=True, vmem_limit_bytes=63 * 2**20
        ),
        cost_estimate=pl.CostEstimate(
            flops=6 * rows * sum(array.size for array in flat_weights),
            bytes_accessed=800 * 2**20,
            transcendentals=0,
        ),
        name="layer",
    )(normed, tokens, cotangent, *flat_heads, *flat_weights, gain)
    out, grad, small = outs[:3]
    return out, grad, small[0], small[1], small[2, : columns[0]], outs[3 : 3 + arrays]


def body(
    tokens,
    lengths,
    norm_gain,
    norm_shift,
    qkv_weight,
    qkv_bias,
    out_weight,
    gate_weight,
    up_weight,
    down_weight,
    cotangent,
):
    tensor_size = lax.axis_size("tensor")
    dp_size = lax.axis_size("dp")
    count = tensor_size // 2
    where = lax.axis_index("tensor")
    dp_place = lax.axis_index("dp")
    side = where % 2
    across = [(i, i ^ 1) for i in range(tensor_size)]
    row_count, width = tokens.shape
    rows = row_count // 2
    chunk_count = 8

    def partner(weights, *after):
        parts = []
        for weight in weights:
            part = weight.shape[0] // dp_size
            mine = lax.dynamic_slice_in_dim(weight, dp_place * part, part, 0)
            parts.append(lax.ppermute(mine, "tensor", across))
        parts, _ = lax.optimization_barrier((parts, after))
        return [lax.all_gather(part, "dp", axis=0, tiled=True) for part in parts]

    head_weights = (qkv_weight, out_weight)
    mid_weights = (gate_weight.T, up_weight.T, down_weight)
    biases = (qkv_bias, lax.ppermute(qkv_bias, "tensor", across))

    own_tokens = lax.dynamic_slice_in_dim(tokens, side * rows, rows, 0)
    own_cot = lax.dynamic_slice_in_dim(cotangent, side * rows, rows, 0)
    length = lax.dynamic_slice_in_dim(lengths, side, 1, 0)
    unit_rows, _ = norm_parts(own_tokens.astype(F32))
    normed = (unit_rows * norm_gain + norm_shift).astype(BF16)

    tables = rotary_tables(rows)
    even = (out_weight.shape[0] // HEAD) % 2 == 0

    def project(weights, bias):
        return (
            product(normed, weights[0]) + bias.astype(F32),
            cols_product(own_cot, weights[1]).astype(BF16),
        )

    own_group = project(head_weights, biases[0])
    other_heads = partner(head_weights, normed)
    if even:
        heads = [attention(length, *own_group, *tables)]
        other_mid = partner(mid_weights, heads[0])
        heads.append(attention(length, *project(other_heads, biases[1]), *tables))
    else:
        other_mid = partner(mid_weights, normed)
        pairs = zip(own_group, project(other_heads, biases[1]))
        attended, qkv_back = attention(
            length, *[jnp.concatenate(pair, axis=1) for pair in pairs], *tables
        )
        cut, wide = out_weight.shape[0], qkv_weight.shape[1]
        heads = [
            (attended[:, s * cut : (s + 1) * cut], qkv_back[:, s * wide : (s + 1) * wide])
            for s in range(2)
        ]
    weights = [(*head_weights, *mid_weights), (*other_heads, *other_mid)]
    layer_out, grad_tokens, gain_part, shift_part, grad_bias, grads = layer(
        normed, tokens, cotangent, heads, weights, norm_gain[None, :], count, chunk_count, dp_size
    )
    grad_qkv, grad_gate, grad_up, grad_down, grad_out = [grad.astype(F32) for grad in grads]
    grad_gate, grad_up = grad_gate.T, grad_up.T
    return (
        layer_out,
        grad_tokens,
        gain_part,
        shift_part,
        grad_qkv,
        grad_bias,
        grad_out,
        grad_gate,
        grad_up,
        grad_down,
    )


def solution(mesh):
    placed = (
        P("dp", None),
        P("dp"),
        P(),
        P(),
        P(None, "tensor"),
        P("tensor"),
        P("tensor", None),
        P(None, "tensor"),
        P(None, "tensor"),
        P("tensor", None),
        P("dp", None),
    )
    return jax.shard_map(
        body,
        mesh=mesh,
        in_specs=placed,
        out_specs=(
            P("dp", None),
            P("dp", None),
            P(),
            P(),
            P(None, "tensor"),
            P("tensor"),
            P("tensor", None),
            P(None, "tensor"),
            P(None, "tensor"),
            P("tensor", None),
        ),
        check_vma=False,
    )
```

```python
import functools

import jax
import jax.numpy as jnp
from jax import lax
from jax.experimental import pallas as pl
from jax.experimental.pallas import tpu as pltpu
from jax.sharding import PartitionSpec as P

HEAD = 64
ROT = 16
PAIR = 2 * HEAD
TRIPLE = 6 * HEAD

EPSILON = 1e-05
NEGATIVE = -1e30
F32 = jnp.float32
BF16 = jnp.bfloat16


def rows_product(former, latter):
    return lax.dot_general(
        former, latter, (((0,), (0,)), ((), ())), preferred_element_type=F32
    )


def cols_product(former, latter):
    return lax.dot_general(
        former, latter, (((1,), (1,)), ((), ())), preferred_element_type=F32
    )


def product(former, latter):
    return jnp.dot(former, latter, preferred_element_type=F32)


def rotary_tables(seq_len):
    frequency = 10000.0 ** (-jnp.arange(0, ROT, 2).astype(F32) / ROT)
    angles = jnp.arange(seq_len).astype(F32)[:, None] * frequency[None, :]
    cosine, sine = jnp.cos(angles), jnp.sin(angles)
    still = HEAD - ROT
    cos_head = jnp.concatenate([cosine, cosine, jnp.ones((seq_len, still), F32)], axis=1)
    sin_head = jnp.concatenate([-sine, sine, jnp.zeros((seq_len, still), F32)], axis=1)
    return jnp.tile(cos_head, (1, 2)), jnp.tile(sin_head, (1, 2))


def attention_kernel(
    len_ref, qkv_ref, grad_ref, cos_ref, sin_ref, att_ref, back_ref,
    score, expo, query, key_value, key_value_t, query_t, grad_query, grad_kv_t,
):
    seq_len = qkv_ref.shape[0]
    block = score.shape[1]
    steps = seq_len // block
    length = len_ref[0]
    lane = lax.broadcasted_iota(jnp.int32, (block, PAIR), 1)
    left = lane < HEAD
    near = lax.rem(lane, HEAD) < ROT // 2

    def turn(tile, cosine, sine):
        swapped = jnp.where(
            near, pltpu.roll(tile, PAIR - ROT // 2, 1), pltpu.roll(tile, ROT // 2, 1)
        )
        return tile * cosine + swapped * sine

    def tables(rows):
        cosine, sine = cos_ref[rows, :], sin_ref[rows, :]
        return (
            (cosine, sine),
            (jnp.where(left, 1.0, cosine), jnp.where(left, 0.0, sine)),
            (jnp.where(left, cosine, 1.0), jnp.where(left, sine, 0.0)),
        )

    def prepare(i, carry):
        rows = pl.ds(pl.multiple_of(i * block, block), block)
        tabs = tables(rows)
        first = turn(qkv_ref[rows, 0:PAIR], *tabs[0])
        second = turn(qkv_ref[rows, PAIR : 2 * PAIR], *tabs[1])
        third = turn(qkv_ref[rows, 2 * PAIR : 3 * PAIR], *tabs[2])
        scale = HEAD**-0.5
        first_q = first.astype(BF16).astype(F32) * scale
        second_q = second.astype(BF16).astype(F32) * scale
        query[0, rows, :] = jnp.where(left, 0.0, pltpu.roll(first_q, HEAD, 1)).astype(BF16)
        query[1, rows, :] = jnp.where(left, pltpu.roll(second_q, HEAD, 1), 0.0).astype(BF16)
        for h, tile in enumerate((jnp.where(left, second, first), third)):
            key_value[h, rows, :] = tile.astype(BF16)
            key_value_t[h, :, rows] = tile.T.astype(BF16)
        query_t[0, :, rows] = first_q.T[0:HEAD, :].astype(BF16)
        query_t[1, :, rows] = second_q.T[HEAD:PAIR, :].astype(BF16)
        zero = jnp.zeros((block, PAIR), F32)
        grad_query[rows, :] = zero
        att_ref[rows, :] = zero.astype(BF16)
        for h in range(2):
            grad_kv_t[h, :, rows] = jnp.zeros((PAIR, block), F32)
        return carry

    lax.fori_loop(0, steps, prepare, 0)

    def fold(tile, op):
        out = tile[:, 0:PAIR]
        for c in range(1, block // PAIR):
            out = op(out, tile[:, c * PAIR : (c + 1) * PAIR])
        return out

    def block_rows(i):
        rows = pl.ds(i * block, block)
        spans = [pl.ds(j * block, block) for j in range(i + 1)]
        q_block = [query[h, rows, :] for h in range(2)]
        below = lax.broadcasted_iota(jnp.int32, (block, block), 1) <= lax.broadcasted_iota(
            jnp.int32, (block, block), 0
        )
        maxima = []
        for h in range(2):
            top = None
            for j, cols in enumerate(spans):
                tile = product(q_block[h], key_value_t[h, :, cols])
                if j == i:
                    tile = jnp.where(below, tile, NEGATIVE)
                score[h, :, cols] = tile
                high = fold(tile, jnp.maximum)
                top = high if top is None else jnp.maximum(top, high)
            maxima.append(jnp.max(top, axis=1, keepdims=True))

        mixed, inverse = [], []
        for h in range(2):
            mixture = total = None
            for cols in spans:
                tile = jnp.exp(score[h, :, cols] - maxima[h])
                low = tile.astype(BF16)
                expo[h, :, cols] = low
                part = product(low, key_value[h, cols, :])
                amount = fold(tile, jnp.add)
                mixture = part if mixture is None else mixture + part
                total = amount if total is None else total + amount
            mixed.append(mixture)
            inverse.append(1.0 / jnp.sum(total, axis=1, keepdims=True))

        place = i * block + lax.broadcasted_iota(jnp.int32, (block, 1), 0)
        valid = (place < length).astype(F32)
        mixture = jnp.where(left, mixed[0] * inverse[0], mixed[1] * inverse[1]) * valid
        att_ref[rows, :] = mixture.astype(BF16)
        upstream = grad_ref[rows, :].astype(F32) * valid
        inner = upstream * mixture
        scale = HEAD**-0.5
        turned = []
        for h in range(2):
            own = left if h == 0 else jnp.logical_not(left)
            inner_sum = jnp.sum(jnp.where(own, inner, 0.0), axis=1, keepdims=True) * inverse[h]
            mine = jnp.where(own, upstream * inverse[h], 0.0)
            scaled = mine.astype(BF16)
            half = slice(0, HEAD) if h == 0 else slice(HEAD, PAIR)
            scaled_t = mine.T[half, :].astype(BF16)
            queries_t = query_t[h, :, rows]
            grad = None
            for cols in spans:
                low = expo[h, :, cols]
                grad_weight = product(scaled, key_value_t[h, :, cols])
                grad_score = (low.astype(F32) * (grad_weight - inner_sum)).astype(BF16)
                part = product(grad_score, key_value[h, cols, :])
                grad = part if grad is None else grad + part
                key_at, value_at = (HEAD, 0) if h == 0 else (0, HEAD)
                grad_kv_t[h, key_at : key_at + HEAD, cols] += product(queries_t, grad_score)
                grad_kv_t[h, value_at : value_at + HEAD, cols] += product(scaled_t, low)
            turned.append(pltpu.roll(grad, HEAD, 1))
        grad_query[rows, :] = jnp.where(left, turned[0], turned[1]) * scale

    for i in range(steps):
        pl.when(i * block < length)(functools.partial(block_rows, i))

    def finish(i, carry):
        rows = pl.ds(pl.multiple_of(i * block, block), block)
        tabs = tables(rows)
        gq = grad_query[rows, :]
        low_kv = grad_kv_t[0, :, rows].T
        high_kv = grad_kv_t[1, :, rows].T
        tiles = (jnp.where(left, gq, low_kv), jnp.where(left, low_kv, gq), high_kv)
        for c in range(3):
            back_ref[rows, c * PAIR : (c + 1) * PAIR] = turn(
                tiles[c], tabs[c][0], -tabs[c][1]
            ).astype(BF16)
        return carry

    lax.fori_loop(0, steps, finish, 0)


def attention(length, qkv, grad_mixture, cosine, sine):
    seq_len, width = qkv.shape
    pairs = width // TRIPLE
    block = min(512, seq_len)
    flops = 6 * 2 * (2 * pairs) * seq_len * seq_len * PAIR
    return pl.pallas_call(
        attention_kernel,
        grid=(pairs,),
        in_specs=[
            pl.BlockSpec(memory_space=pltpu.SMEM),
            pl.BlockSpec((seq_len, TRIPLE), lambda g: (0, g)),
            pl.BlockSpec((seq_len, PAIR), lambda g: (0, g)),
            pl.BlockSpec((seq_len, PAIR), lambda g: (0, 0)),
            pl.BlockSpec((seq_len, PAIR), lambda g: (0, 0)),
        ],
        out_specs=[
            pl.BlockSpec((seq_len, PAIR), lambda g: (0, g)),
            pl.BlockSpec((seq_len, TRIPLE), lambda g: (0, g)),
        ],
        out_shape=[
            jax.ShapeDtypeStruct((seq_len, pairs * PAIR), BF16),
            jax.ShapeDtypeStruct((seq_len, width), BF16),
        ],
        scratch_shapes=[
            pltpu.VMEM((2, block, seq_len), F32),
            pltpu.VMEM((2, block, seq_len), BF16),
            pltpu.VMEM((2, seq_len, PAIR), BF16),
            pltpu.VMEM((2, seq_len, PAIR), BF16),
            pltpu.VMEM((2, PAIR, seq_len), BF16),
            pltpu.VMEM((2, HEAD, seq_len), BF16),
            pltpu.VMEM((seq_len, PAIR), F32),
            pltpu.VMEM((2, PAIR, seq_len), F32),
        ],
        compiler_params=pltpu.CompilerParams(vmem_limit_bytes=48 * 2**20),
        cost_estimate=pl.CostEstimate(
            flops=flops,
            bytes_accessed=seq_len * width * 8,
            transcendentals=2 * pairs * seq_len * seq_len // 2,
        ),
        name="attention",
    )(length, qkv, grad_mixture, cosine, sine)


def start_kernel(
    side_ref, tok_ref, cot_ref, gain_ref, shift_ref, qkv_w, bias_ref, out_w,
    normed_ref, qkv_ref, grad_ref,
):
    wide = tok_ref[...].astype(F32)
    centred = wide - jnp.mean(wide, axis=1, keepdims=True)
    variance = jnp.mean(centred * centred, axis=1, keepdims=True)
    unit = centred * lax.rsqrt(variance + EPSILON)
    normed = (unit * gain_ref[...] + shift_ref[...]).astype(BF16)
    normed_ref[...] = normed
    qkv_ref[...] = product(normed, qkv_w[...]) + bias_ref[...]
    grad_ref[...] = cols_product(cot_ref[...], out_w[...]).astype(BF16)


def start(side, tokens, cotangent, gain, shift, qkv_weight, qkv_bias, out_weight):
    rows, width = tokens.shape[0] // 2, tokens.shape[1]
    tile = min(256, rows)
    tiles = rows // tile
    heads, wide = out_weight.shape[0], qkv_weight.shape[1]

    def sided(i, side_ref):
        return (side_ref[0] * tiles + i, 0)

    def fixed(i, side_ref):
        return (0, 0)

    def rowed(i, side_ref):
        return (i, 0)

    return pl.pallas_call(
        start_kernel,
        grid_spec=pltpu.PrefetchScalarGridSpec(
            num_scalar_prefetch=1,
            grid=(tiles,),
            in_specs=[
                pl.BlockSpec((tile, width), sided),
                pl.BlockSpec((tile, width), sided),
                pl.BlockSpec((1, width), fixed),
                pl.BlockSpec((1, width), fixed),
                pl.BlockSpec((width, wide), fixed),
                pl.BlockSpec((1, wide), fixed),
                pl.BlockSpec((heads, width), fixed),
            ],
            out_specs=[
                pl.BlockSpec((tile, width), rowed),
                pl.BlockSpec((tile, wide), rowed),
                pl.BlockSpec((tile, heads), rowed),
            ],
        ),
        out_shape=[
            jax.ShapeDtypeStruct((rows, width), BF16),
            jax.ShapeDtypeStruct((rows, wide), F32),
            jax.ShapeDtypeStruct((rows, heads), BF16),
        ],
        compiler_params=pltpu.CompilerParams(vmem_limit_bytes=40 * 2**20),
        cost_estimate=pl.CostEstimate(
            flops=2 * rows * width * (wide + heads),
            bytes_accessed=rows * (6 * width + 4 * wide),
            transcendentals=rows,
        ),
        name="start",
    )(
        side[None], tokens, cotangent, gain[None, :], shift[None, :], qkv_weight,
        qkv_bias.astype(F32)[None, :], out_weight,
    )


def layer_kernel(chunks, sides, *refs):
    normed_ref, tok_ref, cot_ref = refs[:3]
    head_refs, refs = refs[3 : 3 + 2 * sides], refs[3 + 2 * sides :]
    weight_refs, gain_ref = refs[: 5 * sides], refs[5 * sides]
    refs = refs[5 * sides + 1 :]
    out_ref, grad_ref, small_ref = refs[:3]
    refs = refs[3:]
    arrays = 5
    grad_outs, core_land = refs[:arrays], refs[arrays : 3 * arrays]
    far_land, side_land = refs[3 * arrays : 5 * arrays], refs[5 * arrays : 6 * arrays]
    refs = refs[6 * arrays :]
    f_ref, g_ref = refs[:2]
    mid_refs, refs = refs[2 : 2 + 3 * sides], refs[2 + 3 * sides :]
    (
        terms, landed, ready, tok_buf, cot_buf,
        term_sem, share_sem, sum_send, sum_recv,
        line_send, line_recv, side_send, side_recv, keep_sem,
        core_send, core_recv, far_send, far_recv, over_send, over_recv,
        back_send, back_recv, load_sem, save_sem,
        part_ref, bias_part, stages, came, small_send, small_recv,
    ) = refs
    share, width = landed.shape[4:]
    count = landed.shape[3] + 1
    chunk_rows = count * share
    rows = chunks * chunk_rows
    where = lax.axis_index("tensor")
    group = lax.axis_index("dp")
    place, side = where // 2, where % 2
    half, core = group // 2, group % 2
    whole_refs = (out_ref, grad_ref)
    factors = []
    for s in range(sides):
        hidden_ref, gate_ref, up_ref = mid_refs[3 * s : 3 * s + 3]
        factors.append(
            (head_refs[2 * s + 1], gate_ref, up_ref, hidden_ref, head_refs[2 * s])
        )
    factors = [factors[x % sides][x // sides] for x in range(arrays * sides)]

    above, below = (group, where + 2), (group, where - 2)
    across = (group, where + 1 - 2 * side)
    other_core = (half * 2 + 1 - core, where)
    other_half = ((1 - half) * 2 + core, where)
    has_above, has_below = place < count - 1, place > 0

    barrier = pltpu.get_barrier_semaphore()

    def greet(target):
        pl.semaphore_signal(barrier, inc=1, device_id=target, device_id_type=pl.DeviceIdType.MESH)

    pl.when(has_above)(lambda: greet(above))
    pl.when(has_below)(lambda: greet(below))
    for target in (across, other_core, other_half):
        greet(target)

    def span(begin, size):
        return pl.ds(pl.multiple_of(begin, size), size)

    def load(c, k):
        source = (f_ref, g_ref)[k].at[span(c * chunk_rows, chunk_rows), :]
        return pltpu.make_async_copy(
            source, terms.at[lax.rem(c, 2), k], term_sem.at[lax.rem(c, 2), k]
        )

    def load_share(c, k):
        begin = span(side * rows + c * chunk_rows + place * share, share)
        source, target = ((tok_ref, tok_buf), (cot_ref, cot_buf))[k]
        return pltpu.make_async_copy(
            source.at[begin, :], target.at[lax.rem(c, 2)], share_sem.at[lax.rem(c, 2), k]
        )

    def remote(source, target, send, recv, device_id):
        return pltpu.make_async_remote_copy(
            src_ref=source, dst_ref=target, send_sem=send, recv_sem=recv,
            device_id=device_id, device_id_type=pl.DeviceIdType.MESH,
        )


    def sum_copy(c, k, way, b, first):
        slot = lax.rem(c, 2)
        target = landed.at[slot, k, way, b - 1 + way]
        source = terms.at[slot, k, span(b * share, share), :] if first else target
        return remote(
            source, target, sum_send.at[slot, k, way, b], sum_recv.at[slot, k, way, b],
            (above, below)[way],
        )

    def place_of(c, b, on_side):
        return span(on_side * rows + c * chunk_rows + b * share, share)

    def line_copy(c, k, b, way, first):
        target = whole_refs[k].at[place_of(c, b, side), :]
        source = ready.at[lax.rem(c, 2), k] if first else target
        return remote(
            source, target, line_send.at[c, k, way, b], line_recv.at[c, k, b],
            (above, below)[way],
        )

    def side_copy(c, k, b, first):
        target = whole_refs[k].at[place_of(c, b, side), :]
        source = ready.at[lax.rem(c, 2), k] if first else target
        return remote(
            source, target, side_send.at[c, k, b], side_recv.at[c, k, b], across
        )

    def keep_copy(c, k):
        return pltpu.make_async_copy(
            ready.at[lax.rem(c, 2), k], whole_refs[k].at[place_of(c, place, side), :],
            keep_sem.at[c, k],
        )

    def each_first(c, k, act):
        @pl.when(jnp.logical_not(has_below))
        def _():
            for b in range(count - 1, 0, -1):
                act(sum_copy(c, k, 0, b, True))

        @pl.when(jnp.logical_not(has_above))
        def _():
            for b in range(count - 1):
                act(sum_copy(c, k, 1, b, True))

    def send_ends(c, k):
        load(c, k).wait()
        each_first(c, k, lambda copy: copy.start())

    def sums_left(c, k):
        for b in range(count):

            @pl.when(has_below & (place < b))
            def _(b=b):
                sum_copy(c, k, 0, b, False).wait_send()

            @pl.when(has_above & (place > b))
            def _(b=b):
                sum_copy(c, k, 1, b, False).wait_send()

    step = min(16, share)

    def add_on(c, k, way, b):
        slot = lax.rem(c, 2)

        def body(i, carry):
            at = span(i * step, step)
            mine = terms[slot, k, span(b * share + i * step, step), :].astype(F32)
            landed[slot, k, way, b - 1 + way, at, :] = (
                mine + landed[slot, k, way, b - 1 + way, at, :].astype(F32)
            ).astype(BF16)
            return carry

        lax.fori_loop(0, share // step, body, 0)

    def sums(c, k, wave):
        ahead = count - 2 - wave
        for way, b, here in (
            (0, place + ahead, has_below & (place + ahead < count)),
            (1, place - ahead, has_above & (place >= ahead)),
        ):

            @pl.when(here)
            def _(way=way, b=b):
                sum_copy(c, k, way, b, False).wait_recv()

                @pl.when(ahead > 0)
                def _():
                    add_on(c, k, way, b)
                    sum_copy(c, k, way, b, False).start()

    def own_left(c, k):
        pl.when(has_above)(lambda: line_copy(c, k, place, 0, True).wait_send())
        pl.when(has_below)(lambda: line_copy(c, k, place, 1, True).wait_send())
        side_copy(c, k, place, True).wait_send()
        keep_copy(c, k).wait()

    def finish(c, k):
        load_share(c, k).wait()
        pl.when(c > 1)(lambda: own_left(c - 2, k))
        slot = lax.rem(c, 2)

        def body(i, carry):
            at = span(i * step, step)
            up = landed[slot, k, 0, jnp.maximum(place - 1, 0), at, :].astype(F32)
            down = landed[slot, k, 1, jnp.minimum(place, count - 2), at, :].astype(F32)
            total = (
                terms[slot, k, span(place * share + i * step, step), :].astype(F32)
                + jnp.where(has_below, up, 0.0)
                + jnp.where(has_above, down, 0.0)
            )
            wide = tok_buf[slot, at, :].astype(F32)
            if k == 0:
                ready[slot, k, at, :] = (wide + total).astype(BF16)
                return carry
            scale = 1.0 / width
            centred = wide - jnp.sum(wide, axis=1, keepdims=True) * scale
            variance = jnp.sum(centred * centred, axis=1, keepdims=True) * scale
            inverse = lax.rsqrt(variance + EPSILON)
            unit = centred * inverse
            scaled = total * gain_ref[0:1, :]
            mean_scaled = jnp.sum(scaled, axis=1, keepdims=True) * scale
            mean_cross = jnp.sum(scaled * unit, axis=1, keepdims=True) * scale
            ready[slot, k, at, :] = (
                cot_buf[slot, at, :].astype(F32)
                + inverse * (scaled - mean_scaled - unit * mean_cross)
            ).astype(BF16)
            gain_term = total * unit
            for r in range(0, step, 8):
                part_ref[0:8, :] += gain_term[r : r + 8, :]
                part_ref[8:16, :] += total[r : r + 8, :]
            return carry

        lax.fori_loop(0, share // step, body, 0)
        pl.when(has_above)(lambda: line_copy(c, k, place, 0, True).start())
        pl.when(has_below)(lambda: line_copy(c, k, place, 1, True).start())
        side_copy(c, k, place, True).start()
        keep_copy(c, k).start()

    def pass_on(c, k, distance):
        for way, b, here in (
            (0, place - distance, place >= distance),
            (1, place + distance, place + distance < count),
        ):

            @pl.when(here)
            def _(way=way, b=b):
                line_copy(c, k, b, way, False).wait_recv()
                pl.when((has_above, has_below)[way])(
                    lambda: line_copy(c, k, b, way, False).start()
                )
                side_copy(c, k, b, False).start()

    def small_copy(n, target):
        return remote(stages.at[n], came.at[n], small_send.at[n], small_recv.at[n], target)

    def small_sums():
        wide = bias_part.shape[2]
        stages[...] = jnp.zeros_like(stages)
        stages[0, 0:1, :] = jnp.sum(part_ref[0:8, :], axis=0, keepdims=True)
        stages[0, 1:2, :] = jnp.sum(part_ref[8:16, :], axis=0, keepdims=True)
        for s in range(sides):
            stages[0, 2 + s : 3 + s, 0:wide] = jnp.sum(bias_part[s], axis=0, keepdims=True)
        for n, target in enumerate((across, other_core, other_half)):
            copy = small_copy(n, target)
            copy.start()
            copy.wait_recv()
            if n == 0:
                stages[1, 0:2, :] = stages[0, 0:2, :] + came[0, 0:2, :]
                stages[1, 2:3, :] = stages[0, 2:3, :] + came[0, 3:4, :]
            else:
                stages[n + 1] = stages[n] + came[n]

        @pl.when(has_below)
        def _():
            small_copy(3, above).wait_recv()
            stages[3] = stages[3] + came[3]

        pl.when(has_above)(lambda: small_copy(3, above).start())
        stages[4] = stages[3]

        @pl.when(has_above)
        def _():
            small_copy(4, below).wait_recv()
            stages[4] = came[4]

        pl.when(has_below)(lambda: small_copy(4, below).start())
        small_ref[...] = stages[4]
        small_ref[2:3, :] = stages[2, 2:3, :] + came[2, 2:3, :]
        for n, target in enumerate((across, other_core, other_half)):
            small_copy(n, target).wait_send()
        pl.when(has_above)(lambda: small_copy(3, above).wait_send())
        pl.when(has_below)(lambda: small_copy(4, below).wait_send())

    waves = count - 1
    every = max(1, waves // 3)
    works = waves // every

    def half_steps(h, live, work):
        c = h // 2

        def one(wave, carry):
            pl.when(lax.rem(wave, every) == 0)(lambda: work(wave // every))
            for k in range(2):

                @pl.when(live & (lax.rem(h, 2) == k))
                def _(k=k):
                    more = c + 1 < chunks

                    @pl.when(wave == 0)
                    def _():
                        @pl.when(c > 0)
                        def _():
                            sums_left(c - 1, k)
                            each_first(c - 1, k, lambda copy: copy.wait_send())

                        pl.when(more)(lambda: load_share(c + 1, k).start())

                    sums(c, k, wave)
                    pl.when(c > 0)(lambda: pass_on(c - 1, k, wave + 1))

                    @pl.when(wave == waves - 1)
                    def _():
                        pl.when(more)(lambda: load(c + 1, k).start())
                        finish(c, k)
                        pl.when(more)(lambda: send_ends(c + 1, k))

            return carry

        lax.fori_loop(0, waves, one, 0)

    tile_halves = -(-sides * (chunks - 1) // works)

    def tiles_scope(*scratch):
        weights = scratch[: 5 * sides]
        scratch = scratch[5 * sides :]
        normed_buf, tile_cot = scratch[:2]
        head_bufs = scratch[2 : 2 + 2 * sides]
        scratch = scratch[2 + 2 * sides :]
        mids, f_buf, g_buf = scratch[: 3 * sides], scratch[3 * sides], scratch[3 * sides + 1]
        f_total, g_total, weight_sem, in_sem, out_sem = scratch[3 * sides + 2 :]

        def weight_copy(x):
            return pltpu.make_async_copy(weight_refs[x], weights[x], weight_sem.at[x])

        def tile_in(i):
            slot = lax.rem(i, 2)
            at = span(i * chunk_rows, chunk_rows)
            at_side = span(side * rows + i * chunk_rows, chunk_rows)
            pairs = [(normed_ref.at[at, :], normed_buf), (cot_ref.at[at_side, :], tile_cot)]
            pairs += [(ref.at[at, :], buf) for ref, buf in zip(head_refs, head_bufs)]
            return [
                pltpu.make_async_copy(ref, buf.at[slot], in_sem.at[slot, x])
                for x, (ref, buf) in enumerate(pairs)
            ]

        def tile_out(i):
            at = span(i * chunk_rows, chunk_rows)
            pairs = list(zip(mids, mid_refs)) + [(f_buf, f_ref), (g_buf, g_ref)]
            return [
                pltpu.make_async_copy(buf, ref.at[at, :], out_sem.at[x])
                for x, (buf, ref) in enumerate(pairs)
            ]

        def wait_out(i):
            for copy in tile_out(i):
                copy.wait()

        def tile(i, s):
            slot = lax.rem(i, 2)
            if s == 0:
                for copy in tile_in(i):
                    copy.wait()

                @pl.when(i + 1 < chunks)
                def _():
                    for copy in tile_in(i + 1):
                        copy.start()

                pl.when(i > 1)(lambda: wait_out(i - 1))

            @pl.when(i == 0)
            def _():
                for x in range(5 * s, 5 * s + 5):
                    weight_copy(x).wait()

            qkv_w, out_w, gate_w, up_w, down_w = weights[5 * s : 5 * s + 5]
            hidden_buf, gate_buf, up_buf = mids[3 * s : 3 * s + 3]
            normed, cot = normed_buf[slot], tile_cot[slot]
            gate = cols_product(normed, gate_w[...])
            up = cols_product(normed, up_w[...])
            sig = 1.0 / (1.0 + jnp.exp(-gate))
            silu = gate * sig
            hidden = (silu * up).astype(BF16)
            hidden_buf[...] = hidden
            grad_hidden = cols_product(cot, down_w[...])
            gate_back = (grad_hidden * up * sig * (1.0 + gate * (1.0 - sig))).astype(BF16)
            up_back = (grad_hidden * silu).astype(BF16)
            gate_buf[...] = gate_back
            up_buf[...] = up_back
            forward = product(hidden, down_w[...])
            forward += product(head_bufs[2 * s][slot], out_w[...])
            backward = product(gate_back, gate_w[...])
            backward += product(up_back, up_w[...])
            qkv_back = head_bufs[2 * s + 1][slot]
            backward += cols_product(qkv_back, qkv_w[...])
            bias_part[s] += (
                qkv_back.astype(F32).reshape(chunk_rows // 8, 8, qkv_back.shape[1]).sum(axis=0)
            )
            if s > 0:
                forward += f_total[...]
                backward += g_total[...]
            if s < sides - 1:
                f_total[...] = forward
                g_total[...] = backward
                return
            f_buf[...] = forward.astype(BF16)
            g_buf[...] = backward.astype(BF16)
            for copy in tile_out(i):
                copy.start()

        def work(turn, n):
            first = turn == 0
            unit = jnp.maximum(works * turn - works, 0) + n
            i = jnp.where(first, 0, 1 + unit // sides)
            part = jnp.where(first, n - works + sides, lax.rem(unit, sides))
            for s in range(sides):
                pl.when((part == s) & (i < chunks))(lambda: tile(i, s))

        for x in range(5 * sides):
            weight_copy(x).start()
        for copy in tile_in(0):
            copy.start()
        for k in range(2):
            load_share(0, k).start()
        part_ref[...] = jnp.zeros_like(part_ref)
        bias_part[...] = jnp.zeros_like(bias_part)
        pl.semaphore_wait(
            barrier, 3 + has_above.astype(jnp.int32) + has_below.astype(jnp.int32)
        )

        def chunk(turn, carry):
            half_steps(
                jnp.maximum(turn, 1) - 1, turn > 0, lambda n: work(turn, n)
            )

            @pl.when(turn == 0)
            def _():
                wait_out(0)
                for k in range(2):
                    load(0, k).start()
                for k in range(2):
                    send_ends(0, k)

            return carry

        lax.fori_loop(0, tile_halves + 1, chunk, 0)
        wait_out(chunks - 1)

    tall = width
    hidden_cols = mid_refs[0].shape[1]
    pl.run_scoped(
        tiles_scope,
        *[pltpu.VMEM(ref.shape, BF16) for ref in weight_refs],
        pltpu.VMEM((2, chunk_rows, width), BF16),
        pltpu.VMEM((2, chunk_rows, width), BF16),
        *[pltpu.VMEM((2, chunk_rows, ref.shape[1]), BF16) for ref in head_refs],
        *[pltpu.VMEM((chunk_rows, hidden_cols), BF16) for _ in mid_refs],
        pltpu.VMEM((chunk_rows, width), BF16),
        pltpu.VMEM((chunk_rows, width), BF16),
        pltpu.VMEM((chunk_rows, width), F32),
        pltpu.VMEM((chunk_rows, width), F32),
        pltpu.SemaphoreType.DMA((5 * sides,)),
        pltpu.SemaphoreType.DMA((2, 2 + 2 * sides)),
        pltpu.SemaphoreType.DMA((3 * sides + 2,)),
    )


    pieces = core_send.shape[2]
    each = 2
    size = tall // pieces

    def grads_scope(*scratch):
        factor_bufs, scratch = scratch[: arrays * sides], scratch[arrays * sides :]
        held, scratch = scratch[: arrays * sides], scratch[arrays * sides :]
        extra, scratch = scratch[: arrays * sides], scratch[arrays * sides :]
        turned, scratch = scratch[: arrays - 1], scratch[arrays - 1 :]
        left_bufs, factor_sem, left_sem = scratch[:2], scratch[2], scratch[3]

        def factor_copy(x):
            return pltpu.make_async_copy(factors[x], factor_bufs[x], factor_sem.at[x])

        def piece(ref, j):
            return ref.at[span(j * size, size), :]

        def piece_of(u):
            owner_core = jnp.where(u < 2 * each, 1 - core, core)
            owner_half = jnp.where((u // each) % 2 == 0, 1 - half, half)
            return (owner_half * 2 + owner_core) * each + lax.rem(u, each)

        def slot_of(u):
            return jnp.where(u < 3 * each, lax.rem(u, each), each + lax.rem(u, each))

        def left_copy(u, which):
            at = span(piece_of(u) * size, size)
            source = (
                normed_ref.at[:, at] if which == 0 else cot_ref.at[span(side * rows, rows), at]
            )
            return pltpu.make_async_copy(
                source, left_bufs[which].at[lax.rem(u, 2)], left_sem.at[which, lax.rem(u, 2)]
            )

        def to_core(a, s, j, slot):
            x = 2 * a + s
            return remote(
                held[x].at[slot], piece(core_land[x], j),
                core_send.at[a, s, j], core_recv.at[a, s, j], other_core,
            )

        def to_far(a, s, i, j):
            x = 2 * a + s
            return remote(
                held[x].at[i], piece(far_land[x], j),
                far_send.at[a, s, j], far_recv.at[a, s, j], other_half,
            )

        def to_over(a, i, j):
            return remote(
                held[2 * a + 1].at[each + i], piece(side_land[a], j),
                over_send.at[a, j], over_recv.at[a, j], across,
            )

        def final_piece(a, j):
            at = span(j * size, size)
            return grad_outs[a].at[:, at] if a else grad_outs[a].at[at, :]

        def final_source(a, i):
            return turned[a - 1].at[i] if a else held[0].at[each + i]

        def back_copy(a, i, j, way, first):
            target = final_piece(a, j)
            source = final_source(a, i) if first else target
            return remote(
                source, target, back_send.at[a, way, j], back_recv.at[a, j],
                (other_core, other_half)[way],
            )

        def save_copy(a, i, j):
            return pltpu.make_async_copy(
                final_source(a, i), final_piece(a, j), save_sem.at[a, i]
            )

        def their_piece(i):
            return ((1 - half) * 2 + core) * each + i

        def my_piece(i):
            return (half * 2 + core) * each + i

        def add_into(target, slot, source):
            def body(i, carry):
                at = span(i * 16, 16)
                target[slot, at, :] = (
                    target[slot, at, :].astype(F32) + source[at, :].astype(F32)
                ).astype(BF16)
                return carry

            lax.fori_loop(0, size // 16, body, 0)

        def fetch(lands, j, ids):
            copies = [
                pltpu.make_async_copy(piece(lands[n], j), extra[x], load_sem.at[x])
                for n, x in enumerate(ids)
            ]
            for copy in copies:
                copy.start()
            for copy in copies:
                copy.wait()

        everything = range(2 * arrays)

        def make(u, which):
            @pl.when(u == 0)
            def _():
                for x in everything:
                    if (x // 2 < 3) == (which == 0):
                        factor_copy(x).wait()

            left_copy(u, which).wait()
            pl.when(u + 1 < pieces)(lambda: left_copy(u + 1, which).start())
            slot = slot_of(u)
            left = left_bufs[which][lax.rem(u, 2)].T

            @pl.when((u >= each) & (u < 3 * each))
            def _():
                for x in everything:
                    if (x // 2 < 3) == (which == 0):
                        to_core(x // 2, x % 2, piece_of(u - each), slot).wait_send()

            for x in everything:
                if (x // 2 < 3) == (which == 0):
                    held[x][slot] = product(left, factor_bufs[x][...]).astype(BF16)

            @pl.when(u < 2 * each)
            def _():
                for x in everything:
                    if (x // 2 < 3) == (which == 0):
                        to_core(x // 2, x % 2, piece_of(u), slot).start()

        def gather_terms(slot, j):
            for x in everything:
                to_core(x // 2, x % 2, j, 0).wait_recv()
            fetch(core_land, j, everything)
            for x in everything:
                add_into(held[x], slot, extra[x])

        def grads_far(i):
            j = their_piece(i)
            gather_terms(i, j)
            for x in everything:
                to_far(x // 2, x % 2, i, j).start()

        def grads_over(i):
            j = my_piece(i)
            gather_terms(each + i, j)
            for x in everything:
                to_far(x // 2, x % 2, i, j).wait_recv()
            fetch(far_land, j, everything)
            for a in range(arrays):
                add_into(held[2 * a + 1], each + i, extra[2 * a + 1])
                to_over(a, i, j).start()
            for a in range(arrays):
                add_into(held[2 * a], each + i, extra[2 * a])

        def grads_back(i):
            j = my_piece(i)
            for a in range(arrays):
                to_over(a, i, j).wait_recv()
            fetch(side_land, j, range(0, 2 * arrays, 2))
            for a in range(arrays):
                if a:
                    total = held[2 * a][each + i].astype(F32) + extra[2 * a][...].astype(F32)
                    turned[a - 1][i] = total.T.astype(BF16)
                else:
                    add_into(held[0], each + i, extra[0])
                back_copy(a, i, j, 1, True).start()
                back_copy(a, i, j, 0, True).start()
                save_copy(a, i, j).start()

        def grads_pass(i):
            j = their_piece(i)
            for a in range(arrays):
                back_copy(a, i, j, 1, False).wait_recv()
                back_copy(a, i, j, 0, False).start()

        def grads_drain():
            for i in range(each):
                mine, theirs = my_piece(i), their_piece(i)
                for a in range(arrays):
                    for s in range(2):
                        to_far(a, s, i, theirs).wait_send()
                    to_over(a, i, mine).wait_send()
                    back_copy(a, i, mine, 1, True).wait_send()
                    back_copy(a, i, mine, 0, True).wait_send()
                    back_copy(a, i, theirs, 0, False).wait_send()
                    save_copy(a, i, mine).wait()
            for u in range(2 * each):
                for a in range(arrays):
                    back_copy(a, 0, piece_of(u), 0, False).wait_recv()

        events = {
            25: (grads_far, 0),
            28: (grads_far, 1),
            34: (grads_over, 0),
            39: (grads_over, 1),
            41: (grads_back, 0),
            46: (grads_back, 1),
        }

        def work(h, n):
            v = works * (h - tile_halves) + n
            for which in range(2):
                pl.when((v < 2 * pieces) & (lax.rem(v, 2) == which))(
                    lambda: make(v // 2, which)
                )
            for at, (act, i) in events.items():
                pl.when(works * h + n == at)(lambda: act(i))

        for x in everything:
            factor_copy(x).start()
        for which in range(2):
            left_copy(0, which).start()

        def chunk(c, carry):
            half_steps(c, c >= 0, lambda n: work(c, n))
            return carry

        lax.fori_loop(tile_halves, 2 * chunks, chunk, 0)
        for distance in range(1, count):
            pass_on(chunks - 1, 0, distance)
            pass_on(chunks - 1, 1, distance)
        small_sums()
        for i in range(each):
            grads_pass(i)
        grads_drain()

    factor_shapes = [ref.shape for ref in factors]
    pl.run_scoped(
        grads_scope,
        *[pltpu.VMEM(shape, BF16) for shape in factor_shapes],
        *[pltpu.VMEM((2 * each, size, shape[1]), BF16) for shape in factor_shapes],
        *[pltpu.VMEM((size, shape[1]), BF16) for shape in factor_shapes],
        *[pltpu.VMEM((each, shape[1], size), BF16) for shape in factor_shapes[2::2]],
        pltpu.VMEM((2, rows, size), BF16),
        pltpu.VMEM((2, rows, size), BF16),
        pltpu.SemaphoreType.DMA((2 * arrays,)),
        pltpu.SemaphoreType.DMA((2, 2)),
    )

    for k in range(2):
        sums_left(chunks - 1, k)
        each_first(chunks - 1, k, lambda copy: copy.wait_send())
        own_left(chunks - 2, k)
        own_left(chunks - 1, k)

    def drain(c, carry):
        for k in range(2):
            for b in range(count):
                pl.when((place > b) & has_above)(
                    lambda: line_copy(c, k, b, 0, False).wait_send()
                )
                pl.when((place < b) & has_below)(
                    lambda: line_copy(c, k, b, 1, False).wait_send()
                )
                pl.when(place != b)(lambda: side_copy(c, k, b, False).wait_send())
                side_copy(c, k, b, False).wait_recv()
        return carry

    lax.fori_loop(0, chunks, drain, 0)


def layer(normed, tokens, cotangent, heads, weights, gain, count, chunks, dp_size):
    row_count, width = tokens.shape
    rows = row_count // 2
    share = rows // chunks // count
    sides, arrays = len(weights), 5
    pieces = 2 * dp_size
    sem = pltpu.SemaphoreType.DMA
    flat_heads = [array for group in heads for array in group]
    flat_weights = [array for side in weights for array in side]
    hidden = weights[0][2].shape[0]
    columns = [heads[0][1].shape[1], hidden, hidden, hidden, heads[0][0].shape[1]]
    whole = jax.ShapeDtypeStruct(tokens.shape, BF16)
    half_sums = [jax.ShapeDtypeStruct((width, n), BF16) for n in columns]
    finals = half_sums[:1] + [jax.ShapeDtypeStruct((n, width), BF16) for n in columns[1:]]
    lands = [shape for shape in half_sums for _ in range(sides)]
    anywhere = pl.BlockSpec(memory_space=pl.ANY)
    vmem = pl.BlockSpec(memory_space=pltpu.VMEM)
    own_rows = [jax.ShapeDtypeStruct((rows, width), BF16)] * 2
    own_rows += [jax.ShapeDtypeStruct((rows, hidden), BF16)] * (3 * sides)
    outs = pl.pallas_call(
        functools.partial(layer_kernel, chunks, sides),
        in_specs=[anywhere] * (3 + len(flat_heads) + len(flat_weights)) + [vmem],
        out_specs=[anywhere, anywhere, vmem] + [anywhere] * (6 * arrays + len(own_rows)),
        out_shape=[whole, whole, jax.ShapeDtypeStruct((8, width), F32)]
        + finals + lands + lands + half_sums + own_rows,
        scratch_shapes=[
            pltpu.VMEM((2, 2, count * share, width), BF16),
            pltpu.VMEM((2, 2, 2, count - 1, share, width), BF16),
            pltpu.VMEM((2, 2, share, width), BF16),
            pltpu.VMEM((2, share, width), BF16),
            pltpu.VMEM((2, share, width), BF16),
            sem((2, 2)),
            sem((2, 2)),
            sem((2, 2, 2, count)),
            sem((2, 2, 2, count)),
            sem((chunks, 2, 2, count)),
            sem((chunks, 2, count)),
            sem((chunks, 2, count)),
            sem((chunks, 2, count)),
            sem((chunks, 2)),
            sem((arrays, 2, pieces)),
            sem((arrays, 2, pieces)),
            sem((arrays, 2, pieces)),
            sem((arrays, 2, pieces)),
            sem((arrays, pieces)),
            sem((arrays, pieces)),
            sem((arrays, 2, pieces)),
            sem((arrays, pieces)),
            sem((2 * arrays,)),
            sem((arrays, 2)),
            pltpu.VMEM((16, width), F32),
            pltpu.VMEM((sides, 8, columns[0]), F32),
            pltpu.VMEM((5, 8, width), F32),
            pltpu.VMEM((5, 8, width), F32),
            sem((5,)),
            sem((5,)),
        ],
        compiler_params=pltpu.CompilerParams(
            collective_id=0, has_side_effects=True, vmem_limit_bytes=63 * 2**20
        ),
        cost_estimate=pl.CostEstimate(
            flops=6 * rows * sum(array.size for array in flat_weights),
            bytes_accessed=800 * 2**20,
            transcendentals=0,
        ),
        name="layer",
    )(normed, tokens, cotangent, *flat_heads, *flat_weights, gain)
    out, grad, small = outs[:3]
    return out, grad, small[0], small[1], small[2, : columns[0]], outs[3 : 3 + arrays]


def body(
    tokens,
    lengths,
    norm_gain,
    norm_shift,
    qkv_weight,
    qkv_bias,
    out_weight,
    gate_weight,
    up_weight,
    down_weight,
    cotangent,
):
    tensor_size = lax.axis_size("tensor")
    dp_size = lax.axis_size("dp")
    count = tensor_size // 2
    where = lax.axis_index("tensor")
    dp_place = lax.axis_index("dp")
    side = where % 2
    across = [(i, i ^ 1) for i in range(tensor_size)]
    row_count, width = tokens.shape
    rows = row_count // 2
    chunk_count = 8

    def partner(weights, before, after):
        parts = []
        for weight in weights:
            part = weight.shape[0] // dp_size
            parts.append(lax.dynamic_slice_in_dim(weight, dp_place * part, part, 0))
        parts, _ = lax.optimization_barrier((parts, before))
        parts = [lax.ppermute(part, "tensor", across) for part in parts]
        parts, _ = lax.optimization_barrier((parts, after))
        return [lax.all_gather(part, "dp", axis=0, tiled=True) for part in parts]

    head_weights = (qkv_weight, out_weight)
    mid_weights = (gate_weight.T, up_weight.T, down_weight)
    biases = (qkv_bias, lax.ppermute(qkv_bias, "tensor", across))

    length = lax.dynamic_slice_in_dim(lengths, side, 1, 0)
    normed, *own_group = start(
        side, tokens, cotangent, norm_gain, norm_shift, qkv_weight, qkv_bias, out_weight
    )
    own_cot = lax.dynamic_slice_in_dim(cotangent, side * rows, rows, 0)
    tables = rotary_tables(rows)
    even = (out_weight.shape[0] // HEAD) % 2 == 0

    def project(weights, bias):
        return (
            product(normed, weights[0]) + bias.astype(F32),
            cols_product(own_cot, weights[1]).astype(BF16),
        )

    other_heads = partner(head_weights, (), normed)
    if even:
        heads = [attention(length, *own_group, *tables)]
        other_mid = partner(mid_weights, normed, heads[0])
        heads.append(attention(length, *project(other_heads, biases[1]), *tables))
    else:
        other_mid = partner(mid_weights, normed, ())
        pairs = zip(own_group, project(other_heads, biases[1]))
        attended, qkv_back = attention(
            length, *[jnp.concatenate(pair, axis=1) for pair in pairs], *tables
        )
        cut, wide = out_weight.shape[0], qkv_weight.shape[1]
        heads = [
            (attended[:, s * cut : (s + 1) * cut], qkv_back[:, s * wide : (s + 1) * wide])
            for s in range(2)
        ]
    weights = [(*head_weights, *mid_weights), (*other_heads, *other_mid)]
    layer_out, grad_tokens, gain_part, shift_part, grad_bias, grads = layer(
        normed, tokens, cotangent, heads, weights, norm_gain[None, :], count, chunk_count, dp_size
    )
    grad_qkv, grad_gate, grad_up, grad_down, grad_out = [grad.astype(F32) for grad in grads]
    grad_gate, grad_up = grad_gate.T, grad_up.T
    return (
        layer_out,
        grad_tokens,
        gain_part,
        shift_part,
        grad_qkv,
        grad_bias,
        grad_out,
        grad_gate,
        grad_up,
        grad_down,
    )


def solution(mesh):
    placed = (
        P("dp", None),
        P("dp"),
        P(),
        P(),
        P(None, "tensor"),
        P("tensor"),
        P("tensor", None),
        P(None, "tensor"),
        P(None, "tensor"),
        P("tensor", None),
        P("dp", None),
    )
    return jax.shard_map(
        body,
        mesh=mesh,
        in_specs=placed,
        out_specs=(
            P("dp", None),
            P("dp", None),
            P(),
            P(),
            P(None, "tensor"),
            P("tensor"),
            P("tensor", None),
            P(None, "tensor"),
            P(None, "tensor"),
            P("tensor", None),
        ),
        check_vma=False,
    )
```

```python
import functools

import jax
import jax.numpy as jnp
from jax import lax
from jax.experimental import pallas as pl
from jax.experimental.pallas import tpu as pltpu
from jax.sharding import PartitionSpec as P

HEAD = 64
ROT = 16
PAIR = 2 * HEAD
TRIPLE = 6 * HEAD

EPSILON = 1e-05
NEGATIVE = -1e30
F32 = jnp.float32
BF16 = jnp.bfloat16


def rows_product(former, latter):
    return lax.dot_general(
        former, latter, (((0,), (0,)), ((), ())), preferred_element_type=F32
    )


def cols_product(former, latter):
    return lax.dot_general(
        former, latter, (((1,), (1,)), ((), ())), preferred_element_type=F32
    )


def product(former, latter):
    return jnp.dot(former, latter, preferred_element_type=F32)


def rotary_tables(seq_len):
    frequency = 10000.0 ** (-jnp.arange(0, ROT, 2).astype(F32) / ROT)
    angles = jnp.arange(seq_len).astype(F32)[:, None] * frequency[None, :]
    cosine, sine = jnp.cos(angles), jnp.sin(angles)
    still = HEAD - ROT
    cos_head = jnp.concatenate([cosine, cosine, jnp.ones((seq_len, still), F32)], axis=1)
    sin_head = jnp.concatenate([-sine, sine, jnp.zeros((seq_len, still), F32)], axis=1)
    return jnp.tile(cos_head, (1, 2)), jnp.tile(sin_head, (1, 2))


def attention_kernel(
    len_ref, qkv_ref, grad_ref, cos_ref, sin_ref, att_ref, back_ref,
    score, expo, query, key_value, key_value_t, query_t, grad_query, grad_kv_t,
):
    seq_len = qkv_ref.shape[0]
    block = score.shape[1]
    steps = seq_len // block
    length = len_ref[0]
    lane = lax.broadcasted_iota(jnp.int32, (block, PAIR), 1)
    left = lane < HEAD
    near = lax.rem(lane, HEAD) < ROT // 2

    def turn(tile, cosine, sine):
        swapped = jnp.where(
            near, pltpu.roll(tile, PAIR - ROT // 2, 1), pltpu.roll(tile, ROT // 2, 1)
        )
        return tile * cosine + swapped * sine

    def tables(rows):
        cosine, sine = cos_ref[rows, :], sin_ref[rows, :]
        return (
            (cosine, sine),
            (jnp.where(left, 1.0, cosine), jnp.where(left, 0.0, sine)),
            (jnp.where(left, cosine, 1.0), jnp.where(left, sine, 0.0)),
        )

    def prepare(i, carry):
        rows = pl.ds(pl.multiple_of(i * block, block), block)
        tabs = tables(rows)
        first = turn(qkv_ref[rows, 0:PAIR], *tabs[0])
        second = turn(qkv_ref[rows, PAIR : 2 * PAIR], *tabs[1])
        third = turn(qkv_ref[rows, 2 * PAIR : 3 * PAIR], *tabs[2])
        scale = HEAD**-0.5
        first_q = first.astype(BF16).astype(F32) * scale
        second_q = second.astype(BF16).astype(F32) * scale
        query[0, rows, :] = jnp.where(left, 0.0, pltpu.roll(first_q, HEAD, 1)).astype(BF16)
        query[1, rows, :] = jnp.where(left, pltpu.roll(second_q, HEAD, 1), 0.0).astype(BF16)
        for h, tile in enumerate((jnp.where(left, second, first), third)):
            key_value[h, rows, :] = tile.astype(BF16)
            key_value_t[h, :, rows] = tile.T.astype(BF16)
        query_t[0, :, rows] = first_q.T[0:HEAD, :].astype(BF16)
        query_t[1, :, rows] = second_q.T[HEAD:PAIR, :].astype(BF16)
        zero = jnp.zeros((block, PAIR), F32)
        grad_query[rows, :] = zero
        att_ref[rows, :] = zero.astype(BF16)
        for h in range(2):
            grad_kv_t[h, :, rows] = jnp.zeros((PAIR, block), F32)
        return carry

    lax.fori_loop(0, steps, prepare, 0)

    def fold(tile, op):
        out = tile[:, 0:PAIR]
        for c in range(1, block // PAIR):
            out = op(out, tile[:, c * PAIR : (c + 1) * PAIR])
        return out

    def block_rows(i):
        rows = pl.ds(i * block, block)
        spans = [pl.ds(j * block, block) for j in range(i + 1)]
        q_block = [query[h, rows, :] for h in range(2)]
        below = lax.broadcasted_iota(jnp.int32, (block, block), 1) <= lax.broadcasted_iota(
            jnp.int32, (block, block), 0
        )
        maxima = []
        for h in range(2):
            top = None
            for j, cols in enumerate(spans):
                tile = product(q_block[h], key_value_t[h, :, cols])
                if j == i:
                    tile = jnp.where(below, tile, NEGATIVE)
                score[h, :, cols] = tile
                high = fold(tile, jnp.maximum)
                top = high if top is None else jnp.maximum(top, high)
            maxima.append(jnp.max(top, axis=1, keepdims=True))

        mixed, inverse = [], []
        for h in range(2):
            mixture = total = None
            for cols in spans:
                tile = jnp.exp(score[h, :, cols] - maxima[h])
                low = tile.astype(BF16)
                expo[h, :, cols] = low
                part = product(low, key_value[h, cols, :])
                amount = fold(tile, jnp.add)
                mixture = part if mixture is None else mixture + part
                total = amount if total is None else total + amount
            mixed.append(mixture)
            inverse.append(1.0 / jnp.sum(total, axis=1, keepdims=True))

        place = i * block + lax.broadcasted_iota(jnp.int32, (block, 1), 0)
        valid = (place < length).astype(F32)
        mixture = jnp.where(left, mixed[0] * inverse[0], mixed[1] * inverse[1]) * valid
        att_ref[rows, :] = mixture.astype(BF16)
        upstream = grad_ref[rows, :].astype(F32) * valid
        inner = upstream * mixture
        scale = HEAD**-0.5
        turned = []
        for h in range(2):
            own = left if h == 0 else jnp.logical_not(left)
            inner_sum = jnp.sum(jnp.where(own, inner, 0.0), axis=1, keepdims=True) * inverse[h]
            mine = jnp.where(own, upstream * inverse[h], 0.0)
            scaled = mine.astype(BF16)
            half = slice(0, HEAD) if h == 0 else slice(HEAD, PAIR)
            scaled_t = mine.T[half, :].astype(BF16)
            queries_t = query_t[h, :, rows]
            grad = None
            for cols in spans:
                low = expo[h, :, cols]
                grad_weight = product(scaled, key_value_t[h, :, cols])
                grad_score = (low.astype(F32) * (grad_weight - inner_sum)).astype(BF16)
                part = product(grad_score, key_value[h, cols, :])
                grad = part if grad is None else grad + part
                key_at, value_at = (HEAD, 0) if h == 0 else (0, HEAD)
                grad_kv_t[h, key_at : key_at + HEAD, cols] += product(queries_t, grad_score)
                grad_kv_t[h, value_at : value_at + HEAD, cols] += product(scaled_t, low)
            turned.append(pltpu.roll(grad, HEAD, 1))
        grad_query[rows, :] = jnp.where(left, turned[0], turned[1]) * scale

    for i in range(steps):
        pl.when(i * block < length)(functools.partial(block_rows, i))

    def finish(i, carry):
        rows = pl.ds(pl.multiple_of(i * block, block), block)
        tabs = tables(rows)
        gq = grad_query[rows, :]
        low_kv = grad_kv_t[0, :, rows].T
        high_kv = grad_kv_t[1, :, rows].T
        tiles = (jnp.where(left, gq, low_kv), jnp.where(left, low_kv, gq), high_kv)
        for c in range(3):
            back_ref[rows, c * PAIR : (c + 1) * PAIR] = turn(
                tiles[c], tabs[c][0], -tabs[c][1]
            ).astype(BF16)
        return carry

    lax.fori_loop(0, steps, finish, 0)


def attention(length, qkv, grad_mixture, cosine, sine):
    seq_len, width = qkv.shape
    pairs = width // TRIPLE
    block = min(512, seq_len)
    flops = 6 * 2 * (2 * pairs) * seq_len * seq_len * PAIR
    return pl.pallas_call(
        attention_kernel,
        grid=(pairs,),
        in_specs=[
            pl.BlockSpec(memory_space=pltpu.SMEM),
            pl.BlockSpec((seq_len, TRIPLE), lambda g: (0, g)),
            pl.BlockSpec((seq_len, PAIR), lambda g: (0, g)),
            pl.BlockSpec((seq_len, PAIR), lambda g: (0, 0)),
            pl.BlockSpec((seq_len, PAIR), lambda g: (0, 0)),
        ],
        out_specs=[
            pl.BlockSpec((seq_len, PAIR), lambda g: (0, g)),
            pl.BlockSpec((seq_len, TRIPLE), lambda g: (0, g)),
        ],
        out_shape=[
            jax.ShapeDtypeStruct((seq_len, pairs * PAIR), BF16),
            jax.ShapeDtypeStruct((seq_len, width), BF16),
        ],
        scratch_shapes=[
            pltpu.VMEM((2, block, seq_len), F32),
            pltpu.VMEM((2, block, seq_len), BF16),
            pltpu.VMEM((2, seq_len, PAIR), BF16),
            pltpu.VMEM((2, seq_len, PAIR), BF16),
            pltpu.VMEM((2, PAIR, seq_len), BF16),
            pltpu.VMEM((2, HEAD, seq_len), BF16),
            pltpu.VMEM((seq_len, PAIR), F32),
            pltpu.VMEM((2, PAIR, seq_len), F32),
        ],
        compiler_params=pltpu.CompilerParams(vmem_limit_bytes=48 * 2**20),
        cost_estimate=pl.CostEstimate(
            flops=flops,
            bytes_accessed=seq_len * width * 8,
            transcendentals=2 * pairs * seq_len * seq_len // 2,
        ),
        name="attention",
    )(length, qkv, grad_mixture, cosine, sine)


def start_kernel(
    side_ref, tok_ref, cot_ref, gain_ref, shift_ref, qkv_w, bias_ref, out_w,
    normed_ref, qkv_ref, grad_ref,
):
    wide = tok_ref[...].astype(F32)
    centred = wide - jnp.mean(wide, axis=1, keepdims=True)
    variance = jnp.mean(centred * centred, axis=1, keepdims=True)
    unit = centred * lax.rsqrt(variance + EPSILON)
    normed = (unit * gain_ref[...] + shift_ref[...]).astype(BF16)
    normed_ref[...] = normed
    qkv_ref[...] = product(normed, qkv_w[...]) + bias_ref[...]
    grad_ref[...] = cols_product(cot_ref[...], out_w[...]).astype(BF16)


def project_kernel(side_ref, normed_ref, cot_ref, qkv_w, bias_ref, out_w, qkv_ref, grad_ref):
    qkv_ref[...] = product(normed_ref[...], qkv_w[...]) + bias_ref[...]
    grad_ref[...] = cols_product(cot_ref[...], out_w[...]).astype(BF16)


def project(side, rows_in, cotangent, norm, weights, bias):
    rows, width = cotangent.shape[0] // 2, cotangent.shape[1]
    tile = min(256, rows)
    tiles = rows // tile
    qkv_weight, out_weight = weights
    heads, wide = out_weight.shape[0], qkv_weight.shape[1]

    def sided(i, side_ref):
        return (side_ref[0] * tiles + i, 0)

    def fixed(i, side_ref):
        return (0, 0)

    def rowed(i, side_ref):
        return (i, 0)

    flat = [part[None, :] for part in norm]
    flat += [qkv_weight, bias.astype(F32)[None, :], out_weight]
    outs = [((rows, wide), F32), ((rows, heads), BF16)]
    if norm:
        outs = [((rows, width), BF16)] + outs
    return pl.pallas_call(
        start_kernel if norm else project_kernel,
        grid_spec=pltpu.PrefetchScalarGridSpec(
            num_scalar_prefetch=1,
            grid=(tiles,),
            in_specs=[
                pl.BlockSpec((tile, width), sided if norm else rowed),
                pl.BlockSpec((tile, width), sided),
            ]
            + [pl.BlockSpec(array.shape, fixed) for array in flat],
            out_specs=[pl.BlockSpec((tile, shape[1]), rowed) for shape, _ in outs],
        ),
        out_shape=[jax.ShapeDtypeStruct(*out) for out in outs],
        compiler_params=pltpu.CompilerParams(vmem_limit_bytes=40 * 2**20),
        cost_estimate=pl.CostEstimate(
            flops=2 * rows * width * (wide + heads),
            bytes_accessed=rows * (6 * width + 4 * wide),
            transcendentals=rows,
        ),
        name="project",
    )(side[None], rows_in, cotangent, *flat)


def layer_kernel(chunks, sides, *refs):
    normed_ref, tok_ref, cot_ref = refs[:3]
    head_refs, refs = refs[3 : 3 + 2 * sides], refs[3 + 2 * sides :]
    own_weights, other_heads, other_mid, gain_ref = refs[:5], refs[5:7], refs[7], refs[8]
    refs = refs[9:]
    out_ref, grad_ref, small_ref = refs[:3]
    refs = refs[3:]
    arrays = 5
    grad_outs, core_land = refs[:arrays], refs[arrays : 3 * arrays]
    far_land, side_land = refs[3 * arrays : 5 * arrays], refs[5 * arrays : 6 * arrays]
    refs = refs[6 * arrays :]
    f_ref, g_ref = refs[:2]
    mid_refs, refs = refs[2 : 2 + 3 * sides], refs[2 + 3 * sides :]
    (
        terms, landed, ready, tok_buf, cot_buf,
        term_sem, share_sem, sum_send, sum_recv,
        line_send, line_recv, side_send, side_recv, keep_sem,
        core_send, core_recv, far_send, far_recv, over_send, over_recv,
        back_send, back_recv, load_sem, save_sem,
        part_ref, bias_part, stages, came, small_send, small_recv,
    ) = refs
    share, width = landed.shape[4:]
    count = landed.shape[3] + 1
    chunk_rows = count * share
    rows = chunks * chunk_rows
    where = lax.axis_index("tensor")
    group = lax.axis_index("dp")
    place, side = where // 2, where % 2
    half, core = group // 2, group % 2
    whole_refs = (out_ref, grad_ref)
    factors = []
    for s in range(sides):
        hidden_ref, gate_ref, up_ref = mid_refs[3 * s : 3 * s + 3]
        factors.append(
            (head_refs[2 * s + 1], gate_ref, up_ref, hidden_ref, head_refs[2 * s])
        )
    factors = [factors[x % sides][x // sides] for x in range(arrays * sides)]

    above, below = (group, where + 2), (group, where - 2)
    across = (group, where + 1 - 2 * side)
    other_core = (half * 2 + 1 - core, where)
    other_half = ((1 - half) * 2 + core, where)
    has_above, has_below = place < count - 1, place > 0

    barrier = pltpu.get_barrier_semaphore()

    def greet(target):
        pl.semaphore_signal(barrier, inc=1, device_id=target, device_id_type=pl.DeviceIdType.MESH)

    pl.when(has_above)(lambda: greet(above))
    pl.when(has_below)(lambda: greet(below))
    for target in (across, other_core, other_half):
        greet(target)

    def span(begin, size):
        return pl.ds(pl.multiple_of(begin, size), size)

    def load(c, k):
        source = (f_ref, g_ref)[k].at[span(c * chunk_rows, chunk_rows), :]
        return pltpu.make_async_copy(
            source, terms.at[lax.rem(c, 2), k], term_sem.at[lax.rem(c, 2), k]
        )

    def load_share(c, k):
        begin = span(side * rows + c * chunk_rows + place * share, share)
        source, target = ((tok_ref, tok_buf), (cot_ref, cot_buf))[k]
        return pltpu.make_async_copy(
            source.at[begin, :], target.at[lax.rem(c, 2)], share_sem.at[lax.rem(c, 2), k]
        )

    def remote(source, target, send, recv, device_id):
        return pltpu.make_async_remote_copy(
            src_ref=source, dst_ref=target, send_sem=send, recv_sem=recv,
            device_id=device_id, device_id_type=pl.DeviceIdType.MESH,
        )


    def sum_copy(c, k, way, b, first):
        slot = lax.rem(c, 2)
        target = landed.at[slot, k, way, b - 1 + way]
        source = terms.at[slot, k, span(b * share, share), :] if first else target
        return remote(
            source, target, sum_send.at[slot, k, way, b], sum_recv.at[slot, k, way, b],
            (above, below)[way],
        )

    def place_of(c, b, on_side):
        return span(on_side * rows + c * chunk_rows + b * share, share)

    def line_copy(c, k, b, way, first):
        target = whole_refs[k].at[place_of(c, b, side), :]
        source = ready.at[lax.rem(c, 2), k] if first else target
        return remote(
            source, target, line_send.at[c, k, way, b], line_recv.at[c, k, b],
            (above, below)[way],
        )

    def side_copy(c, k, b, first):
        target = whole_refs[k].at[place_of(c, b, side), :]
        source = ready.at[lax.rem(c, 2), k] if first else target
        return remote(
            source, target, side_send.at[c, k, b], side_recv.at[c, k, b], across
        )

    def keep_copy(c, k):
        return pltpu.make_async_copy(
            ready.at[lax.rem(c, 2), k], whole_refs[k].at[place_of(c, place, side), :],
            keep_sem.at[c, k],
        )

    def each_first(c, k, act):
        @pl.when(jnp.logical_not(has_below))
        def _():
            for b in range(count - 1, 0, -1):
                act(sum_copy(c, k, 0, b, True))

        @pl.when(jnp.logical_not(has_above))
        def _():
            for b in range(count - 1):
                act(sum_copy(c, k, 1, b, True))

    def send_ends(c, k):
        load(c, k).wait()
        each_first(c, k, lambda copy: copy.start())

    def sums_left(c, k):
        for b in range(count):

            @pl.when(has_below & (place < b))
            def _(b=b):
                sum_copy(c, k, 0, b, False).wait_send()

            @pl.when(has_above & (place > b))
            def _(b=b):
                sum_copy(c, k, 1, b, False).wait_send()

    step = min(16, share)

    def add_on(c, k, way, b):
        slot = lax.rem(c, 2)

        def body(i, carry):
            at = span(i * step, step)
            mine = terms[slot, k, span(b * share + i * step, step), :].astype(F32)
            landed[slot, k, way, b - 1 + way, at, :] = (
                mine + landed[slot, k, way, b - 1 + way, at, :].astype(F32)
            ).astype(BF16)
            return carry

        lax.fori_loop(0, share // step, body, 0)

    def sums(c, k, wave):
        ahead = count - 2 - wave
        for way, b, here in (
            (0, place + ahead, has_below & (place + ahead < count)),
            (1, place - ahead, has_above & (place >= ahead)),
        ):

            @pl.when(here)
            def _(way=way, b=b):
                sum_copy(c, k, way, b, False).wait_recv()

                @pl.when(ahead > 0)
                def _():
                    add_on(c, k, way, b)
                    sum_copy(c, k, way, b, False).start()

    def own_left(c, k):
        pl.when(has_above)(lambda: line_copy(c, k, place, 0, True).wait_send())
        pl.when(has_below)(lambda: line_copy(c, k, place, 1, True).wait_send())
        side_copy(c, k, place, True).wait_send()
        keep_copy(c, k).wait()

    def finish(c, k):
        load_share(c, k).wait()
        pl.when(c > 1)(lambda: own_left(c - 2, k))
        slot = lax.rem(c, 2)

        def body(i, carry):
            at = span(i * step, step)
            up = landed[slot, k, 0, jnp.maximum(place - 1, 0), at, :].astype(F32)
            down = landed[slot, k, 1, jnp.minimum(place, count - 2), at, :].astype(F32)
            total = (
                terms[slot, k, span(place * share + i * step, step), :].astype(F32)
                + jnp.where(has_below, up, 0.0)
                + jnp.where(has_above, down, 0.0)
            )
            wide = tok_buf[slot, at, :].astype(F32)
            if k == 0:
                ready[slot, k, at, :] = (wide + total).astype(BF16)
                return carry
            scale = 1.0 / width
            centred = wide - jnp.sum(wide, axis=1, keepdims=True) * scale
            variance = jnp.sum(centred * centred, axis=1, keepdims=True) * scale
            inverse = lax.rsqrt(variance + EPSILON)
            unit = centred * inverse
            scaled = total * gain_ref[0:1, :]
            mean_scaled = jnp.sum(scaled, axis=1, keepdims=True) * scale
            mean_cross = jnp.sum(scaled * unit, axis=1, keepdims=True) * scale
            ready[slot, k, at, :] = (
                cot_buf[slot, at, :].astype(F32)
                + inverse * (scaled - mean_scaled - unit * mean_cross)
            ).astype(BF16)
            gain_term = total * unit
            for r in range(0, step, 8):
                part_ref[0:8, :] += gain_term[r : r + 8, :]
                part_ref[8:16, :] += total[r : r + 8, :]
            return carry

        lax.fori_loop(0, share // step, body, 0)
        pl.when(has_above)(lambda: line_copy(c, k, place, 0, True).start())
        pl.when(has_below)(lambda: line_copy(c, k, place, 1, True).start())
        side_copy(c, k, place, True).start()
        keep_copy(c, k).start()

    def pass_on(c, k, distance):
        for way, b, here in (
            (0, place - distance, place >= distance),
            (1, place + distance, place + distance < count),
        ):

            @pl.when(here)
            def _(way=way, b=b):
                line_copy(c, k, b, way, False).wait_recv()
                pl.when((has_above, has_below)[way])(
                    lambda: line_copy(c, k, b, way, False).start()
                )
                side_copy(c, k, b, False).start()

    def small_copy(n, target):
        return remote(stages.at[n], came.at[n], small_send.at[n], small_recv.at[n], target)

    def small_sums():
        wide = bias_part.shape[2]
        stages[...] = jnp.zeros_like(stages)
        stages[0, 0:1, :] = jnp.sum(part_ref[0:8, :], axis=0, keepdims=True)
        stages[0, 1:2, :] = jnp.sum(part_ref[8:16, :], axis=0, keepdims=True)
        for s in range(sides):
            stages[0, 2 + s : 3 + s, 0:wide] = jnp.sum(bias_part[s], axis=0, keepdims=True)
        for n, target in enumerate((across, other_core, other_half)):
            copy = small_copy(n, target)
            copy.start()
            copy.wait_recv()
            if n == 0:
                stages[1, 0:2, :] = stages[0, 0:2, :] + came[0, 0:2, :]
                stages[1, 2:3, :] = stages[0, 2:3, :] + came[0, 3:4, :]
            else:
                stages[n + 1] = stages[n] + came[n]

        @pl.when(has_below)
        def _():
            small_copy(3, above).wait_recv()
            stages[3] = stages[3] + came[3]

        pl.when(has_above)(lambda: small_copy(3, above).start())
        stages[4] = stages[3]

        @pl.when(has_above)
        def _():
            small_copy(4, below).wait_recv()
            stages[4] = came[4]

        pl.when(has_below)(lambda: small_copy(4, below).start())
        small_ref[...] = stages[4]
        small_ref[2:3, :] = stages[2, 2:3, :] + came[2, 2:3, :]
        for n, target in enumerate((across, other_core, other_half)):
            small_copy(n, target).wait_send()
        pl.when(has_above)(lambda: small_copy(3, above).wait_send())
        pl.when(has_below)(lambda: small_copy(4, below).wait_send())

    waves = count - 1
    every = max(1, waves // 3)
    works = waves // every

    if count == 4:
        order = ((2, 2, 0), (1, 1, 1), (2, 3, 1))
    else:
        order = tuple((2, distance, distance - 1) for distance in range(1, count))

    def pass_steps(h, live, wave):
        for behind, distance, step in order:
            item = jnp.maximum(h - behind, 0)
            for k in range(2):
                pl.when(
                    live & (wave == step) & (h >= behind) & (lax.rem(item, 2) == k)
                )(lambda: pass_on(item // 2, k, distance))

    def pass_rest():
        for item in range(2 * chunks - 2, 2 * chunks):
            for distance, behind in sorted((step[1], step[0]) for step in order):
                if item + behind >= 2 * chunks:
                    pass_on(item // 2, item % 2, distance)

    def half_steps(h, live, work):
        c = h // 2

        def one(wave, carry):
            pl.when(lax.rem(wave, every) == 0)(lambda: work(wave // every))
            for k in range(2):

                @pl.when(live & (lax.rem(h, 2) == k))
                def _(k=k):
                    more = c + 1 < chunks

                    @pl.when(wave == 0)
                    def _():
                        @pl.when(c > 0)
                        def _():
                            sums_left(c - 1, k)
                            each_first(c - 1, k, lambda copy: copy.wait_send())

                        pl.when(more)(lambda: load_share(c + 1, k).start())

                    sums(c, k, wave)

            pass_steps(h, live, wave)
            for k in range(2):

                @pl.when(live & (lax.rem(h, 2) == k) & (wave == waves - 1))
                def _(k=k):
                    more = c + 1 < chunks
                    pl.when(more)(lambda: load(c + 1, k).start())
                    finish(c, k)
                    pl.when(more)(lambda: send_ends(c + 1, k))

            return carry

        lax.fori_loop(0, waves, one, 0)

    tile_halves = -(-sides * (chunks - 1) // works)

    def tiles_scope(*scratch):
        weights = scratch[: 5 * sides]
        scratch = scratch[5 * sides :]
        normed_buf, tile_cot = scratch[:2]
        head_bufs = scratch[2 : 2 + 2 * sides]
        scratch = scratch[2 + 2 * sides :]
        mids, f_buf, g_buf = scratch[: 3 * sides], scratch[3 * sides], scratch[3 * sides + 1]
        f_total, g_total, weight_sem, in_sem, out_sem = scratch[3 * sides + 2 :]

        def weight_copies(s):
            if s == 0:
                pairs = list(zip(own_weights, weights[:5]))
            else:
                pairs = list(zip(other_heads, weights[5:7]))
                parts, kinds, size = other_mid.shape[:3]
                for part in range(parts):
                    for kind in range(kinds):
                        target = weights[7 + kind].at[pl.ds(part * size, size), :]
                        pairs.append((other_mid.at[part, kind], target))
            return [
                pltpu.make_async_copy(source, target, weight_sem.at[5 * s + x])
                for x, (source, target) in enumerate(pairs)
            ]

        def tile_in(i):
            slot = lax.rem(i, 2)
            at = span(i * chunk_rows, chunk_rows)
            at_side = span(side * rows + i * chunk_rows, chunk_rows)
            pairs = [(normed_ref.at[at, :], normed_buf), (cot_ref.at[at_side, :], tile_cot)]
            pairs += [(ref.at[at, :], buf) for ref, buf in zip(head_refs, head_bufs)]
            return [
                pltpu.make_async_copy(ref, buf.at[slot], in_sem.at[slot, x])
                for x, (ref, buf) in enumerate(pairs)
            ]

        def tile_out(i):
            at = span(i * chunk_rows, chunk_rows)
            pairs = list(zip(mids, mid_refs)) + [(f_buf, f_ref), (g_buf, g_ref)]
            return [
                pltpu.make_async_copy(buf, ref.at[at, :], out_sem.at[x])
                for x, (buf, ref) in enumerate(pairs)
            ]

        def wait_out(i):
            for copy in tile_out(i):
                copy.wait()

        def tile(i, s):
            slot = lax.rem(i, 2)
            if s == 0:
                for copy in tile_in(i):
                    copy.wait()

                @pl.when(i + 1 < chunks)
                def _():
                    for copy in tile_in(i + 1):
                        copy.start()

                pl.when(i > 1)(lambda: wait_out(i - 1))

            @pl.when(i == 0)
            def _():
                for copy in weight_copies(s):
                    copy.wait()

            qkv_w, out_w, gate_w, up_w, down_w = weights[5 * s : 5 * s + 5]
            hidden_buf, gate_buf, up_buf = mids[3 * s : 3 * s + 3]
            normed, cot = normed_buf[slot], tile_cot[slot]
            gate = cols_product(normed, gate_w[...])
            up = cols_product(normed, up_w[...])
            sig = 1.0 / (1.0 + jnp.exp(-gate))
            silu = gate * sig
            hidden = (silu * up).astype(BF16)
            hidden_buf[...] = hidden
            grad_hidden = cols_product(cot, down_w[...])
            gate_back = (grad_hidden * up * sig * (1.0 + gate * (1.0 - sig))).astype(BF16)
            up_back = (grad_hidden * silu).astype(BF16)
            gate_buf[...] = gate_back
            up_buf[...] = up_back
            forward = product(hidden, down_w[...])
            forward += product(head_bufs[2 * s][slot], out_w[...])
            backward = product(gate_back, gate_w[...])
            backward += product(up_back, up_w[...])
            qkv_back = head_bufs[2 * s + 1][slot]
            backward += cols_product(qkv_back, qkv_w[...])
            bias_part[s] += (
                qkv_back.astype(F32).reshape(chunk_rows // 8, 8, qkv_back.shape[1]).sum(axis=0)
            )
            if s > 0:
                forward += f_total[...]
                backward += g_total[...]
            if s < sides - 1:
                f_total[...] = forward
                g_total[...] = backward
                return
            f_buf[...] = forward.astype(BF16)
            g_buf[...] = backward.astype(BF16)
            for copy in tile_out(i):
                copy.start()

        def work(turn, n):
            first = turn == 0
            unit = jnp.maximum(works * turn - works, 0) + n
            i = jnp.where(first, 0, 1 + unit // sides)
            part = jnp.where(first, n - works + sides, lax.rem(unit, sides))
            for s in range(sides):
                pl.when((part == s) & (i < chunks))(lambda: tile(i, s))

        for s in range(sides):
            for copy in weight_copies(s):
                copy.start()
        for copy in tile_in(0):
            copy.start()
        for k in range(2):
            load_share(0, k).start()
        part_ref[...] = jnp.zeros_like(part_ref)
        bias_part[...] = jnp.zeros_like(bias_part)
        pl.semaphore_wait(
            barrier, 3 + has_above.astype(jnp.int32) + has_below.astype(jnp.int32)
        )

        def chunk(turn, carry):
            half_steps(
                jnp.maximum(turn, 1) - 1, turn > 0, lambda n: work(turn, n)
            )

            @pl.when(turn == 0)
            def _():
                wait_out(0)
                for k in range(2):
                    load(0, k).start()
                for k in range(2):
                    send_ends(0, k)

            return carry

        lax.fori_loop(0, tile_halves + 1, chunk, 0)
        wait_out(chunks - 1)

    tall = width
    hidden_cols = mid_refs[0].shape[1]
    pl.run_scoped(
        tiles_scope,
        *[pltpu.VMEM(ref.shape, BF16) for ref in own_weights * sides],
        pltpu.VMEM((2, chunk_rows, width), BF16),
        pltpu.VMEM((2, chunk_rows, width), BF16),
        *[pltpu.VMEM((2, chunk_rows, ref.shape[1]), BF16) for ref in head_refs],
        *[pltpu.VMEM((chunk_rows, hidden_cols), BF16) for _ in mid_refs],
        pltpu.VMEM((chunk_rows, width), BF16),
        pltpu.VMEM((chunk_rows, width), BF16),
        pltpu.VMEM((chunk_rows, width), F32),
        pltpu.VMEM((chunk_rows, width), F32),
        pltpu.SemaphoreType.DMA((7 + 3 * other_mid.shape[0],)),
        pltpu.SemaphoreType.DMA((2, 2 + 2 * sides)),
        pltpu.SemaphoreType.DMA((3 * sides + 2,)),
    )


    pieces = core_send.shape[2]
    each = 2
    size = tall // pieces

    def grads_scope(*scratch):
        factor_bufs, scratch = scratch[: arrays * sides], scratch[arrays * sides :]
        held, scratch = scratch[: arrays * sides], scratch[arrays * sides :]
        extra, scratch = scratch[: arrays * sides], scratch[arrays * sides :]
        turned, scratch = scratch[: arrays - 1], scratch[arrays - 1 :]
        left_bufs, factor_sem, left_sem = scratch[:2], scratch[2], scratch[3]

        def factor_copy(x):
            return pltpu.make_async_copy(factors[x], factor_bufs[x], factor_sem.at[x])

        def piece(ref, j):
            return ref.at[span(j * size, size), :]

        def piece_of(u):
            owner_core = jnp.where(u < 2 * each, 1 - core, core)
            owner_half = jnp.where((u // each) % 2 == 0, 1 - half, half)
            return (owner_half * 2 + owner_core) * each + lax.rem(u, each)

        def slot_of(u):
            return jnp.where(u < 3 * each, lax.rem(u, each), each + lax.rem(u, each))

        def left_copy(u, which):
            at = span(piece_of(u) * size, size)
            source = (
                normed_ref.at[:, at] if which == 0 else cot_ref.at[span(side * rows, rows), at]
            )
            return pltpu.make_async_copy(
                source, left_bufs[which].at[lax.rem(u, 2)], left_sem.at[which, lax.rem(u, 2)]
            )

        def to_core(a, s, j, slot):
            x = 2 * a + s
            return remote(
                held[x].at[slot], piece(core_land[x], j),
                core_send.at[a, s, j], core_recv.at[a, s, j], other_core,
            )

        def to_far(a, s, i, j):
            x = 2 * a + s
            return remote(
                held[x].at[i], piece(far_land[x], j),
                far_send.at[a, s, j], far_recv.at[a, s, j], other_half,
            )

        def to_over(a, i, j):
            return remote(
                held[2 * a + 1].at[each + i], piece(side_land[a], j),
                over_send.at[a, j], over_recv.at[a, j], across,
            )

        def final_piece(a, j):
            return grad_outs[a].at[j] if a else grad_outs[a].at[span(j * size, size), :]

        def final_source(a, i):
            return turned[a - 1].at[i] if a else held[0].at[each + i]

        def back_copy(a, i, j, way, first):
            target = final_piece(a, j)
            source = final_source(a, i) if first else target
            return remote(
                source, target, back_send.at[a, way, j], back_recv.at[a, j],
                (other_core, other_half)[way],
            )

        def save_copy(a, i, j):
            return pltpu.make_async_copy(
                final_source(a, i), final_piece(a, j), save_sem.at[a, i]
            )

        def their_piece(i):
            return ((1 - half) * 2 + core) * each + i

        def my_piece(i):
            return (half * 2 + core) * each + i

        def add_into(target, slot, source):
            def body(i, carry):
                at = span(i * 16, 16)
                target[slot, at, :] = (
                    target[slot, at, :].astype(F32) + source[at, :].astype(F32)
                ).astype(BF16)
                return carry

            lax.fori_loop(0, size // 16, body, 0)

        def fetch(lands, j, ids):
            copies = [
                pltpu.make_async_copy(piece(lands[n], j), extra[x], load_sem.at[x])
                for n, x in enumerate(ids)
            ]
            for copy in copies:
                copy.start()
            for copy in copies:
                copy.wait()

        everything = range(2 * arrays)

        def make(u, which):
            @pl.when(u == 0)
            def _():
                for x in everything:
                    if (x // 2 < 3) == (which == 0):
                        factor_copy(x).wait()

            left_copy(u, which).wait()
            pl.when(u + 1 < pieces)(lambda: left_copy(u + 1, which).start())
            slot = slot_of(u)
            left = left_bufs[which][lax.rem(u, 2)].T

            @pl.when((u >= each) & (u < 3 * each))
            def _():
                for x in everything:
                    if (x // 2 < 3) == (which == 0):
                        to_core(x // 2, x % 2, piece_of(u - each), slot).wait_send()

            for x in everything:
                if (x // 2 < 3) == (which == 0):
                    held[x][slot] = product(left, factor_bufs[x][...]).astype(BF16)

            @pl.when(u < 2 * each)
            def _():
                for x in everything:
                    if (x // 2 < 3) == (which == 0):
                        to_core(x // 2, x % 2, piece_of(u), slot).start()

        def gather_terms(slot, j):
            for x in everything:
                to_core(x // 2, x % 2, j, 0).wait_recv()
            fetch(core_land, j, everything)
            for x in everything:
                add_into(held[x], slot, extra[x])

        def grads_far(i):
            j = their_piece(i)
            gather_terms(i, j)
            for x in everything:
                to_far(x // 2, x % 2, i, j).start()

        def grads_over(i):
            j = my_piece(i)
            gather_terms(each + i, j)
            for x in everything:
                to_far(x // 2, x % 2, i, j).wait_recv()
            fetch(far_land, j, everything)
            for a in range(arrays):
                add_into(held[2 * a + 1], each + i, extra[2 * a + 1])
                to_over(a, i, j).start()
            for a in range(arrays):
                add_into(held[2 * a], each + i, extra[2 * a])

        def grads_back(i):
            j = my_piece(i)
            for a in range(arrays):
                to_over(a, i, j).wait_recv()
            fetch(side_land, j, range(0, 2 * arrays, 2))
            for a in range(arrays):
                if a:
                    total = held[2 * a][each + i].astype(F32) + extra[2 * a][...].astype(F32)
                    turned[a - 1][i] = total.T.astype(BF16)
                else:
                    add_into(held[0], each + i, extra[0])
                back_copy(a, i, j, 1, True).start()
                back_copy(a, i, j, 0, True).start()
                save_copy(a, i, j).start()

        def grads_pass(i):
            j = their_piece(i)
            for a in range(arrays):
                back_copy(a, i, j, 1, False).wait_recv()
                back_copy(a, i, j, 0, False).start()

        def grads_drain():
            for i in range(each):
                mine, theirs = my_piece(i), their_piece(i)
                for a in range(arrays):
                    for s in range(2):
                        to_far(a, s, i, theirs).wait_send()
                    to_over(a, i, mine).wait_send()
                    back_copy(a, i, mine, 1, True).wait_send()
                    back_copy(a, i, mine, 0, True).wait_send()
                    back_copy(a, i, theirs, 0, False).wait_send()
                    save_copy(a, i, mine).wait()
            for u in range(2 * each):
                for a in range(arrays):
                    back_copy(a, 0, piece_of(u), 0, False).wait_recv()

        events = {
            26: (grads_far, 0),
            28: (grads_far, 1),
            35: (grads_over, 0),
            40: (grads_back, 0),
            43: (grads_over, 1),
        }

        def work(h, n):
            v = works * (h - tile_halves) + n
            for which in range(2):
                pl.when((v < 2 * pieces) & (lax.rem(v, 2) == which))(
                    lambda: make(v // 2, which)
                )
            for at, (act, i) in events.items():
                pl.when(works * h + n == at)(lambda: act(i))

        for x in everything:
            factor_copy(x).start()
        for which in range(2):
            left_copy(0, which).start()

        def chunk(c, carry):
            half_steps(c, c >= 0, lambda n: work(c, n))
            return carry

        lax.fori_loop(tile_halves, 2 * chunks, chunk, 0)
        pass_rest()
        grads_back(1)
        small_sums()
        for i in range(each):
            grads_pass(i)
        grads_drain()

    factor_shapes = [ref.shape for ref in factors]
    pl.run_scoped(
        grads_scope,
        *[pltpu.VMEM(shape, BF16) for shape in factor_shapes],
        *[pltpu.VMEM((2 * each, size, shape[1]), BF16) for shape in factor_shapes],
        *[pltpu.VMEM((size, shape[1]), BF16) for shape in factor_shapes],
        *[pltpu.VMEM((each, shape[1], size), BF16) for shape in factor_shapes[2::2]],
        pltpu.VMEM((2, rows, size), BF16),
        pltpu.VMEM((2, rows, size), BF16),
        pltpu.SemaphoreType.DMA((2 * arrays,)),
        pltpu.SemaphoreType.DMA((2, 2)),
    )

    for k in range(2):
        sums_left(chunks - 1, k)
        each_first(chunks - 1, k, lambda copy: copy.wait_send())
        own_left(chunks - 2, k)
        own_left(chunks - 1, k)

    def drain(c, carry):
        for k in range(2):
            for b in range(count):
                pl.when((place > b) & has_above)(
                    lambda: line_copy(c, k, b, 0, False).wait_send()
                )
                pl.when((place < b) & has_below)(
                    lambda: line_copy(c, k, b, 1, False).wait_send()
                )
                pl.when(place != b)(lambda: side_copy(c, k, b, False).wait_send())
                side_copy(c, k, b, False).wait_recv()
        return carry

    lax.fori_loop(0, chunks, drain, 0)


def layer(normed, tokens, cotangent, heads, weights, gain, count, chunks, dp_size):
    row_count, width = tokens.shape
    rows = row_count // 2
    share = rows // chunks // count
    sides, arrays = 2, 5
    pieces = 2 * dp_size
    sem = pltpu.SemaphoreType.DMA
    flat_heads = [array for group in heads for array in group]
    own_weights, other_heads, other_mid = weights
    flat_weights = [*own_weights, *other_heads, other_mid]
    hidden = own_weights[2].shape[0]
    columns = [heads[0][1].shape[1], hidden, hidden, hidden, heads[0][0].shape[1]]
    whole = jax.ShapeDtypeStruct(tokens.shape, BF16)
    half_sums = [jax.ShapeDtypeStruct((width, n), BF16) for n in columns]
    finals = half_sums[:1] + [
        jax.ShapeDtypeStruct((pieces, n, width // pieces), BF16) for n in columns[1:]
    ]
    lands = [shape for shape in half_sums for _ in range(sides)]
    anywhere = pl.BlockSpec(memory_space=pl.ANY)
    vmem = pl.BlockSpec(memory_space=pltpu.VMEM)
    own_rows = [jax.ShapeDtypeStruct((rows, width), BF16)] * 2
    own_rows += [jax.ShapeDtypeStruct((rows, hidden), BF16)] * (3 * sides)
    outs = pl.pallas_call(
        functools.partial(layer_kernel, chunks, sides),
        in_specs=[anywhere] * (3 + len(flat_heads) + len(flat_weights)) + [vmem],
        out_specs=[anywhere, anywhere, vmem] + [anywhere] * (6 * arrays + len(own_rows)),
        out_shape=[whole, whole, jax.ShapeDtypeStruct((8, width), F32)]
        + finals + lands + lands + half_sums + own_rows,
        scratch_shapes=[
            pltpu.VMEM((2, 2, count * share, width), BF16),
            pltpu.VMEM((2, 2, 2, count - 1, share, width), BF16),
            pltpu.VMEM((2, 2, share, width), BF16),
            pltpu.VMEM((2, share, width), BF16),
            pltpu.VMEM((2, share, width), BF16),
            sem((2, 2)),
            sem((2, 2)),
            sem((2, 2, 2, count)),
            sem((2, 2, 2, count)),
            sem((chunks, 2, 2, count)),
            sem((chunks, 2, count)),
            sem((chunks, 2, count)),
            sem((chunks, 2, count)),
            sem((chunks, 2)),
            sem((arrays, 2, pieces)),
            sem((arrays, 2, pieces)),
            sem((arrays, 2, pieces)),
            sem((arrays, 2, pieces)),
            sem((arrays, pieces)),
            sem((arrays, pieces)),
            sem((arrays, 2, pieces)),
            sem((arrays, pieces)),
            sem((2 * arrays,)),
            sem((arrays, 2)),
            pltpu.VMEM((16, width), F32),
            pltpu.VMEM((sides, 8, columns[0]), F32),
            pltpu.VMEM((5, 8, width), F32),
            pltpu.VMEM((5, 8, width), F32),
            sem((5,)),
            sem((5,)),
        ],
        compiler_params=pltpu.CompilerParams(
            collective_id=0, has_side_effects=True, vmem_limit_bytes=63 * 2**20
        ),
        cost_estimate=pl.CostEstimate(
            flops=6 * rows * sum(array.size for array in flat_weights),
            bytes_accessed=800 * 2**20,
            transcendentals=0,
        ),
        name="layer",
    )(normed, tokens, cotangent, *flat_heads, *flat_weights, gain)
    out, grad, small = outs[:3]
    grads = [outs[3].astype(F32)]
    for blocks in outs[4 : 3 + arrays]:
        grads.append(blocks.transpose(1, 0, 2).reshape(blocks.shape[1], width).astype(F32))
    return out, grad, small[0], small[1], small[2, : columns[0]], grads


def body(
    tokens,
    lengths,
    norm_gain,
    norm_shift,
    qkv_weight,
    qkv_bias,
    out_weight,
    gate_weight,
    up_weight,
    down_weight,
    cotangent,
):
    tensor_size = lax.axis_size("tensor")
    dp_size = lax.axis_size("dp")
    count = tensor_size // 2
    where = lax.axis_index("tensor")
    dp_place = lax.axis_index("dp")
    side = where % 2
    across = [(i, i ^ 1) for i in range(tensor_size)]
    row_count, width = tokens.shape
    rows = row_count // 2
    chunk_count = 8

    def own_part(weight):
        part = weight.shape[0] // dp_size
        return lax.dynamic_slice_in_dim(weight, dp_place * part, part, 0)

    def partner(parts, before, after):
        parts, _ = lax.optimization_barrier((parts, before))
        parts = [lax.ppermute(part, "tensor", across) for part in parts]
        parts, _ = lax.optimization_barrier((parts, after))
        return [lax.all_gather(part, "dp") for part in parts]

    head_weights = (qkv_weight, out_weight)
    mid_weights = (gate_weight.T, up_weight.T, down_weight)
    biases = (qkv_bias, lax.ppermute(qkv_bias, "tensor", across))

    length = lax.dynamic_slice_in_dim(lengths, side, 1, 0)
    norm = (norm_gain, norm_shift)
    normed, *own_group = project(side, tokens, cotangent, norm, head_weights, biases[0])
    tables = rotary_tables(rows)
    even = (out_weight.shape[0] // HEAD) % 2 == 0
    other_heads = [
        parts.reshape(-1, parts.shape[-1])
        for parts in partner([own_part(weight) for weight in head_weights], (), normed)
    ]
    mid_parts = [jnp.stack([own_part(weight) for weight in mid_weights])]
    if even:
        heads = [attention(length, *own_group, *tables)]
        (other_mid,) = partner(mid_parts, normed, heads[0])
        other_group = project(side, normed, cotangent, (), other_heads, biases[1])
        heads.append(attention(length, *other_group, *tables))
    else:
        (other_mid,) = partner(mid_parts, normed, ())
        other_group = project(side, normed, cotangent, (), other_heads, biases[1])
        pairs = zip(own_group, other_group)
        attended, qkv_back = attention(
            length, *[jnp.concatenate(pair, axis=1) for pair in pairs], *tables
        )
        cut, wide = out_weight.shape[0], qkv_weight.shape[1]
        heads = [
            (attended[:, s * cut : (s + 1) * cut], qkv_back[:, s * wide : (s + 1) * wide])
            for s in range(2)
        ]
    if other_mid.shape[2] % 16:
        other_mid = other_mid.transpose(1, 0, 2, 3).reshape(1, 3, -1, width)
    weights = ((*head_weights, *mid_weights), other_heads, other_mid)
    layer_out, grad_tokens, gain_part, shift_part, grad_bias, grads = layer(
        normed, tokens, cotangent, heads, weights, norm_gain[None, :], count, chunk_count, dp_size
    )
    grad_qkv, grad_gate, grad_up, grad_down, grad_out = grads
    grad_gate, grad_up = grad_gate.T, grad_up.T
    return (
        layer_out,
        grad_tokens,
        gain_part,
        shift_part,
        grad_qkv,
        grad_bias,
        grad_out,
        grad_gate,
        grad_up,
        grad_down,
    )


def solution(mesh):
    placed = (
        P("dp", None),
        P("dp"),
        P(),
        P(),
        P(None, "tensor"),
        P("tensor"),
        P("tensor", None),
        P(None, "tensor"),
        P(None, "tensor"),
        P("tensor", None),
        P("dp", None),
    )
    return jax.shard_map(
        body,
        mesh=mesh,
        in_specs=placed,
        out_specs=(
            P("dp", None),
            P("dp", None),
            P(),
            P(),
            P(None, "tensor"),
            P("tensor"),
            P("tensor", None),
            P(None, "tensor"),
            P(None, "tensor"),
            P("tensor", None),
        ),
        check_vma=False,
    )
```

```python
import functools

import jax
import jax.numpy as jnp
import numpy as np
from jax import lax
from jax.experimental import pallas as pl
from jax.experimental.pallas import tpu as pltpu
from jax.sharding import PartitionSpec as P

HEAD = 64
ROT = 16
PAIR = 2 * HEAD
TRIPLE = 6 * HEAD

EPSILON = 1e-05
NEGATIVE = -1e30
F32 = jnp.float32
BF16 = jnp.bfloat16


def rows_product(former, latter):
    return lax.dot_general(
        former, latter, (((0,), (0,)), ((), ())), preferred_element_type=F32
    )


def cols_product(former, latter):
    return lax.dot_general(
        former, latter, (((1,), (1,)), ((), ())), preferred_element_type=F32
    )


def product(former, latter):
    return jnp.dot(former, latter, preferred_element_type=F32)


def rotary_tables(seq_len):
    frequency = np.float32(10000.0) ** (-np.arange(0, ROT, 2).astype(np.float32) / ROT)
    angles = np.arange(seq_len).astype(np.float32)[:, None] * frequency[None, :]
    cosine, sine = np.cos(angles), np.sin(angles)
    still = HEAD - ROT
    cos_head = np.concatenate([cosine, cosine, np.ones((seq_len, still))], axis=1)
    sin_head = np.concatenate([-sine, sine, np.zeros((seq_len, still))], axis=1)
    return [jnp.asarray(np.tile(table, (1, 2)), F32) for table in (cos_head, sin_head)]


def attention_kernel(
    len_ref, qkv_ref, grad_ref, cos_ref, sin_ref, att_ref, back_ref,
    score, expo, query, key_value, key_value_t, query_t, grad_query, grad_kv_t,
):
    seq_len = qkv_ref.shape[0]
    block = score.shape[1]
    steps = seq_len // block
    length = len_ref[0]
    lane = lax.broadcasted_iota(jnp.int32, (block, PAIR), 1)
    left = lane < HEAD
    near = lax.rem(lane, HEAD) < ROT // 2

    def turn(tile, cosine, sine):
        swapped = jnp.where(
            near, pltpu.roll(tile, PAIR - ROT // 2, 1), pltpu.roll(tile, ROT // 2, 1)
        )
        return tile * cosine + swapped * sine

    def tables(rows):
        cosine, sine = cos_ref[rows, :], sin_ref[rows, :]
        return (
            (cosine, sine),
            (jnp.where(left, 1.0, cosine), jnp.where(left, 0.0, sine)),
            (jnp.where(left, cosine, 1.0), jnp.where(left, sine, 0.0)),
        )

    def prepare(i, carry):
        rows = pl.ds(pl.multiple_of(i * block, block), block)
        tabs = tables(rows)
        first = turn(qkv_ref[rows, 0:PAIR], *tabs[0])
        second = turn(qkv_ref[rows, PAIR : 2 * PAIR], *tabs[1])
        third = turn(qkv_ref[rows, 2 * PAIR : 3 * PAIR], *tabs[2])
        scale = HEAD**-0.5
        first_q = first.astype(BF16).astype(F32) * scale
        second_q = second.astype(BF16).astype(F32) * scale
        query[0, rows, :] = jnp.where(left, 0.0, pltpu.roll(first_q, HEAD, 1)).astype(BF16)
        query[1, rows, :] = jnp.where(left, pltpu.roll(second_q, HEAD, 1), 0.0).astype(BF16)
        for h, tile in enumerate((jnp.where(left, second, first), third)):
            key_value[h, rows, :] = tile.astype(BF16)
            key_value_t[h, :, rows] = tile.T.astype(BF16)
        query_t[0, :, rows] = first_q.T[0:HEAD, :].astype(BF16)
        query_t[1, :, rows] = second_q.T[HEAD:PAIR, :].astype(BF16)
        zero = jnp.zeros((block, PAIR), F32)
        grad_query[rows, :] = zero
        att_ref[rows, :] = zero.astype(BF16)
        for h in range(2):
            grad_kv_t[h, :, rows] = jnp.zeros((PAIR, block), F32)
        return carry

    lax.fori_loop(0, steps, prepare, 0)

    def fold(tile, op):
        out = tile[:, 0:PAIR]
        for c in range(1, block // PAIR):
            out = op(out, tile[:, c * PAIR : (c + 1) * PAIR])
        return out

    def block_rows(i):
        rows = pl.ds(i * block, block)
        spans = [pl.ds(j * block, block) for j in range(i + 1)]
        q_block = [query[h, rows, :] for h in range(2)]
        below = lax.broadcasted_iota(jnp.int32, (block, block), 1) <= lax.broadcasted_iota(
            jnp.int32, (block, block), 0
        )
        maxima = []
        for h in range(2):
            top = None
            for j, cols in enumerate(spans):
                tile = product(q_block[h], key_value_t[h, :, cols])
                if j == i:
                    tile = jnp.where(below, tile, NEGATIVE)
                score[h, :, cols] = tile
                high = fold(tile, jnp.maximum)
                top = high if top is None else jnp.maximum(top, high)
            maxima.append(jnp.max(top, axis=1, keepdims=True))

        mixed, inverse = [], []
        for h in range(2):
            mixture = total = None
            for cols in spans:
                tile = jnp.exp(score[h, :, cols] - maxima[h])
                low = tile.astype(BF16)
                expo[h, :, cols] = low
                part = product(low, key_value[h, cols, :])
                amount = fold(tile, jnp.add)
                mixture = part if mixture is None else mixture + part
                total = amount if total is None else total + amount
            mixed.append(mixture)
            inverse.append(1.0 / jnp.sum(total, axis=1, keepdims=True))

        place = i * block + lax.broadcasted_iota(jnp.int32, (block, 1), 0)
        valid = (place < length).astype(F32)
        mixture = jnp.where(left, mixed[0] * inverse[0], mixed[1] * inverse[1]) * valid
        att_ref[rows, :] = mixture.astype(BF16)
        upstream = grad_ref[rows, :].astype(F32) * valid
        inner = upstream * mixture
        scale = HEAD**-0.5
        turned = []
        for h in range(2):
            own = left if h == 0 else jnp.logical_not(left)
            inner_sum = jnp.sum(jnp.where(own, inner, 0.0), axis=1, keepdims=True) * inverse[h]
            mine = jnp.where(own, upstream * inverse[h], 0.0)
            scaled = mine.astype(BF16)
            half = slice(0, HEAD) if h == 0 else slice(HEAD, PAIR)
            scaled_t = mine.T[half, :].astype(BF16)
            queries_t = query_t[h, :, rows]
            grad = None
            for cols in spans:
                low = expo[h, :, cols]
                grad_weight = product(scaled, key_value_t[h, :, cols])
                grad_score = (low.astype(F32) * (grad_weight - inner_sum)).astype(BF16)
                part = product(grad_score, key_value[h, cols, :])
                grad = part if grad is None else grad + part
                key_at, value_at = (HEAD, 0) if h == 0 else (0, HEAD)
                grad_kv_t[h, key_at : key_at + HEAD, cols] += product(queries_t, grad_score)
                grad_kv_t[h, value_at : value_at + HEAD, cols] += product(scaled_t, low)
            turned.append(pltpu.roll(grad, HEAD, 1))
        grad_query[rows, :] = jnp.where(left, turned[0], turned[1]) * scale

    for i in range(steps):
        pl.when(i * block < length)(functools.partial(block_rows, i))

    def finish(i, carry):
        rows = pl.ds(pl.multiple_of(i * block, block), block)
        tabs = tables(rows)
        gq = grad_query[rows, :]
        low_kv = grad_kv_t[0, :, rows].T
        high_kv = grad_kv_t[1, :, rows].T
        tiles = (jnp.where(left, gq, low_kv), jnp.where(left, low_kv, gq), high_kv)
        for c in range(3):
            back_ref[rows, c * PAIR : (c + 1) * PAIR] = turn(
                tiles[c], tabs[c][0], -tabs[c][1]
            ).astype(BF16)
        return carry

    lax.fori_loop(0, steps, finish, 0)


def attention(length, qkv, grad_mixture, cosine, sine):
    seq_len, width = qkv.shape
    pairs = width // TRIPLE
    block = min(512, seq_len)
    flops = 6 * 2 * (2 * pairs) * seq_len * seq_len * PAIR
    return pl.pallas_call(
        attention_kernel,
        grid=(pairs,),
        in_specs=[
            pl.BlockSpec(memory_space=pltpu.SMEM),
            pl.BlockSpec((seq_len, TRIPLE), lambda g: (0, g)),
            pl.BlockSpec((seq_len, PAIR), lambda g: (0, g)),
            pl.BlockSpec((seq_len, PAIR), lambda g: (0, 0)),
            pl.BlockSpec((seq_len, PAIR), lambda g: (0, 0)),
        ],
        out_specs=[
            pl.BlockSpec((seq_len, PAIR), lambda g: (0, g)),
            pl.BlockSpec((seq_len, TRIPLE), lambda g: (0, g)),
        ],
        out_shape=[
            jax.ShapeDtypeStruct((seq_len, pairs * PAIR), BF16),
            jax.ShapeDtypeStruct((seq_len, width), BF16),
        ],
        scratch_shapes=[
            pltpu.VMEM((2, block, seq_len), F32),
            pltpu.VMEM((2, block, seq_len), BF16),
            pltpu.VMEM((2, seq_len, PAIR), BF16),
            pltpu.VMEM((2, seq_len, PAIR), BF16),
            pltpu.VMEM((2, PAIR, seq_len), BF16),
            pltpu.VMEM((2, HEAD, seq_len), BF16),
            pltpu.VMEM((seq_len, PAIR), F32),
            pltpu.VMEM((2, PAIR, seq_len), F32),
        ],
        compiler_params=pltpu.CompilerParams(vmem_limit_bytes=48 * 2**20),
        cost_estimate=pl.CostEstimate(
            flops=flops,
            bytes_accessed=seq_len * width * 8,
            transcendentals=2 * pairs * seq_len * seq_len // 2,
        ),
        name="attention",
    )(length, qkv, grad_mixture, cosine, sine)


def start_kernel(
    side_ref, tok_ref, cot_ref, gain_ref, shift_ref, qkv_w, bias_ref, out_w,
    normed_ref, qkv_ref, grad_ref,
):
    wide = tok_ref[...].astype(F32)
    centred = wide - jnp.mean(wide, axis=1, keepdims=True)
    variance = jnp.mean(centred * centred, axis=1, keepdims=True)
    unit = centred * lax.rsqrt(variance + EPSILON)
    normed = (unit * gain_ref[...] + shift_ref[...]).astype(BF16)
    normed_ref[...] = normed
    qkv_ref[...] = product(normed, qkv_w[...]) + bias_ref[...]
    grad_ref[...] = cols_product(cot_ref[...], out_w[...]).astype(BF16)


def project_kernel(side_ref, normed_ref, cot_ref, qkv_w, bias_ref, out_w, qkv_ref, grad_ref):
    qkv_ref[...] = product(normed_ref[...], qkv_w[...]) + bias_ref[...]
    grad_ref[...] = cols_product(cot_ref[...], out_w[...]).astype(BF16)


def project(side, rows_in, cotangent, norm, weights, bias):
    rows, width = cotangent.shape[0] // 2, cotangent.shape[1]
    tile = min(256, rows)
    tiles = rows // tile
    qkv_weight, out_weight = weights
    heads, wide = out_weight.shape[0], qkv_weight.shape[1]

    def sided(i, side_ref):
        return (side_ref[0] * tiles + i, 0)

    def fixed(i, side_ref):
        return (0, 0)

    def rowed(i, side_ref):
        return (i, 0)

    flat = [part[None, :] for part in norm]
    flat += [qkv_weight, bias.astype(F32)[None, :], out_weight]
    outs = [((rows, wide), F32), ((rows, heads), BF16)]
    if norm:
        outs = [((rows, width), BF16)] + outs
    return pl.pallas_call(
        start_kernel if norm else project_kernel,
        grid_spec=pltpu.PrefetchScalarGridSpec(
            num_scalar_prefetch=1,
            grid=(tiles,),
            in_specs=[
                pl.BlockSpec((tile, width), sided if norm else rowed),
                pl.BlockSpec((tile, width), sided),
            ]
            + [pl.BlockSpec(array.shape, fixed) for array in flat],
            out_specs=[pl.BlockSpec((tile, shape[1]), rowed) for shape, _ in outs],
        ),
        out_shape=[jax.ShapeDtypeStruct(*out) for out in outs],
        compiler_params=pltpu.CompilerParams(vmem_limit_bytes=40 * 2**20),
        cost_estimate=pl.CostEstimate(
            flops=2 * rows * width * (wide + heads),
            bytes_accessed=rows * (6 * width + 4 * wide),
            transcendentals=rows,
        ),
        name="project",
    )(side[None], rows_in, cotangent, *flat)


def layer_kernel(chunks, sides, *refs):
    normed_ref, tok_ref, cot_ref = refs[:3]
    head_refs, refs = refs[3 : 3 + 2 * sides], refs[3 + 2 * sides :]
    weight_refs, gain_ref = refs[: 5 * sides], refs[5 * sides]
    refs = refs[5 * sides + 1 :]
    out_ref, grad_ref, small_ref = refs[:3]
    refs = refs[3:]
    arrays = 5
    grad_outs, core_land = refs[:arrays], refs[arrays : 3 * arrays]
    far_land, side_land = refs[3 * arrays : 5 * arrays], refs[5 * arrays : 6 * arrays]
    refs = refs[6 * arrays :]
    f_ref, g_ref = refs[:2]
    mid_refs, refs = refs[2 : 2 + 3 * sides], refs[2 + 3 * sides :]
    (
        terms, landed, ready, tok_buf, cot_buf,
        term_sem, share_sem, sum_send, sum_recv,
        line_send, line_recv, side_send, side_recv, keep_sem,
        core_send, core_recv, far_send, far_recv, over_send, over_recv,
        back_send, back_recv, load_sem, save_sem,
        part_ref, bias_part, stages, came, small_send, small_recv,
    ) = refs
    share, width = landed.shape[4:]
    count = landed.shape[3] + 1
    chunk_rows = count * share
    rows = chunks * chunk_rows
    where = lax.axis_index("tensor")
    group = lax.axis_index("dp")
    place, side = where // 2, where % 2
    half, core = group // 2, group % 2
    whole_refs = (out_ref, grad_ref)
    factors = []
    for s in range(sides):
        hidden_ref, gate_ref, up_ref = mid_refs[3 * s : 3 * s + 3]
        factors.append(
            (head_refs[2 * s + 1], gate_ref, up_ref, hidden_ref, head_refs[2 * s])
        )
    factors = [factors[x % sides][x // sides] for x in range(arrays * sides)]

    above, below = (group, where + 2), (group, where - 2)
    across = (group, where + 1 - 2 * side)
    other_core = (half * 2 + 1 - core, where)
    other_half = ((1 - half) * 2 + core, where)
    has_above, has_below = place < count - 1, place > 0

    barrier = pltpu.get_barrier_semaphore()

    def greet(target):
        pl.semaphore_signal(barrier, inc=1, device_id=target, device_id_type=pl.DeviceIdType.MESH)

    pl.when(has_above)(lambda: greet(above))
    pl.when(has_below)(lambda: greet(below))
    for target in (across, other_core, other_half):
        greet(target)

    def span(begin, size):
        return pl.ds(pl.multiple_of(begin, size), size)

    def load(c, k):
        source = (f_ref, g_ref)[k].at[span(c * chunk_rows, chunk_rows), :]
        return pltpu.make_async_copy(
            source, terms.at[lax.rem(c, 2), k], term_sem.at[lax.rem(c, 2), k]
        )

    def load_share(c, k):
        begin = span(side * rows + c * chunk_rows + place * share, share)
        source, target = ((tok_ref, tok_buf), (cot_ref, cot_buf))[k]
        return pltpu.make_async_copy(
            source.at[begin, :], target.at[lax.rem(c, 2)], share_sem.at[lax.rem(c, 2), k]
        )

    def remote(source, target, send, recv, device_id):
        return pltpu.make_async_remote_copy(
            src_ref=source, dst_ref=target, send_sem=send, recv_sem=recv,
            device_id=device_id, device_id_type=pl.DeviceIdType.MESH,
        )


    def sum_copy(c, k, way, b, first):
        slot = lax.rem(c, 2)
        target = landed.at[slot, k, way, b - 1 + way]
        source = terms.at[slot, k, span(b * share, share), :] if first else target
        return remote(
            source, target, sum_send.at[slot, k, way, b], sum_recv.at[slot, k, way, b],
            (above, below)[way],
        )

    def place_of(c, b, on_side):
        return span(on_side * rows + c * chunk_rows + b * share, share)

    def line_copy(c, k, b, way, first):
        target = whole_refs[k].at[place_of(c, b, side), :]
        source = ready.at[lax.rem(c, 2), k] if first else target
        return remote(
            source, target, line_send.at[c, k, way, b], line_recv.at[c, k, b],
            (above, below)[way],
        )

    def side_copy(c, k, b, first):
        target = whole_refs[k].at[place_of(c, b, side), :]
        source = ready.at[lax.rem(c, 2), k] if first else target
        return remote(
            source, target, side_send.at[c, k, b], side_recv.at[c, k, b], across
        )

    def keep_copy(c, k):
        return pltpu.make_async_copy(
            ready.at[lax.rem(c, 2), k], whole_refs[k].at[place_of(c, place, side), :],
            keep_sem.at[c, k],
        )

    def each_first(c, k, act):
        @pl.when(jnp.logical_not(has_below))
        def _():
            for b in range(count - 1, 0, -1):
                act(sum_copy(c, k, 0, b, True))

        @pl.when(jnp.logical_not(has_above))
        def _():
            for b in range(count - 1):
                act(sum_copy(c, k, 1, b, True))

    def send_ends(c, k):
        load(c, k).wait()
        each_first(c, k, lambda copy: copy.start())

    def sums_left(c, k):
        for b in range(count):

            @pl.when(has_below & (place < b))
            def _(b=b):
                sum_copy(c, k, 0, b, False).wait_send()

            @pl.when(has_above & (place > b))
            def _(b=b):
                sum_copy(c, k, 1, b, False).wait_send()

    step = min(16, share)

    def add_on(c, k, way, b):
        slot = lax.rem(c, 2)

        def body(i, carry):
            at = span(i * step, step)
            mine = terms[slot, k, span(b * share + i * step, step), :].astype(F32)
            landed[slot, k, way, b - 1 + way, at, :] = (
                mine + landed[slot, k, way, b - 1 + way, at, :].astype(F32)
            ).astype(BF16)
            return carry

        lax.fori_loop(0, share // step, body, 0)

    def sums(c, k, wave):
        ahead = count - 2 - wave
        for way, b, here in (
            (0, place + ahead, has_below & (place + ahead < count)),
            (1, place - ahead, has_above & (place >= ahead)),
        ):

            @pl.when(here)
            def _(way=way, b=b):
                sum_copy(c, k, way, b, False).wait_recv()

                @pl.when(ahead > 0)
                def _():
                    add_on(c, k, way, b)
                    sum_copy(c, k, way, b, False).start()

    def own_left(c, k):
        pl.when(has_above)(lambda: line_copy(c, k, place, 0, True).wait_send())
        pl.when(has_below)(lambda: line_copy(c, k, place, 1, True).wait_send())
        side_copy(c, k, place, True).wait_send()
        keep_copy(c, k).wait()

    def finish(c, k):
        load_share(c, k).wait()
        pl.when(c > 1)(lambda: own_left(c - 2, k))
        slot = lax.rem(c, 2)

        def body(i, carry):
            at = span(i * step, step)
            up = landed[slot, k, 0, jnp.maximum(place - 1, 0), at, :].astype(F32)
            down = landed[slot, k, 1, jnp.minimum(place, count - 2), at, :].astype(F32)
            total = (
                terms[slot, k, span(place * share + i * step, step), :].astype(F32)
                + jnp.where(has_below, up, 0.0)
                + jnp.where(has_above, down, 0.0)
            )
            wide = tok_buf[slot, at, :].astype(F32)
            if k == 0:
                ready[slot, k, at, :] = (wide + total).astype(BF16)
                return carry
            scale = 1.0 / width
            centred = wide - jnp.sum(wide, axis=1, keepdims=True) * scale
            variance = jnp.sum(centred * centred, axis=1, keepdims=True) * scale
            inverse = lax.rsqrt(variance + EPSILON)
            unit = centred * inverse
            scaled = total * gain_ref[0:1, :]
            mean_scaled = jnp.sum(scaled, axis=1, keepdims=True) * scale
            mean_cross = jnp.sum(scaled * unit, axis=1, keepdims=True) * scale
            ready[slot, k, at, :] = (
                cot_buf[slot, at, :].astype(F32)
                + inverse * (scaled - mean_scaled - unit * mean_cross)
            ).astype(BF16)
            gain_term = total * unit
            for r in range(0, step, 8):
                part_ref[0:8, :] += gain_term[r : r + 8, :]
                part_ref[8:16, :] += total[r : r + 8, :]
            return carry

        lax.fori_loop(0, share // step, body, 0)
        pl.when(has_above)(lambda: line_copy(c, k, place, 0, True).start())
        pl.when(has_below)(lambda: line_copy(c, k, place, 1, True).start())
        side_copy(c, k, place, True).start()
        keep_copy(c, k).start()

    def pass_on(c, k, distance):
        for way, b, here in (
            (0, place - distance, place >= distance),
            (1, place + distance, place + distance < count),
        ):

            @pl.when(here)
            def _(way=way, b=b):
                line_copy(c, k, b, way, False).wait_recv()
                pl.when((has_above, has_below)[way])(
                    lambda: line_copy(c, k, b, way, False).start()
                )
                side_copy(c, k, b, False).start()

    def small_copy(n, target):
        return remote(stages.at[n], came.at[n], small_send.at[n], small_recv.at[n], target)

    def small_sums():
        wide = bias_part.shape[2]
        stages[...] = jnp.zeros_like(stages)
        stages[0, 0:1, :] = jnp.sum(part_ref[0:8, :], axis=0, keepdims=True)
        stages[0, 1:2, :] = jnp.sum(part_ref[8:16, :], axis=0, keepdims=True)
        for s in range(sides):
            stages[0, 2 + s : 3 + s, 0:wide] = jnp.sum(bias_part[s], axis=0, keepdims=True)
        for n, target in enumerate((across, other_core, other_half)):
            copy = small_copy(n, target)
            copy.start()
            copy.wait_recv()
            if n == 0:
                stages[1, 0:2, :] = stages[0, 0:2, :] + came[0, 0:2, :]
                stages[1, 2:3, :] = stages[0, 2:3, :] + came[0, 3:4, :]
            else:
                stages[n + 1] = stages[n] + came[n]

        @pl.when(has_below)
        def _():
            small_copy(3, above).wait_recv()
            stages[3] = stages[3] + came[3]

        pl.when(has_above)(lambda: small_copy(3, above).start())
        stages[4] = stages[3]

        @pl.when(has_above)
        def _():
            small_copy(4, below).wait_recv()
            stages[4] = came[4]

        pl.when(has_below)(lambda: small_copy(4, below).start())
        small_ref[...] = stages[4]
        small_ref[2:3, :] = stages[2, 2:3, :] + came[2, 2:3, :]
        for n, target in enumerate((across, other_core, other_half)):
            small_copy(n, target).wait_send()
        pl.when(has_above)(lambda: small_copy(3, above).wait_send())
        pl.when(has_below)(lambda: small_copy(4, below).wait_send())

    waves = count - 1
    every = max(1, waves // 3)
    works = waves // every

    if count == 4:
        order = ((2, 2, 0), (1, 1, 1), (2, 3, 1))
    else:
        order = tuple((2, distance, distance - 1) for distance in range(1, count))

    def pass_steps(h, live, wave):
        for behind, distance, step in order:
            item = jnp.maximum(h - behind, 0)
            for k in range(2):
                pl.when(
                    live & (wave == step) & (h >= behind) & (lax.rem(item, 2) == k)
                )(lambda: pass_on(item // 2, k, distance))

    def pass_rest():
        for item in range(2 * chunks - 2, 2 * chunks):
            for distance, behind in sorted((step[1], step[0]) for step in order):
                if item + behind >= 2 * chunks:
                    pass_on(item // 2, item % 2, distance)

    def half_steps(h, live, work):
        c = h // 2

        def one(wave, carry):
            pl.when(lax.rem(wave, every) == 0)(lambda: work(wave // every))
            for k in range(2):

                @pl.when(live & (lax.rem(h, 2) == k))
                def _(k=k):
                    more = c + 1 < chunks

                    @pl.when(wave == 0)
                    def _():
                        @pl.when(c > 0)
                        def _():
                            sums_left(c - 1, k)
                            each_first(c - 1, k, lambda copy: copy.wait_send())

                        pl.when(more)(lambda: load_share(c + 1, k).start())

                    sums(c, k, wave)

            pass_steps(h, live, wave)
            for k in range(2):

                @pl.when(live & (lax.rem(h, 2) == k) & (wave == waves - 1))
                def _(k=k):
                    more = c + 1 < chunks
                    pl.when(more)(lambda: load(c + 1, k).start())
                    finish(c, k)
                    pl.when(more)(lambda: send_ends(c + 1, k))

            return carry

        lax.fori_loop(0, waves, one, 0)

    tile_halves = -(-sides * (chunks - 1) // works)

    def tiles_scope(*scratch):
        weights = scratch[: 5 * sides]
        scratch = scratch[5 * sides :]
        normed_buf, tile_cot = scratch[:2]
        head_bufs = scratch[2 : 2 + 2 * sides]
        scratch = scratch[2 + 2 * sides :]
        mids, f_buf, g_buf = scratch[: 3 * sides], scratch[3 * sides], scratch[3 * sides + 1]
        f_total, g_total, weight_sem, in_sem, out_sem = scratch[3 * sides + 2 :]

        def weight_copies(s):
            return [
                pltpu.make_async_copy(weight_refs[x], weights[x], weight_sem.at[x])
                for x in range(5 * s, 5 * s + 5)
            ]

        def tile_in(i):
            slot = lax.rem(i, 2)
            at = span(i * chunk_rows, chunk_rows)
            at_side = span(side * rows + i * chunk_rows, chunk_rows)
            pairs = [(normed_ref.at[at, :], normed_buf), (cot_ref.at[at_side, :], tile_cot)]
            pairs += [(ref.at[at, :], buf) for ref, buf in zip(head_refs, head_bufs)]
            return [
                pltpu.make_async_copy(ref, buf.at[slot], in_sem.at[slot, x])
                for x, (ref, buf) in enumerate(pairs)
            ]

        def tile_out(i):
            at = span(i * chunk_rows, chunk_rows)
            pairs = list(zip(mids, mid_refs)) + [(f_buf, f_ref), (g_buf, g_ref)]
            return [
                pltpu.make_async_copy(buf, ref.at[at, :], out_sem.at[x])
                for x, (buf, ref) in enumerate(pairs)
            ]

        def wait_out(i):
            for copy in tile_out(i):
                copy.wait()

        def tile(i, s):
            slot = lax.rem(i, 2)
            if s == 0:
                for copy in tile_in(i):
                    copy.wait()

                @pl.when(i + 1 < chunks)
                def _():
                    for copy in tile_in(i + 1):
                        copy.start()

                pl.when(i > 1)(lambda: wait_out(i - 1))

            @pl.when(i == 0)
            def _():
                for copy in weight_copies(s):
                    copy.wait()

            qkv_w, out_w, gate_w, up_w, down_w = weights[5 * s : 5 * s + 5]
            hidden_buf, gate_buf, up_buf = mids[3 * s : 3 * s + 3]
            normed, cot = normed_buf[slot], tile_cot[slot]
            gate = product(normed, gate_w[...])
            up = product(normed, up_w[...])
            sig = 1.0 / (1.0 + jnp.exp(-gate))
            silu = gate * sig
            hidden = (silu * up).astype(BF16)
            hidden_buf[...] = hidden
            grad_hidden = cols_product(cot, down_w[...])
            gate_back = (grad_hidden * up * sig * (1.0 + gate * (1.0 - sig))).astype(BF16)
            up_back = (grad_hidden * silu).astype(BF16)
            gate_buf[...] = gate_back
            up_buf[...] = up_back
            forward = product(hidden, down_w[...])
            forward += product(head_bufs[2 * s][slot], out_w[...])
            backward = cols_product(gate_back, gate_w[...])
            backward += cols_product(up_back, up_w[...])
            qkv_back = head_bufs[2 * s + 1][slot]
            backward += cols_product(qkv_back, qkv_w[...])
            bias_part[s] += (
                qkv_back.astype(F32).reshape(chunk_rows // 8, 8, qkv_back.shape[1]).sum(axis=0)
            )
            if s > 0:
                forward += f_total[...]
                backward += g_total[...]
            if s < sides - 1:
                f_total[...] = forward
                g_total[...] = backward
                return
            f_buf[...] = forward.astype(BF16)
            g_buf[...] = backward.astype(BF16)
            for copy in tile_out(i):
                copy.start()

        def work(turn, n):
            first = turn == 0
            unit = jnp.maximum(works * turn - works, 0) + n
            i = jnp.where(first, 0, 1 + unit // sides)
            part = jnp.where(first, n - works + sides, lax.rem(unit, sides))
            for s in range(sides):
                pl.when((part == s) & (i < chunks))(lambda: tile(i, s))

        for s in range(sides):
            for copy in weight_copies(s):
                copy.start()
        for copy in tile_in(0):
            copy.start()
        for k in range(2):
            load_share(0, k).start()
        part_ref[...] = jnp.zeros_like(part_ref)
        bias_part[...] = jnp.zeros_like(bias_part)
        pl.semaphore_wait(
            barrier, 3 + has_above.astype(jnp.int32) + has_below.astype(jnp.int32)
        )

        def chunk(turn, carry):
            half_steps(
                jnp.maximum(turn, 1) - 1, turn > 0, lambda n: work(turn, n)
            )

            @pl.when(turn == 0)
            def _():
                wait_out(0)
                for k in range(2):
                    load(0, k).start()
                for k in range(2):
                    send_ends(0, k)

            return carry

        lax.fori_loop(0, tile_halves + 1, chunk, 0)
        wait_out(chunks - 1)

    tall = width
    hidden_cols = mid_refs[0].shape[1]
    pl.run_scoped(
        tiles_scope,
        *[pltpu.VMEM(ref.shape, BF16) for ref in weight_refs],
        pltpu.VMEM((2, chunk_rows, width), BF16),
        pltpu.VMEM((2, chunk_rows, width), BF16),
        *[pltpu.VMEM((2, chunk_rows, ref.shape[1]), BF16) for ref in head_refs],
        *[pltpu.VMEM((chunk_rows, hidden_cols), BF16) for _ in mid_refs],
        pltpu.VMEM((chunk_rows, width), BF16),
        pltpu.VMEM((chunk_rows, width), BF16),
        pltpu.VMEM((chunk_rows, width), F32),
        pltpu.VMEM((chunk_rows, width), F32),
        pltpu.SemaphoreType.DMA((5 * sides,)),
        pltpu.SemaphoreType.DMA((2, 2 + 2 * sides)),
        pltpu.SemaphoreType.DMA((3 * sides + 2,)),
    )


    pieces = core_send.shape[2]
    each = 2
    size = tall // pieces

    def grads_scope(*scratch):
        factor_bufs, scratch = scratch[: arrays * sides], scratch[arrays * sides :]
        held, scratch = scratch[: arrays * sides], scratch[arrays * sides :]
        extra, scratch = scratch[: arrays * sides], scratch[arrays * sides :]
        turned, scratch = scratch[: arrays - 1], scratch[arrays - 1 :]
        left_bufs, factor_sem, left_sem = scratch[:2], scratch[2], scratch[3]

        def factor_copy(x):
            return pltpu.make_async_copy(factors[x], factor_bufs[x], factor_sem.at[x])

        def piece(ref, j):
            return ref.at[span(j * size, size), :]

        def piece_of(u):
            owner_core = jnp.where(u < 2 * each, 1 - core, core)
            owner_half = jnp.where((u // each) % 2 == 0, 1 - half, half)
            return (owner_half * 2 + owner_core) * each + lax.rem(u, each)

        def slot_of(u):
            return jnp.where(u < 3 * each, lax.rem(u, each), each + lax.rem(u, each))

        def left_copy(u, which):
            at = span(piece_of(u) * size, size)
            source = (
                normed_ref.at[:, at] if which == 0 else cot_ref.at[span(side * rows, rows), at]
            )
            return pltpu.make_async_copy(
                source, left_bufs[which].at[lax.rem(u, 2)], left_sem.at[which, lax.rem(u, 2)]
            )

        def to_core(a, s, j, slot):
            x = 2 * a + s
            return remote(
                held[x].at[slot], piece(core_land[x], j),
                core_send.at[a, s, j], core_recv.at[a, s, j], other_core,
            )

        def to_far(a, s, i, j):
            x = 2 * a + s
            return remote(
                held[x].at[i], piece(far_land[x], j),
                far_send.at[a, s, j], far_recv.at[a, s, j], other_half,
            )

        def to_over(a, i, j):
            return remote(
                held[2 * a + 1].at[each + i], piece(side_land[a], j),
                over_send.at[a, j], over_recv.at[a, j], across,
            )

        def final_piece(a, j):
            return grad_outs[a].at[j] if a else grad_outs[a].at[span(j * size, size), :]

        def final_source(a, i):
            return turned[a - 1].at[i] if a else held[0].at[each + i]

        def back_copy(a, i, j, way, first):
            target = final_piece(a, j)
            source = final_source(a, i) if first else target
            return remote(
                source, target, back_send.at[a, way, j], back_recv.at[a, j],
                (other_core, other_half)[way],
            )

        def save_copy(a, i, j):
            return pltpu.make_async_copy(
                final_source(a, i), final_piece(a, j), save_sem.at[a, i]
            )

        def their_piece(i):
            return ((1 - half) * 2 + core) * each + i

        def my_piece(i):
            return (half * 2 + core) * each + i

        def add_into(target, slot, source):
            def body(i, carry):
                at = span(i * 16, 16)
                target[slot, at, :] = (
                    target[slot, at, :].astype(F32) + source[at, :].astype(F32)
                ).astype(BF16)
                return carry

            lax.fori_loop(0, size // 16, body, 0)

        def fetch(lands, j, ids):
            copies = [
                pltpu.make_async_copy(piece(lands[n], j), extra[x], load_sem.at[x])
                for n, x in enumerate(ids)
            ]
            for copy in copies:
                copy.start()
            for copy in copies:
                copy.wait()

        everything = range(2 * arrays)

        def make(u, which):
            @pl.when(u == 0)
            def _():
                for x in everything:
                    if (x // 2 < 3) == (which == 0):
                        factor_copy(x).wait()

            left_copy(u, which).wait()
            pl.when(u + 1 < pieces)(lambda: left_copy(u + 1, which).start())
            slot = slot_of(u)
            left = left_bufs[which][lax.rem(u, 2)].T

            @pl.when((u >= each) & (u < 3 * each))
            def _():
                for x in everything:
                    if (x // 2 < 3) == (which == 0):
                        to_core(x // 2, x % 2, piece_of(u - each), slot).wait_send()

            for x in everything:
                if (x // 2 < 3) == (which == 0):
                    held[x][slot] = product(left, factor_bufs[x][...]).astype(BF16)

            @pl.when(u < 2 * each)
            def _():
                for x in everything:
                    if (x // 2 < 3) == (which == 0):
                        to_core(x // 2, x % 2, piece_of(u), slot).start()

        def gather_terms(slot, j):
            for x in everything:
                to_core(x // 2, x % 2, j, 0).wait_recv()
            fetch(core_land, j, everything)
            for x in everything:
                add_into(held[x], slot, extra[x])

        def grads_far(i):
            j = their_piece(i)
            gather_terms(i, j)
            for x in everything:
                to_far(x // 2, x % 2, i, j).start()

        def grads_over(i):
            j = my_piece(i)
            gather_terms(each + i, j)
            for x in everything:
                to_far(x // 2, x % 2, i, j).wait_recv()
            fetch(far_land, j, everything)
            for a in range(arrays):
                add_into(held[2 * a + 1], each + i, extra[2 * a + 1])
                to_over(a, i, j).start()
            for a in range(arrays):
                add_into(held[2 * a], each + i, extra[2 * a])

        def grads_back(i):
            j = my_piece(i)
            for a in range(arrays):
                to_over(a, i, j).wait_recv()
            fetch(side_land, j, range(0, 2 * arrays, 2))
            for a in range(arrays):
                if a:
                    total = held[2 * a][each + i].astype(F32) + extra[2 * a][...].astype(F32)
                    turned[a - 1][i] = total.T.astype(BF16)
                else:
                    add_into(held[0], each + i, extra[0])
                back_copy(a, i, j, 1, True).start()
                back_copy(a, i, j, 0, True).start()
                save_copy(a, i, j).start()

        def grads_pass(i):
            j = their_piece(i)
            for a in range(arrays):
                back_copy(a, i, j, 1, False).wait_recv()
                back_copy(a, i, j, 0, False).start()

        def grads_drain():
            for i in range(each):
                mine, theirs = my_piece(i), their_piece(i)
                for a in range(arrays):
                    for s in range(2):
                        to_far(a, s, i, theirs).wait_send()
                    to_over(a, i, mine).wait_send()
                    back_copy(a, i, mine, 1, True).wait_send()
                    back_copy(a, i, mine, 0, True).wait_send()
                    back_copy(a, i, theirs, 0, False).wait_send()
                    save_copy(a, i, mine).wait()
            for u in range(2 * each):
                for a in range(arrays):
                    back_copy(a, 0, piece_of(u), 0, False).wait_recv()

        events = {
            26: (grads_far, 0),
            28: (grads_far, 1),
            35: (grads_over, 0),
            40: (grads_back, 0),
            43: (grads_over, 1),
        }

        def work(h, n):
            v = works * (h - tile_halves) + n
            for which in range(2):
                pl.when((v < 2 * pieces) & (lax.rem(v, 2) == which))(
                    lambda: make(v // 2, which)
                )
            for at, (act, i) in events.items():
                pl.when(works * h + n == at)(lambda: act(i))

        for x in everything:
            factor_copy(x).start()
        for which in range(2):
            left_copy(0, which).start()

        def chunk(c, carry):
            half_steps(c, c >= 0, lambda n: work(c, n))
            return carry

        lax.fori_loop(tile_halves, 2 * chunks, chunk, 0)
        pass_rest()
        grads_back(1)
        small_sums()
        for i in range(each):
            grads_pass(i)
        grads_drain()

    factor_shapes = [ref.shape for ref in factors]
    pl.run_scoped(
        grads_scope,
        *[pltpu.VMEM(shape, BF16) for shape in factor_shapes],
        *[pltpu.VMEM((2 * each, size, shape[1]), BF16) for shape in factor_shapes],
        *[pltpu.VMEM((size, shape[1]), BF16) for shape in factor_shapes],
        *[pltpu.VMEM((each, shape[1], size), BF16) for shape in factor_shapes[2::2]],
        pltpu.VMEM((2, rows, size), BF16),
        pltpu.VMEM((2, rows, size), BF16),
        pltpu.SemaphoreType.DMA((2 * arrays,)),
        pltpu.SemaphoreType.DMA((2, 2)),
    )

    for k in range(2):
        sums_left(chunks - 1, k)
        each_first(chunks - 1, k, lambda copy: copy.wait_send())
        own_left(chunks - 2, k)
        own_left(chunks - 1, k)

    def drain(c, carry):
        for k in range(2):
            for b in range(count):
                pl.when((place > b) & has_above)(
                    lambda: line_copy(c, k, b, 0, False).wait_send()
                )
                pl.when((place < b) & has_below)(
                    lambda: line_copy(c, k, b, 1, False).wait_send()
                )
                pl.when(place != b)(lambda: side_copy(c, k, b, False).wait_send())
                side_copy(c, k, b, False).wait_recv()
        return carry

    lax.fori_loop(0, chunks, drain, 0)


def layer(normed, tokens, cotangent, heads, weights, gain, count, chunks, dp_size):
    row_count, width = tokens.shape
    rows = row_count // 2
    share = rows // chunks // count
    sides, arrays = len(weights), 5
    pieces = 2 * dp_size
    sem = pltpu.SemaphoreType.DMA
    flat_heads = [array for group in heads for array in group]
    flat_weights = [array for group in weights for array in group]
    hidden = weights[0][2].shape[1]
    columns = [heads[0][1].shape[1], hidden, hidden, hidden, heads[0][0].shape[1]]
    whole = jax.ShapeDtypeStruct(tokens.shape, BF16)
    half_sums = [jax.ShapeDtypeStruct((width, n), BF16) for n in columns]
    finals = half_sums[:1] + [
        jax.ShapeDtypeStruct((pieces, n, width // pieces), BF16) for n in columns[1:]
    ]
    lands = [shape for shape in half_sums for _ in range(sides)]
    anywhere = pl.BlockSpec(memory_space=pl.ANY)
    vmem = pl.BlockSpec(memory_space=pltpu.VMEM)
    own_rows = [jax.ShapeDtypeStruct((rows, width), BF16)] * 2
    own_rows += [jax.ShapeDtypeStruct((rows, hidden), BF16)] * (3 * sides)
    outs = pl.pallas_call(
        functools.partial(layer_kernel, chunks, sides),
        in_specs=[anywhere] * (3 + len(flat_heads) + len(flat_weights)) + [vmem],
        out_specs=[anywhere, anywhere, vmem] + [anywhere] * (6 * arrays + len(own_rows)),
        out_shape=[whole, whole, jax.ShapeDtypeStruct((8, width), F32)]
        + finals + lands + lands + half_sums + own_rows,
        scratch_shapes=[
            pltpu.VMEM((2, 2, count * share, width), BF16),
            pltpu.VMEM((2, 2, 2, count - 1, share, width), BF16),
            pltpu.VMEM((2, 2, share, width), BF16),
            pltpu.VMEM((2, share, width), BF16),
            pltpu.VMEM((2, share, width), BF16),
            sem((2, 2)),
            sem((2, 2)),
            sem((2, 2, 2, count)),
            sem((2, 2, 2, count)),
            sem((chunks, 2, 2, count)),
            sem((chunks, 2, count)),
            sem((chunks, 2, count)),
            sem((chunks, 2, count)),
            sem((chunks, 2)),
            sem((arrays, 2, pieces)),
            sem((arrays, 2, pieces)),
            sem((arrays, 2, pieces)),
            sem((arrays, 2, pieces)),
            sem((arrays, pieces)),
            sem((arrays, pieces)),
            sem((arrays, 2, pieces)),
            sem((arrays, pieces)),
            sem((2 * arrays,)),
            sem((arrays, 2)),
            pltpu.VMEM((16, width), F32),
            pltpu.VMEM((sides, 8, columns[0]), F32),
            pltpu.VMEM((5, 8, width), F32),
            pltpu.VMEM((5, 8, width), F32),
            sem((5,)),
            sem((5,)),
        ],
        compiler_params=pltpu.CompilerParams(
            collective_id=0, has_side_effects=True, vmem_limit_bytes=63 * 2**20
        ),
        cost_estimate=pl.CostEstimate(
            flops=6 * rows * sum(array.size for array in flat_weights),
            bytes_accessed=800 * 2**20,
            transcendentals=0,
        ),
        name="layer",
    )(normed, tokens, cotangent, *flat_heads, *flat_weights, gain)
    out, grad, small = outs[:3]
    grads = [outs[3].astype(F32)]
    for blocks in outs[4 : 3 + arrays]:
        grads.append(blocks.transpose(1, 0, 2).reshape(blocks.shape[1], width).astype(F32))
    return out, grad, small[0], small[1], small[2, : columns[0]], grads


def body(
    tokens,
    lengths,
    norm_gain,
    norm_shift,
    qkv_weight,
    qkv_bias,
    out_weight,
    gate_weight,
    up_weight,
    down_weight,
    cotangent,
):
    tensor_size = lax.axis_size("tensor")
    dp_size = lax.axis_size("dp")
    count = tensor_size // 2
    where = lax.axis_index("tensor")
    dp_place = lax.axis_index("dp")
    side = where % 2
    across = [(i, i ^ 1) for i in range(tensor_size)]
    row_count, width = tokens.shape
    rows = row_count // 2
    chunk_count = 8

    def own_part(weight):
        part = weight.shape[0] // dp_size
        return lax.dynamic_slice_in_dim(weight, dp_place * part, part, 0)

    def partner(parts, before, after):
        parts, _ = lax.optimization_barrier((parts, before))
        parts = [lax.ppermute(part, "tensor", across) for part in parts]
        parts, _ = lax.optimization_barrier((parts, after))
        return [lax.all_gather(part, "dp", axis=0, tiled=True) for part in parts]

    head_weights = (qkv_weight, out_weight)
    mid_weights = (gate_weight, up_weight, down_weight)
    biases = (qkv_bias, lax.ppermute(qkv_bias, "tensor", across))

    length = lax.dynamic_slice_in_dim(lengths, side, 1, 0)
    norm = (norm_gain, norm_shift)
    normed, *own_group = project(side, tokens, cotangent, norm, head_weights, biases[0])
    tables = rotary_tables(rows)
    even = (out_weight.shape[0] // HEAD) % 2 == 0
    other_heads = partner([own_part(weight) for weight in head_weights], (), normed)
    mid_parts = [own_part(weight) for weight in mid_weights]
    if even:
        heads = [attention(length, *own_group, *tables)]
        other_mids = partner(mid_parts, normed, heads[0])
        other_group = project(side, normed, cotangent, (), other_heads, biases[1])
        heads.append(attention(length, *other_group, *tables))
    else:
        other_mids = partner(mid_parts, normed, ())
        other_group = project(side, normed, cotangent, (), other_heads, biases[1])
        pairs = zip(own_group, other_group)
        attended, qkv_back = attention(
            length, *[jnp.concatenate(pair, axis=1) for pair in pairs], *tables
        )
        cut, wide = out_weight.shape[0], qkv_weight.shape[1]
        heads = [
            (attended[:, s * cut : (s + 1) * cut], qkv_back[:, s * wide : (s + 1) * wide])
            for s in range(2)
        ]
    weights = ((*head_weights, *mid_weights), (*other_heads, *other_mids))
    layer_out, grad_tokens, gain_part, shift_part, grad_bias, grads = layer(
        normed, tokens, cotangent, heads, weights, norm_gain[None, :], count, chunk_count, dp_size
    )
    grad_qkv, grad_gate, grad_up, grad_down, grad_out = grads
    grad_gate, grad_up = grad_gate.T, grad_up.T
    return (
        layer_out,
        grad_tokens,
        gain_part,
        shift_part,
        grad_qkv,
        grad_bias,
        grad_out,
        grad_gate,
        grad_up,
        grad_down,
    )


def solution(mesh):
    placed = (
        P("dp", None),
        P("dp"),
        P(),
        P(),
        P(None, "tensor"),
        P("tensor"),
        P("tensor", None),
        P(None, "tensor"),
        P(None, "tensor"),
        P("tensor", None),
        P("dp", None),
    )
    return jax.shard_map(
        body,
        mesh=mesh,
        in_specs=placed,
        out_specs=(
            P("dp", None),
            P("dp", None),
            P(),
            P(),
            P(None, "tensor"),
            P("tensor"),
            P("tensor", None),
            P(None, "tensor"),
            P(None, "tensor"),
            P("tensor", None),
        ),
        check_vma=False,
    )
```

```python
import functools

import jax
import jax.numpy as jnp
import numpy as np
from jax import lax
from jax.experimental import pallas as pl
from jax.experimental.pallas import tpu as pltpu
from jax.sharding import PartitionSpec as P

HEAD = 64
ROT = 16
PAIR = 2 * HEAD
TRIPLE = 6 * HEAD

EPSILON = 1e-05
NEGATIVE = -1e30
F32 = jnp.float32
BF16 = jnp.bfloat16


def rows_product(former, latter):
    return lax.dot_general(
        former, latter, (((0,), (0,)), ((), ())), preferred_element_type=F32
    )


def cols_product(former, latter):
    return lax.dot_general(
        former, latter, (((1,), (1,)), ((), ())), preferred_element_type=F32
    )


def product(former, latter):
    return jnp.dot(former, latter, preferred_element_type=F32)


def rotary_tables(seq_len):
    frequency = np.float32(10000.0) ** (-np.arange(0, ROT, 2).astype(np.float32) / ROT)
    angles = np.arange(seq_len).astype(np.float32)[:, None] * frequency[None, :]
    cosine, sine = np.cos(angles), np.sin(angles)
    still = HEAD - ROT
    cos_head = np.concatenate([cosine, cosine, np.ones((seq_len, still))], axis=1)
    sin_head = np.concatenate([-sine, sine, np.zeros((seq_len, still))], axis=1)
    return [jnp.asarray(np.tile(table, (1, 2)), F32) for table in (cos_head, sin_head)]


def attention_kernel(
    len_ref, qkv_ref, grad_ref, cos_ref, sin_ref, att_ref, back_ref,
    score, expo, query, key_value, key_value_t, query_t, grad_query, grad_kv_t,
):
    seq_len = qkv_ref.shape[0]
    block = score.shape[1]
    steps = seq_len // block
    length = len_ref[0]
    lane = lax.broadcasted_iota(jnp.int32, (block, PAIR), 1)
    left = lane < HEAD
    near = lax.rem(lane, HEAD) < ROT // 2

    def turn(tile, cosine, sine):
        swapped = jnp.where(
            near, pltpu.roll(tile, PAIR - ROT // 2, 1), pltpu.roll(tile, ROT // 2, 1)
        )
        return tile * cosine + swapped * sine

    def tables(rows):
        cosine, sine = cos_ref[rows, :], sin_ref[rows, :]
        return (
            (cosine, sine),
            (jnp.where(left, 1.0, cosine), jnp.where(left, 0.0, sine)),
            (jnp.where(left, cosine, 1.0), jnp.where(left, sine, 0.0)),
        )

    def prepare(i, carry):
        rows = pl.ds(pl.multiple_of(i * block, block), block)
        tabs = tables(rows)
        first = turn(qkv_ref[rows, 0:PAIR], *tabs[0])
        second = turn(qkv_ref[rows, PAIR : 2 * PAIR], *tabs[1])
        third = turn(qkv_ref[rows, 2 * PAIR : 3 * PAIR], *tabs[2])
        scale = HEAD**-0.5
        first_q = first.astype(BF16).astype(F32) * scale
        second_q = second.astype(BF16).astype(F32) * scale
        query[0, rows, :] = jnp.where(left, 0.0, pltpu.roll(first_q, HEAD, 1)).astype(BF16)
        query[1, rows, :] = jnp.where(left, pltpu.roll(second_q, HEAD, 1), 0.0).astype(BF16)
        for h, tile in enumerate((jnp.where(left, second, first), third)):
            key_value[h, rows, :] = tile.astype(BF16)
            key_value_t[h, :, rows] = tile.T.astype(BF16)
        query_t[0, :, rows] = first_q.T[0:HEAD, :].astype(BF16)
        query_t[1, :, rows] = second_q.T[HEAD:PAIR, :].astype(BF16)
        zero = jnp.zeros((block, PAIR), F32)
        grad_query[rows, :] = zero
        att_ref[rows, :] = zero.astype(BF16)
        for h in range(2):
            grad_kv_t[h, :, rows] = jnp.zeros((PAIR, block), F32)
        return carry

    lax.fori_loop(0, steps, prepare, 0)

    def fold(tile, op):
        out = tile[:, 0:PAIR]
        for c in range(1, block // PAIR):
            out = op(out, tile[:, c * PAIR : (c + 1) * PAIR])
        return out

    def block_rows(i):
        rows = pl.ds(i * block, block)
        spans = [pl.ds(j * block, block) for j in range(i + 1)]
        q_block = [query[h, rows, :] for h in range(2)]
        below = lax.broadcasted_iota(jnp.int32, (block, block), 1) <= lax.broadcasted_iota(
            jnp.int32, (block, block), 0
        )
        maxima = []
        for h in range(2):
            top = None
            for j, cols in enumerate(spans):
                tile = product(q_block[h], key_value_t[h, :, cols])
                if j == i:
                    tile = jnp.where(below, tile, NEGATIVE)
                score[h, :, cols] = tile
                high = fold(tile, jnp.maximum)
                top = high if top is None else jnp.maximum(top, high)
            maxima.append(jnp.max(top, axis=1, keepdims=True))

        mixed, inverse = [], []
        for h in range(2):
            mixture = total = None
            for cols in spans:
                tile = jnp.exp(score[h, :, cols] - maxima[h])
                low = tile.astype(BF16)
                expo[h, :, cols] = low
                part = product(low, key_value[h, cols, :])
                amount = fold(tile, jnp.add)
                mixture = part if mixture is None else mixture + part
                total = amount if total is None else total + amount
            mixed.append(mixture)
            inverse.append(1.0 / jnp.sum(total, axis=1, keepdims=True))

        place = i * block + lax.broadcasted_iota(jnp.int32, (block, 1), 0)
        valid = (place < length).astype(F32)
        mixture = jnp.where(left, mixed[0] * inverse[0], mixed[1] * inverse[1]) * valid
        att_ref[rows, :] = mixture.astype(BF16)
        upstream = grad_ref[rows, :].astype(F32) * valid
        inner = upstream * mixture
        scale = HEAD**-0.5
        turned = []
        for h in range(2):
            own = left if h == 0 else jnp.logical_not(left)
            inner_sum = jnp.sum(jnp.where(own, inner, 0.0), axis=1, keepdims=True) * inverse[h]
            mine = jnp.where(own, upstream * inverse[h], 0.0)
            scaled = mine.astype(BF16)
            half = slice(0, HEAD) if h == 0 else slice(HEAD, PAIR)
            scaled_t = mine.T[half, :].astype(BF16)
            queries_t = query_t[h, :, rows]
            grad = None
            for cols in spans:
                low = expo[h, :, cols]
                grad_weight = product(scaled, key_value_t[h, :, cols])
                grad_score = (low.astype(F32) * (grad_weight - inner_sum)).astype(BF16)
                part = product(grad_score, key_value[h, cols, :])
                grad = part if grad is None else grad + part
                key_at, value_at = (HEAD, 0) if h == 0 else (0, HEAD)
                grad_kv_t[h, key_at : key_at + HEAD, cols] += product(queries_t, grad_score)
                grad_kv_t[h, value_at : value_at + HEAD, cols] += product(scaled_t, low)
            turned.append(pltpu.roll(grad, HEAD, 1))
        grad_query[rows, :] = jnp.where(left, turned[0], turned[1]) * scale

    for i in range(steps):
        pl.when(i * block < length)(functools.partial(block_rows, i))

    def finish(i, carry):
        rows = pl.ds(pl.multiple_of(i * block, block), block)
        tabs = tables(rows)
        gq = grad_query[rows, :]
        low_kv = grad_kv_t[0, :, rows].T
        high_kv = grad_kv_t[1, :, rows].T
        tiles = (jnp.where(left, gq, low_kv), jnp.where(left, low_kv, gq), high_kv)
        for c in range(3):
            back_ref[rows, c * PAIR : (c + 1) * PAIR] = turn(
                tiles[c], tabs[c][0], -tabs[c][1]
            ).astype(BF16)
        return carry

    lax.fori_loop(0, steps, finish, 0)


def attention(length, qkv, grad_mixture, cosine, sine):
    seq_len, width = qkv.shape
    pairs = width // TRIPLE
    block = min(512, seq_len)
    flops = 6 * 2 * (2 * pairs) * seq_len * seq_len * PAIR
    return pl.pallas_call(
        attention_kernel,
        grid=(pairs,),
        in_specs=[
            pl.BlockSpec(memory_space=pltpu.SMEM),
            pl.BlockSpec((seq_len, TRIPLE), lambda g: (0, g)),
            pl.BlockSpec((seq_len, PAIR), lambda g: (0, g)),
            pl.BlockSpec((seq_len, PAIR), lambda g: (0, 0)),
            pl.BlockSpec((seq_len, PAIR), lambda g: (0, 0)),
        ],
        out_specs=[
            pl.BlockSpec((seq_len, PAIR), lambda g: (0, g)),
            pl.BlockSpec((seq_len, TRIPLE), lambda g: (0, g)),
        ],
        out_shape=[
            jax.ShapeDtypeStruct((seq_len, pairs * PAIR), BF16),
            jax.ShapeDtypeStruct((seq_len, width), BF16),
        ],
        scratch_shapes=[
            pltpu.VMEM((2, block, seq_len), F32),
            pltpu.VMEM((2, block, seq_len), BF16),
            pltpu.VMEM((2, seq_len, PAIR), BF16),
            pltpu.VMEM((2, seq_len, PAIR), BF16),
            pltpu.VMEM((2, PAIR, seq_len), BF16),
            pltpu.VMEM((2, HEAD, seq_len), BF16),
            pltpu.VMEM((seq_len, PAIR), F32),
            pltpu.VMEM((2, PAIR, seq_len), F32),
        ],
        compiler_params=pltpu.CompilerParams(vmem_limit_bytes=48 * 2**20),
        cost_estimate=pl.CostEstimate(
            flops=flops,
            bytes_accessed=seq_len * width * 8,
            transcendentals=2 * pairs * seq_len * seq_len // 2,
        ),
        name="attention",
    )(length, qkv, grad_mixture, cosine, sine)


def start_kernel(
    side_ref, tok_ref, cot_ref, gain_ref, shift_ref, qkv_w, bias_ref, out_w,
    qkv_ref, grad_ref, normed_ref, normed_t_ref, cot_t_ref,
):
    wide = tok_ref[...].astype(F32)
    centred = wide - jnp.mean(wide, axis=1, keepdims=True)
    variance = jnp.mean(centred * centred, axis=1, keepdims=True)
    unit = centred * lax.rsqrt(variance + EPSILON)
    normed = (unit * gain_ref[...] + shift_ref[...]).astype(BF16)
    normed_ref[...] = normed
    normed_t_ref[...] = normed.T
    cot_t_ref[...] = cot_ref[...].T
    qkv_ref[...] = product(normed, qkv_w[...]) + bias_ref[...]
    grad_ref[...] = cols_product(cot_ref[...], out_w[...]).astype(BF16)


def project_kernel(side_ref, normed_ref, cot_ref, qkv_w, bias_ref, out_w, qkv_ref, grad_ref):
    qkv_ref[...] = product(normed_ref[...], qkv_w[...]) + bias_ref[...]
    grad_ref[...] = cols_product(cot_ref[...], out_w[...]).astype(BF16)


def project(side, rows_in, cotangent, norm, weights, bias):
    rows, width = cotangent.shape[0] // 2, cotangent.shape[1]
    tile = min(256, rows)
    tiles = rows // tile
    qkv_weight, out_weight = weights
    heads, wide = out_weight.shape[0], qkv_weight.shape[1]

    def sided(i, side_ref):
        return (side_ref[0] * tiles + i, 0)

    def fixed(i, side_ref):
        return (0, 0)

    def rowed(i, side_ref):
        return (i, 0)

    flat = [part[None, :] for part in norm]
    flat += [qkv_weight, bias.astype(F32)[None, :], out_weight]
    outs = [((rows, wide), F32), ((rows, heads), BF16)]
    out_specs = [pl.BlockSpec((tile, shape[1]), rowed) for shape, _ in outs]
    if norm:
        outs += [((rows, width), BF16)] + [((width, rows), BF16)] * 2
        out_specs += [pl.BlockSpec((tile, width), rowed)]
        out_specs += [pl.BlockSpec((width, tile), lambda i, side_ref: (0, i))] * 2
    return pl.pallas_call(
        start_kernel if norm else project_kernel,
        grid_spec=pltpu.PrefetchScalarGridSpec(
            num_scalar_prefetch=1,
            grid=(tiles,),
            in_specs=[
                pl.BlockSpec((tile, width), sided if norm else rowed),
                pl.BlockSpec((tile, width), sided),
            ]
            + [pl.BlockSpec(array.shape, fixed) for array in flat],
            out_specs=out_specs,
        ),
        out_shape=[jax.ShapeDtypeStruct(*out) for out in outs],
        compiler_params=pltpu.CompilerParams(vmem_limit_bytes=40 * 2**20),
        cost_estimate=pl.CostEstimate(
            flops=2 * rows * width * (wide + heads),
            bytes_accessed=rows * (6 * width + 4 * wide),
            transcendentals=rows,
        ),
        name="project",
    )(side[None], rows_in, cotangent, *flat)


def layer_kernel(chunks, sides, *refs):
    normed_ref, tok_ref, cot_ref = refs[:3]
    left_refs, refs = refs[3:5], refs[5:]
    head_refs, refs = refs[: 2 * sides], refs[2 * sides :]
    weight_refs, gain_ref = refs[: 5 * sides], refs[5 * sides]
    refs = refs[5 * sides + 1 :]
    out_ref, grad_ref, small_ref = refs[:3]
    refs = refs[3:]
    arrays = 5
    grad_outs, core_land = refs[:arrays], refs[arrays : 3 * arrays]
    far_land, side_land = refs[3 * arrays : 5 * arrays], refs[5 * arrays : 6 * arrays]
    refs = refs[6 * arrays :]
    f_ref, g_ref = refs[:2]
    mid_refs, refs = refs[2 : 2 + 3 * sides], refs[2 + 3 * sides :]
    (
        terms, landed, ready, tok_buf, cot_buf,
        term_sem, share_sem, sum_send, sum_recv,
        line_send, line_recv, side_send, side_recv, keep_sem,
        core_send, core_recv, far_send, far_recv, over_send, over_recv,
        back_send, back_recv, load_sem, save_sem,
        part_ref, bias_part, stages, came, small_send, small_recv,
    ) = refs
    share, width = landed.shape[4:]
    count = landed.shape[3] + 1
    chunk_rows = count * share
    rows = chunks * chunk_rows
    where = lax.axis_index("tensor")
    group = lax.axis_index("dp")
    place, side = where // 2, where % 2
    half, core = group // 2, group % 2
    whole_refs = (out_ref, grad_ref)
    factors = []
    for s in range(sides):
        hidden_ref, gate_ref, up_ref = mid_refs[3 * s : 3 * s + 3]
        factors.append(
            (head_refs[2 * s + 1], gate_ref, up_ref, hidden_ref, head_refs[2 * s])
        )
    factors = [factors[x % sides][x // sides] for x in range(arrays * sides)]

    above, below = (group, where + 2), (group, where - 2)
    across = (group, where + 1 - 2 * side)
    other_core = (half * 2 + 1 - core, where)
    other_half = ((1 - half) * 2 + core, where)
    has_above, has_below = place < count - 1, place > 0

    barrier = pltpu.get_barrier_semaphore()

    def greet(target):
        pl.semaphore_signal(barrier, inc=1, device_id=target, device_id_type=pl.DeviceIdType.MESH)

    pl.when(has_above)(lambda: greet(above))
    pl.when(has_below)(lambda: greet(below))
    for target in (across, other_core, other_half):
        greet(target)

    def span(begin, size):
        return pl.ds(pl.multiple_of(begin, size), size)

    def load(c, k):
        source = (f_ref, g_ref)[k].at[span(c * chunk_rows, chunk_rows), :]
        return pltpu.make_async_copy(
            source, terms.at[lax.rem(c, 2), k], term_sem.at[lax.rem(c, 2), k]
        )

    def load_share(c, k):
        begin = span(side * rows + c * chunk_rows + place * share, share)
        source, target = ((tok_ref, tok_buf), (cot_ref, cot_buf))[k]
        return pltpu.make_async_copy(
            source.at[begin, :], target.at[lax.rem(c, 2)], share_sem.at[lax.rem(c, 2), k]
        )

    def remote(source, target, send, recv, device_id):
        return pltpu.make_async_remote_copy(
            src_ref=source, dst_ref=target, send_sem=send, recv_sem=recv,
            device_id=device_id, device_id_type=pl.DeviceIdType.MESH,
        )


    def sum_copy(c, k, way, b, first):
        slot = lax.rem(c, 2)
        target = landed.at[slot, k, way, b - 1 + way]
        source = terms.at[slot, k, span(b * share, share), :] if first else target
        return remote(
            source, target, sum_send.at[slot, k, way, b], sum_recv.at[slot, k, way, b],
            (above, below)[way],
        )

    def place_of(c, b, on_side):
        return span(on_side * rows + c * chunk_rows + b * share, share)

    def line_copy(c, k, b, way, first):
        target = whole_refs[k].at[place_of(c, b, side), :]
        source = ready.at[lax.rem(c, 2), k] if first else target
        return remote(
            source, target, line_send.at[c, k, way, b], line_recv.at[c, k, b],
            (above, below)[way],
        )

    def side_copy(c, k, b, first):
        target = whole_refs[k].at[place_of(c, b, side), :]
        source = ready.at[lax.rem(c, 2), k] if first else target
        return remote(
            source, target, side_send.at[c, k, b], side_recv.at[c, k, b], across
        )

    def keep_copy(c, k):
        return pltpu.make_async_copy(
            ready.at[lax.rem(c, 2), k], whole_refs[k].at[place_of(c, place, side), :],
            keep_sem.at[c, k],
        )

    def each_first(c, k, act):
        @pl.when(jnp.logical_not(has_below))
        def _():
            for b in range(count - 1, 0, -1):
                act(sum_copy(c, k, 0, b, True))

        @pl.when(jnp.logical_not(has_above))
        def _():
            for b in range(count - 1):
                act(sum_copy(c, k, 1, b, True))

    def send_ends(c, k):
        load(c, k).wait()
        each_first(c, k, lambda copy: copy.start())

    def sums_left(c, k):
        for b in range(count):

            @pl.when(has_below & (place < b))
            def _(b=b):
                sum_copy(c, k, 0, b, False).wait_send()

            @pl.when(has_above & (place > b))
            def _(b=b):
                sum_copy(c, k, 1, b, False).wait_send()

    step = min(16, share)

    def add_on(c, k, way, b):
        slot = lax.rem(c, 2)

        def body(i, carry):
            at = span(i * step, step)
            mine = terms[slot, k, span(b * share + i * step, step), :].astype(F32)
            landed[slot, k, way, b - 1 + way, at, :] = (
                mine + landed[slot, k, way, b - 1 + way, at, :].astype(F32)
            ).astype(BF16)
            return carry

        lax.fori_loop(0, share // step, body, 0)

    def sums(c, k, wave):
        ahead = count - 2 - wave
        for way, b, here in (
            (0, place + ahead, has_below & (place + ahead < count)),
            (1, place - ahead, has_above & (place >= ahead)),
        ):

            @pl.when(here)
            def _(way=way, b=b):
                sum_copy(c, k, way, b, False).wait_recv()

                @pl.when(ahead > 0)
                def _():
                    add_on(c, k, way, b)
                    sum_copy(c, k, way, b, False).start()

    def own_left(c, k):
        pl.when(has_above)(lambda: line_copy(c, k, place, 0, True).wait_send())
        pl.when(has_below)(lambda: line_copy(c, k, place, 1, True).wait_send())
        side_copy(c, k, place, True).wait_send()
        keep_copy(c, k).wait()

    def finish(c, k):
        load_share(c, k).wait()
        pl.when(c > 1)(lambda: own_left(c - 2, k))
        slot = lax.rem(c, 2)

        def body(i, carry):
            at = span(i * step, step)
            up = landed[slot, k, 0, jnp.maximum(place - 1, 0), at, :].astype(F32)
            down = landed[slot, k, 1, jnp.minimum(place, count - 2), at, :].astype(F32)
            total = (
                terms[slot, k, span(place * share + i * step, step), :].astype(F32)
                + jnp.where(has_below, up, 0.0)
                + jnp.where(has_above, down, 0.0)
            )
            wide = tok_buf[slot, at, :].astype(F32)
            if k == 0:
                ready[slot, k, at, :] = (wide + total).astype(BF16)
                return carry
            scale = 1.0 / width
            centred = wide - jnp.sum(wide, axis=1, keepdims=True) * scale
            variance = jnp.sum(centred * centred, axis=1, keepdims=True) * scale
            inverse = lax.rsqrt(variance + EPSILON)
            unit = centred * inverse
            scaled = total * gain_ref[0:1, :]
            mean_scaled = jnp.sum(scaled, axis=1, keepdims=True) * scale
            mean_cross = jnp.sum(scaled * unit, axis=1, keepdims=True) * scale
            ready[slot, k, at, :] = (
                cot_buf[slot, at, :].astype(F32)
                + inverse * (scaled - mean_scaled - unit * mean_cross)
            ).astype(BF16)
            gain_term = total * unit
            for r in range(0, step, 8):
                part_ref[0:8, :] += gain_term[r : r + 8, :]
                part_ref[8:16, :] += total[r : r + 8, :]
            return carry

        lax.fori_loop(0, share // step, body, 0)
        pl.when(has_above)(lambda: line_copy(c, k, place, 0, True).start())
        pl.when(has_below)(lambda: line_copy(c, k, place, 1, True).start())
        side_copy(c, k, place, True).start()
        keep_copy(c, k).start()

    def pass_on(c, k, distance):
        for way, b, here in (
            (0, place - distance, place >= distance),
            (1, place + distance, place + distance < count),
        ):

            @pl.when(here)
            def _(way=way, b=b):
                line_copy(c, k, b, way, False).wait_recv()
                pl.when((has_above, has_below)[way])(
                    lambda: line_copy(c, k, b, way, False).start()
                )
                side_copy(c, k, b, False).start()

    def small_copy(n, target):
        return remote(stages.at[n], came.at[n], small_send.at[n], small_recv.at[n], target)

    def small_sums():
        wide = bias_part.shape[2]
        stages[...] = jnp.zeros_like(stages)
        stages[0, 0:1, :] = jnp.sum(part_ref[0:8, :], axis=0, keepdims=True)
        stages[0, 1:2, :] = jnp.sum(part_ref[8:16, :], axis=0, keepdims=True)
        for s in range(sides):
            stages[0, 2 + s : 3 + s, 0:wide] = bias_part[s, 0:1, :]
        for n, target in enumerate((across, other_core, other_half)):
            copy = small_copy(n, target)
            copy.start()
            copy.wait_recv()
            if n == 0:
                stages[1, 0:2, :] = stages[0, 0:2, :] + came[0, 0:2, :]
                stages[1, 2:3, :] = stages[0, 2:3, :] + came[0, 3:4, :]
            else:
                stages[n + 1] = stages[n] + came[n]

        @pl.when(has_below)
        def _():
            small_copy(3, above).wait_recv()
            stages[3] = stages[3] + came[3]

        pl.when(has_above)(lambda: small_copy(3, above).start())
        stages[4] = stages[3]

        @pl.when(has_above)
        def _():
            small_copy(4, below).wait_recv()
            stages[4] = came[4]

        pl.when(has_below)(lambda: small_copy(4, below).start())
        small_ref[...] = stages[4]
        small_ref[2:3, :] = stages[2, 2:3, :] + came[2, 2:3, :]
        for n, target in enumerate((across, other_core, other_half)):
            small_copy(n, target).wait_send()
        pl.when(has_above)(lambda: small_copy(3, above).wait_send())
        pl.when(has_below)(lambda: small_copy(4, below).wait_send())

    waves = count - 1
    every = max(1, waves // 3)
    works = waves // every

    if count == 4:
        order = ((2, 2, 0), (1, 1, 1), (2, 3, 1))
    else:
        order = tuple((2, distance, distance - 1) for distance in range(1, count))

    def pass_steps(h, live, wave):
        for behind, distance, step in order:
            item = jnp.maximum(h - behind, 0)
            for k in range(2):
                pl.when(
                    live & (wave == step) & (h >= behind) & (lax.rem(item, 2) == k)
                )(lambda: pass_on(item // 2, k, distance))

    def pass_rest():
        for item in range(2 * chunks - 2, 2 * chunks):
            for distance, behind in sorted((step[1], step[0]) for step in order):
                if item + behind >= 2 * chunks:
                    pass_on(item // 2, item % 2, distance)

    def half_steps(h, live, work):
        c = h // 2

        def one(wave, carry):
            pl.when(lax.rem(wave, every) == 0)(lambda: work(wave // every))
            for k in range(2):

                @pl.when(live & (lax.rem(h, 2) == k))
                def _(k=k):
                    more = c + 1 < chunks

                    @pl.when(wave == 0)
                    def _():
                        @pl.when(c > 0)
                        def _():
                            sums_left(c - 1, k)
                            each_first(c - 1, k, lambda copy: copy.wait_send())

                        pl.when(more)(lambda: load_share(c + 1, k).start())

                    sums(c, k, wave)

            pass_steps(h, live, wave)
            for k in range(2):

                @pl.when(live & (lax.rem(h, 2) == k) & (wave == waves - 1))
                def _(k=k):
                    more = c + 1 < chunks
                    pl.when(more)(lambda: load(c + 1, k).start())
                    finish(c, k)
                    pl.when(more)(lambda: send_ends(c + 1, k))

            return carry

        lax.fori_loop(0, waves, one, 0)

    tile_halves = -(-sides * (chunks - 1) // works)

    def tiles_scope(*scratch):
        weights = scratch[: 5 * sides]
        scratch = scratch[5 * sides :]
        normed_buf, tile_cot = scratch[:2]
        head_bufs = scratch[2 : 2 + 2 * sides]
        scratch = scratch[2 + 2 * sides :]
        mids, f_buf, g_buf = scratch[: 3 * sides], scratch[3 * sides], scratch[3 * sides + 1]
        f_total, g_total, weight_sem, in_sem, out_sem = scratch[3 * sides + 2 :]

        def weight_copies(s):
            return [
                pltpu.make_async_copy(weight_refs[x], weights[x], weight_sem.at[x])
                for x in range(5 * s, 5 * s + 5)
            ]

        def tile_in(i):
            slot = lax.rem(i, 2)
            at = span(i * chunk_rows, chunk_rows)
            at_side = span(side * rows + i * chunk_rows, chunk_rows)
            pairs = [(normed_ref.at[at, :], normed_buf), (cot_ref.at[at_side, :], tile_cot)]
            pairs += [(ref.at[at, :], buf) for ref, buf in zip(head_refs, head_bufs)]
            return [
                pltpu.make_async_copy(ref, buf.at[slot], in_sem.at[slot, x])
                for x, (ref, buf) in enumerate(pairs)
            ]

        def tile_out(i):
            at = span(i * chunk_rows, chunk_rows)
            pairs = list(zip(mids, mid_refs)) + [(f_buf, f_ref), (g_buf, g_ref)]
            return [
                pltpu.make_async_copy(buf, ref.at[at, :], out_sem.at[x])
                for x, (buf, ref) in enumerate(pairs)
            ]

        def wait_out(i):
            for copy in tile_out(i):
                copy.wait()

        def tile(i, s):
            slot = lax.rem(i, 2)
            if s == 0:
                for copy in tile_in(i):
                    copy.wait()

                @pl.when(i + 1 < chunks)
                def _():
                    for copy in tile_in(i + 1):
                        copy.start()

                pl.when(i > 1)(lambda: wait_out(i - 1))

            @pl.when(i == 0)
            def _():
                for copy in weight_copies(s):
                    copy.wait()

            qkv_w, out_w, gate_w, up_w, down_w = weights[5 * s : 5 * s + 5]
            hidden_buf, gate_buf, up_buf = mids[3 * s : 3 * s + 3]
            normed, cot = normed_buf[slot], tile_cot[slot]
            gate = product(normed, gate_w[...])
            up = product(normed, up_w[...])
            sig = 1.0 / (1.0 + jnp.exp(-gate))
            silu = gate * sig
            hidden = (silu * up).astype(BF16)
            hidden_buf[...] = hidden
            grad_hidden = cols_product(cot, down_w[...])
            gate_back = (grad_hidden * up * sig * (1.0 + gate * (1.0 - sig))).astype(BF16)
            up_back = (grad_hidden * silu).astype(BF16)
            gate_buf[...] = gate_back
            up_buf[...] = up_back
            forward = product(hidden, down_w[...])
            forward += product(head_bufs[2 * s][slot], out_w[...])
            backward = cols_product(gate_back, gate_w[...])
            backward += cols_product(up_back, up_w[...])
            qkv_back = head_bufs[2 * s + 1][slot]
            backward += cols_product(qkv_back, qkv_w[...])
            bias_part[s] += product(jnp.ones((16, chunk_rows), BF16), qkv_back)
            if s > 0:
                forward += f_total[...]
                backward += g_total[...]
            if s < sides - 1:
                f_total[...] = forward
                g_total[...] = backward
                return
            f_buf[...] = forward.astype(BF16)
            g_buf[...] = backward.astype(BF16)
            for copy in tile_out(i):
                copy.start()

        def work(turn, n):
            first = turn == 0
            unit = jnp.maximum(works * turn - works, 0) + n
            i = jnp.where(first, 0, 1 + unit // sides)
            part = jnp.where(first, n - works + sides, lax.rem(unit, sides))
            for s in range(sides):
                pl.when((part == s) & (i < chunks))(lambda: tile(i, s))

        for s in range(sides):
            for copy in weight_copies(s):
                copy.start()
        for copy in tile_in(0):
            copy.start()
        for k in range(2):
            load_share(0, k).start()
        part_ref[...] = jnp.zeros_like(part_ref)
        bias_part[...] = jnp.zeros_like(bias_part)
        pl.semaphore_wait(
            barrier, 3 + has_above.astype(jnp.int32) + has_below.astype(jnp.int32)
        )

        def chunk(turn, carry):
            half_steps(
                jnp.maximum(turn, 1) - 1, turn > 0, lambda n: work(turn, n)
            )

            @pl.when(turn == 0)
            def _():
                wait_out(0)
                for k in range(2):
                    load(0, k).start()
                for k in range(2):
                    send_ends(0, k)

            return carry

        lax.fori_loop(0, tile_halves + 1, chunk, 0)
        wait_out(chunks - 1)

    tall = width
    hidden_cols = mid_refs[0].shape[1]
    pl.run_scoped(
        tiles_scope,
        *[pltpu.VMEM(ref.shape, BF16) for ref in weight_refs],
        pltpu.VMEM((2, chunk_rows, width), BF16),
        pltpu.VMEM((2, chunk_rows, width), BF16),
        *[pltpu.VMEM((2, chunk_rows, ref.shape[1]), BF16) for ref in head_refs],
        *[pltpu.VMEM((chunk_rows, hidden_cols), BF16) for _ in mid_refs],
        pltpu.VMEM((chunk_rows, width), BF16),
        pltpu.VMEM((chunk_rows, width), BF16),
        pltpu.VMEM((chunk_rows, width), F32),
        pltpu.VMEM((chunk_rows, width), F32),
        pltpu.SemaphoreType.DMA((5 * sides,)),
        pltpu.SemaphoreType.DMA((2, 2 + 2 * sides)),
        pltpu.SemaphoreType.DMA((3 * sides + 2,)),
    )


    pieces = core_send.shape[2]
    each = 2
    size = tall // pieces

    def grads_scope(*scratch):
        factor_bufs, scratch = scratch[: arrays * sides], scratch[arrays * sides :]
        held, scratch = scratch[: arrays * sides], scratch[arrays * sides :]
        extra, scratch = scratch[: arrays * sides], scratch[arrays * sides :]
        turned, scratch = scratch[: arrays - 1], scratch[arrays - 1 :]
        left_bufs, factor_sem, left_sem = scratch[:2], scratch[2], scratch[3]

        def factor_copy(x):
            return pltpu.make_async_copy(factors[x], factor_bufs[x], factor_sem.at[x])

        def piece(ref, j):
            return ref.at[span(j * size, size), :]

        def piece_of(u):
            owner_core = jnp.where(u < 2 * each, 1 - core, core)
            owner_half = jnp.where((u // each) % 2 == 0, 1 - half, half)
            return (owner_half * 2 + owner_core) * each + lax.rem(u, each)

        def slot_of(u):
            return jnp.where(u < 3 * each, lax.rem(u, each), each + lax.rem(u, each))

        def left_copy(u, which):
            source = left_refs[which].at[span(piece_of(u) * size, size), :]
            return pltpu.make_async_copy(
                source, left_bufs[which].at[lax.rem(u, 2)], left_sem.at[which, lax.rem(u, 2)]
            )

        def to_core(a, s, j, slot):
            x = 2 * a + s
            return remote(
                held[x].at[slot], piece(core_land[x], j),
                core_send.at[a, s, j], core_recv.at[a, s, j], other_core,
            )

        def to_far(a, s, i, j):
            x = 2 * a + s
            return remote(
                held[x].at[i], piece(far_land[x], j),
                far_send.at[a, s, j], far_recv.at[a, s, j], other_half,
            )

        def to_over(a, i, j):
            return remote(
                held[2 * a + 1].at[each + i], piece(side_land[a], j),
                over_send.at[a, j], over_recv.at[a, j], across,
            )

        def final_piece(a, j):
            return grad_outs[a].at[j] if a else grad_outs[a].at[span(j * size, size), :]

        def final_source(a, i):
            return turned[a - 1].at[i] if a else held[0].at[each + i]

        def back_copy(a, i, j, way, first):
            target = final_piece(a, j)
            source = final_source(a, i) if first else target
            return remote(
                source, target, back_send.at[a, way, j], back_recv.at[a, j],
                (other_core, other_half)[way],
            )

        def save_copy(a, i, j):
            return pltpu.make_async_copy(
                final_source(a, i), final_piece(a, j), save_sem.at[a, i]
            )

        def their_piece(i):
            return ((1 - half) * 2 + core) * each + i

        def my_piece(i):
            return (half * 2 + core) * each + i

        def add_into(target, slot, source):
            def body(i, carry):
                at = span(i * 16, 16)
                target[slot, at, :] = (
                    target[slot, at, :].astype(F32) + source[at, :].astype(F32)
                ).astype(BF16)
                return carry

            lax.fori_loop(0, size // 16, body, 0)

        def fetch(lands, j, ids):
            copies = [
                pltpu.make_async_copy(piece(lands[n], j), extra[x], load_sem.at[x])
                for n, x in enumerate(ids)
            ]
            for copy in copies:
                copy.start()
            for copy in copies:
                copy.wait()

        everything = range(2 * arrays)

        def make(u, which):
            @pl.when(u == 0)
            def _():
                for x in everything:
                    if (x // 2 < 3) == (which == 0):
                        factor_copy(x).wait()

            left_copy(u, which).wait()
            pl.when(u + 1 < pieces)(lambda: left_copy(u + 1, which).start())
            slot = slot_of(u)
            left = left_bufs[which][lax.rem(u, 2)]

            @pl.when((u >= each) & (u < 3 * each))
            def _():
                for x in everything:
                    if (x // 2 < 3) == (which == 0):
                        to_core(x // 2, x % 2, piece_of(u - each), slot).wait_send()

            for x in everything:
                if (x // 2 < 3) == (which == 0):
                    held[x][slot] = product(left, factor_bufs[x][...]).astype(BF16)

            @pl.when(u < 2 * each)
            def _():
                for x in everything:
                    if (x // 2 < 3) == (which == 0):
                        to_core(x // 2, x % 2, piece_of(u), slot).start()

        def gather_terms(slot, j):
            for x in everything:
                to_core(x // 2, x % 2, j, 0).wait_recv()
            fetch(core_land, j, everything)
            for x in everything:
                add_into(held[x], slot, extra[x])

        def grads_far(i):
            j = their_piece(i)
            gather_terms(i, j)
            for x in everything:
                to_far(x // 2, x % 2, i, j).start()

        def grads_over(i):
            j = my_piece(i)
            gather_terms(each + i, j)
            for x in everything:
                to_far(x // 2, x % 2, i, j).wait_recv()
            fetch(far_land, j, everything)
            for a in range(arrays):
                add_into(held[2 * a + 1], each + i, extra[2 * a + 1])
                to_over(a, i, j).start()
            for a in range(arrays):
                add_into(held[2 * a], each + i, extra[2 * a])

        def grads_back(i):
            j = my_piece(i)
            for a in range(arrays):
                to_over(a, i, j).wait_recv()
            fetch(side_land, j, range(0, 2 * arrays, 2))
            for a in range(arrays):
                if a:
                    total = held[2 * a][each + i].astype(F32) + extra[2 * a][...].astype(F32)
                    turned[a - 1][i] = total.T.astype(BF16)
                else:
                    add_into(held[0], each + i, extra[0])
                back_copy(a, i, j, 1, True).start()
                back_copy(a, i, j, 0, True).start()
                save_copy(a, i, j).start()

        def grads_pass(i):
            j = their_piece(i)
            for a in range(arrays):
                back_copy(a, i, j, 1, False).wait_recv()
                back_copy(a, i, j, 0, False).start()

        def grads_drain():
            for i in range(each):
                mine, theirs = my_piece(i), their_piece(i)
                for a in range(arrays):
                    for s in range(2):
                        to_far(a, s, i, theirs).wait_send()
                    to_over(a, i, mine).wait_send()
                    back_copy(a, i, mine, 1, True).wait_send()
                    back_copy(a, i, mine, 0, True).wait_send()
                    back_copy(a, i, theirs, 0, False).wait_send()
                    save_copy(a, i, mine).wait()
            for u in range(2 * each):
                for a in range(arrays):
                    back_copy(a, 0, piece_of(u), 0, False).wait_recv()

        events = {
            26: (grads_far, 0),
            28: (grads_far, 1),
            35: (grads_over, 0),
            40: (grads_back, 0),
            43: (grads_over, 1),
        }

        def work(h, n):
            v = works * (h - tile_halves) + n
            for which in range(2):
                pl.when((v < 2 * pieces) & (lax.rem(v, 2) == which))(
                    lambda: make(v // 2, which)
                )
            for at, (act, i) in events.items():
                pl.when(works * h + n == at)(lambda: act(i))

        for x in everything:
            factor_copy(x).start()
        for which in range(2):
            left_copy(0, which).start()

        def chunk(c, carry):
            half_steps(c, c >= 0, lambda n: work(c, n))
            return carry

        lax.fori_loop(tile_halves, 2 * chunks, chunk, 0)
        pass_rest()
        grads_back(1)
        small_sums()
        for i in range(each):
            grads_pass(i)
        grads_drain()

    factor_shapes = [ref.shape for ref in factors]
    pl.run_scoped(
        grads_scope,
        *[pltpu.VMEM(shape, BF16) for shape in factor_shapes],
        *[pltpu.VMEM((2 * each, size, shape[1]), BF16) for shape in factor_shapes],
        *[pltpu.VMEM((size, shape[1]), BF16) for shape in factor_shapes],
        *[pltpu.VMEM((each, shape[1], size), BF16) for shape in factor_shapes[2::2]],
        pltpu.VMEM((2, size, rows), BF16),
        pltpu.VMEM((2, size, rows), BF16),
        pltpu.SemaphoreType.DMA((2 * arrays,)),
        pltpu.SemaphoreType.DMA((2, 2)),
    )

    for k in range(2):
        sums_left(chunks - 1, k)
        each_first(chunks - 1, k, lambda copy: copy.wait_send())
        own_left(chunks - 2, k)
        own_left(chunks - 1, k)

    def drain(c, carry):
        for k in range(2):
            for b in range(count):
                pl.when((place > b) & has_above)(
                    lambda: line_copy(c, k, b, 0, False).wait_send()
                )
                pl.when((place < b) & has_below)(
                    lambda: line_copy(c, k, b, 1, False).wait_send()
                )
                pl.when(place != b)(lambda: side_copy(c, k, b, False).wait_send())
                side_copy(c, k, b, False).wait_recv()
        return carry

    lax.fori_loop(0, chunks, drain, 0)


def layer(normed, lefts, tokens, cotangent, heads, weights, gain, count, chunks, dp_size):
    row_count, width = tokens.shape
    rows = row_count // 2
    share = rows // chunks // count
    sides, arrays = len(weights), 5
    pieces = 2 * dp_size
    sem = pltpu.SemaphoreType.DMA
    flat_heads = [array for group in heads for array in group]
    flat_weights = [array for group in weights for array in group]
    hidden = weights[0][2].shape[1]
    columns = [heads[0][1].shape[1], hidden, hidden, hidden, heads[0][0].shape[1]]
    whole = jax.ShapeDtypeStruct(tokens.shape, BF16)
    half_sums = [jax.ShapeDtypeStruct((width, n), BF16) for n in columns]
    finals = half_sums[:1] + [
        jax.ShapeDtypeStruct((pieces, n, width // pieces), BF16) for n in columns[1:]
    ]
    lands = [shape for shape in half_sums for _ in range(sides)]
    anywhere = pl.BlockSpec(memory_space=pl.ANY)
    vmem = pl.BlockSpec(memory_space=pltpu.VMEM)
    own_rows = [jax.ShapeDtypeStruct((rows, width), BF16)] * 2
    own_rows += [jax.ShapeDtypeStruct((rows, hidden), BF16)] * (3 * sides)
    outs = pl.pallas_call(
        functools.partial(layer_kernel, chunks, sides),
        in_specs=[anywhere] * (5 + len(flat_heads) + len(flat_weights)) + [vmem],
        out_specs=[anywhere, anywhere, vmem] + [anywhere] * (6 * arrays + len(own_rows)),
        out_shape=[whole, whole, jax.ShapeDtypeStruct((8, width), F32)]
        + finals + lands + lands + half_sums + own_rows,
        scratch_shapes=[
            pltpu.VMEM((2, 2, count * share, width), BF16),
            pltpu.VMEM((2, 2, 2, count - 1, share, width), BF16),
            pltpu.VMEM((2, 2, share, width), BF16),
            pltpu.VMEM((2, share, width), BF16),
            pltpu.VMEM((2, share, width), BF16),
            sem((2, 2)),
            sem((2, 2)),
            sem((2, 2, 2, count)),
            sem((2, 2, 2, count)),
            sem((chunks, 2, 2, count)),
            sem((chunks, 2, count)),
            sem((chunks, 2, count)),
            sem((chunks, 2, count)),
            sem((chunks, 2)),
            sem((arrays, 2, pieces)),
            sem((arrays, 2, pieces)),
            sem((arrays, 2, pieces)),
            sem((arrays, 2, pieces)),
            sem((arrays, pieces)),
            sem((arrays, pieces)),
            sem((arrays, 2, pieces)),
            sem((arrays, pieces)),
            sem((2 * arrays,)),
            sem((arrays, 2)),
            pltpu.VMEM((16, width), F32),
            pltpu.VMEM((sides, 16, columns[0]), F32),
            pltpu.VMEM((5, 8, width), F32),
            pltpu.VMEM((5, 8, width), F32),
            sem((5,)),
            sem((5,)),
        ],
        compiler_params=pltpu.CompilerParams(
            collective_id=0, has_side_effects=True, vmem_limit_bytes=63 * 2**20
        ),
        cost_estimate=pl.CostEstimate(
            flops=6 * rows * sum(array.size for array in flat_weights),
            bytes_accessed=800 * 2**20,
            transcendentals=0,
        ),
        name="layer",
    )(normed, tokens, cotangent, *lefts, *flat_heads, *flat_weights, gain)
    out, grad, small = outs[:3]
    grads = [outs[3].astype(F32)]
    for blocks in outs[4 : 3 + arrays]:
        grads.append(blocks.transpose(1, 0, 2).reshape(blocks.shape[1], width).astype(F32))
    return out, grad, small[0], small[1], small[2, : columns[0]], grads


def body(
    tokens,
    lengths,
    norm_gain,
    norm_shift,
    qkv_weight,
    qkv_bias,
    out_weight,
    gate_weight,
    up_weight,
    down_weight,
    cotangent,
):
    tensor_size = lax.axis_size("tensor")
    dp_size = lax.axis_size("dp")
    count = tensor_size // 2
    where = lax.axis_index("tensor")
    dp_place = lax.axis_index("dp")
    side = where % 2
    across = [(i, i ^ 1) for i in range(tensor_size)]
    row_count, width = tokens.shape
    rows = row_count // 2
    chunk_count = 8

    def own_part(weight):
        part = weight.shape[0] // dp_size
        return lax.dynamic_slice_in_dim(weight, dp_place * part, part, 0)

    def partner(parts, before, after):
        parts, _ = lax.optimization_barrier((parts, before))
        parts = [lax.ppermute(part, "tensor", across) for part in parts]
        parts, _ = lax.optimization_barrier((parts, after))
        return [lax.all_gather(part, "dp", axis=0, tiled=True) for part in parts]

    head_weights = (qkv_weight, out_weight)
    mid_weights = (gate_weight, up_weight, down_weight)
    biases = (qkv_bias, lax.ppermute(qkv_bias, "tensor", across))

    length = lax.dynamic_slice_in_dim(lengths, side, 1, 0)
    norm = (norm_gain, norm_shift)
    *own_group, normed, normed_t, cot_t = project(side, tokens, cotangent, norm, head_weights, biases[0])
    tables = rotary_tables(rows)
    even = (out_weight.shape[0] // HEAD) % 2 == 0
    other_heads = partner([own_part(weight) for weight in head_weights], (), normed)
    mid_parts = [own_part(weight) for weight in mid_weights]
    if even:
        heads = [attention(length, *own_group, *tables)]
        other_mids = partner(mid_parts, normed, heads[0])
        other_group = project(side, normed, cotangent, (), other_heads, biases[1])
        heads.append(attention(length, *other_group, *tables))
    else:
        other_mids = partner(mid_parts, normed, ())
        other_group = project(side, normed, cotangent, (), other_heads, biases[1])
        pairs = zip(own_group, other_group)
        attended, qkv_back = attention(
            length, *[jnp.concatenate(pair, axis=1) for pair in pairs], *tables
        )
        cut, wide = out_weight.shape[0], qkv_weight.shape[1]
        heads = [
            (attended[:, s * cut : (s + 1) * cut], qkv_back[:, s * wide : (s + 1) * wide])
            for s in range(2)
        ]
    weights = ((*head_weights, *mid_weights), (*other_heads, *other_mids))
    layer_out, grad_tokens, gain_part, shift_part, grad_bias, grads = layer(
        normed, (normed_t, cot_t), tokens, cotangent, heads, weights, norm_gain[None, :], count,
        chunk_count, dp_size,
    )
    grad_qkv, grad_gate, grad_up, grad_down, grad_out = grads
    grad_gate, grad_up = grad_gate.T, grad_up.T
    return (
        layer_out,
        grad_tokens,
        gain_part,
        shift_part,
        grad_qkv,
        grad_bias,
        grad_out,
        grad_gate,
        grad_up,
        grad_down,
    )


def solution(mesh):
    placed = (
        P("dp", None),
        P("dp"),
        P(),
        P(),
        P(None, "tensor"),
        P("tensor"),
        P("tensor", None),
        P(None, "tensor"),
        P(None, "tensor"),
        P("tensor", None),
        P("dp", None),
    )
    return jax.shard_map(
        body,
        mesh=mesh,
        in_specs=placed,
        out_specs=(
            P("dp", None),
            P("dp", None),
            P(),
            P(),
            P(None, "tensor"),
            P("tensor"),
            P("tensor", None),
            P(None, "tensor"),
            P(None, "tensor"),
            P("tensor", None),
        ),
        check_vma=False,
    )
```

```python
import functools

import jax
import jax.numpy as jnp
import numpy as np
from jax import lax
from jax.experimental import pallas as pl
from jax.experimental.pallas import tpu as pltpu
from jax.sharding import PartitionSpec as P

HEAD = 64
ROT = 16
PAIR = 2 * HEAD
TRIPLE = 6 * HEAD

EPSILON = 1e-05
NEGATIVE = -1e30
F32 = jnp.float32
BF16 = jnp.bfloat16


def rows_product(former, latter):
    return lax.dot_general(
        former, latter, (((0,), (0,)), ((), ())), preferred_element_type=F32
    )


def cols_product(former, latter):
    return lax.dot_general(
        former, latter, (((1,), (1,)), ((), ())), preferred_element_type=F32
    )


def product(former, latter):
    return jnp.dot(former, latter, preferred_element_type=F32)


def rotary_tables(seq_len):
    frequency = np.float32(10000.0) ** (-np.arange(0, ROT, 2).astype(np.float32) / ROT)
    angles = np.arange(seq_len).astype(np.float32)[:, None] * frequency[None, :]
    cosine, sine = np.cos(angles), np.sin(angles)
    still = HEAD - ROT
    cos_head = np.concatenate([cosine, cosine, np.ones((seq_len, still))], axis=1)
    sin_head = np.concatenate([-sine, sine, np.zeros((seq_len, still))], axis=1)
    return [jnp.asarray(np.tile(table, (1, 2)), F32) for table in (cos_head, sin_head)]


def attention_kernel(
    len_ref, qkv_ref, grad_ref, cos_ref, sin_ref, att_ref, back_ref,
    score, expo, query, key_value, key_value_t, query_t, grad_query, grad_kv_t,
):
    seq_len = qkv_ref.shape[0]
    block = score.shape[1]
    steps = seq_len // block
    length = len_ref[0]
    lane = lax.broadcasted_iota(jnp.int32, (block, PAIR), 1)
    left = lane < HEAD
    near = lax.rem(lane, HEAD) < ROT // 2

    def turn(tile, cosine, sine):
        swapped = jnp.where(
            near, pltpu.roll(tile, PAIR - ROT // 2, 1), pltpu.roll(tile, ROT // 2, 1)
        )
        return tile * cosine + swapped * sine

    def tables(rows):
        cosine, sine = cos_ref[rows, :], sin_ref[rows, :]
        return (
            (cosine, sine),
            (jnp.where(left, 1.0, cosine), jnp.where(left, 0.0, sine)),
            (jnp.where(left, cosine, 1.0), jnp.where(left, sine, 0.0)),
        )

    def prepare(i, carry):
        rows = pl.ds(pl.multiple_of(i * block, block), block)
        tabs = tables(rows)
        first = turn(qkv_ref[rows, 0:PAIR], *tabs[0])
        second = turn(qkv_ref[rows, PAIR : 2 * PAIR], *tabs[1])
        third = turn(qkv_ref[rows, 2 * PAIR : 3 * PAIR], *tabs[2])
        scale = HEAD**-0.5
        first_q = first.astype(BF16).astype(F32) * scale
        second_q = second.astype(BF16).astype(F32) * scale
        query[0, rows, :] = jnp.where(left, 0.0, pltpu.roll(first_q, HEAD, 1)).astype(BF16)
        query[1, rows, :] = jnp.where(left, pltpu.roll(second_q, HEAD, 1), 0.0).astype(BF16)
        for h, tile in enumerate((jnp.where(left, second, first), third)):
            key_value[h, rows, :] = tile.astype(BF16)
            key_value_t[h, :, rows] = tile.T.astype(BF16)
        query_t[0, :, rows] = first_q.T[0:HEAD, :].astype(BF16)
        query_t[1, :, rows] = second_q.T[HEAD:PAIR, :].astype(BF16)
        zero = jnp.zeros((block, PAIR), F32)
        grad_query[rows, :] = zero
        att_ref[rows, :] = zero.astype(BF16)
        for h in range(2):
            grad_kv_t[h, :, rows] = jnp.zeros((PAIR, block), F32)
        return carry

    lax.fori_loop(0, steps, prepare, 0)

    def fold(tile, op):
        out = tile[:, 0:PAIR]
        for c in range(1, block // PAIR):
            out = op(out, tile[:, c * PAIR : (c + 1) * PAIR])
        return out

    def block_rows(i):
        rows = pl.ds(i * block, block)
        spans = [pl.ds(j * block, block) for j in range(i + 1)]
        q_block = [query[h, rows, :] for h in range(2)]
        below = lax.broadcasted_iota(jnp.int32, (block, block), 1) <= lax.broadcasted_iota(
            jnp.int32, (block, block), 0
        )
        maxima = []
        for h in range(2):
            top = None
            for j, cols in enumerate(spans):
                tile = product(q_block[h], key_value_t[h, :, cols])
                if j == i:
                    tile = jnp.where(below, tile, NEGATIVE)
                score[h, :, cols] = tile
                high = fold(tile, jnp.maximum)
                top = high if top is None else jnp.maximum(top, high)
            maxima.append(jnp.max(top, axis=1, keepdims=True))

        mixed, inverse = [], []
        for h in range(2):
            mixture = total = None
            for cols in spans:
                tile = jnp.exp(score[h, :, cols] - maxima[h])
                low = tile.astype(BF16)
                expo[h, :, cols] = low
                part = product(low, key_value[h, cols, :])
                amount = fold(tile, jnp.add)
                mixture = part if mixture is None else mixture + part
                total = amount if total is None else total + amount
            mixed.append(mixture)
            inverse.append(1.0 / jnp.sum(total, axis=1, keepdims=True))

        place = i * block + lax.broadcasted_iota(jnp.int32, (block, 1), 0)
        valid = (place < length).astype(F32)
        mixture = jnp.where(left, mixed[0] * inverse[0], mixed[1] * inverse[1]) * valid
        att_ref[rows, :] = mixture.astype(BF16)
        upstream = grad_ref[rows, :].astype(F32) * valid
        inner = upstream * mixture
        scale = HEAD**-0.5
        turned = []
        for h in range(2):
            own = left if h == 0 else jnp.logical_not(left)
            inner_sum = jnp.sum(jnp.where(own, inner, 0.0), axis=1, keepdims=True) * inverse[h]
            mine = jnp.where(own, upstream * inverse[h], 0.0)
            scaled = mine.astype(BF16)
            half = slice(0, HEAD) if h == 0 else slice(HEAD, PAIR)
            scaled_t = mine.T[half, :].astype(BF16)
            queries_t = query_t[h, :, rows]
            grad = None
            for cols in spans:
                low = expo[h, :, cols]
                grad_weight = product(scaled, key_value_t[h, :, cols])
                grad_score = (low.astype(F32) * (grad_weight - inner_sum)).astype(BF16)
                part = product(grad_score, key_value[h, cols, :])
                grad = part if grad is None else grad + part
                key_at, value_at = (HEAD, 0) if h == 0 else (0, HEAD)
                grad_kv_t[h, key_at : key_at + HEAD, cols] += product(queries_t, grad_score)
                grad_kv_t[h, value_at : value_at + HEAD, cols] += product(scaled_t, low)
            turned.append(pltpu.roll(grad, HEAD, 1))
        grad_query[rows, :] = jnp.where(left, turned[0], turned[1]) * scale

    for i in range(steps):
        pl.when(i * block < length)(functools.partial(block_rows, i))

    def finish(i, carry):
        rows = pl.ds(pl.multiple_of(i * block, block), block)
        tabs = tables(rows)
        gq = grad_query[rows, :]
        low_kv = grad_kv_t[0, :, rows].T
        high_kv = grad_kv_t[1, :, rows].T
        tiles = (jnp.where(left, gq, low_kv), jnp.where(left, low_kv, gq), high_kv)
        for c in range(3):
            back_ref[rows, c * PAIR : (c + 1) * PAIR] = turn(
                tiles[c], tabs[c][0], -tabs[c][1]
            ).astype(BF16)
        return carry

    lax.fori_loop(0, steps, finish, 0)


def attention(length, qkv, grad_mixture, cosine, sine):
    seq_len, width = qkv.shape
    pairs = width // TRIPLE
    block = min(512, seq_len)
    flops = 6 * 2 * (2 * pairs) * seq_len * seq_len * PAIR
    return pl.pallas_call(
        attention_kernel,
        grid=(pairs,),
        in_specs=[
            pl.BlockSpec(memory_space=pltpu.SMEM),
            pl.BlockSpec((seq_len, TRIPLE), lambda g: (0, g)),
            pl.BlockSpec((seq_len, PAIR), lambda g: (0, g)),
            pl.BlockSpec((seq_len, PAIR), lambda g: (0, 0)),
            pl.BlockSpec((seq_len, PAIR), lambda g: (0, 0)),
        ],
        out_specs=[
            pl.BlockSpec((seq_len, PAIR), lambda g: (0, g)),
            pl.BlockSpec((seq_len, TRIPLE), lambda g: (0, g)),
        ],
        out_shape=[
            jax.ShapeDtypeStruct((seq_len, pairs * PAIR), BF16),
            jax.ShapeDtypeStruct((seq_len, width), BF16),
        ],
        scratch_shapes=[
            pltpu.VMEM((2, block, seq_len), F32),
            pltpu.VMEM((2, block, seq_len), BF16),
            pltpu.VMEM((2, seq_len, PAIR), BF16),
            pltpu.VMEM((2, seq_len, PAIR), BF16),
            pltpu.VMEM((2, PAIR, seq_len), BF16),
            pltpu.VMEM((2, HEAD, seq_len), BF16),
            pltpu.VMEM((seq_len, PAIR), F32),
            pltpu.VMEM((2, PAIR, seq_len), F32),
        ],
        compiler_params=pltpu.CompilerParams(vmem_limit_bytes=48 * 2**20),
        cost_estimate=pl.CostEstimate(
            flops=flops,
            bytes_accessed=seq_len * width * 8,
            transcendentals=2 * pairs * seq_len * seq_len // 2,
        ),
        name="attention",
    )(length, qkv, grad_mixture, cosine, sine)


def start_kernel(
    side_ref, tok_ref, cot_ref, gain_ref, shift_ref, qkv_w, bias_ref, out_w,
    qkv_ref, grad_ref, normed_ref,
):
    wide = tok_ref[...].astype(F32)
    centred = wide - jnp.mean(wide, axis=1, keepdims=True)
    variance = jnp.mean(centred * centred, axis=1, keepdims=True)
    unit = centred * lax.rsqrt(variance + EPSILON)
    normed = (unit * gain_ref[...] + shift_ref[...]).astype(BF16)
    normed_ref[...] = normed
    qkv_ref[...] = product(normed, qkv_w[...]) + bias_ref[...]
    grad_ref[...] = cols_product(cot_ref[...], out_w[...]).astype(BF16)


def project_kernel(side_ref, normed_ref, cot_ref, qkv_w, bias_ref, out_w, qkv_ref, grad_ref):
    qkv_ref[...] = product(normed_ref[...], qkv_w[...]) + bias_ref[...]
    grad_ref[...] = cols_product(cot_ref[...], out_w[...]).astype(BF16)


def project(side, rows_in, cotangent, norm, weights, bias):
    rows, width = cotangent.shape[0] // 2, cotangent.shape[1]
    tile = min(256, rows)
    tiles = rows // tile
    qkv_weight, out_weight = weights
    heads, wide = out_weight.shape[0], qkv_weight.shape[1]

    def sided(i, side_ref):
        return (side_ref[0] * tiles + i, 0)

    def fixed(i, side_ref):
        return (0, 0)

    def rowed(i, side_ref):
        return (i, 0)

    flat = [part[None, :] for part in norm]
    flat += [qkv_weight, bias.astype(F32)[None, :], out_weight]
    outs = [((rows, wide), F32), ((rows, heads), BF16)]
    out_specs = [pl.BlockSpec((tile, shape[1]), rowed) for shape, _ in outs]
    if norm:
        outs.append(((rows, width), BF16))
        out_specs.append(pl.BlockSpec((tile, width), rowed))
    return pl.pallas_call(
        start_kernel if norm else project_kernel,
        grid_spec=pltpu.PrefetchScalarGridSpec(
            num_scalar_prefetch=1,
            grid=(tiles,),
            in_specs=[
                pl.BlockSpec((tile, width), sided if norm else rowed),
                pl.BlockSpec((tile, width), sided),
            ]
            + [pl.BlockSpec(array.shape, fixed) for array in flat],
            out_specs=out_specs,
        ),
        out_shape=[jax.ShapeDtypeStruct(*out) for out in outs],
        compiler_params=pltpu.CompilerParams(vmem_limit_bytes=40 * 2**20),
        cost_estimate=pl.CostEstimate(
            flops=2 * rows * width * (wide + heads),
            bytes_accessed=rows * (6 * width + 4 * wide),
            transcendentals=rows,
        ),
        name="project",
    )(side[None], rows_in, cotangent, *flat)


def layer_kernel(chunks, sides, *refs):
    normed_ref, tok_ref, cot_ref = refs[:3]
    head_refs, refs = refs[3 : 3 + 2 * sides], refs[3 + 2 * sides :]
    weight_refs, gain_ref = refs[: 5 * sides], refs[5 * sides]
    refs = refs[5 * sides + 1 :]
    out_ref, grad_ref, small_ref = refs[:3]
    refs = refs[3:]
    arrays = 5
    grad_outs, core_land = refs[:arrays], refs[arrays : 3 * arrays]
    far_land, side_land = refs[3 * arrays : 5 * arrays], refs[5 * arrays : 6 * arrays]
    refs = refs[6 * arrays :]
    f_ref, g_ref = refs[:2]
    mid_refs, refs = refs[2 : 2 + 3 * sides], refs[2 + 3 * sides :]
    (
        terms, landed, ready, tok_buf, cot_buf,
        term_sem, share_sem, sum_send, sum_recv,
        line_send, line_recv, side_send, side_recv, keep_sem,
        core_send, core_recv, far_send, far_recv, over_send, over_recv,
        back_send, back_recv, load_sem, save_sem,
        part_ref, bias_part, stages, came, small_send, small_recv,
    ) = refs
    share, width = landed.shape[4:]
    count = landed.shape[3] + 1
    chunk_rows = count * share
    rows = chunks * chunk_rows
    where = lax.axis_index("tensor")
    group = lax.axis_index("dp")
    place, side = where // 2, where % 2
    half, core = group // 2, group % 2
    whole_refs = (out_ref, grad_ref)
    factors = []
    for s in range(sides):
        hidden_ref, gate_ref, up_ref = mid_refs[3 * s : 3 * s + 3]
        factors.append(
            (head_refs[2 * s + 1], gate_ref, up_ref, hidden_ref, head_refs[2 * s])
        )
    factors = [factors[x % sides][x // sides] for x in range(arrays * sides)]

    above, below = (group, where + 2), (group, where - 2)
    across = (group, where + 1 - 2 * side)
    other_core = (half * 2 + 1 - core, where)
    other_half = ((1 - half) * 2 + core, where)
    has_above, has_below = place < count - 1, place > 0

    barrier = pltpu.get_barrier_semaphore()

    def greet(target):
        pl.semaphore_signal(barrier, inc=1, device_id=target, device_id_type=pl.DeviceIdType.MESH)

    pl.when(has_above)(lambda: greet(above))
    pl.when(has_below)(lambda: greet(below))
    for target in (across, other_core, other_half):
        greet(target)

    def span(begin, size):
        return pl.ds(pl.multiple_of(begin, size), size)

    def load(c, k):
        source = (f_ref, g_ref)[k].at[span(c * chunk_rows, chunk_rows), :]
        return pltpu.make_async_copy(
            source, terms.at[lax.rem(c, 2), k], term_sem.at[lax.rem(c, 2), k]
        )

    def load_share(c, k):
        begin = span(side * rows + c * chunk_rows + place * share, share)
        source, target = ((tok_ref, tok_buf), (cot_ref, cot_buf))[k]
        return pltpu.make_async_copy(
            source.at[begin, :], target.at[lax.rem(c, 2)], share_sem.at[lax.rem(c, 2), k]
        )

    def remote(source, target, send, recv, device_id):
        return pltpu.make_async_remote_copy(
            src_ref=source, dst_ref=target, send_sem=send, recv_sem=recv,
            device_id=device_id, device_id_type=pl.DeviceIdType.MESH,
        )


    def sum_copy(c, k, way, b, first):
        slot = lax.rem(c, 2)
        target = landed.at[slot, k, way, b - 1 + way]
        source = terms.at[slot, k, span(b * share, share), :] if first else target
        return remote(
            source, target, sum_send.at[slot, k, way, b], sum_recv.at[slot, k, way, b],
            (above, below)[way],
        )

    def place_of(c, b, on_side):
        return span(on_side * rows + c * chunk_rows + b * share, share)

    def line_copy(c, k, b, way, first):
        target = whole_refs[k].at[place_of(c, b, side), :]
        source = ready.at[lax.rem(c, 2), k] if first else target
        return remote(
            source, target, line_send.at[c, k, way, b], line_recv.at[c, k, b],
            (above, below)[way],
        )

    def side_copy(c, k, b, first):
        target = whole_refs[k].at[place_of(c, b, side), :]
        source = ready.at[lax.rem(c, 2), k] if first else target
        return remote(
            source, target, side_send.at[c, k, b], side_recv.at[c, k, b], across
        )

    def keep_copy(c, k):
        return pltpu.make_async_copy(
            ready.at[lax.rem(c, 2), k], whole_refs[k].at[place_of(c, place, side), :],
            keep_sem.at[c, k],
        )

    def each_first(c, k, act):
        @pl.when(jnp.logical_not(has_below))
        def _():
            for b in range(count - 1, 0, -1):
                act(sum_copy(c, k, 0, b, True))

        @pl.when(jnp.logical_not(has_above))
        def _():
            for b in range(count - 1):
                act(sum_copy(c, k, 1, b, True))

    def send_ends(c, k):
        load(c, k).wait()
        each_first(c, k, lambda copy: copy.start())

    def sums_left(c, k):
        for b in range(count):

            @pl.when(has_below & (place < b))
            def _(b=b):
                sum_copy(c, k, 0, b, False).wait_send()

            @pl.when(has_above & (place > b))
            def _(b=b):
                sum_copy(c, k, 1, b, False).wait_send()

    step = min(16, share)

    def add_on(c, k, way, b):
        slot = lax.rem(c, 2)

        def body(i, carry):
            at = span(i * step, step)
            mine = terms[slot, k, span(b * share + i * step, step), :].astype(F32)
            landed[slot, k, way, b - 1 + way, at, :] = (
                mine + landed[slot, k, way, b - 1 + way, at, :].astype(F32)
            ).astype(BF16)
            return carry

        lax.fori_loop(0, share // step, body, 0)

    def sums(c, k, wave):
        ahead = count - 2 - wave
        for way, b, here in (
            (0, place + ahead, has_below & (place + ahead < count)),
            (1, place - ahead, has_above & (place >= ahead)),
        ):

            @pl.when(here)
            def _(way=way, b=b):
                sum_copy(c, k, way, b, False).wait_recv()

                @pl.when(ahead > 0)
                def _():
                    add_on(c, k, way, b)
                    sum_copy(c, k, way, b, False).start()

    def own_left(c, k):
        pl.when(has_above)(lambda: line_copy(c, k, place, 0, True).wait_send())
        pl.when(has_below)(lambda: line_copy(c, k, place, 1, True).wait_send())
        side_copy(c, k, place, True).wait_send()
        keep_copy(c, k).wait()

    def finish(c, k):
        load_share(c, k).wait()
        pl.when(c > 1)(lambda: own_left(c - 2, k))
        slot = lax.rem(c, 2)

        def body(i, carry):
            at = span(i * step, step)
            up = landed[slot, k, 0, jnp.maximum(place - 1, 0), at, :].astype(F32)
            down = landed[slot, k, 1, jnp.minimum(place, count - 2), at, :].astype(F32)
            total = (
                terms[slot, k, span(place * share + i * step, step), :].astype(F32)
                + jnp.where(has_below, up, 0.0)
                + jnp.where(has_above, down, 0.0)
            )
            wide = tok_buf[slot, at, :].astype(F32)
            if k == 0:
                ready[slot, k, at, :] = (wide + total).astype(BF16)
                return carry
            scale = 1.0 / width
            centred = wide - jnp.sum(wide, axis=1, keepdims=True) * scale
            variance = jnp.sum(centred * centred, axis=1, keepdims=True) * scale
            inverse = lax.rsqrt(variance + EPSILON)
            unit = centred * inverse
            scaled = total * gain_ref[0:1, :]
            mean_scaled = jnp.sum(scaled, axis=1, keepdims=True) * scale
            mean_cross = jnp.sum(scaled * unit, axis=1, keepdims=True) * scale
            ready[slot, k, at, :] = (
                cot_buf[slot, at, :].astype(F32)
                + inverse * (scaled - mean_scaled - unit * mean_cross)
            ).astype(BF16)
            gain_term = total * unit
            for r in range(0, step, 8):
                part_ref[0:8, :] += gain_term[r : r + 8, :]
                part_ref[8:16, :] += total[r : r + 8, :]
            return carry

        lax.fori_loop(0, share // step, body, 0)
        pl.when(has_above)(lambda: line_copy(c, k, place, 0, True).start())
        pl.when(has_below)(lambda: line_copy(c, k, place, 1, True).start())
        side_copy(c, k, place, True).start()
        keep_copy(c, k).start()

    def pass_on(c, k, distance):
        for way, b, here in (
            (0, place - distance, place >= distance),
            (1, place + distance, place + distance < count),
        ):

            @pl.when(here)
            def _(way=way, b=b):
                line_copy(c, k, b, way, False).wait_recv()
                pl.when((has_above, has_below)[way])(
                    lambda: line_copy(c, k, b, way, False).start()
                )
                side_copy(c, k, b, False).start()

    def small_copy(n, target):
        return remote(stages.at[n], came.at[n], small_send.at[n], small_recv.at[n], target)

    def small_sums():
        wide = bias_part.shape[2]
        stages[...] = jnp.zeros_like(stages)
        stages[0, 0:1, :] = jnp.sum(part_ref[0:8, :], axis=0, keepdims=True)
        stages[0, 1:2, :] = jnp.sum(part_ref[8:16, :], axis=0, keepdims=True)
        for s in range(sides):
            stages[0, 2 + s : 3 + s, 0:wide] = jnp.sum(bias_part[s], axis=0, keepdims=True)
        for n, target in enumerate((across, other_core, other_half)):
            copy = small_copy(n, target)
            copy.start()
            copy.wait_recv()
            if n == 0:
                stages[1, 0:2, :] = stages[0, 0:2, :] + came[0, 0:2, :]
                stages[1, 2:3, :] = stages[0, 2:3, :] + came[0, 3:4, :]
            else:
                stages[n + 1] = stages[n] + came[n]

        @pl.when(has_below)
        def _():
            small_copy(3, above).wait_recv()
            stages[3] = stages[3] + came[3]

        pl.when(has_above)(lambda: small_copy(3, above).start())
        stages[4] = stages[3]

        @pl.when(has_above)
        def _():
            small_copy(4, below).wait_recv()
            stages[4] = came[4]

        pl.when(has_below)(lambda: small_copy(4, below).start())
        small_ref[...] = stages[4]
        small_ref[2:3, :] = stages[2, 2:3, :] + came[2, 2:3, :]
        for n, target in enumerate((across, other_core, other_half)):
            small_copy(n, target).wait_send()
        pl.when(has_above)(lambda: small_copy(3, above).wait_send())
        pl.when(has_below)(lambda: small_copy(4, below).wait_send())

    waves = count - 1
    every = max(1, waves // 3)
    works = waves // every

    if count == 4:
        order = ((2, 2, 0), (1, 1, 1), (2, 3, 1))
    else:
        order = tuple((2, distance, distance - 1) for distance in range(1, count))

    def pass_steps(h, live, wave):
        for behind, distance, step in order:
            item = jnp.maximum(h - behind, 0)
            for k in range(2):
                pl.when(
                    live & (wave == step) & (h >= behind) & (lax.rem(item, 2) == k)
                )(lambda: pass_on(item // 2, k, distance))

    def pass_rest():
        for item in range(2 * chunks - 2, 2 * chunks):
            for distance, behind in sorted((step[1], step[0]) for step in order):
                if item + behind >= 2 * chunks:
                    pass_on(item // 2, item % 2, distance)

    def half_steps(h, live, work):
        c = h // 2

        def one(wave, carry):
            pl.when(lax.rem(wave, every) == 0)(lambda: work(wave // every))
            for k in range(2):

                @pl.when(live & (lax.rem(h, 2) == k))
                def _(k=k):
                    more = c + 1 < chunks

                    @pl.when(wave == 0)
                    def _():
                        @pl.when(c > 0)
                        def _():
                            sums_left(c - 1, k)
                            each_first(c - 1, k, lambda copy: copy.wait_send())

                        pl.when(more)(lambda: load_share(c + 1, k).start())

                    sums(c, k, wave)

            pass_steps(h, live, wave)
            for k in range(2):

                @pl.when(live & (lax.rem(h, 2) == k) & (wave == waves - 1))
                def _(k=k):
                    more = c + 1 < chunks
                    pl.when(more)(lambda: load(c + 1, k).start())
                    finish(c, k)
                    pl.when(more)(lambda: send_ends(c + 1, k))

            return carry

        lax.fori_loop(0, waves, one, 0)

    tile_halves = -(-sides * (chunks - 1) // works)

    def tiles_scope(*scratch):
        weights = scratch[: 5 * sides]
        scratch = scratch[5 * sides :]
        normed_buf, tile_cot = scratch[:2]
        head_bufs = scratch[2 : 2 + 2 * sides]
        scratch = scratch[2 + 2 * sides :]
        mids, f_buf, g_buf = scratch[: 3 * sides], scratch[3 * sides], scratch[3 * sides + 1]
        f_total, g_total, weight_sem, in_sem, out_sem = scratch[3 * sides + 2 :]

        def weight_copies(s):
            return [
                pltpu.make_async_copy(weight_refs[x], weights[x], weight_sem.at[x])
                for x in range(5 * s, 5 * s + 5)
            ]

        def tile_in(i):
            slot = lax.rem(i, 2)
            at = span(i * chunk_rows, chunk_rows)
            at_side = span(side * rows + i * chunk_rows, chunk_rows)
            pairs = [(normed_ref.at[at, :], normed_buf), (cot_ref.at[at_side, :], tile_cot)]
            pairs += [(ref.at[at, :], buf) for ref, buf in zip(head_refs, head_bufs)]
            return [
                pltpu.make_async_copy(ref, buf.at[slot], in_sem.at[slot, x])
                for x, (ref, buf) in enumerate(pairs)
            ]

        def tile_out(i):
            at = span(i * chunk_rows, chunk_rows)
            pairs = list(zip(mids, mid_refs)) + [(f_buf, f_ref), (g_buf, g_ref)]
            return [
                pltpu.make_async_copy(buf, ref.at[at, :], out_sem.at[x])
                for x, (buf, ref) in enumerate(pairs)
            ]

        def wait_out(i):
            for copy in tile_out(i):
                copy.wait()

        def tile(i, s):
            slot = lax.rem(i, 2)
            if s == 0:
                for copy in tile_in(i):
                    copy.wait()

                @pl.when(i + 1 < chunks)
                def _():
                    for copy in tile_in(i + 1):
                        copy.start()

                pl.when(i > 1)(lambda: wait_out(i - 1))

            @pl.when(i == 0)
            def _():
                for copy in weight_copies(s):
                    copy.wait()

            qkv_w, out_w, gate_w, up_w, down_w = weights[5 * s : 5 * s + 5]
            hidden_buf, gate_buf, up_buf = mids[3 * s : 3 * s + 3]
            normed, cot = normed_buf[slot], tile_cot[slot]
            gate = cols_product(normed, gate_w[...])
            up = cols_product(normed, up_w[...])
            sig = 1.0 / (1.0 + jnp.exp(-gate))
            silu = gate * sig
            hidden = (silu * up).astype(BF16)
            hidden_buf[...] = hidden
            grad_hidden = cols_product(cot, down_w[...])
            gate_back = (grad_hidden * up * sig * (1.0 + gate * (1.0 - sig))).astype(BF16)
            up_back = (grad_hidden * silu).astype(BF16)
            gate_buf[...] = gate_back
            up_buf[...] = up_back
            forward = product(hidden, down_w[...])
            forward += product(head_bufs[2 * s][slot], out_w[...])
            backward = product(gate_back, gate_w[...])
            backward += product(up_back, up_w[...])
            qkv_back = head_bufs[2 * s + 1][slot]
            backward += cols_product(qkv_back, qkv_w[...])
            bias_part[s] += (
                qkv_back.astype(F32).reshape(chunk_rows // 8, 8, qkv_back.shape[1]).sum(axis=0)
            )
            if s > 0:
                forward += f_total[...]
                backward += g_total[...]
            if s < sides - 1:
                f_total[...] = forward
                g_total[...] = backward
                return
            f_buf[...] = forward.astype(BF16)
            g_buf[...] = backward.astype(BF16)
            for copy in tile_out(i):
                copy.start()

        def work(turn, n):
            first = turn == 0
            unit = jnp.maximum(works * turn - works, 0) + n
            i = jnp.where(first, 0, 1 + unit // sides)
            part = jnp.where(first, n - works + sides, lax.rem(unit, sides))
            for s in range(sides):
                pl.when((part == s) & (i < chunks))(lambda: tile(i, s))

        for s in range(sides):
            for copy in weight_copies(s):
                copy.start()
        for copy in tile_in(0):
            copy.start()
        for k in range(2):
            load_share(0, k).start()
        part_ref[...] = jnp.zeros_like(part_ref)
        bias_part[...] = jnp.zeros_like(bias_part)
        pl.semaphore_wait(
            barrier, 3 + has_above.astype(jnp.int32) + has_below.astype(jnp.int32)
        )

        def chunk(turn, carry):
            half_steps(
                jnp.maximum(turn, 1) - 1, turn > 0, lambda n: work(turn, n)
            )

            @pl.when(turn == 0)
            def _():
                wait_out(0)
                for k in range(2):
                    load(0, k).start()
                for k in range(2):
                    send_ends(0, k)

            return carry

        lax.fori_loop(0, tile_halves + 1, chunk, 0)
        wait_out(chunks - 1)

    tall = width
    hidden_cols = mid_refs[0].shape[1]
    pl.run_scoped(
        tiles_scope,
        *[pltpu.VMEM(ref.shape, BF16) for ref in weight_refs],
        pltpu.VMEM((2, chunk_rows, width), BF16),
        pltpu.VMEM((2, chunk_rows, width), BF16),
        *[pltpu.VMEM((2, chunk_rows, ref.shape[1]), BF16) for ref in head_refs],
        *[pltpu.VMEM((chunk_rows, hidden_cols), BF16) for _ in mid_refs],
        pltpu.VMEM((chunk_rows, width), BF16),
        pltpu.VMEM((chunk_rows, width), BF16),
        pltpu.VMEM((chunk_rows, width), F32),
        pltpu.VMEM((chunk_rows, width), F32),
        pltpu.SemaphoreType.DMA((5 * sides,)),
        pltpu.SemaphoreType.DMA((2, 2 + 2 * sides)),
        pltpu.SemaphoreType.DMA((3 * sides + 2,)),
    )


    pieces = core_send.shape[2]
    each = 2
    size = tall // pieces

    def grads_scope(*scratch):
        factor_bufs, scratch = scratch[: arrays * sides], scratch[arrays * sides :]
        held, scratch = scratch[: arrays * sides], scratch[arrays * sides :]
        extra, scratch = scratch[: arrays * sides], scratch[arrays * sides :]
        turned, scratch = scratch[: arrays - 1], scratch[arrays - 1 :]
        left_bufs, factor_sem, left_sem = scratch[:2], scratch[2], scratch[3]

        def factor_copy(x):
            return pltpu.make_async_copy(factors[x], factor_bufs[x], factor_sem.at[x])

        def piece(ref, j):
            return ref.at[span(j * size, size), :]

        def piece_of(u):
            owner_core = jnp.where((u // each) % 2 == 0, 1 - core, core)
            owner_half = jnp.where(u < 2 * each, 1 - half, half)
            return (owner_half * 2 + owner_core) * each + lax.rem(u, each)

        def slot_of(u):
            return jnp.where(u < 2 * each, lax.rem(u, each), each + lax.rem(u, each))

        def left_copy(u, which):
            at = span(piece_of(u) * size, size)
            source = (
                normed_ref.at[:, at] if which == 0 else cot_ref.at[span(side * rows, rows), at]
            )
            return pltpu.make_async_copy(
                source, left_bufs[which].at[lax.rem(u, 2)], left_sem.at[which, lax.rem(u, 2)]
            )

        def to_core(a, s, j, slot):
            x = 2 * a + s
            return remote(
                held[x].at[slot], piece(core_land[x], j),
                core_send.at[a, s, j], core_recv.at[a, s, j], other_core,
            )

        def to_far(a, s, i, j):
            x = 2 * a + s
            return remote(
                held[x].at[i], piece(far_land[x], j),
                far_send.at[a, s, j], far_recv.at[a, s, j], other_half,
            )

        def to_over(a, i, j):
            return remote(
                held[2 * a + 1].at[each + i], piece(side_land[a], j),
                over_send.at[a, j], over_recv.at[a, j], across,
            )

        def final_piece(a, j):
            return grad_outs[a].at[j] if a else grad_outs[a].at[span(j * size, size), :]

        def final_source(a, i):
            return turned[a - 1].at[i] if a else held[0].at[each + i]

        def back_copy(a, i, j, way, first):
            target = final_piece(a, j)
            source = final_source(a, i) if first else target
            return remote(
                source, target, back_send.at[a, way, j], back_recv.at[a, j],
                (other_core, other_half)[way],
            )

        def save_copy(a, i, j):
            return pltpu.make_async_copy(
                final_source(a, i), final_piece(a, j), save_sem.at[a, i]
            )

        def their_piece(i):
            return ((1 - half) * 2 + core) * each + i

        def my_piece(i):
            return (half * 2 + core) * each + i

        def add_into(target, slot, source):
            def body(i, carry):
                at = span(i * 16, 16)
                target[slot, at, :] = (
                    target[slot, at, :].astype(F32) + source[at, :].astype(F32)
                ).astype(BF16)
                return carry

            lax.fori_loop(0, size // 16, body, 0)

        def fetch(lands, j, ids):
            copies = [
                pltpu.make_async_copy(piece(lands[n], j), extra[x], load_sem.at[x])
                for n, x in enumerate(ids)
            ]
            for copy in copies:
                copy.start()
            for copy in copies:
                copy.wait()

        everything = range(2 * arrays)

        def make(u, which):
            @pl.when(u == 0)
            def _():
                for x in everything:
                    if (x // 2 < 3) == (which == 0):
                        factor_copy(x).wait()

            left_copy(u, which).wait()
            pl.when(u + 1 < pieces)(lambda: left_copy(u + 1, which).start())
            slot = slot_of(u)
            left = left_bufs[which][lax.rem(u, 2)].T

            @pl.when((u // each) % 2 == 1)
            def _():
                for x in everything:
                    if (x // 2 < 3) == (which == 0):
                        to_core(x // 2, x % 2, piece_of(u - each), slot).wait_send()

            for x in everything:
                if (x // 2 < 3) == (which == 0):
                    held[x][slot] = product(left, factor_bufs[x][...]).astype(BF16)

            @pl.when((u // each) % 2 == 0)
            def _():
                for x in everything:
                    if (x // 2 < 3) == (which == 0):
                        to_core(x // 2, x % 2, piece_of(u), slot).start()

        def gather_terms(slot, j):
            for x in everything:
                to_core(x // 2, x % 2, j, 0).wait_recv()
            fetch(core_land, j, everything)
            for x in everything:
                add_into(held[x], slot, extra[x])

        def grads_far(i):
            j = their_piece(i)
            gather_terms(i, j)
            for x in everything:
                to_far(x // 2, x % 2, i, j).start()

        def grads_over(i):
            j = my_piece(i)
            gather_terms(each + i, j)
            for x in everything:
                to_far(x // 2, x % 2, i, j).wait_recv()
            fetch(far_land, j, everything)
            for a in range(arrays):
                add_into(held[2 * a + 1], each + i, extra[2 * a + 1])
                to_over(a, i, j).start()
            for a in range(arrays):
                add_into(held[2 * a], each + i, extra[2 * a])

        def grads_back(i):
            j = my_piece(i)
            for a in range(arrays):
                to_over(a, i, j).wait_recv()
            fetch(side_land, j, range(0, 2 * arrays, 2))
            for a in range(arrays):
                if a:
                    total = held[2 * a][each + i].astype(F32) + extra[2 * a][...].astype(F32)
                    turned[a - 1][i] = total.T.astype(BF16)
                else:
                    add_into(held[0], each + i, extra[0])
                back_copy(a, i, j, 1, True).start()
                back_copy(a, i, j, 0, True).start()
                save_copy(a, i, j).start()

        def grads_pass(i):
            j = their_piece(i)
            for a in range(arrays):
                back_copy(a, i, j, 1, False).wait_recv()
                back_copy(a, i, j, 0, False).start()

        def grads_drain():
            for i in range(each):
                mine, theirs = my_piece(i), their_piece(i)
                for a in range(arrays):
                    for s in range(2):
                        to_far(a, s, i, theirs).wait_send()
                    to_over(a, i, mine).wait_send()
                    back_copy(a, i, mine, 1, True).wait_send()
                    back_copy(a, i, mine, 0, True).wait_send()
                    back_copy(a, i, theirs, 0, False).wait_send()
                    save_copy(a, i, mine).wait()
            for u in (*range(each), *range(2 * each, 3 * each)):
                for a in range(arrays):
                    back_copy(a, 0, piece_of(u), 0, False).wait_recv()

        events = {
            7: (grads_far, 0),
            8: (grads_far, 1),
            11: (grads_over, 0),
            12: (grads_over, 1),
            14: (grads_back, 0),
        }

        def work(h, n):
            u = h - tile_halves
            for which in range(2):
                pl.when((u < pieces) & (n == which))(lambda: make(u, which))
            for at, (act, i) in events.items():
                pl.when((h == at) & (n == works - 1))(lambda: act(i))

        for x in everything:
            factor_copy(x).start()
        for which in range(2):
            left_copy(0, which).start()

        def chunk(c, carry):
            half_steps(c, c >= 0, lambda n: work(c, n))
            return carry

        lax.fori_loop(tile_halves, 2 * chunks, chunk, 0)
        pass_rest()
        grads_back(1)
        small_sums()
        for i in range(each):
            grads_pass(i)
        grads_drain()

    factor_shapes = [ref.shape for ref in factors]
    pl.run_scoped(
        grads_scope,
        *[pltpu.VMEM(shape, BF16) for shape in factor_shapes],
        *[pltpu.VMEM((2 * each, size, shape[1]), BF16) for shape in factor_shapes],
        *[pltpu.VMEM((size, shape[1]), BF16) for shape in factor_shapes],
        *[pltpu.VMEM((each, shape[1], size), BF16) for shape in factor_shapes[2::2]],
        pltpu.VMEM((2, rows, size), BF16),
        pltpu.VMEM((2, rows, size), BF16),
        pltpu.SemaphoreType.DMA((2 * arrays,)),
        pltpu.SemaphoreType.DMA((2, 2)),
    )

    for k in range(2):
        sums_left(chunks - 1, k)
        each_first(chunks - 1, k, lambda copy: copy.wait_send())
        own_left(chunks - 2, k)
        own_left(chunks - 1, k)

    def drain(c, carry):
        for k in range(2):
            for b in range(count):
                pl.when((place > b) & has_above)(
                    lambda: line_copy(c, k, b, 0, False).wait_send()
                )
                pl.when((place < b) & has_below)(
                    lambda: line_copy(c, k, b, 1, False).wait_send()
                )
                pl.when(place != b)(lambda: side_copy(c, k, b, False).wait_send())
                side_copy(c, k, b, False).wait_recv()
        return carry

    lax.fori_loop(0, chunks, drain, 0)


def layer(normed, tokens, cotangent, heads, weights, gain, count, chunks, dp_size):
    row_count, width = tokens.shape
    rows = row_count // 2
    share = rows // chunks // count
    sides, arrays = len(weights), 5
    pieces = 2 * dp_size
    sem = pltpu.SemaphoreType.DMA
    flat_heads = [array for group in heads for array in group]
    flat_weights = [array for group in weights for array in group]
    hidden = weights[0][2].shape[0]
    columns = [heads[0][1].shape[1], hidden, hidden, hidden, heads[0][0].shape[1]]
    whole = jax.ShapeDtypeStruct(tokens.shape, BF16)
    half_sums = [jax.ShapeDtypeStruct((width, n), BF16) for n in columns]
    finals = half_sums[:1] + [
        jax.ShapeDtypeStruct((pieces, n, width // pieces), BF16) for n in columns[1:]
    ]
    lands = [shape for shape in half_sums for _ in range(sides)]
    anywhere = pl.BlockSpec(memory_space=pl.ANY)
    vmem = pl.BlockSpec(memory_space=pltpu.VMEM)
    own_rows = [jax.ShapeDtypeStruct((rows, width), BF16)] * 2
    own_rows += [jax.ShapeDtypeStruct((rows, hidden), BF16)] * (3 * sides)
    outs = pl.pallas_call(
        functools.partial(layer_kernel, chunks, sides),
        in_specs=[anywhere] * (3 + len(flat_heads) + len(flat_weights)) + [vmem],
        out_specs=[anywhere, anywhere, vmem] + [anywhere] * (6 * arrays + len(own_rows)),
        out_shape=[whole, whole, jax.ShapeDtypeStruct((8, width), F32)]
        + finals + lands + lands + half_sums + own_rows,
        scratch_shapes=[
            pltpu.VMEM((2, 2, count * share, width), BF16),
            pltpu.VMEM((2, 2, 2, count - 1, share, width), BF16),
            pltpu.VMEM((2, 2, share, width), BF16),
            pltpu.VMEM((2, share, width), BF16),
            pltpu.VMEM((2, share, width), BF16),
            sem((2, 2)),
            sem((2, 2)),
            sem((2, 2, 2, count)),
            sem((2, 2, 2, count)),
            sem((chunks, 2, 2, count)),
            sem((chunks, 2, count)),
            sem((chunks, 2, count)),
            sem((chunks, 2, count)),
            sem((chunks, 2)),
            sem((arrays, 2, pieces)),
            sem((arrays, 2, pieces)),
            sem((arrays, 2, pieces)),
            sem((arrays, 2, pieces)),
            sem((arrays, pieces)),
            sem((arrays, pieces)),
            sem((arrays, 2, pieces)),
            sem((arrays, pieces)),
            sem((2 * arrays,)),
            sem((arrays, 2)),
            pltpu.VMEM((16, width), F32),
            pltpu.VMEM((sides, 8, columns[0]), F32),
            pltpu.VMEM((5, 8, width), F32),
            pltpu.VMEM((5, 8, width), F32),
            sem((5,)),
            sem((5,)),
        ],
        compiler_params=pltpu.CompilerParams(
            collective_id=0, has_side_effects=True, vmem_limit_bytes=63 * 2**20
        ),
        cost_estimate=pl.CostEstimate(
            flops=6 * rows * sum(array.size for array in flat_weights),
            bytes_accessed=800 * 2**20,
            transcendentals=0,
        ),
        name="layer",
    )(normed, tokens, cotangent, *flat_heads, *flat_weights, gain)
    out, grad, small = outs[:3]
    grads = [outs[3].astype(F32)]
    for blocks in outs[4 : 3 + arrays]:
        grads.append(blocks.transpose(1, 0, 2).reshape(blocks.shape[1], width).astype(F32))
    return out, grad, small[0], small[1], small[2, : columns[0]], grads


def body(
    tokens,
    lengths,
    norm_gain,
    norm_shift,
    qkv_weight,
    qkv_bias,
    out_weight,
    gate_weight,
    up_weight,
    down_weight,
    cotangent,
):
    tensor_size = lax.axis_size("tensor")
    dp_size = lax.axis_size("dp")
    count = tensor_size // 2
    where = lax.axis_index("tensor")
    dp_place = lax.axis_index("dp")
    side = where % 2
    across = [(i, i ^ 1) for i in range(tensor_size)]
    row_count, width = tokens.shape
    rows = row_count // 2
    chunk_count = 8

    def own_part(weight):
        part = weight.shape[0] // dp_size
        return lax.dynamic_slice_in_dim(weight, dp_place * part, part, 0)

    def partner(parts, before, after):
        parts, _ = lax.optimization_barrier((parts, before))
        parts = [lax.ppermute(part, "tensor", across) for part in parts]
        parts, _ = lax.optimization_barrier((parts, after))
        return [lax.all_gather(part, "dp", axis=0, tiled=True) for part in parts]

    head_weights = (qkv_weight, out_weight)
    mid_weights = (gate_weight.T, up_weight.T, down_weight)
    biases = (qkv_bias, lax.ppermute(qkv_bias, "tensor", across))

    length = lax.dynamic_slice_in_dim(lengths, side, 1, 0)
    norm = (norm_gain, norm_shift)
    *own_group, normed = project(side, tokens, cotangent, norm, head_weights, biases[0])
    tables = rotary_tables(rows)
    even = (out_weight.shape[0] // HEAD) % 2 == 0
    other_heads = partner([own_part(weight) for weight in head_weights], (), normed)
    mid_parts = [own_part(weight) for weight in mid_weights]
    if even:
        heads = [attention(length, *own_group, *tables)]
        other_mids = partner(mid_parts, normed, heads[0])
        other_group = project(side, normed, cotangent, (), other_heads, biases[1])
        heads.append(attention(length, *other_group, *tables))
    else:
        other_mids = partner(mid_parts, normed, ())
        other_group = project(side, normed, cotangent, (), other_heads, biases[1])
        pairs = zip(own_group, other_group)
        attended, qkv_back = attention(
            length, *[jnp.concatenate(pair, axis=1) for pair in pairs], *tables
        )
        cut, wide = out_weight.shape[0], qkv_weight.shape[1]
        heads = [
            (attended[:, s * cut : (s + 1) * cut], qkv_back[:, s * wide : (s + 1) * wide])
            for s in range(2)
        ]
    weights = ((*head_weights, *mid_weights), (*other_heads, *other_mids))
    layer_out, grad_tokens, gain_part, shift_part, grad_bias, grads = layer(
        normed, tokens, cotangent, heads, weights, norm_gain[None, :], count, chunk_count, dp_size
    )
    grad_qkv, grad_gate, grad_up, grad_down, grad_out = grads
    grad_gate, grad_up = grad_gate.T, grad_up.T
    return (
        layer_out,
        grad_tokens,
        gain_part,
        shift_part,
        grad_qkv,
        grad_bias,
        grad_out,
        grad_gate,
        grad_up,
        grad_down,
    )


def solution(mesh):
    placed = (
        P("dp", None),
        P("dp"),
        P(),
        P(),
        P(None, "tensor"),
        P("tensor"),
        P("tensor", None),
        P(None, "tensor"),
        P(None, "tensor"),
        P("tensor", None),
        P("dp", None),
    )
    return jax.shard_map(
        body,
        mesh=mesh,
        in_specs=placed,
        out_specs=(
            P("dp", None),
            P("dp", None),
            P(),
            P(),
            P(None, "tensor"),
            P("tensor"),
            P("tensor", None),
            P(None, "tensor"),
            P(None, "tensor"),
            P("tensor", None),
        ),
        check_vma=False,
    )
```

```python
import functools

import jax
import jax.numpy as jnp
import numpy as np
from jax import lax
from jax.experimental import pallas as pl
from jax.experimental.pallas import tpu as pltpu
from jax.sharding import PartitionSpec as P

HEAD = 64
ROT = 16
PAIR = 2 * HEAD
TRIPLE = 6 * HEAD

EPSILON = 1e-05
NEGATIVE = -1e30
F32 = jnp.float32
BF16 = jnp.bfloat16


def rows_product(former, latter):
    return lax.dot_general(
        former, latter, (((0,), (0,)), ((), ())), preferred_element_type=F32
    )


def cols_product(former, latter):
    return lax.dot_general(
        former, latter, (((1,), (1,)), ((), ())), preferred_element_type=F32
    )


def product(former, latter):
    return jnp.dot(former, latter, preferred_element_type=F32)


def rotary_tables(seq_len):
    frequency = np.float32(10000.0) ** (-np.arange(0, ROT, 2).astype(np.float32) / ROT)
    angles = np.arange(seq_len).astype(np.float32)[:, None] * frequency[None, :]
    cosine, sine = np.cos(angles), np.sin(angles)
    still = HEAD - ROT
    cos_head = np.concatenate([cosine, cosine, np.ones((seq_len, still))], axis=1)
    sin_head = np.concatenate([-sine, sine, np.zeros((seq_len, still))], axis=1)
    return [jnp.asarray(np.tile(table, (1, 2)), F32) for table in (cos_head, sin_head)]


def attention_kernel(
    len_ref, qkv_ref, grad_ref, cos_ref, sin_ref, att_ref, back_ref,
    score, expo, query, key_value, key_value_t, query_t, grad_query, grad_kv_t,
):
    seq_len = qkv_ref.shape[0]
    block = score.shape[1]
    steps = seq_len // block
    length = len_ref[0]
    lane = lax.broadcasted_iota(jnp.int32, (block, PAIR), 1)
    left = lane < HEAD
    near = lax.rem(lane, HEAD) < ROT // 2

    def turn(tile, cosine, sine):
        swapped = jnp.where(
            near, pltpu.roll(tile, PAIR - ROT // 2, 1), pltpu.roll(tile, ROT // 2, 1)
        )
        return tile * cosine + swapped * sine

    def tables(rows):
        cosine, sine = cos_ref[rows, :], sin_ref[rows, :]
        return (
            (cosine, sine),
            (jnp.where(left, 1.0, cosine), jnp.where(left, 0.0, sine)),
            (jnp.where(left, cosine, 1.0), jnp.where(left, sine, 0.0)),
        )

    def prepare(i, carry):
        rows = pl.ds(pl.multiple_of(i * block, block), block)
        tabs = tables(rows)
        first = turn(qkv_ref[rows, 0:PAIR], *tabs[0])
        second = turn(qkv_ref[rows, PAIR : 2 * PAIR], *tabs[1])
        third = turn(qkv_ref[rows, 2 * PAIR : 3 * PAIR], *tabs[2])
        scale = HEAD**-0.5
        first_q = first.astype(BF16).astype(F32) * scale
        second_q = second.astype(BF16).astype(F32) * scale
        query[0, rows, :] = jnp.where(left, 0.0, pltpu.roll(first_q, HEAD, 1)).astype(BF16)
        query[1, rows, :] = jnp.where(left, pltpu.roll(second_q, HEAD, 1), 0.0).astype(BF16)
        for h, tile in enumerate((jnp.where(left, second, first), third)):
            key_value[h, rows, :] = tile.astype(BF16)
            key_value_t[h, :, rows] = tile.T.astype(BF16)
        query_t[0, :, rows] = first_q.T[0:HEAD, :].astype(BF16)
        query_t[1, :, rows] = second_q.T[HEAD:PAIR, :].astype(BF16)
        zero = jnp.zeros((block, PAIR), F32)
        grad_query[rows, :] = zero
        att_ref[rows, :] = zero.astype(BF16)
        for h in range(2):
            grad_kv_t[h, :, rows] = jnp.zeros((PAIR, block), F32)
        return carry

    lax.fori_loop(0, steps, prepare, 0)

    def fold(tile, op):
        out = tile[:, 0:PAIR]
        for c in range(1, block // PAIR):
            out = op(out, tile[:, c * PAIR : (c + 1) * PAIR])
        return out

    def block_rows(i):
        rows = pl.ds(i * block, block)
        spans = [pl.ds(j * block, block) for j in range(i + 1)]
        q_block = [query[h, rows, :] for h in range(2)]
        below = lax.broadcasted_iota(jnp.int32, (block, block), 1) <= lax.broadcasted_iota(
            jnp.int32, (block, block), 0
        )
        maxima = []
        for h in range(2):
            top = None
            for j, cols in enumerate(spans):
                tile = product(q_block[h], key_value_t[h, :, cols])
                if j == i:
                    tile = jnp.where(below, tile, NEGATIVE)
                score[h, :, cols] = tile
                high = fold(tile, jnp.maximum)
                top = high if top is None else jnp.maximum(top, high)
            maxima.append(jnp.max(top, axis=1, keepdims=True))

        mixed, inverse = [], []
        for h in range(2):
            mixture = total = None
            for cols in spans:
                tile = jnp.exp(score[h, :, cols] - maxima[h])
                low = tile.astype(BF16)
                expo[h, :, cols] = low
                part = product(low, key_value[h, cols, :])
                amount = fold(tile, jnp.add)
                mixture = part if mixture is None else mixture + part
                total = amount if total is None else total + amount
            mixed.append(mixture)
            inverse.append(1.0 / jnp.sum(total, axis=1, keepdims=True))

        place = i * block + lax.broadcasted_iota(jnp.int32, (block, 1), 0)
        valid = (place < length).astype(F32)
        mixture = jnp.where(left, mixed[0] * inverse[0], mixed[1] * inverse[1]) * valid
        att_ref[rows, :] = mixture.astype(BF16)
        upstream = grad_ref[rows, :].astype(F32) * valid
        inner = upstream * mixture
        scale = HEAD**-0.5
        turned = []
        for h in range(2):
            own = left if h == 0 else jnp.logical_not(left)
            inner_sum = jnp.sum(jnp.where(own, inner, 0.0), axis=1, keepdims=True) * inverse[h]
            mine = jnp.where(own, upstream * inverse[h], 0.0)
            scaled = mine.astype(BF16)
            half = slice(0, HEAD) if h == 0 else slice(HEAD, PAIR)
            scaled_t = mine.T[half, :].astype(BF16)
            queries_t = query_t[h, :, rows]
            grad = None
            for cols in spans:
                low = expo[h, :, cols]
                grad_weight = product(scaled, key_value_t[h, :, cols])
                grad_score = (low.astype(F32) * (grad_weight - inner_sum)).astype(BF16)
                part = product(grad_score, key_value[h, cols, :])
                grad = part if grad is None else grad + part
                key_at, value_at = (HEAD, 0) if h == 0 else (0, HEAD)
                grad_kv_t[h, key_at : key_at + HEAD, cols] += product(queries_t, grad_score)
                grad_kv_t[h, value_at : value_at + HEAD, cols] += product(scaled_t, low)
            turned.append(pltpu.roll(grad, HEAD, 1))
        grad_query[rows, :] = jnp.where(left, turned[0], turned[1]) * scale

    for i in range(steps):
        pl.when(i * block < length)(functools.partial(block_rows, i))

    def finish(i, carry):
        rows = pl.ds(pl.multiple_of(i * block, block), block)
        tabs = tables(rows)
        gq = grad_query[rows, :]
        low_kv = grad_kv_t[0, :, rows].T
        high_kv = grad_kv_t[1, :, rows].T
        tiles = (jnp.where(left, gq, low_kv), jnp.where(left, low_kv, gq), high_kv)
        for c in range(3):
            back_ref[rows, c * PAIR : (c + 1) * PAIR] = turn(
                tiles[c], tabs[c][0], -tabs[c][1]
            ).astype(BF16)
        return carry

    lax.fori_loop(0, steps, finish, 0)


def attention(length, qkv, grad_mixture, cosine, sine):
    seq_len, width = qkv.shape
    pairs = width // TRIPLE
    block = min(512, seq_len)
    flops = 6 * 2 * (2 * pairs) * seq_len * seq_len * PAIR
    return pl.pallas_call(
        attention_kernel,
        grid=(pairs,),
        in_specs=[
            pl.BlockSpec(memory_space=pltpu.SMEM),
            pl.BlockSpec((seq_len, TRIPLE), lambda g: (0, g)),
            pl.BlockSpec((seq_len, PAIR), lambda g: (0, g)),
            pl.BlockSpec((seq_len, PAIR), lambda g: (0, 0)),
            pl.BlockSpec((seq_len, PAIR), lambda g: (0, 0)),
        ],
        out_specs=[
            pl.BlockSpec((seq_len, PAIR), lambda g: (0, g)),
            pl.BlockSpec((seq_len, TRIPLE), lambda g: (0, g)),
        ],
        out_shape=[
            jax.ShapeDtypeStruct((seq_len, pairs * PAIR), BF16),
            jax.ShapeDtypeStruct((seq_len, width), BF16),
        ],
        scratch_shapes=[
            pltpu.VMEM((2, block, seq_len), F32),
            pltpu.VMEM((2, block, seq_len), BF16),
            pltpu.VMEM((2, seq_len, PAIR), BF16),
            pltpu.VMEM((2, seq_len, PAIR), BF16),
            pltpu.VMEM((2, PAIR, seq_len), BF16),
            pltpu.VMEM((2, HEAD, seq_len), BF16),
            pltpu.VMEM((seq_len, PAIR), F32),
            pltpu.VMEM((2, PAIR, seq_len), F32),
        ],
        compiler_params=pltpu.CompilerParams(vmem_limit_bytes=48 * 2**20),
        cost_estimate=pl.CostEstimate(
            flops=flops,
            bytes_accessed=seq_len * width * 8,
            transcendentals=2 * pairs * seq_len * seq_len // 2,
        ),
        name="attention",
    )(length, qkv, grad_mixture, cosine, sine)


def start_kernel(
    side_ref, tok_ref, cot_ref, gain_ref, shift_ref, qkv_w, bias_ref, out_w,
    qkv_ref, grad_ref, normed_ref,
):
    wide = tok_ref[...].astype(F32)
    centred = wide - jnp.mean(wide, axis=1, keepdims=True)
    variance = jnp.mean(centred * centred, axis=1, keepdims=True)
    unit = centred * lax.rsqrt(variance + EPSILON)
    normed = (unit * gain_ref[...] + shift_ref[...]).astype(BF16)
    normed_ref[...] = normed
    qkv_ref[...] = product(normed, qkv_w[...]) + bias_ref[...]
    grad_ref[...] = cols_product(cot_ref[...], out_w[...]).astype(BF16)


def project_kernel(side_ref, normed_ref, cot_ref, qkv_w, bias_ref, out_w, qkv_ref, grad_ref):
    qkv_ref[...] = product(normed_ref[...], qkv_w[...]) + bias_ref[...]
    grad_ref[...] = cols_product(cot_ref[...], out_w[...]).astype(BF16)


def project(side, rows_in, cotangent, norm, weights, bias):
    rows, width = cotangent.shape[0] // 2, cotangent.shape[1]
    tile = min(256, rows)
    tiles = rows // tile
    qkv_weight, out_weight = weights
    heads, wide = out_weight.shape[0], qkv_weight.shape[1]

    def sided(i, side_ref):
        return (side_ref[0] * tiles + i, 0)

    def fixed(i, side_ref):
        return (0, 0)

    def rowed(i, side_ref):
        return (i, 0)

    flat = [part[None, :] for part in norm]
    flat += [qkv_weight, bias.astype(F32)[None, :], out_weight]
    outs = [((rows, wide), F32), ((rows, heads), BF16)]
    out_specs = [pl.BlockSpec((tile, shape[1]), rowed) for shape, _ in outs]
    if norm:
        outs.append(((rows, width), BF16))
        out_specs.append(pl.BlockSpec((tile, width), rowed))
    return pl.pallas_call(
        start_kernel if norm else project_kernel,
        grid_spec=pltpu.PrefetchScalarGridSpec(
            num_scalar_prefetch=1,
            grid=(tiles,),
            in_specs=[
                pl.BlockSpec((tile, width), sided if norm else rowed),
                pl.BlockSpec((tile, width), sided),
            ]
            + [pl.BlockSpec(array.shape, fixed) for array in flat],
            out_specs=out_specs,
        ),
        out_shape=[jax.ShapeDtypeStruct(*out) for out in outs],
        compiler_params=pltpu.CompilerParams(vmem_limit_bytes=40 * 2**20),
        cost_estimate=pl.CostEstimate(
            flops=2 * rows * width * (wide + heads),
            bytes_accessed=rows * (6 * width + 4 * wide),
            transcendentals=rows,
        ),
        name="project",
    )(side[None], rows_in, cotangent, *flat)


def layer_kernel(chunks, sides, *refs):
    normed_ref, tok_ref, cot_ref = refs[:3]
    head_refs, refs = refs[3 : 3 + 2 * sides], refs[3 + 2 * sides :]
    weight_refs, gain_ref = refs[: 5 * sides], refs[5 * sides]
    refs = refs[5 * sides + 1 :]
    out_ref, grad_ref, small_ref = refs[:3]
    refs = refs[3:]
    arrays = 5
    grad_outs, core_land = refs[:arrays], refs[arrays : 3 * arrays]
    far_land, side_land = refs[3 * arrays : 5 * arrays], refs[5 * arrays : 6 * arrays]
    refs = refs[6 * arrays :]
    f_ref, g_ref = refs[:2]
    mid_refs, refs = refs[2 : 2 + 3 * sides], refs[2 + 3 * sides :]
    (
        terms, landed, ready, tok_buf, cot_buf,
        term_sem, share_sem, sum_send, sum_recv,
        line_send, line_recv, side_send, side_recv, keep_sem,
        core_send, core_recv, far_send, far_recv, over_send, over_recv,
        back_send, back_recv, load_sem, save_sem,
        part_ref, bias_part, stages, came, small_send, small_recv,
    ) = refs
    share, width = landed.shape[4:]
    count = landed.shape[3] + 1
    chunk_rows = count * share
    rows = chunks * chunk_rows
    where = lax.axis_index("tensor")
    group = lax.axis_index("dp")
    place, side = where // 2, where % 2
    half, core = group // 2, group % 2
    whole_refs = (out_ref, grad_ref)
    factors = []
    for s in range(sides):
        hidden_ref, gate_ref, up_ref = mid_refs[3 * s : 3 * s + 3]
        factors.append(
            (head_refs[2 * s + 1], gate_ref, up_ref, hidden_ref, head_refs[2 * s])
        )
    factors = [factors[x % sides][x // sides] for x in range(arrays * sides)]

    above, below = (group, where + 2), (group, where - 2)
    across = (group, where + 1 - 2 * side)
    other_core = (half * 2 + 1 - core, where)
    other_half = ((1 - half) * 2 + core, where)
    has_above, has_below = place < count - 1, place > 0

    barrier = pltpu.get_barrier_semaphore()

    def greet(target):
        pl.semaphore_signal(barrier, inc=1, device_id=target, device_id_type=pl.DeviceIdType.MESH)

    pl.when(has_above)(lambda: greet(above))
    pl.when(has_below)(lambda: greet(below))
    for target in (across, other_core, other_half):
        greet(target)

    def span(begin, size):
        return pl.ds(pl.multiple_of(begin, size), size)

    def load(c, k):
        source = (f_ref, g_ref)[k].at[span(c * chunk_rows, chunk_rows), :]
        return pltpu.make_async_copy(
            source, terms.at[lax.rem(c, 2), k], term_sem.at[lax.rem(c, 2), k]
        )

    def load_share(c, k):
        begin = span(side * rows + c * chunk_rows + place * share, share)
        source, target = ((tok_ref, tok_buf), (cot_ref, cot_buf))[k]
        return pltpu.make_async_copy(
            source.at[begin, :], target.at[lax.rem(c, 2)], share_sem.at[lax.rem(c, 2), k]
        )

    def remote(source, target, send, recv, device_id):
        return pltpu.make_async_remote_copy(
            src_ref=source, dst_ref=target, send_sem=send, recv_sem=recv,
            device_id=device_id, device_id_type=pl.DeviceIdType.MESH,
        )


    def sum_copy(c, k, way, b, first):
        slot = lax.rem(c, 2)
        target = landed.at[slot, k, way, b - 1 + way]
        source = terms.at[slot, k, span(b * share, share), :] if first else target
        return remote(
            source, target, sum_send.at[slot, k, way, b], sum_recv.at[slot, k, way, b],
            (above, below)[way],
        )

    def place_of(c, b, on_side):
        return span(on_side * rows + c * chunk_rows + b * share, share)

    def line_copy(c, k, b, way, first):
        target = whole_refs[k].at[place_of(c, b, side), :]
        source = ready.at[lax.rem(c, 2), k] if first else target
        return remote(
            source, target, line_send.at[c, k, way, b], line_recv.at[c, k, b],
            (above, below)[way],
        )

    def side_copy(c, k, b, first):
        target = whole_refs[k].at[place_of(c, b, side), :]
        source = ready.at[lax.rem(c, 2), k] if first else target
        return remote(
            source, target, side_send.at[c, k, b], side_recv.at[c, k, b], across
        )

    def keep_copy(c, k):
        return pltpu.make_async_copy(
            ready.at[lax.rem(c, 2), k], whole_refs[k].at[place_of(c, place, side), :],
            keep_sem.at[c, k],
        )

    def each_first(c, k, act):
        @pl.when(jnp.logical_not(has_below))
        def _():
            for b in range(count - 1, 0, -1):
                act(sum_copy(c, k, 0, b, True))

        @pl.when(jnp.logical_not(has_above))
        def _():
            for b in range(count - 1):
                act(sum_copy(c, k, 1, b, True))

    def send_ends(c, k):
        load(c, k).wait()
        each_first(c, k, lambda copy: copy.start())

    def sums_left(c, k):
        for b in range(count):

            @pl.when(has_below & (place < b))
            def _(b=b):
                sum_copy(c, k, 0, b, False).wait_send()

            @pl.when(has_above & (place > b))
            def _(b=b):
                sum_copy(c, k, 1, b, False).wait_send()

    step = min(16, share)

    def add_on(c, k, way, b):
        slot = lax.rem(c, 2)

        def body(i, carry):
            at = span(i * step, step)
            mine = terms[slot, k, span(b * share + i * step, step), :].astype(F32)
            landed[slot, k, way, b - 1 + way, at, :] = (
                mine + landed[slot, k, way, b - 1 + way, at, :].astype(F32)
            ).astype(BF16)
            return carry

        lax.fori_loop(0, share // step, body, 0)

    def sums(c, k, wave):
        ahead = count - 2 - wave
        for way, b, here in (
            (0, place + ahead, has_below & (place + ahead < count)),
            (1, place - ahead, has_above & (place >= ahead)),
        ):

            @pl.when(here)
            def _(way=way, b=b):
                sum_copy(c, k, way, b, False).wait_recv()

                @pl.when(ahead > 0)
                def _():
                    add_on(c, k, way, b)
                    sum_copy(c, k, way, b, False).start()

    def own_left(c, k):
        pl.when(has_above)(lambda: line_copy(c, k, place, 0, True).wait_send())
        pl.when(has_below)(lambda: line_copy(c, k, place, 1, True).wait_send())
        side_copy(c, k, place, True).wait_send()
        keep_copy(c, k).wait()

    def finish(c, k):
        load_share(c, k).wait()
        pl.when(c > 1)(lambda: own_left(c - 2, k))
        slot = lax.rem(c, 2)

        def body(i, carry):
            at = span(i * step, step)
            up = landed[slot, k, 0, jnp.maximum(place - 1, 0), at, :].astype(F32)
            down = landed[slot, k, 1, jnp.minimum(place, count - 2), at, :].astype(F32)
            total = (
                terms[slot, k, span(place * share + i * step, step), :].astype(F32)
                + jnp.where(has_below, up, 0.0)
                + jnp.where(has_above, down, 0.0)
            )
            wide = tok_buf[slot, at, :].astype(F32)
            if k == 0:
                ready[slot, k, at, :] = (wide + total).astype(BF16)
                return carry
            scale = 1.0 / width
            centred = wide - jnp.sum(wide, axis=1, keepdims=True) * scale
            variance = jnp.sum(centred * centred, axis=1, keepdims=True) * scale
            inverse = lax.rsqrt(variance + EPSILON)
            unit = centred * inverse
            scaled = total * gain_ref[0:1, :]
            mean_scaled = jnp.sum(scaled, axis=1, keepdims=True) * scale
            mean_cross = jnp.sum(scaled * unit, axis=1, keepdims=True) * scale
            ready[slot, k, at, :] = (
                cot_buf[slot, at, :].astype(F32)
                + inverse * (scaled - mean_scaled - unit * mean_cross)
            ).astype(BF16)
            gain_term = total * unit
            for r in range(0, step, 8):
                part_ref[0:8, :] += gain_term[r : r + 8, :]
                part_ref[8:16, :] += total[r : r + 8, :]
            return carry

        lax.fori_loop(0, share // step, body, 0)
        pl.when(has_above)(lambda: line_copy(c, k, place, 0, True).start())
        pl.when(has_below)(lambda: line_copy(c, k, place, 1, True).start())
        side_copy(c, k, place, True).start()
        keep_copy(c, k).start()

    def pass_on(c, k, distance):
        for way, b, here in (
            (0, place - distance, place >= distance),
            (1, place + distance, place + distance < count),
        ):

            @pl.when(here)
            def _(way=way, b=b):
                line_copy(c, k, b, way, False).wait_recv()
                pl.when((has_above, has_below)[way])(
                    lambda: line_copy(c, k, b, way, False).start()
                )
                side_copy(c, k, b, False).start()

    def small_copy(n, target):
        return remote(stages.at[n], came.at[n], small_send.at[n], small_recv.at[n], target)

    def small_sums():
        wide = bias_part.shape[2]
        stages[...] = jnp.zeros_like(stages)
        stages[0, 0:1, :] = jnp.sum(part_ref[0:8, :], axis=0, keepdims=True)
        stages[0, 1:2, :] = jnp.sum(part_ref[8:16, :], axis=0, keepdims=True)
        for s in range(sides):
            stages[0, 2 + s : 3 + s, 0:wide] = jnp.sum(bias_part[s], axis=0, keepdims=True)
        for n, target in enumerate((across, other_core, other_half)):
            copy = small_copy(n, target)
            copy.start()
            copy.wait_recv()
            if n == 0:
                stages[1, 0:2, :] = stages[0, 0:2, :] + came[0, 0:2, :]
                stages[1, 2:3, :] = stages[0, 2:3, :] + came[0, 3:4, :]
            else:
                stages[n + 1] = stages[n] + came[n]

        @pl.when(has_below)
        def _():
            small_copy(3, above).wait_recv()
            stages[3] = stages[3] + came[3]

        pl.when(has_above)(lambda: small_copy(3, above).start())
        stages[4] = stages[3]

        @pl.when(has_above)
        def _():
            small_copy(4, below).wait_recv()
            stages[4] = came[4]

        pl.when(has_below)(lambda: small_copy(4, below).start())
        small_ref[...] = stages[4]
        small_ref[2:3, :] = stages[2, 2:3, :] + came[2, 2:3, :]
        for n, target in enumerate((across, other_core, other_half)):
            small_copy(n, target).wait_send()
        pl.when(has_above)(lambda: small_copy(3, above).wait_send())
        pl.when(has_below)(lambda: small_copy(4, below).wait_send())

    waves = count - 1
    every = max(1, waves // 3)
    works = waves // every

    if count == 4:
        order = ((2, 2, 0), (1, 1, 1), (2, 3, 1))
    else:
        order = tuple((2, distance, distance - 1) for distance in range(1, count))

    def pass_steps(h, live, wave):
        for behind, distance, step in order:
            item = jnp.maximum(h - behind, 0)
            for k in range(2):
                pl.when(
                    live & (wave == step) & (h >= behind) & (lax.rem(item, 2) == k)
                )(lambda: pass_on(item // 2, k, distance))

    def pass_rest():
        for item in range(2 * chunks - 2, 2 * chunks):
            for distance, behind in sorted((step[1], step[0]) for step in order):
                if item + behind >= 2 * chunks:
                    pass_on(item // 2, item % 2, distance)

    def half_steps(h, live, work):
        c = h // 2

        def one(wave, carry):
            pl.when(lax.rem(wave, every) == 0)(lambda: work(wave // every))
            for k in range(2):

                @pl.when(live & (lax.rem(h, 2) == k))
                def _(k=k):
                    more = c + 1 < chunks

                    @pl.when(wave == 0)
                    def _():
                        @pl.when(c > 0)
                        def _():
                            sums_left(c - 1, k)
                            each_first(c - 1, k, lambda copy: copy.wait_send())

                        pl.when(more)(lambda: load_share(c + 1, k).start())
                        pl.when(more & (c > 0))(lambda: load(c + 1, k).start())

                    sums(c, k, wave)

            pass_steps(h, live, wave)
            for k in range(2):

                @pl.when(live & (lax.rem(h, 2) == k) & (wave == waves - 1))
                def _(k=k):
                    more = c + 1 < chunks
                    pl.when(c == 0)(lambda: load(c + 1, k).start())
                    finish(c, k)
                    pl.when(more)(lambda: send_ends(c + 1, k))

            return carry

        lax.fori_loop(0, waves, one, 0)

    tile_halves = -(-sides * (chunks - 1) // works)

    def tiles_scope(*scratch):
        weights = scratch[: 5 * sides]
        scratch = scratch[5 * sides :]
        normed_buf, tile_cot = scratch[:2]
        head_bufs = scratch[2 : 2 + 2 * sides]
        scratch = scratch[2 + 2 * sides :]
        mids, f_buf, g_buf = scratch[: 3 * sides], scratch[3 * sides], scratch[3 * sides + 1]
        f_total, g_total, weight_sem, in_sem, out_sem = scratch[3 * sides + 2 :]

        def weight_copies(s):
            return [
                pltpu.make_async_copy(weight_refs[x], weights[x], weight_sem.at[x])
                for x in range(5 * s, 5 * s + 5)
            ]

        def tile_in(i):
            slot = lax.rem(i, 2)
            at = span(i * chunk_rows, chunk_rows)
            at_side = span(side * rows + i * chunk_rows, chunk_rows)
            pairs = [(normed_ref.at[at, :], normed_buf), (cot_ref.at[at_side, :], tile_cot)]
            pairs += [(ref.at[at, :], buf) for ref, buf in zip(head_refs, head_bufs)]
            return [
                pltpu.make_async_copy(ref, buf.at[slot], in_sem.at[slot, x])
                for x, (ref, buf) in enumerate(pairs)
            ]

        def tile_out(i):
            at = span(i * chunk_rows, chunk_rows)
            pairs = list(zip(mids, mid_refs)) + [(f_buf, f_ref), (g_buf, g_ref)]
            return [
                pltpu.make_async_copy(buf, ref.at[at, :], out_sem.at[x])
                for x, (buf, ref) in enumerate(pairs)
            ]

        def wait_out(i):
            for copy in tile_out(i):
                copy.wait()

        def tile(i, s):
            slot = lax.rem(i, 2)
            if s == 0:
                for copy in tile_in(i):
                    copy.wait()

                @pl.when(i + 1 < chunks)
                def _():
                    for copy in tile_in(i + 1):
                        copy.start()

            @pl.when(i == 0)
            def _():
                for copy in weight_copies(s):
                    copy.wait()

            qkv_w, out_w, gate_w, up_w, down_w = weights[5 * s : 5 * s + 5]
            hidden_buf, gate_buf, up_buf = mids[3 * s : 3 * s + 3]
            normed, cot = normed_buf[slot], tile_cot[slot]
            gate = cols_product(normed, gate_w[...])
            up = cols_product(normed, up_w[...])
            sig = 1.0 / (1.0 + jnp.exp(-gate))
            silu = gate * sig
            hidden = (silu * up).astype(BF16)
            grad_hidden = cols_product(cot, down_w[...])
            if s == 0:
                pl.when(i > 1)(lambda: wait_out(i - 1))
            hidden_buf[...] = hidden
            gate_back = (grad_hidden * up * sig * (1.0 + gate * (1.0 - sig))).astype(BF16)
            up_back = (grad_hidden * silu).astype(BF16)
            gate_buf[...] = gate_back
            up_buf[...] = up_back
            forward = product(hidden, down_w[...])
            forward += product(head_bufs[2 * s][slot], out_w[...])
            backward = product(gate_back, gate_w[...])
            backward += product(up_back, up_w[...])
            qkv_back = head_bufs[2 * s + 1][slot]
            backward += cols_product(qkv_back, qkv_w[...])
            bias_part[s] += (
                qkv_back.astype(F32).reshape(chunk_rows // 8, 8, qkv_back.shape[1]).sum(axis=0)
            )
            if s > 0:
                forward += f_total[...]
                backward += g_total[...]
            if s < sides - 1:
                f_total[...] = forward
                g_total[...] = backward
                return
            f_buf[...] = forward.astype(BF16)
            g_buf[...] = backward.astype(BF16)
            for copy in tile_out(i):
                copy.start()

        def work(turn, n):
            first = turn == 0
            unit = jnp.maximum(works * turn - works, 0) + n
            i = jnp.where(first, 0, 1 + unit // sides)
            part = jnp.where(first, n - works + sides, lax.rem(unit, sides))
            for s in range(sides):
                pl.when((part == s) & (i < chunks))(lambda: tile(i, s))

        for s in range(sides):
            for copy in weight_copies(s):
                copy.start()
        for copy in tile_in(0):
            copy.start()
        for k in range(2):
            load_share(0, k).start()
        part_ref[...] = jnp.zeros_like(part_ref)
        bias_part[...] = jnp.zeros_like(bias_part)
        pl.semaphore_wait(
            barrier, 3 + has_above.astype(jnp.int32) + has_below.astype(jnp.int32)
        )

        def chunk(turn, carry):
            half_steps(
                jnp.maximum(turn, 1) - 1, turn > 0, lambda n: work(turn, n)
            )

            @pl.when(turn == 0)
            def _():
                wait_out(0)
                for k in range(2):
                    load(0, k).start()
                for k in range(2):
                    send_ends(0, k)

            return carry

        lax.fori_loop(0, tile_halves + 1, chunk, 0)
        wait_out(chunks - 1)

    tall = width
    hidden_cols = mid_refs[0].shape[1]
    pl.run_scoped(
        tiles_scope,
        *[pltpu.VMEM(ref.shape, BF16) for ref in weight_refs],
        pltpu.VMEM((2, chunk_rows, width), BF16),
        pltpu.VMEM((2, chunk_rows, width), BF16),
        *[pltpu.VMEM((2, chunk_rows, ref.shape[1]), BF16) for ref in head_refs],
        *[pltpu.VMEM((chunk_rows, hidden_cols), BF16) for _ in mid_refs],
        pltpu.VMEM((chunk_rows, width), BF16),
        pltpu.VMEM((chunk_rows, width), BF16),
        pltpu.VMEM((chunk_rows, width), F32),
        pltpu.VMEM((chunk_rows, width), F32),
        pltpu.SemaphoreType.DMA((5 * sides,)),
        pltpu.SemaphoreType.DMA((2, 2 + 2 * sides)),
        pltpu.SemaphoreType.DMA((3 * sides + 2,)),
    )


    pieces = core_send.shape[2]
    each = 2
    size = tall // pieces

    def grads_scope(*scratch):
        factor_bufs, scratch = scratch[: arrays * sides], scratch[arrays * sides :]
        held, scratch = scratch[: arrays * sides], scratch[arrays * sides :]
        extra, scratch = scratch[: arrays * sides], scratch[arrays * sides :]
        turned, scratch = scratch[: arrays - 1], scratch[arrays - 1 :]
        left_bufs, factor_sem, left_sem = scratch[:2], scratch[2], scratch[3]

        def factor_copy(x):
            return pltpu.make_async_copy(factors[x], factor_bufs[x], factor_sem.at[x])

        def piece(ref, j):
            return ref.at[span(j * size, size), :]

        def piece_of(u):
            owner_core = jnp.where((u // each) % 2 == 0, 1 - core, core)
            owner_half = jnp.where(u < 2 * each, 1 - half, half)
            return (owner_half * 2 + owner_core) * each + lax.rem(u, each)

        def slot_of(u):
            return jnp.where(u < 2 * each, lax.rem(u, each), each + lax.rem(u, each))

        def left_copy(u, which):
            at = span(piece_of(u) * size, size)
            source = (
                normed_ref.at[:, at] if which == 0 else cot_ref.at[span(side * rows, rows), at]
            )
            return pltpu.make_async_copy(
                source, left_bufs[which].at[lax.rem(u, 2)], left_sem.at[which, lax.rem(u, 2)]
            )

        def to_core(a, s, j, slot):
            x = 2 * a + s
            return remote(
                held[x].at[slot], piece(core_land[x], j),
                core_send.at[a, s, j], core_recv.at[a, s, j], other_core,
            )

        def to_far(a, s, i, j):
            x = 2 * a + s
            return remote(
                held[x].at[i], piece(far_land[x], j),
                far_send.at[a, s, j], far_recv.at[a, s, j], other_half,
            )

        def to_over(a, i, j):
            return remote(
                held[2 * a + 1].at[each + i], piece(side_land[a], j),
                over_send.at[a, j], over_recv.at[a, j], across,
            )

        def final_piece(a, j):
            return grad_outs[a].at[j] if a else grad_outs[a].at[span(j * size, size), :]

        def final_source(a, i):
            return turned[a - 1].at[i] if a else held[0].at[each + i]

        def back_copy(a, i, j, way, first):
            target = final_piece(a, j)
            source = final_source(a, i) if first else target
            return remote(
                source, target, back_send.at[a, way, j], back_recv.at[a, j],
                (other_core, other_half)[way],
            )

        def save_copy(a, i, j):
            return pltpu.make_async_copy(
                final_source(a, i), final_piece(a, j), save_sem.at[a, i]
            )

        def their_piece(i):
            return ((1 - half) * 2 + core) * each + i

        def my_piece(i):
            return (half * 2 + core) * each + i

        def add_into(target, slot, source):
            def body(i, carry):
                at = span(i * 16, 16)
                target[slot, at, :] = (
                    target[slot, at, :].astype(F32) + source[at, :].astype(F32)
                ).astype(BF16)
                return carry

            lax.fori_loop(0, size // 16, body, 0)

        def fetch(lands, j, ids, act):
            for n, x in enumerate(ids):
                act(pltpu.make_async_copy(piece(lands[n], j), extra[x], load_sem.at[x]))

        def begin(lands, j, ids):
            fetch(lands, j, ids, lambda copy: copy.start())

        def end(lands, j, ids):
            fetch(lands, j, ids, lambda copy: copy.wait())

        everything = range(2 * arrays)

        def make(u, which):
            @pl.when(u == 0)
            def _():
                for x in everything:
                    if (x // 2 < 3) == (which == 0):
                        factor_copy(x).wait()

            left_copy(u, which).wait()
            pl.when(u + 1 < pieces)(lambda: left_copy(u + 1, which).start())
            slot = slot_of(u)
            left = left_bufs[which][lax.rem(u, 2)].T

            @pl.when((u // each) % 2 == 1)
            def _():
                for x in everything:
                    if (x // 2 < 3) == (which == 0):
                        to_core(x // 2, x % 2, piece_of(u - each), slot).wait_send()

            for x in everything:
                if (x // 2 < 3) == (which == 0):
                    held[x][slot] = product(left, factor_bufs[x][...]).astype(BF16)

            @pl.when((u // each) % 2 == 0)
            def _():
                for x in everything:
                    if (x // 2 < 3) == (which == 0):
                        to_core(x // 2, x % 2, piece_of(u), slot).start()


        def core_begin(j):
            for x in everything:
                to_core(x // 2, x % 2, j, 0).wait_recv()
            begin(core_land, j, everything)

        def core_end(slot, j):
            end(core_land, j, everything)
            for x in everything:
                add_into(held[x], slot, extra[x])

        def far_begin(i):
            core_begin(their_piece(i))

        def far_end(i):
            j = their_piece(i)
            core_end(i, j)
            for x in everything:
                to_far(x // 2, x % 2, i, j).start()

        def over_begin(i):
            core_begin(my_piece(i))

        def over_middle(i):
            j = my_piece(i)
            core_end(each + i, j)
            for x in everything:
                to_far(x // 2, x % 2, i, j).wait_recv()
            begin(far_land, j, everything)

        def over_end(i):
            j = my_piece(i)
            end(far_land, j, everything)
            for a in range(arrays):
                add_into(held[2 * a + 1], each + i, extra[2 * a + 1])
                to_over(a, i, j).start()
            for a in range(arrays):
                add_into(held[2 * a], each + i, extra[2 * a])

        firsts = range(0, 2 * arrays, 2)

        def back_begin(i):
            j = my_piece(i)
            for a in range(arrays):
                to_over(a, i, j).wait_recv()
            begin(side_land, j, firsts)

        def back_end(i):
            j = my_piece(i)
            end(side_land, j, firsts)
            for a in range(arrays):
                if a:
                    total = held[2 * a][each + i].astype(F32) + extra[2 * a][...].astype(F32)
                    turned[a - 1][i] = total.T.astype(BF16)
                else:
                    add_into(held[0], each + i, extra[0])
                back_copy(a, i, j, 1, True).start()
                back_copy(a, i, j, 0, True).start()
                save_copy(a, i, j).start()

        def grads_pass(i):
            j = their_piece(i)
            for a in range(arrays):
                back_copy(a, i, j, 1, False).wait_recv()
                back_copy(a, i, j, 0, False).start()

        def grads_drain():
            for i in range(each):
                mine, theirs = my_piece(i), their_piece(i)
                for a in range(arrays):
                    for s in range(2):
                        to_far(a, s, i, theirs).wait_send()
                    to_over(a, i, mine).wait_send()
                    back_copy(a, i, mine, 1, True).wait_send()
                    back_copy(a, i, mine, 0, True).wait_send()
                    back_copy(a, i, theirs, 0, False).wait_send()
                    save_copy(a, i, mine).wait()
            for u in (*range(each), *range(2 * each, 3 * each)):
                for a in range(arrays):
                    back_copy(a, 0, piece_of(u), 0, False).wait_recv()

        events = {
            (7, 1): (far_begin, 0),
            (7, 2): (far_end, 0),
            (8, 1): (far_begin, 1),
            (8, 2): (far_end, 1),
            (11, 1): (over_begin, 0),
            (11, 2): (over_middle, 0),
            (12, 0): (over_end, 0),
            (12, 1): (over_begin, 1),
            (12, 2): (over_middle, 1),
            (13, 0): (over_end, 1),
            (14, 1): (back_begin, 0),
            (14, 2): (back_end, 0),
        }

        def work(h, n):
            u = h - tile_halves
            for which in range(2):
                pl.when((u < pieces) & (n == which))(lambda: make(u, which))
            for (at, step), (act, i) in events.items():
                pl.when((h == at) & (n == step))(lambda: act(i))

        for x in everything:
            factor_copy(x).start()
        for which in range(2):
            left_copy(0, which).start()

        def chunk(c, carry):
            half_steps(c, c >= 0, lambda n: work(c, n))
            return carry

        lax.fori_loop(tile_halves, 2 * chunks, chunk, 0)
        back_begin(1)
        pass_rest()
        back_end(1)
        small_sums()
        for i in range(each):
            grads_pass(i)
        grads_drain()

    factor_shapes = [ref.shape for ref in factors]
    pl.run_scoped(
        grads_scope,
        *[pltpu.VMEM(shape, BF16) for shape in factor_shapes],
        *[pltpu.VMEM((2 * each, size, shape[1]), BF16) for shape in factor_shapes],
        *[pltpu.VMEM((size, shape[1]), BF16) for shape in factor_shapes],
        *[pltpu.VMEM((each, shape[1], size), BF16) for shape in factor_shapes[2::2]],
        pltpu.VMEM((2, rows, size), BF16),
        pltpu.VMEM((2, rows, size), BF16),
        pltpu.SemaphoreType.DMA((2 * arrays,)),
        pltpu.SemaphoreType.DMA((2, 2)),
    )

    for k in range(2):
        sums_left(chunks - 1, k)
        each_first(chunks - 1, k, lambda copy: copy.wait_send())
        own_left(chunks - 2, k)
        own_left(chunks - 1, k)

    def drain(c, carry):
        for k in range(2):
            for b in range(count):
                pl.when((place > b) & has_above)(
                    lambda: line_copy(c, k, b, 0, False).wait_send()
                )
                pl.when((place < b) & has_below)(
                    lambda: line_copy(c, k, b, 1, False).wait_send()
                )
                pl.when(place != b)(lambda: side_copy(c, k, b, False).wait_send())
                side_copy(c, k, b, False).wait_recv()
        return carry

    lax.fori_loop(0, chunks, drain, 0)


def layer(normed, tokens, cotangent, heads, weights, gain, count, chunks, dp_size):
    row_count, width = tokens.shape
    rows = row_count // 2
    share = rows // chunks // count
    sides, arrays = len(weights), 5
    pieces = 2 * dp_size
    sem = pltpu.SemaphoreType.DMA
    flat_heads = [array for group in heads for array in group]
    flat_weights = [array for group in weights for array in group]
    hidden = weights[0][2].shape[0]
    columns = [heads[0][1].shape[1], hidden, hidden, hidden, heads[0][0].shape[1]]
    whole = jax.ShapeDtypeStruct(tokens.shape, BF16)
    half_sums = [jax.ShapeDtypeStruct((width, n), BF16) for n in columns]
    finals = half_sums[:1] + [
        jax.ShapeDtypeStruct((pieces, n, width // pieces), BF16) for n in columns[1:]
    ]
    lands = [shape for shape in half_sums for _ in range(sides)]
    anywhere = pl.BlockSpec(memory_space=pl.ANY)
    vmem = pl.BlockSpec(memory_space=pltpu.VMEM)
    own_rows = [jax.ShapeDtypeStruct((rows, width), BF16)] * 2
    own_rows += [jax.ShapeDtypeStruct((rows, hidden), BF16)] * (3 * sides)
    outs = pl.pallas_call(
        functools.partial(layer_kernel, chunks, sides),
        in_specs=[anywhere] * (3 + len(flat_heads) + len(flat_weights)) + [vmem],
        out_specs=[anywhere, anywhere, vmem] + [anywhere] * (6 * arrays + len(own_rows)),
        out_shape=[whole, whole, jax.ShapeDtypeStruct((8, width), F32)]
        + finals + lands + lands + half_sums + own_rows,
        scratch_shapes=[
            pltpu.VMEM((2, 2, count * share, width), BF16),
            pltpu.VMEM((2, 2, 2, count - 1, share, width), BF16),
            pltpu.VMEM((2, 2, share, width), BF16),
            pltpu.VMEM((2, share, width), BF16),
            pltpu.VMEM((2, share, width), BF16),
            sem((2, 2)),
            sem((2, 2)),
            sem((2, 2, 2, count)),
            sem((2, 2, 2, count)),
            sem((chunks, 2, 2, count)),
            sem((chunks, 2, count)),
            sem((chunks, 2, count)),
            sem((chunks, 2, count)),
            sem((chunks, 2)),
            sem((arrays, 2, pieces)),
            sem((arrays, 2, pieces)),
            sem((arrays, 2, pieces)),
            sem((arrays, 2, pieces)),
            sem((arrays, pieces)),
            sem((arrays, pieces)),
            sem((arrays, 2, pieces)),
            sem((arrays, pieces)),
            sem((2 * arrays,)),
            sem((arrays, 2)),
            pltpu.VMEM((16, width), F32),
            pltpu.VMEM((sides, 8, columns[0]), F32),
            pltpu.VMEM((5, 8, width), F32),
            pltpu.VMEM((5, 8, width), F32),
            sem((5,)),
            sem((5,)),
        ],
        compiler_params=pltpu.CompilerParams(
            collective_id=0, has_side_effects=True, vmem_limit_bytes=63 * 2**20
        ),
        cost_estimate=pl.CostEstimate(
            flops=6 * rows * sum(array.size for array in flat_weights),
            bytes_accessed=800 * 2**20,
            transcendentals=0,
        ),
        name="layer",
    )(normed, tokens, cotangent, *flat_heads, *flat_weights, gain)
    out, grad, small = outs[:3]
    grads = [outs[3].astype(F32)]
    for blocks in outs[4 : 3 + arrays]:
        grads.append(blocks.transpose(1, 0, 2).reshape(blocks.shape[1], width).astype(F32))
    return out, grad, small[0], small[1], small[2, : columns[0]], grads


def body(
    tokens,
    lengths,
    norm_gain,
    norm_shift,
    qkv_weight,
    qkv_bias,
    out_weight,
    gate_weight,
    up_weight,
    down_weight,
    cotangent,
):
    tensor_size = lax.axis_size("tensor")
    dp_size = lax.axis_size("dp")
    count = tensor_size // 2
    where = lax.axis_index("tensor")
    dp_place = lax.axis_index("dp")
    side = where % 2
    across = [(i, i ^ 1) for i in range(tensor_size)]
    row_count, width = tokens.shape
    rows = row_count // 2
    chunk_count = 8

    def own_part(weight):
        part = weight.shape[0] // dp_size
        return lax.dynamic_slice_in_dim(weight, dp_place * part, part, 0)

    def partner(parts, before, after):
        parts, _ = lax.optimization_barrier((parts, before))
        parts = [lax.ppermute(part, "tensor", across) for part in parts]
        parts, _ = lax.optimization_barrier((parts, after))
        return [lax.all_gather(part, "dp", axis=0, tiled=True) for part in parts]

    head_weights = (qkv_weight, out_weight)
    mid_weights = (gate_weight.T, up_weight.T, down_weight)
    biases = (qkv_bias, lax.ppermute(qkv_bias, "tensor", across))

    length = lax.dynamic_slice_in_dim(lengths, side, 1, 0)
    norm = (norm_gain, norm_shift)
    *own_group, normed = project(side, tokens, cotangent, norm, head_weights, biases[0])
    tables = rotary_tables(rows)
    even = (out_weight.shape[0] // HEAD) % 2 == 0
    other_heads = partner([own_part(weight) for weight in head_weights], (), normed)
    mid_parts = [own_part(weight) for weight in mid_weights]
    if even:
        heads = [attention(length, *own_group, *tables)]
        other_mids = partner(mid_parts, normed, heads[0])
        other_group = project(side, normed, cotangent, (), other_heads, biases[1])
        heads.append(attention(length, *other_group, *tables))
    else:
        other_mids = partner(mid_parts, normed, ())
        other_group = project(side, normed, cotangent, (), other_heads, biases[1])
        pairs = zip(own_group, other_group)
        attended, qkv_back = attention(
            length, *[jnp.concatenate(pair, axis=1) for pair in pairs], *tables
        )
        cut, wide = out_weight.shape[0], qkv_weight.shape[1]
        heads = [
            (attended[:, s * cut : (s + 1) * cut], qkv_back[:, s * wide : (s + 1) * wide])
            for s in range(2)
        ]
    weights = ((*head_weights, *mid_weights), (*other_heads, *other_mids))
    layer_out, grad_tokens, gain_part, shift_part, grad_bias, grads = layer(
        normed, tokens, cotangent, heads, weights, norm_gain[None, :], count, chunk_count, dp_size
    )
    grad_qkv, grad_gate, grad_up, grad_down, grad_out = grads
    grad_gate, grad_up = grad_gate.T, grad_up.T
    return (
        layer_out,
        grad_tokens,
        gain_part,
        shift_part,
        grad_qkv,
        grad_bias,
        grad_out,
        grad_gate,
        grad_up,
        grad_down,
    )


def solution(mesh):
    placed = (
        P("dp", None),
        P("dp"),
        P(),
        P(),
        P(None, "tensor"),
        P("tensor"),
        P("tensor", None),
        P(None, "tensor"),
        P(None, "tensor"),
        P("tensor", None),
        P("dp", None),
    )
    return jax.shard_map(
        body,
        mesh=mesh,
        in_specs=placed,
        out_specs=(
            P("dp", None),
            P("dp", None),
            P(),
            P(),
            P(None, "tensor"),
            P("tensor"),
            P("tensor", None),
            P(None, "tensor"),
            P(None, "tensor"),
            P("tensor", None),
        ),
        check_vma=False,
    )
```

```python
import functools

import jax
import jax.numpy as jnp
import numpy as np
from jax import lax
from jax.experimental import pallas as pl
from jax.experimental.pallas import tpu as pltpu
from jax.sharding import PartitionSpec as P

HEAD = 64
ROT = 16
PAIR = 2 * HEAD
TRIPLE = 6 * HEAD

EPSILON = 1e-05
NEGATIVE = -1e30
F32 = jnp.float32
BF16 = jnp.bfloat16


def rows_product(former, latter):
    return lax.dot_general(
        former, latter, (((0,), (0,)), ((), ())), preferred_element_type=F32
    )


def cols_product(former, latter):
    return lax.dot_general(
        former, latter, (((1,), (1,)), ((), ())), preferred_element_type=F32
    )


def product(former, latter):
    return jnp.dot(former, latter, preferred_element_type=F32)


def rotary_tables(seq_len):
    frequency = np.float32(10000.0) ** (-np.arange(0, ROT, 2).astype(np.float32) / ROT)
    angles = np.arange(seq_len).astype(np.float32)[:, None] * frequency[None, :]
    cosine, sine = np.cos(angles), np.sin(angles)
    still = HEAD - ROT
    cos_head = np.concatenate([cosine, cosine, np.ones((seq_len, still))], axis=1)
    sin_head = np.concatenate([-sine, sine, np.zeros((seq_len, still))], axis=1)
    return [jnp.asarray(np.tile(table, (1, 2)), F32) for table in (cos_head, sin_head)]


def attention_kernel(
    len_ref, qkv_ref, grad_ref, cos_ref, sin_ref, att_ref, back_ref,
    score, expo, query, key_value, key_value_t, query_t, grad_query, grad_kv_t,
):
    seq_len = qkv_ref.shape[0]
    block = score.shape[1]
    steps = seq_len // block
    length = len_ref[0]
    lane = lax.broadcasted_iota(jnp.int32, (block, PAIR), 1)
    left = lane < HEAD
    near = lax.rem(lane, HEAD) < ROT // 2

    def turn(tile, cosine, sine):
        swapped = jnp.where(
            near, pltpu.roll(tile, PAIR - ROT // 2, 1), pltpu.roll(tile, ROT // 2, 1)
        )
        return tile * cosine + swapped * sine

    def tables(rows):
        cosine, sine = cos_ref[rows, :], sin_ref[rows, :]
        return (
            (cosine, sine),
            (jnp.where(left, 1.0, cosine), jnp.where(left, 0.0, sine)),
            (jnp.where(left, cosine, 1.0), jnp.where(left, sine, 0.0)),
        )

    def prepare(i, carry):
        rows = pl.ds(pl.multiple_of(i * block, block), block)
        tabs = tables(rows)
        first = turn(qkv_ref[rows, 0:PAIR], *tabs[0])
        second = turn(qkv_ref[rows, PAIR : 2 * PAIR], *tabs[1])
        third = turn(qkv_ref[rows, 2 * PAIR : 3 * PAIR], *tabs[2])
        scale = HEAD**-0.5
        first_q = first.astype(BF16).astype(F32) * scale
        second_q = second.astype(BF16).astype(F32) * scale
        query[0, rows, :] = jnp.where(left, 0.0, pltpu.roll(first_q, HEAD, 1)).astype(BF16)
        query[1, rows, :] = jnp.where(left, pltpu.roll(second_q, HEAD, 1), 0.0).astype(BF16)
        for h, tile in enumerate((jnp.where(left, second, first), third)):
            key_value[h, rows, :] = tile.astype(BF16)
            key_value_t[h, :, rows] = tile.T.astype(BF16)
        query_t[0, :, rows] = first_q.T[0:HEAD, :].astype(BF16)
        query_t[1, :, rows] = second_q.T[HEAD:PAIR, :].astype(BF16)
        zero = jnp.zeros((block, PAIR), F32)
        grad_query[rows, :] = zero
        att_ref[rows, :] = zero.astype(BF16)
        for h in range(2):
            grad_kv_t[h, :, rows] = jnp.zeros((PAIR, block), F32)
        return carry

    lax.fori_loop(0, steps, prepare, 0)

    def fold(tile, op):
        out = tile[:, 0:PAIR]
        for c in range(1, block // PAIR):
            out = op(out, tile[:, c * PAIR : (c + 1) * PAIR])
        return out

    def block_rows(i):
        rows = pl.ds(i * block, block)
        spans = [pl.ds(j * block, block) for j in range(i + 1)]
        q_block = [query[h, rows, :] for h in range(2)]
        below = lax.broadcasted_iota(jnp.int32, (block, block), 1) <= lax.broadcasted_iota(
            jnp.int32, (block, block), 0
        )
        maxima = []
        for h in range(2):
            top = None
            for j, cols in enumerate(spans):
                tile = product(q_block[h], key_value_t[h, :, cols])
                if j == i:
                    tile = jnp.where(below, tile, NEGATIVE)
                score[h, :, cols] = tile
                high = fold(tile, jnp.maximum)
                top = high if top is None else jnp.maximum(top, high)
            maxima.append(jnp.max(top, axis=1, keepdims=True))

        mixed, inverse = [], []
        for h in range(2):
            mixture = total = None
            for cols in spans:
                tile = jnp.exp(score[h, :, cols] - maxima[h])
                low = tile.astype(BF16)
                expo[h, :, cols] = low
                part = product(low, key_value[h, cols, :])
                amount = fold(tile, jnp.add)
                mixture = part if mixture is None else mixture + part
                total = amount if total is None else total + amount
            mixed.append(mixture)
            inverse.append(1.0 / jnp.sum(total, axis=1, keepdims=True))

        place = i * block + lax.broadcasted_iota(jnp.int32, (block, 1), 0)
        valid = (place < length).astype(F32)
        mixture = jnp.where(left, mixed[0] * inverse[0], mixed[1] * inverse[1]) * valid
        att_ref[rows, :] = mixture.astype(BF16)
        upstream = grad_ref[rows, :].astype(F32) * valid
        inner = upstream * mixture
        scale = HEAD**-0.5
        turned = []
        for h in range(2):
            own = left if h == 0 else jnp.logical_not(left)
            inner_sum = jnp.sum(jnp.where(own, inner, 0.0), axis=1, keepdims=True) * inverse[h]
            mine = jnp.where(own, upstream * inverse[h], 0.0)
            scaled = mine.astype(BF16)
            half = slice(0, HEAD) if h == 0 else slice(HEAD, PAIR)
            scaled_t = mine.T[half, :].astype(BF16)
            queries_t = query_t[h, :, rows]
            grad = None
            for cols in spans:
                low = expo[h, :, cols]
                grad_weight = product(scaled, key_value_t[h, :, cols])
                grad_score = (low.astype(F32) * (grad_weight - inner_sum)).astype(BF16)
                part = product(grad_score, key_value[h, cols, :])
                grad = part if grad is None else grad + part
                key_at, value_at = (HEAD, 0) if h == 0 else (0, HEAD)
                grad_kv_t[h, key_at : key_at + HEAD, cols] += product(queries_t, grad_score)
                grad_kv_t[h, value_at : value_at + HEAD, cols] += product(scaled_t, low)
            turned.append(pltpu.roll(grad, HEAD, 1))
        grad_query[rows, :] = jnp.where(left, turned[0], turned[1]) * scale

    for i in range(steps):
        pl.when(i * block < length)(functools.partial(block_rows, i))

    def finish(i, carry):
        rows = pl.ds(pl.multiple_of(i * block, block), block)
        tabs = tables(rows)
        gq = grad_query[rows, :]
        low_kv = grad_kv_t[0, :, rows].T
        high_kv = grad_kv_t[1, :, rows].T
        tiles = (jnp.where(left, gq, low_kv), jnp.where(left, low_kv, gq), high_kv)
        for c in range(3):
            back_ref[rows, c * PAIR : (c + 1) * PAIR] = turn(
                tiles[c], tabs[c][0], -tabs[c][1]
            ).astype(BF16)
        return carry

    lax.fori_loop(0, steps, finish, 0)


def attention(length, qkv, grad_mixture, cosine, sine):
    seq_len, width = qkv.shape
    pairs = width // TRIPLE
    block = min(512, seq_len)
    flops = 6 * 2 * (2 * pairs) * seq_len * seq_len * PAIR
    return pl.pallas_call(
        attention_kernel,
        grid=(pairs,),
        in_specs=[
            pl.BlockSpec(memory_space=pltpu.SMEM),
            pl.BlockSpec((seq_len, TRIPLE), lambda g: (0, g)),
            pl.BlockSpec((seq_len, PAIR), lambda g: (0, g)),
            pl.BlockSpec((seq_len, PAIR), lambda g: (0, 0)),
            pl.BlockSpec((seq_len, PAIR), lambda g: (0, 0)),
        ],
        out_specs=[
            pl.BlockSpec((seq_len, PAIR), lambda g: (0, g)),
            pl.BlockSpec((seq_len, TRIPLE), lambda g: (0, g)),
        ],
        out_shape=[
            jax.ShapeDtypeStruct((seq_len, pairs * PAIR), BF16),
            jax.ShapeDtypeStruct((seq_len, width), BF16),
        ],
        scratch_shapes=[
            pltpu.VMEM((2, block, seq_len), F32),
            pltpu.VMEM((2, block, seq_len), BF16),
            pltpu.VMEM((2, seq_len, PAIR), BF16),
            pltpu.VMEM((2, seq_len, PAIR), BF16),
            pltpu.VMEM((2, PAIR, seq_len), BF16),
            pltpu.VMEM((2, HEAD, seq_len), BF16),
            pltpu.VMEM((seq_len, PAIR), F32),
            pltpu.VMEM((2, PAIR, seq_len), F32),
        ],
        compiler_params=pltpu.CompilerParams(vmem_limit_bytes=48 * 2**20),
        cost_estimate=pl.CostEstimate(
            flops=flops,
            bytes_accessed=seq_len * width * 8,
            transcendentals=2 * pairs * seq_len * seq_len // 2,
        ),
        name="attention",
    )(length, qkv, grad_mixture, cosine, sine)


def start_kernel(
    side_ref, tok_ref, cot_ref, gain_ref, shift_ref, qkv_w, bias_ref, out_w,
    qkv_ref, grad_ref, normed_ref,
):
    wide = tok_ref[...].astype(F32)
    centred = wide - jnp.mean(wide, axis=1, keepdims=True)
    variance = jnp.mean(centred * centred, axis=1, keepdims=True)
    unit = centred * lax.rsqrt(variance + EPSILON)
    normed = (unit * gain_ref[...] + shift_ref[...]).astype(BF16)
    normed_ref[...] = normed
    qkv_ref[...] = product(normed, qkv_w[...]) + bias_ref[...]
    grad_ref[...] = cols_product(cot_ref[...], out_w[...]).astype(BF16)


def project_kernel(side_ref, normed_ref, cot_ref, qkv_w, bias_ref, out_w, qkv_ref, grad_ref):
    qkv_ref[...] = product(normed_ref[...], qkv_w[...]) + bias_ref[...]
    grad_ref[...] = cols_product(cot_ref[...], out_w[...]).astype(BF16)


def project(side, rows_in, cotangent, norm, weights, bias):
    rows, width = cotangent.shape[0] // 2, cotangent.shape[1]
    tile = min(256, rows)
    tiles = rows // tile
    qkv_weight, out_weight = weights
    heads, wide = out_weight.shape[0], qkv_weight.shape[1]

    def sided(i, side_ref):
        return (side_ref[0] * tiles + i, 0)

    def fixed(i, side_ref):
        return (0, 0)

    def rowed(i, side_ref):
        return (i, 0)

    flat = [part[None, :] for part in norm]
    flat += [qkv_weight, bias.astype(F32)[None, :], out_weight]
    outs = [((rows, wide), F32), ((rows, heads), BF16)]
    out_specs = [pl.BlockSpec((tile, shape[1]), rowed) for shape, _ in outs]
    if norm:
        outs.append(((rows, width), BF16))
        out_specs.append(pl.BlockSpec((tile, width), rowed))
    return pl.pallas_call(
        start_kernel if norm else project_kernel,
        grid_spec=pltpu.PrefetchScalarGridSpec(
            num_scalar_prefetch=1,
            grid=(tiles,),
            in_specs=[
                pl.BlockSpec((tile, width), sided if norm else rowed),
                pl.BlockSpec((tile, width), sided),
            ]
            + [pl.BlockSpec(array.shape, fixed) for array in flat],
            out_specs=out_specs,
        ),
        out_shape=[jax.ShapeDtypeStruct(*out) for out in outs],
        compiler_params=pltpu.CompilerParams(vmem_limit_bytes=40 * 2**20),
        cost_estimate=pl.CostEstimate(
            flops=2 * rows * width * (wide + heads),
            bytes_accessed=rows * (6 * width + 4 * wide),
            transcendentals=rows,
        ),
        name="project",
    )(side[None], rows_in, cotangent, *flat)


def layer_kernel(chunks, sides, *refs):
    normed_ref, tok_ref, cot_ref = refs[:3]
    head_refs, refs = refs[3 : 3 + 2 * sides], refs[3 + 2 * sides :]
    weight_refs, gain_ref = refs[: 5 * sides], refs[5 * sides]
    refs = refs[5 * sides + 1 :]
    out_ref, grad_ref, small_ref = refs[:3]
    refs = refs[3:]
    arrays = 5
    grad_outs, core_land = refs[:arrays], refs[arrays : 3 * arrays]
    far_land, side_land = refs[3 * arrays : 5 * arrays], refs[5 * arrays : 6 * arrays]
    refs = refs[6 * arrays :]
    f_ref, g_ref = refs[:2]
    mid_refs, refs = refs[2 : 2 + 3 * sides], refs[2 + 3 * sides :]
    (
        terms, landed, ready, tok_buf, cot_buf,
        term_sem, share_sem, sum_send, sum_recv,
        line_send, line_recv, side_send, side_recv, keep_sem,
        core_send, core_recv, far_send, far_recv, over_send, over_recv,
        back_send, back_recv, load_sem, save_sem,
        part_ref, bias_part, stages, came, small_send, small_recv,
    ) = refs
    share, width = landed.shape[4:]
    count = landed.shape[3] + 1
    chunk_rows = count * share
    rows = chunks * chunk_rows
    where = lax.axis_index("tensor")
    group = lax.axis_index("dp")
    place, side = where // 2, where % 2
    half, core = group // 2, group % 2
    whole_refs = (out_ref, grad_ref)
    factors = []
    for s in range(sides):
        hidden_ref, gate_ref, up_ref = mid_refs[3 * s : 3 * s + 3]
        factors.append(
            (head_refs[2 * s + 1], gate_ref, up_ref, hidden_ref, head_refs[2 * s])
        )
    factors = [factors[x % sides][x // sides] for x in range(arrays * sides)]

    above, below = (group, where + 2), (group, where - 2)
    across = (group, where + 1 - 2 * side)
    other_core = (half * 2 + 1 - core, where)
    other_half = ((1 - half) * 2 + core, where)
    has_above, has_below = place < count - 1, place > 0

    barrier = pltpu.get_barrier_semaphore()

    def greet(target):
        pl.semaphore_signal(barrier, inc=1, device_id=target, device_id_type=pl.DeviceIdType.MESH)

    pl.when(has_above)(lambda: greet(above))
    pl.when(has_below)(lambda: greet(below))
    for target in (across, other_core, other_half):
        greet(target)

    def span(begin, size):
        return pl.ds(pl.multiple_of(begin, size), size)

    def load(c, k):
        source = (f_ref, g_ref)[k].at[span(c * chunk_rows, chunk_rows), :]
        return pltpu.make_async_copy(
            source, terms.at[lax.rem(c, 2), k], term_sem.at[lax.rem(c, 2), k]
        )

    def load_share(c, k):
        begin = span(side * rows + c * chunk_rows + place * share, share)
        source, target = ((tok_ref, tok_buf), (cot_ref, cot_buf))[k]
        return pltpu.make_async_copy(
            source.at[begin, :], target.at[lax.rem(c, 2)], share_sem.at[lax.rem(c, 2), k]
        )

    def remote(source, target, send, recv, device_id):
        return pltpu.make_async_remote_copy(
            src_ref=source, dst_ref=target, send_sem=send, recv_sem=recv,
            device_id=device_id, device_id_type=pl.DeviceIdType.MESH,
        )


    def sum_copy(c, k, way, b, first):
        slot = lax.rem(c, 2)
        target = landed.at[slot, k, way, b - 1 + way]
        source = terms.at[slot, k, span(b * share, share), :] if first else target
        return remote(
            source, target, sum_send.at[slot, k, way, b], sum_recv.at[slot, k, way, b],
            (above, below)[way],
        )

    def place_of(c, b, on_side):
        return span(on_side * rows + c * chunk_rows + b * share, share)

    def line_copy(c, k, b, way, first):
        target = whole_refs[k].at[place_of(c, b, side), :]
        source = ready.at[lax.rem(c, 2), k] if first else target
        return remote(
            source, target, line_send.at[c, k, way, b], line_recv.at[c, k, b],
            (above, below)[way],
        )

    def side_copy(c, k, b, first):
        target = whole_refs[k].at[place_of(c, b, side), :]
        source = ready.at[lax.rem(c, 2), k] if first else target
        return remote(
            source, target, side_send.at[c, k, b], side_recv.at[c, k, b], across
        )

    def keep_copy(c, k):
        return pltpu.make_async_copy(
            ready.at[lax.rem(c, 2), k], whole_refs[k].at[place_of(c, place, side), :],
            keep_sem.at[c, k],
        )

    def each_first(c, k, act):
        @pl.when(jnp.logical_not(has_below))
        def _():
            for b in range(count - 1, 0, -1):
                act(sum_copy(c, k, 0, b, True))

        @pl.when(jnp.logical_not(has_above))
        def _():
            for b in range(count - 1):
                act(sum_copy(c, k, 1, b, True))

    def send_ends(c, k):
        load(c, k).wait()
        each_first(c, k, lambda copy: copy.start())

    def sums_left(c, k):
        for b in range(count):

            @pl.when(has_below & (place < b))
            def _(b=b):
                sum_copy(c, k, 0, b, False).wait_send()

            @pl.when(has_above & (place > b))
            def _(b=b):
                sum_copy(c, k, 1, b, False).wait_send()

    step = min(16, share)

    def add_on(c, k, way, b):
        slot = lax.rem(c, 2)

        def body(i, carry):
            at = span(i * step, step)
            mine = terms[slot, k, span(b * share + i * step, step), :].astype(F32)
            landed[slot, k, way, b - 1 + way, at, :] = (
                mine + landed[slot, k, way, b - 1 + way, at, :].astype(F32)
            ).astype(BF16)
            return carry

        lax.fori_loop(0, share // step, body, 0)

    def sums(c, k, wave):
        ahead = count - 2 - wave
        for way, b, here in (
            (0, place + ahead, has_below & (place + ahead < count)),
            (1, place - ahead, has_above & (place >= ahead)),
        ):

            @pl.when(here)
            def _(way=way, b=b):
                sum_copy(c, k, way, b, False).wait_recv()

                @pl.when(ahead > 0)
                def _():
                    add_on(c, k, way, b)
                    sum_copy(c, k, way, b, False).start()

    def own_left(c, k):
        pl.when(has_above)(lambda: line_copy(c, k, place, 0, True).wait_send())
        pl.when(has_below)(lambda: line_copy(c, k, place, 1, True).wait_send())
        side_copy(c, k, place, True).wait_send()
        keep_copy(c, k).wait()

    def finish(c, k):
        load_share(c, k).wait()
        pl.when(c > 1)(lambda: own_left(c - 2, k))
        slot = lax.rem(c, 2)

        def body(i, carry):
            at = span(i * step, step)
            up = landed[slot, k, 0, jnp.maximum(place - 1, 0), at, :].astype(F32)
            down = landed[slot, k, 1, jnp.minimum(place, count - 2), at, :].astype(F32)
            total = (
                terms[slot, k, span(place * share + i * step, step), :].astype(F32)
                + jnp.where(has_below, up, 0.0)
                + jnp.where(has_above, down, 0.0)
            )
            wide = tok_buf[slot, at, :].astype(F32)
            if k == 0:
                ready[slot, k, at, :] = (wide + total).astype(BF16)
                return carry
            scale = 1.0 / width
            centred = wide - jnp.sum(wide, axis=1, keepdims=True) * scale
            variance = jnp.sum(centred * centred, axis=1, keepdims=True) * scale
            inverse = lax.rsqrt(variance + EPSILON)
            unit = centred * inverse
            scaled = total * gain_ref[0:1, :]
            mean_scaled = jnp.sum(scaled, axis=1, keepdims=True) * scale
            mean_cross = jnp.sum(scaled * unit, axis=1, keepdims=True) * scale
            ready[slot, k, at, :] = (
                cot_buf[slot, at, :].astype(F32)
                + inverse * (scaled - mean_scaled - unit * mean_cross)
            ).astype(BF16)
            gain_term = total * unit
            for r in range(0, step, 8):
                part_ref[0:8, :] += gain_term[r : r + 8, :]
                part_ref[8:16, :] += total[r : r + 8, :]
            return carry

        lax.fori_loop(0, share // step, body, 0)
        pl.when(has_above)(lambda: line_copy(c, k, place, 0, True).start())
        pl.when(has_below)(lambda: line_copy(c, k, place, 1, True).start())
        side_copy(c, k, place, True).start()
        keep_copy(c, k).start()

    def pass_on(c, k, distance):
        for way, b, here in (
            (0, place - distance, place >= distance),
            (1, place + distance, place + distance < count),
        ):

            @pl.when(here)
            def _(way=way, b=b):
                line_copy(c, k, b, way, False).wait_recv()
                pl.when((has_above, has_below)[way])(
                    lambda: line_copy(c, k, b, way, False).start()
                )
                side_copy(c, k, b, False).start()

    def small_copy(n, target):
        return remote(stages.at[n], came.at[n], small_send.at[n], small_recv.at[n], target)

    def small_sums():
        wide = bias_part.shape[2]
        stages[...] = jnp.zeros_like(stages)
        stages[0, 0:1, :] = jnp.sum(part_ref[0:8, :], axis=0, keepdims=True)
        stages[0, 1:2, :] = jnp.sum(part_ref[8:16, :], axis=0, keepdims=True)
        for s in range(sides):
            stages[0, 2 + s : 3 + s, 0:wide] = jnp.sum(bias_part[s], axis=0, keepdims=True)
        for n, target in enumerate((across, other_core, other_half)):
            copy = small_copy(n, target)
            copy.start()
            copy.wait_recv()
            if n == 0:
                stages[1, 0:2, :] = stages[0, 0:2, :] + came[0, 0:2, :]
                stages[1, 2:3, :] = stages[0, 2:3, :] + came[0, 3:4, :]
            else:
                stages[n + 1] = stages[n] + came[n]

        @pl.when(has_below)
        def _():
            small_copy(3, above).wait_recv()
            stages[3] = stages[3] + came[3]

        pl.when(has_above)(lambda: small_copy(3, above).start())
        stages[4] = stages[3]

        @pl.when(has_above)
        def _():
            small_copy(4, below).wait_recv()
            stages[4] = came[4]

        pl.when(has_below)(lambda: small_copy(4, below).start())
        small_ref[...] = stages[4]
        small_ref[2:3, :] = stages[2, 2:3, :] + came[2, 2:3, :]
        for n, target in enumerate((across, other_core, other_half)):
            small_copy(n, target).wait_send()
        pl.when(has_above)(lambda: small_copy(3, above).wait_send())
        pl.when(has_below)(lambda: small_copy(4, below).wait_send())

    waves = count - 1
    every = max(1, waves // 3)
    works = waves // every

    if count == 4:
        order = ((2, 2, 0), (1, 1, 1), (2, 3, 1))
    else:
        order = tuple((2, distance, distance - 1) for distance in range(1, count))

    def pass_steps(h, live, wave):
        for behind, distance, step in order:
            item = jnp.maximum(h - behind, 0)
            for k in range(2):
                pl.when(
                    live & (wave == step) & (h >= behind) & (lax.rem(item, 2) == k)
                )(lambda: pass_on(item // 2, k, distance))

    def pass_rest():
        for item in range(2 * chunks - 2, 2 * chunks):
            for distance, behind in sorted((step[1], step[0]) for step in order):
                if item + behind >= 2 * chunks:
                    pass_on(item // 2, item % 2, distance)

    def half_steps(h, live, work):
        c = h // 2

        def one(wave, carry):
            pl.when(lax.rem(wave, every) == 0)(lambda: work(wave // every))
            for k in range(2):

                @pl.when(live & (lax.rem(h, 2) == k))
                def _(k=k):
                    more = c + 1 < chunks

                    @pl.when(wave == 0)
                    def _():
                        @pl.when(c > 0)
                        def _():
                            sums_left(c - 1, k)
                            each_first(c - 1, k, lambda copy: copy.wait_send())

                        pl.when(more)(lambda: load_share(c + 1, k).start())
                        pl.when(more & (c > 0))(lambda: load(c + 1, k).start())

                    sums(c, k, wave)

            pass_steps(h, live, wave)
            for k in range(2):

                @pl.when(live & (lax.rem(h, 2) == k) & (wave == waves - 1))
                def _(k=k):
                    more = c + 1 < chunks
                    pl.when(c == 0)(lambda: load(c + 1, k).start())
                    finish(c, k)
                    pl.when(more)(lambda: send_ends(c + 1, k))

            return carry

        lax.fori_loop(0, waves, one, 0)

    tile_halves = -(-sides * (chunks - 1) // works)

    def tiles_scope(*scratch):
        weights = scratch[: 5 * sides]
        scratch = scratch[5 * sides :]
        normed_buf, tile_cot = scratch[:2]
        head_bufs = scratch[2 : 2 + 2 * sides]
        scratch = scratch[2 + 2 * sides :]
        mids, f_buf, g_buf = scratch[: 3 * sides], scratch[3 * sides], scratch[3 * sides + 1]
        f_total, g_total, weight_sem, in_sem, out_sem = scratch[3 * sides + 2 :]

        def weight_copies(s):
            return [
                pltpu.make_async_copy(weight_refs[x], weights[x], weight_sem.at[x])
                for x in range(5 * s, 5 * s + 5)
            ]

        def tile_in(i):
            slot = lax.rem(i, 2)
            at = span(i * chunk_rows, chunk_rows)
            at_side = span(side * rows + i * chunk_rows, chunk_rows)
            pairs = [(normed_ref.at[at, :], normed_buf), (cot_ref.at[at_side, :], tile_cot)]
            pairs += [(ref.at[at, :], buf) for ref, buf in zip(head_refs, head_bufs)]
            return [
                pltpu.make_async_copy(ref, buf.at[slot], in_sem.at[slot, x])
                for x, (ref, buf) in enumerate(pairs)
            ]

        def tile_out(i):
            at = span(i * chunk_rows, chunk_rows)
            pairs = list(zip(mids, mid_refs)) + [(f_buf, f_ref), (g_buf, g_ref)]
            return [
                pltpu.make_async_copy(buf, ref.at[at, :], out_sem.at[x])
                for x, (buf, ref) in enumerate(pairs)
            ]

        def wait_out(i):
            for copy in tile_out(i):
                copy.wait()

        def tile(i, s):
            slot = lax.rem(i, 2)
            if s == 0:
                for copy in tile_in(i):
                    copy.wait()

                @pl.when(i + 1 < chunks)
                def _():
                    for copy in tile_in(i + 1):
                        copy.start()

            @pl.when(i == 0)
            def _():
                for copy in weight_copies(s):
                    copy.wait()

            qkv_w, out_w, gate_w, up_w, down_w = weights[5 * s : 5 * s + 5]
            hidden_buf, gate_buf, up_buf = mids[3 * s : 3 * s + 3]
            normed, cot = normed_buf[slot], tile_cot[slot]
            gate = cols_product(normed, gate_w[...])
            up = cols_product(normed, up_w[...])
            sig = 1.0 / (1.0 + jnp.exp(-gate))
            silu = gate * sig
            hidden = (silu * up).astype(BF16)
            grad_hidden = cols_product(cot, down_w[...])
            if s == 0:
                pl.when(i > 1)(lambda: wait_out(i - 1))
            hidden_buf[...] = hidden
            gate_back = (grad_hidden * up * sig * (1.0 + gate * (1.0 - sig))).astype(BF16)
            up_back = (grad_hidden * silu).astype(BF16)
            gate_buf[...] = gate_back
            up_buf[...] = up_back
            forward = product(hidden, down_w[...])
            forward += product(head_bufs[2 * s][slot], out_w[...])
            backward = product(gate_back, gate_w[...])
            backward += product(up_back, up_w[...])
            qkv_back = head_bufs[2 * s + 1][slot]
            backward += cols_product(qkv_back, qkv_w[...])
            bias_part[s] += (
                qkv_back.astype(F32).reshape(chunk_rows // 8, 8, qkv_back.shape[1]).sum(axis=0)
            )
            if s > 0:
                forward += f_total[...]
                backward += g_total[...]
            if s < sides - 1:
                f_total[...] = forward
                g_total[...] = backward
                return
            f_buf[...] = forward.astype(BF16)
            g_buf[...] = backward.astype(BF16)
            for copy in tile_out(i):
                copy.start()

        def work(turn, n):
            first = turn == 0
            unit = jnp.maximum(works * turn - works, 0) + n
            i = jnp.where(first, 0, 1 + unit // sides)
            part = jnp.where(first, n - works + sides, lax.rem(unit, sides))
            for s in range(sides):
                pl.when((part == s) & (i < chunks))(lambda: tile(i, s))

        for s in range(sides):
            for copy in weight_copies(s):
                copy.start()
        for copy in tile_in(0):
            copy.start()
        for k in range(2):
            load_share(0, k).start()
        part_ref[...] = jnp.zeros_like(part_ref)
        bias_part[...] = jnp.zeros_like(bias_part)
        pl.semaphore_wait(
            barrier, 3 + has_above.astype(jnp.int32) + has_below.astype(jnp.int32)
        )

        def chunk(turn, carry):
            half_steps(
                jnp.maximum(turn, 1) - 1, turn > 0, lambda n: work(turn, n)
            )

            @pl.when(turn == 0)
            def _():
                wait_out(0)
                for k in range(2):
                    load(0, k).start()
                for k in range(2):
                    send_ends(0, k)

            return carry

        lax.fori_loop(0, tile_halves + 1, chunk, 0)
        wait_out(chunks - 1)

    tall = width
    hidden_cols = mid_refs[0].shape[1]
    pl.run_scoped(
        tiles_scope,
        *[pltpu.VMEM(ref.shape, BF16) for ref in weight_refs],
        pltpu.VMEM((2, chunk_rows, width), BF16),
        pltpu.VMEM((2, chunk_rows, width), BF16),
        *[pltpu.VMEM((2, chunk_rows, ref.shape[1]), BF16) for ref in head_refs],
        *[pltpu.VMEM((chunk_rows, hidden_cols), BF16) for _ in mid_refs],
        pltpu.VMEM((chunk_rows, width), BF16),
        pltpu.VMEM((chunk_rows, width), BF16),
        pltpu.VMEM((chunk_rows, width), F32),
        pltpu.VMEM((chunk_rows, width), F32),
        pltpu.SemaphoreType.DMA((5 * sides,)),
        pltpu.SemaphoreType.DMA((2, 2 + 2 * sides)),
        pltpu.SemaphoreType.DMA((3 * sides + 2,)),
    )


    pieces = core_send.shape[2]
    each = 2
    size = tall // pieces

    def grads_scope(*scratch):
        factor_bufs, scratch = scratch[: arrays * sides], scratch[arrays * sides :]
        held, scratch = scratch[: arrays * sides], scratch[arrays * sides :]
        extra, scratch = scratch[: arrays * sides], scratch[arrays * sides :]
        turned, scratch = scratch[: arrays - 1], scratch[arrays - 1 :]
        left_bufs, factor_sem, left_sem = scratch[:2], scratch[2], scratch[3]

        def factor_copy(x):
            return pltpu.make_async_copy(factors[x], factor_bufs[x], factor_sem.at[x])

        def piece(ref, j):
            return ref.at[span(j * size, size), :]

        def piece_of(u):
            owner_core = jnp.where((u // each) % 2 == 0, 1 - core, core)
            owner_half = jnp.where(u < 2 * each, 1 - half, half)
            return (owner_half * 2 + owner_core) * each + lax.rem(u, each)

        def slot_of(u):
            return jnp.where(u < 2 * each, lax.rem(u, each), each + lax.rem(u, each))

        def left_copy(u, which):
            at = span(piece_of(u) * size, size)
            source = (
                normed_ref.at[:, at] if which == 0 else cot_ref.at[span(side * rows, rows), at]
            )
            return pltpu.make_async_copy(
                source, left_bufs[which].at[lax.rem(u, 2)], left_sem.at[which, lax.rem(u, 2)]
            )

        def to_core(a, s, j, slot):
            x = 2 * a + s
            return remote(
                held[x].at[slot], piece(core_land[x], j),
                core_send.at[a, s, j], core_recv.at[a, s, j], other_core,
            )

        def to_far(a, s, i, j):
            x = 2 * a + s
            return remote(
                held[x].at[i], piece(far_land[x], j),
                far_send.at[a, s, j], far_recv.at[a, s, j], other_half,
            )

        def to_over(a, i, j):
            return remote(
                held[2 * a + 1].at[each + i], piece(side_land[a], j),
                over_send.at[a, j], over_recv.at[a, j], across,
            )

        def final_piece(a, j):
            return grad_outs[a].at[j] if a else grad_outs[a].at[span(j * size, size), :]

        def final_source(a, i):
            return turned[a - 1].at[i] if a else held[0].at[each + i]

        def back_copy(a, i, j, way, first):
            target = final_piece(a, j)
            source = final_source(a, i) if first else target
            return remote(
                source, target, back_send.at[a, way, j], back_recv.at[a, j],
                (other_core, other_half)[way],
            )

        def save_copy(a, i, j):
            return pltpu.make_async_copy(
                final_source(a, i), final_piece(a, j), save_sem.at[a, i]
            )

        def their_piece(i):
            return ((1 - half) * 2 + core) * each + i

        def my_piece(i):
            return (half * 2 + core) * each + i

        def add_into(target, slot, source):
            rows_at_once = min(64, size)

            def body(i, carry):
                at = span(i * rows_at_once, rows_at_once)
                target[slot, at, :] = (
                    target[slot, at, :].astype(F32) + source[at, :].astype(F32)
                ).astype(BF16)
                return carry

            lax.fori_loop(0, size // rows_at_once, body, 0)

        def fetch(lands, j, ids, act):
            for n, x in enumerate(ids):
                act(pltpu.make_async_copy(piece(lands[n], j), extra[x], load_sem.at[x]))

        def begin(lands, j, ids):
            fetch(lands, j, ids, lambda copy: copy.start())

        def end(lands, j, ids):
            fetch(lands, j, ids, lambda copy: copy.wait())

        everything = range(2 * arrays)

        def make(u, which):
            @pl.when(u == 0)
            def _():
                for x in everything:
                    if (x // 2 < 3) == (which == 0):
                        factor_copy(x).wait()

            left_copy(u, which).wait()
            pl.when(u + 1 < pieces)(lambda: left_copy(u + 1, which).start())
            slot = slot_of(u)
            left = left_bufs[which][lax.rem(u, 2)].T

            @pl.when((u // each) % 2 == 1)
            def _():
                for x in everything:
                    if (x // 2 < 3) == (which == 0):
                        to_core(x // 2, x % 2, piece_of(u - each), slot).wait_send()

            for x in everything:
                if (x // 2 < 3) == (which == 0):
                    held[x][slot] = product(left, factor_bufs[x][...]).astype(BF16)

            @pl.when((u // each) % 2 == 0)
            def _():
                for x in everything:
                    if (x // 2 < 3) == (which == 0):
                        to_core(x // 2, x % 2, piece_of(u), slot).start()


        def core_begin(j):
            for x in everything:
                to_core(x // 2, x % 2, j, 0).wait_recv()
            begin(core_land, j, everything)

        def core_end(slot, j):
            end(core_land, j, everything)
            for x in everything:
                add_into(held[x], slot, extra[x])

        def far_begin(i):
            core_begin(their_piece(i))

        def far_end(i):
            j = their_piece(i)
            core_end(i, j)
            for x in everything:
                to_far(x // 2, x % 2, i, j).start()

        def over_begin(i):
            core_begin(my_piece(i))

        def over_middle(i):
            j = my_piece(i)
            core_end(each + i, j)
            for x in everything:
                to_far(x // 2, x % 2, i, j).wait_recv()
            begin(far_land, j, everything)

        def over_end(i):
            j = my_piece(i)
            end(far_land, j, everything)
            for a in range(arrays):
                add_into(held[2 * a + 1], each + i, extra[2 * a + 1])
                to_over(a, i, j).start()
            for a in range(arrays):
                add_into(held[2 * a], each + i, extra[2 * a])

        firsts = range(0, 2 * arrays, 2)

        def back_begin(i):
            j = my_piece(i)
            for a in range(arrays):
                to_over(a, i, j).wait_recv()
            begin(side_land, j, firsts)

        def back_end(i):
            j = my_piece(i)
            end(side_land, j, firsts)
            for a in range(arrays):
                if a:
                    total = held[2 * a][each + i].astype(F32) + extra[2 * a][...].astype(F32)
                    turned[a - 1][i] = total.T.astype(BF16)
                else:
                    add_into(held[0], each + i, extra[0])
                back_copy(a, i, j, 1, True).start()
                back_copy(a, i, j, 0, True).start()
                save_copy(a, i, j).start()

        def grads_pass(i):
            j = their_piece(i)
            for a in range(arrays):
                back_copy(a, i, j, 1, False).wait_recv()
                back_copy(a, i, j, 0, False).start()

        def grads_drain():
            for i in range(each):
                mine, theirs = my_piece(i), their_piece(i)
                for a in range(arrays):
                    for s in range(2):
                        to_far(a, s, i, theirs).wait_send()
                    to_over(a, i, mine).wait_send()
                    back_copy(a, i, mine, 1, True).wait_send()
                    back_copy(a, i, mine, 0, True).wait_send()
                    back_copy(a, i, theirs, 0, False).wait_send()
                    save_copy(a, i, mine).wait()
            for u in (*range(each), *range(2 * each, 3 * each)):
                for a in range(arrays):
                    back_copy(a, 0, piece_of(u), 0, False).wait_recv()

        events = {
            (7, 1): (far_begin, 0),
            (7, 2): (far_end, 0),
            (8, 1): (far_begin, 1),
            (8, 2): (far_end, 1),
            (11, 1): (over_begin, 0),
            (11, 2): (over_middle, 0),
            (12, 0): (over_end, 0),
            (12, 1): (over_begin, 1),
            (12, 2): (over_middle, 1),
            (13, 0): (over_end, 1),
            (14, 1): (back_begin, 0),
            (14, 2): (back_end, 0),
        }

        def work(h, n):
            u = h - tile_halves
            for which in range(2):
                pl.when((u < pieces) & (n == which))(lambda: make(u, which))
            for (at, step), (act, i) in events.items():
                pl.when((h == at) & (n == step))(lambda: act(i))

        for x in everything:
            factor_copy(x).start()
        for which in range(2):
            left_copy(0, which).start()

        def chunk(c, carry):
            half_steps(c, c >= 0, lambda n: work(c, n))
            return carry

        lax.fori_loop(tile_halves, 2 * chunks, chunk, 0)
        back_begin(1)
        pass_rest()
        back_end(1)
        small_sums()
        for i in range(each):
            grads_pass(i)
        grads_drain()

    factor_shapes = [ref.shape for ref in factors]
    pl.run_scoped(
        grads_scope,
        *[pltpu.VMEM(shape, BF16) for shape in factor_shapes],
        *[pltpu.VMEM((2 * each, size, shape[1]), BF16) for shape in factor_shapes],
        *[pltpu.VMEM((size, shape[1]), BF16) for shape in factor_shapes],
        *[pltpu.VMEM((each, shape[1], size), BF16) for shape in factor_shapes[2::2]],
        pltpu.VMEM((2, rows, size), BF16),
        pltpu.VMEM((2, rows, size), BF16),
        pltpu.SemaphoreType.DMA((2 * arrays,)),
        pltpu.SemaphoreType.DMA((2, 2)),
    )

    for k in range(2):
        sums_left(chunks - 1, k)
        each_first(chunks - 1, k, lambda copy: copy.wait_send())
        own_left(chunks - 2, k)
        own_left(chunks - 1, k)

    def drain(c, carry):
        for k in range(2):
            for b in range(count):
                pl.when((place > b) & has_above)(
                    lambda: line_copy(c, k, b, 0, False).wait_send()
                )
                pl.when((place < b) & has_below)(
                    lambda: line_copy(c, k, b, 1, False).wait_send()
                )
                pl.when(place != b)(lambda: side_copy(c, k, b, False).wait_send())
                side_copy(c, k, b, False).wait_recv()
        return carry

    lax.fori_loop(0, chunks, drain, 0)


def layer(normed, tokens, cotangent, heads, weights, gain, count, chunks, dp_size):
    row_count, width = tokens.shape
    rows = row_count // 2
    share = rows // chunks // count
    sides, arrays = len(weights), 5
    pieces = 2 * dp_size
    sem = pltpu.SemaphoreType.DMA
    flat_heads = [array for group in heads for array in group]
    flat_weights = [array for group in weights for array in group]
    hidden = weights[0][2].shape[0]
    columns = [heads[0][1].shape[1], hidden, hidden, hidden, heads[0][0].shape[1]]
    whole = jax.ShapeDtypeStruct(tokens.shape, BF16)
    half_sums = [jax.ShapeDtypeStruct((width, n), BF16) for n in columns]
    finals = half_sums[:1] + [
        jax.ShapeDtypeStruct((pieces, n, width // pieces), BF16) for n in columns[1:]
    ]
    lands = [shape for shape in half_sums for _ in range(sides)]
    anywhere = pl.BlockSpec(memory_space=pl.ANY)
    vmem = pl.BlockSpec(memory_space=pltpu.VMEM)
    own_rows = [jax.ShapeDtypeStruct((rows, width), BF16)] * 2
    own_rows += [jax.ShapeDtypeStruct((rows, hidden), BF16)] * (3 * sides)
    outs = pl.pallas_call(
        functools.partial(layer_kernel, chunks, sides),
        in_specs=[anywhere] * (3 + len(flat_heads) + len(flat_weights)) + [vmem],
        out_specs=[anywhere, anywhere, vmem] + [anywhere] * (6 * arrays + len(own_rows)),
        out_shape=[whole, whole, jax.ShapeDtypeStruct((8, width), F32)]
        + finals + lands + lands + half_sums + own_rows,
        scratch_shapes=[
            pltpu.VMEM((2, 2, count * share, width), BF16),
            pltpu.VMEM((2, 2, 2, count - 1, share, width), BF16),
            pltpu.VMEM((2, 2, share, width), BF16),
            pltpu.VMEM((2, share, width), BF16),
            pltpu.VMEM((2, share, width), BF16),
            sem((2, 2)),
            sem((2, 2)),
            sem((2, 2, 2, count)),
            sem((2, 2, 2, count)),
            sem((chunks, 2, 2, count)),
            sem((chunks, 2, count)),
            sem((chunks, 2, count)),
            sem((chunks, 2, count)),
            sem((chunks, 2)),
            sem((arrays, 2, pieces)),
            sem((arrays, 2, pieces)),
            sem((arrays, 2, pieces)),
            sem((arrays, 2, pieces)),
            sem((arrays, pieces)),
            sem((arrays, pieces)),
            sem((arrays, 2, pieces)),
            sem((arrays, pieces)),
            sem((2 * arrays,)),
            sem((arrays, 2)),
            pltpu.VMEM((16, width), F32),
            pltpu.VMEM((sides, 8, columns[0]), F32),
            pltpu.VMEM((5, 8, width), F32),
            pltpu.VMEM((5, 8, width), F32),
            sem((5,)),
            sem((5,)),
        ],
        compiler_params=pltpu.CompilerParams(
            collective_id=0, has_side_effects=True, vmem_limit_bytes=63 * 2**20
        ),
        cost_estimate=pl.CostEstimate(
            flops=6 * rows * sum(array.size for array in flat_weights),
            bytes_accessed=800 * 2**20,
            transcendentals=0,
        ),
        name="layer",
    )(normed, tokens, cotangent, *flat_heads, *flat_weights, gain)
    out, grad, small = outs[:3]
    grads = [outs[3].astype(F32)]
    for blocks in outs[4 : 3 + arrays]:
        grads.append(blocks.transpose(1, 0, 2).reshape(blocks.shape[1], width).astype(F32))
    return out, grad, small[0], small[1], small[2, : columns[0]], grads


def body(
    tokens,
    lengths,
    norm_gain,
    norm_shift,
    qkv_weight,
    qkv_bias,
    out_weight,
    gate_weight,
    up_weight,
    down_weight,
    cotangent,
):
    tensor_size = lax.axis_size("tensor")
    dp_size = lax.axis_size("dp")
    count = tensor_size // 2
    where = lax.axis_index("tensor")
    dp_place = lax.axis_index("dp")
    side = where % 2
    across = [(i, i ^ 1) for i in range(tensor_size)]
    row_count, width = tokens.shape
    rows = row_count // 2
    chunk_count = 8

    def own_part(weight):
        part = weight.shape[0] // dp_size
        return lax.dynamic_slice_in_dim(weight, dp_place * part, part, 0)

    def partner(parts, before, after):
        parts, _ = lax.optimization_barrier((parts, before))
        parts = [lax.ppermute(part, "tensor", across) for part in parts]
        parts, after = lax.optimization_barrier((parts, after))
        return [lax.all_gather(part, "dp", axis=0, tiled=True) for part in parts], after

    head_weights = (qkv_weight, out_weight)
    mid_weights = (gate_weight.T, up_weight.T, down_weight)
    other_bias = lax.ppermute(qkv_bias, "tensor", across)

    length = lax.dynamic_slice_in_dim(lengths, side, 1, 0)
    norm = (norm_gain, norm_shift)
    *own_group, normed = project(side, tokens, cotangent, norm, head_weights, qkv_bias)
    tables = rotary_tables(rows)
    even = (out_weight.shape[0] // HEAD) % 2 == 0
    other_heads, (_, other_bias) = partner(
        [own_part(weight) for weight in head_weights], (), (normed, other_bias)
    )
    mid_parts = [own_part(weight) for weight in mid_weights]
    if even:
        heads = [attention(length, *own_group, *tables)]
        other_mids, _ = partner(mid_parts, normed, heads[0])
        other_group = project(side, normed, cotangent, (), other_heads, other_bias)
        heads.append(attention(length, *other_group, *tables))
    else:
        other_mids, _ = partner(mid_parts, normed, ())
        other_group = project(side, normed, cotangent, (), other_heads, other_bias)
        pairs = zip(own_group, other_group)
        attended, qkv_back = attention(
            length, *[jnp.concatenate(pair, axis=1) for pair in pairs], *tables
        )
        cut, wide = out_weight.shape[0], qkv_weight.shape[1]
        heads = [
            (attended[:, s * cut : (s + 1) * cut], qkv_back[:, s * wide : (s + 1) * wide])
            for s in range(2)
        ]
    weights = ((*head_weights, *mid_weights), (*other_heads, *other_mids))
    layer_out, grad_tokens, gain_part, shift_part, grad_bias, grads = layer(
        normed, tokens, cotangent, heads, weights, norm_gain[None, :], count, chunk_count, dp_size
    )
    grad_qkv, grad_gate, grad_up, grad_down, grad_out = grads
    grad_gate, grad_up = grad_gate.T, grad_up.T
    return (
        layer_out,
        grad_tokens,
        gain_part,
        shift_part,
        grad_qkv,
        grad_bias,
        grad_out,
        grad_gate,
        grad_up,
        grad_down,
    )


def solution(mesh):
    placed = (
        P("dp", None),
        P("dp"),
        P(),
        P(),
        P(None, "tensor"),
        P("tensor"),
        P("tensor", None),
        P(None, "tensor"),
        P(None, "tensor"),
        P("tensor", None),
        P("dp", None),
    )
    return jax.shard_map(
        body,
        mesh=mesh,
        in_specs=placed,
        out_specs=(
            P("dp", None),
            P("dp", None),
            P(),
            P(),
            P(None, "tensor"),
            P("tensor"),
            P("tensor", None),
            P(None, "tensor"),
            P(None, "tensor"),
            P("tensor", None),
        ),
        check_vma=False,
    )
```

```python
import functools

import jax
import jax.numpy as jnp
import numpy as np
from jax import lax
from jax.experimental import pallas as pl
from jax.experimental.pallas import tpu as pltpu
from jax.sharding import PartitionSpec as P

HEAD = 64
ROT = 16
PAIR = 2 * HEAD
TRIPLE = 6 * HEAD

EPSILON = 1e-05
NEGATIVE = -1e30
F32 = jnp.float32
BF16 = jnp.bfloat16


def rows_product(former, latter):
    return lax.dot_general(
        former, latter, (((0,), (0,)), ((), ())), preferred_element_type=F32
    )


def cols_product(former, latter):
    return lax.dot_general(
        former, latter, (((1,), (1,)), ((), ())), preferred_element_type=F32
    )


def product(former, latter):
    return jnp.dot(former, latter, preferred_element_type=F32)


def rotary_tables(seq_len):
    frequency = np.float32(10000.0) ** (-np.arange(0, ROT, 2).astype(np.float32) / ROT)
    angles = np.arange(seq_len).astype(np.float32)[:, None] * frequency[None, :]
    cosine, sine = np.cos(angles), np.sin(angles)
    still = HEAD - ROT
    cos_head = np.concatenate([cosine, cosine, np.ones((seq_len, still))], axis=1)
    sin_head = np.concatenate([-sine, sine, np.zeros((seq_len, still))], axis=1)
    return [jnp.asarray(np.tile(table, (1, 2)), F32) for table in (cos_head, sin_head)]


def attention_kernel(
    len_ref, qkv_ref, grad_ref, cos_ref, sin_ref, att_ref, back_ref,
    score, expo, query, key_value, key_value_t, query_t, grad_query, grad_kv_t,
):
    seq_len = qkv_ref.shape[0]
    block = score.shape[1]
    steps = seq_len // block
    length = len_ref[0]
    lane = lax.broadcasted_iota(jnp.int32, (block, PAIR), 1)
    left = lane < HEAD
    near = lax.rem(lane, HEAD) < ROT // 2

    def turn(tile, cosine, sine):
        swapped = jnp.where(
            near, pltpu.roll(tile, PAIR - ROT // 2, 1), pltpu.roll(tile, ROT // 2, 1)
        )
        return tile * cosine + swapped * sine

    def tables(rows):
        cosine, sine = cos_ref[rows, :], sin_ref[rows, :]
        return (
            (cosine, sine),
            (jnp.where(left, 1.0, cosine), jnp.where(left, 0.0, sine)),
            (jnp.where(left, cosine, 1.0), jnp.where(left, sine, 0.0)),
        )

    def prepare(i, carry):
        rows = pl.ds(pl.multiple_of(i * block, block), block)
        tabs = tables(rows)
        first = turn(qkv_ref[rows, 0:PAIR], *tabs[0])
        second = turn(qkv_ref[rows, PAIR : 2 * PAIR], *tabs[1])
        third = turn(qkv_ref[rows, 2 * PAIR : 3 * PAIR], *tabs[2])
        scale = HEAD**-0.5
        first_q = first.astype(BF16).astype(F32) * scale
        second_q = second.astype(BF16).astype(F32) * scale
        query[0, rows, :] = jnp.where(left, 0.0, pltpu.roll(first_q, HEAD, 1)).astype(BF16)
        query[1, rows, :] = jnp.where(left, pltpu.roll(second_q, HEAD, 1), 0.0).astype(BF16)
        for h, tile in enumerate((jnp.where(left, second, first), third)):
            key_value[h, rows, :] = tile.astype(BF16)
            key_value_t[h, :, rows] = tile.T.astype(BF16)
        query_t[0, :, rows] = first_q.T[0:HEAD, :].astype(BF16)
        query_t[1, :, rows] = second_q.T[HEAD:PAIR, :].astype(BF16)
        zero = jnp.zeros((block, PAIR), F32)
        grad_query[rows, :] = zero
        att_ref[rows, :] = zero.astype(BF16)
        for h in range(2):
            grad_kv_t[h, :, rows] = jnp.zeros((PAIR, block), F32)
        return carry

    lax.fori_loop(0, steps, prepare, 0)

    def fold(tile, op):
        out = tile[:, 0:PAIR]
        for c in range(1, block // PAIR):
            out = op(out, tile[:, c * PAIR : (c + 1) * PAIR])
        return out

    def block_rows(i):
        rows = pl.ds(i * block, block)
        spans = [pl.ds(j * block, block) for j in range(i + 1)]
        q_block = [query[h, rows, :] for h in range(2)]
        below = lax.broadcasted_iota(jnp.int32, (block, block), 1) <= lax.broadcasted_iota(
            jnp.int32, (block, block), 0
        )
        maxima = []
        for h in range(2):
            top = None
            for j, cols in enumerate(spans):
                tile = product(q_block[h], key_value_t[h, :, cols])
                if j == i:
                    tile = jnp.where(below, tile, NEGATIVE)
                score[h, :, cols] = tile
                high = fold(tile, jnp.maximum)
                top = high if top is None else jnp.maximum(top, high)
            maxima.append(jnp.max(top, axis=1, keepdims=True))

        mixed, inverse = [], []
        for h in range(2):
            mixture = total = None
            for cols in spans:
                tile = jnp.exp(score[h, :, cols] - maxima[h])
                low = tile.astype(BF16)
                expo[h, :, cols] = low
                part = product(low, key_value[h, cols, :])
                amount = fold(tile, jnp.add)
                mixture = part if mixture is None else mixture + part
                total = amount if total is None else total + amount
            mixed.append(mixture)
            inverse.append(1.0 / jnp.sum(total, axis=1, keepdims=True))

        place = i * block + lax.broadcasted_iota(jnp.int32, (block, 1), 0)
        valid = (place < length).astype(F32)
        mixture = jnp.where(left, mixed[0] * inverse[0], mixed[1] * inverse[1]) * valid
        att_ref[rows, :] = mixture.astype(BF16)
        upstream = grad_ref[rows, :].astype(F32) * valid
        inner = upstream * mixture
        scale = HEAD**-0.5
        turned = []
        for h in range(2):
            own = left if h == 0 else jnp.logical_not(left)
            inner_sum = jnp.sum(jnp.where(own, inner, 0.0), axis=1, keepdims=True) * inverse[h]
            mine = jnp.where(own, upstream * inverse[h], 0.0)
            scaled = mine.astype(BF16)
            half = slice(0, HEAD) if h == 0 else slice(HEAD, PAIR)
            scaled_t = mine.T[half, :].astype(BF16)
            queries_t = query_t[h, :, rows]
            grad = None
            for cols in spans:
                low = expo[h, :, cols]
                grad_weight = product(scaled, key_value_t[h, :, cols])
                grad_score = (low.astype(F32) * (grad_weight - inner_sum)).astype(BF16)
                part = product(grad_score, key_value[h, cols, :])
                grad = part if grad is None else grad + part
                key_at, value_at = (HEAD, 0) if h == 0 else (0, HEAD)
                grad_kv_t[h, key_at : key_at + HEAD, cols] += product(queries_t, grad_score)
                grad_kv_t[h, value_at : value_at + HEAD, cols] += product(scaled_t, low)
            turned.append(pltpu.roll(grad, HEAD, 1))
        grad_query[rows, :] = jnp.where(left, turned[0], turned[1]) * scale

    for i in range(steps):
        pl.when(i * block < length)(functools.partial(block_rows, i))

    def finish(i, carry):
        rows = pl.ds(pl.multiple_of(i * block, block), block)
        tabs = tables(rows)
        gq = grad_query[rows, :]
        low_kv = grad_kv_t[0, :, rows].T
        high_kv = grad_kv_t[1, :, rows].T
        tiles = (jnp.where(left, gq, low_kv), jnp.where(left, low_kv, gq), high_kv)
        for c in range(3):
            back_ref[rows, c * PAIR : (c + 1) * PAIR] = turn(
                tiles[c], tabs[c][0], -tabs[c][1]
            ).astype(BF16)
        return carry

    lax.fori_loop(0, steps, finish, 0)


def attention(length, qkv, grad_mixture, cosine, sine):
    seq_len, width = qkv.shape
    pairs = width // TRIPLE
    block = min(512, seq_len)
    flops = 6 * 2 * (2 * pairs) * seq_len * seq_len * PAIR
    return pl.pallas_call(
        attention_kernel,
        grid=(pairs,),
        in_specs=[
            pl.BlockSpec(memory_space=pltpu.SMEM),
            pl.BlockSpec((seq_len, TRIPLE), lambda g: (0, g)),
            pl.BlockSpec((seq_len, PAIR), lambda g: (0, g)),
            pl.BlockSpec((seq_len, PAIR), lambda g: (0, 0)),
            pl.BlockSpec((seq_len, PAIR), lambda g: (0, 0)),
        ],
        out_specs=[
            pl.BlockSpec((seq_len, PAIR), lambda g: (0, g)),
            pl.BlockSpec((seq_len, TRIPLE), lambda g: (0, g)),
        ],
        out_shape=[
            jax.ShapeDtypeStruct((seq_len, pairs * PAIR), BF16),
            jax.ShapeDtypeStruct((seq_len, width), BF16),
        ],
        scratch_shapes=[
            pltpu.VMEM((2, block, seq_len), F32),
            pltpu.VMEM((2, block, seq_len), BF16),
            pltpu.VMEM((2, seq_len, PAIR), BF16),
            pltpu.VMEM((2, seq_len, PAIR), BF16),
            pltpu.VMEM((2, PAIR, seq_len), BF16),
            pltpu.VMEM((2, HEAD, seq_len), BF16),
            pltpu.VMEM((seq_len, PAIR), F32),
            pltpu.VMEM((2, PAIR, seq_len), F32),
        ],
        compiler_params=pltpu.CompilerParams(vmem_limit_bytes=48 * 2**20),
        cost_estimate=pl.CostEstimate(
            flops=flops,
            bytes_accessed=seq_len * width * 8,
            transcendentals=2 * pairs * seq_len * seq_len // 2,
        ),
        name="attention",
    )(length, qkv, grad_mixture, cosine, sine)


def start_kernel(
    side_ref, tok_ref, cot_ref, gain_ref, shift_ref, qkv_w, bias_ref, out_w,
    qkv_ref, grad_ref, normed_ref,
):
    wide = tok_ref[...].astype(F32)
    centred = wide - jnp.mean(wide, axis=1, keepdims=True)
    variance = jnp.mean(centred * centred, axis=1, keepdims=True)
    unit = centred * lax.rsqrt(variance + EPSILON)
    normed = (unit * gain_ref[...] + shift_ref[...]).astype(BF16)
    normed_ref[...] = normed
    qkv_ref[...] = product(normed, qkv_w[...]) + bias_ref[...]
    grad_ref[...] = cols_product(cot_ref[...], out_w[...]).astype(BF16)


def project_kernel(side_ref, normed_ref, cot_ref, qkv_w, bias_ref, out_w, qkv_ref, grad_ref):
    qkv_ref[...] = product(normed_ref[...], qkv_w[...]) + bias_ref[...]
    grad_ref[...] = cols_product(cot_ref[...], out_w[...]).astype(BF16)


def project(side, rows_in, cotangent, norm, weights, bias):
    rows, width = cotangent.shape[0] // 2, cotangent.shape[1]
    tile = min(256, rows)
    tiles = rows // tile
    qkv_weight, out_weight = weights
    heads, wide = out_weight.shape[0], qkv_weight.shape[1]

    def sided(i, side_ref):
        return (side_ref[0] * tiles + i, 0)

    def fixed(i, side_ref):
        return (0, 0)

    def rowed(i, side_ref):
        return (i, 0)

    flat = [part[None, :] for part in norm]
    flat += [qkv_weight, bias.astype(F32)[None, :], out_weight]
    outs = [((rows, wide), F32), ((rows, heads), BF16)]
    out_specs = [pl.BlockSpec((tile, shape[1]), rowed) for shape, _ in outs]
    if norm:
        outs.append(((rows, width), BF16))
        out_specs.append(pl.BlockSpec((tile, width), rowed))
    return pl.pallas_call(
        start_kernel if norm else project_kernel,
        grid_spec=pltpu.PrefetchScalarGridSpec(
            num_scalar_prefetch=1,
            grid=(tiles,),
            in_specs=[
                pl.BlockSpec((tile, width), sided if norm else rowed),
                pl.BlockSpec((tile, width), sided),
            ]
            + [pl.BlockSpec(array.shape, fixed) for array in flat],
            out_specs=out_specs,
        ),
        out_shape=[jax.ShapeDtypeStruct(*out) for out in outs],
        compiler_params=pltpu.CompilerParams(vmem_limit_bytes=40 * 2**20),
        cost_estimate=pl.CostEstimate(
            flops=2 * rows * width * (wide + heads),
            bytes_accessed=rows * (6 * width + 4 * wide),
            transcendentals=rows,
        ),
        name="project",
    )(side[None], rows_in, cotangent, *flat)


def layer_kernel(chunks, sides, *refs):
    normed_ref, tok_ref, cot_ref = refs[:3]
    head_refs, refs = refs[3 : 3 + 2 * sides], refs[3 + 2 * sides :]
    weight_refs, gain_ref = refs[: 5 * sides], refs[5 * sides]
    refs = refs[5 * sides + 1 :]
    out_ref, grad_ref, small_ref = refs[:3]
    refs = refs[3:]
    arrays = 5
    grad_outs, core_land = refs[:arrays], refs[arrays : 3 * arrays]
    far_land, side_land = refs[3 * arrays : 5 * arrays], refs[5 * arrays : 6 * arrays]
    refs = refs[6 * arrays :]
    f_ref, g_ref = refs[:2]
    mid_refs, refs = refs[2 : 2 + 3 * sides], refs[2 + 3 * sides :]
    (
        terms, landed, ready, tok_buf, cot_buf,
        term_sem, share_sem, sum_send, sum_recv,
        line_send, line_recv, side_send, side_recv, keep_sem,
        core_send, core_recv, far_send, far_recv, over_send, over_recv,
        back_send, back_recv, load_sem, save_sem,
        part_ref, bias_part, stages, came, small_send, small_recv,
    ) = refs
    share, width = landed.shape[4:]
    count = landed.shape[3] + 1
    chunk_rows = count * share
    rows = chunks * chunk_rows
    where = lax.axis_index("tensor")
    group = lax.axis_index("dp")
    place, side = where // 2, where % 2
    half, core = group // 2, group % 2
    whole_refs = (out_ref, grad_ref)
    factors = []
    for s in range(sides):
        hidden_ref, gate_ref, up_ref = mid_refs[3 * s : 3 * s + 3]
        factors.append(
            (head_refs[2 * s + 1], gate_ref, up_ref, hidden_ref, head_refs[2 * s])
        )
    factors = [factors[x % sides][x // sides] for x in range(arrays * sides)]

    above, below = (group, where + 2), (group, where - 2)
    across = (group, where + 1 - 2 * side)
    other_core = (half * 2 + 1 - core, where)
    other_half = ((1 - half) * 2 + core, where)
    has_above, has_below = place < count - 1, place > 0

    barrier = pltpu.get_barrier_semaphore()

    def greet(target):
        pl.semaphore_signal(barrier, inc=1, device_id=target, device_id_type=pl.DeviceIdType.MESH)

    pl.when(has_above)(lambda: greet(above))
    pl.when(has_below)(lambda: greet(below))
    for target in (across, other_core, other_half):
        greet(target)

    def span(begin, size):
        return pl.ds(pl.multiple_of(begin, size), size)

    def load(c, k):
        source = (f_ref, g_ref)[k].at[span(c * chunk_rows, chunk_rows), :]
        return pltpu.make_async_copy(
            source, terms.at[lax.rem(c, 2), k], term_sem.at[lax.rem(c, 2), k]
        )

    def load_share(c, k):
        begin = span(side * rows + c * chunk_rows + place * share, share)
        source, target = ((tok_ref, tok_buf), (cot_ref, cot_buf))[k]
        return pltpu.make_async_copy(
            source.at[begin, :], target.at[lax.rem(c, 2)], share_sem.at[lax.rem(c, 2), k]
        )

    def remote(source, target, send, recv, device_id):
        return pltpu.make_async_remote_copy(
            src_ref=source, dst_ref=target, send_sem=send, recv_sem=recv,
            device_id=device_id, device_id_type=pl.DeviceIdType.MESH,
        )


    def sum_copy(c, k, way, b, first):
        slot = lax.rem(c, 2)
        target = landed.at[slot, k, way, b - 1 + way]
        source = terms.at[slot, k, span(b * share, share), :] if first else target
        return remote(
            source, target, sum_send.at[slot, k, way, b], sum_recv.at[slot, k, way, b],
            (above, below)[way],
        )

    def place_of(c, b, on_side):
        return span(on_side * rows + c * chunk_rows + b * share, share)

    def line_copy(c, k, b, way, first):
        target = whole_refs[k].at[place_of(c, b, side), :]
        source = ready.at[lax.rem(c, 2), k] if first else target
        return remote(
            source, target, line_send.at[c, k, way, b], line_recv.at[c, k, b],
            (above, below)[way],
        )

    def side_copy(c, k, b, first):
        target = whole_refs[k].at[place_of(c, b, side), :]
        source = ready.at[lax.rem(c, 2), k] if first else target
        return remote(
            source, target, side_send.at[c, k, b], side_recv.at[c, k, b], across
        )

    def keep_copy(c, k):
        return pltpu.make_async_copy(
            ready.at[lax.rem(c, 2), k], whole_refs[k].at[place_of(c, place, side), :],
            keep_sem.at[c, k],
        )

    def each_first(c, k, act):
        @pl.when(jnp.logical_not(has_below))
        def _():
            for b in range(count - 1, 0, -1):
                act(sum_copy(c, k, 0, b, True))

        @pl.when(jnp.logical_not(has_above))
        def _():
            for b in range(count - 1):
                act(sum_copy(c, k, 1, b, True))

    def send_ends(c, k):
        load(c, k).wait()
        each_first(c, k, lambda copy: copy.start())

    def sums_left(c, k):
        for b in range(count):

            @pl.when(has_below & (place < b))
            def _(b=b):
                sum_copy(c, k, 0, b, False).wait_send()

            @pl.when(has_above & (place > b))
            def _(b=b):
                sum_copy(c, k, 1, b, False).wait_send()

    step = min(16, share)

    def add_on(c, k, way, b):
        slot = lax.rem(c, 2)

        def body(i, carry):
            at = span(i * step, step)
            mine = terms[slot, k, span(b * share + i * step, step), :].astype(F32)
            landed[slot, k, way, b - 1 + way, at, :] = (
                mine + landed[slot, k, way, b - 1 + way, at, :].astype(F32)
            ).astype(BF16)
            return carry

        lax.fori_loop(0, share // step, body, 0)

    def sums(c, k, wave):
        ahead = count - 2 - wave
        for way, b, here in (
            (0, place + ahead, has_below & (place + ahead < count)),
            (1, place - ahead, has_above & (place >= ahead)),
        ):

            @pl.when(here)
            def _(way=way, b=b):
                sum_copy(c, k, way, b, False).wait_recv()

                @pl.when(ahead > 0)
                def _():
                    add_on(c, k, way, b)
                    sum_copy(c, k, way, b, False).start()

    def own_left(c, k):
        pl.when(has_above)(lambda: line_copy(c, k, place, 0, True).wait_send())
        pl.when(has_below)(lambda: line_copy(c, k, place, 1, True).wait_send())
        side_copy(c, k, place, True).wait_send()
        keep_copy(c, k).wait()

    def finish(c, k):
        load_share(c, k).wait()
        pl.when(c > 1)(lambda: own_left(c - 2, k))
        slot = lax.rem(c, 2)

        def body(i, carry):
            at = span(i * step, step)
            up = landed[slot, k, 0, jnp.maximum(place - 1, 0), at, :].astype(F32)
            down = landed[slot, k, 1, jnp.minimum(place, count - 2), at, :].astype(F32)
            total = (
                terms[slot, k, span(place * share + i * step, step), :].astype(F32)
                + jnp.where(has_below, up, 0.0)
                + jnp.where(has_above, down, 0.0)
            )
            wide = tok_buf[slot, at, :].astype(F32)
            if k == 0:
                ready[slot, k, at, :] = (wide + total).astype(BF16)
                return carry
            scale = 1.0 / width
            centred = wide - jnp.sum(wide, axis=1, keepdims=True) * scale
            variance = jnp.sum(centred * centred, axis=1, keepdims=True) * scale
            inverse = lax.rsqrt(variance + EPSILON)
            unit = centred * inverse
            scaled = total * gain_ref[0:1, :]
            mean_scaled = jnp.sum(scaled, axis=1, keepdims=True) * scale
            mean_cross = jnp.sum(scaled * unit, axis=1, keepdims=True) * scale
            ready[slot, k, at, :] = (
                cot_buf[slot, at, :].astype(F32)
                + inverse * (scaled - mean_scaled - unit * mean_cross)
            ).astype(BF16)
            gain_term = total * unit
            for r in range(0, step, 8):
                part_ref[0:8, :] += gain_term[r : r + 8, :]
                part_ref[8:16, :] += total[r : r + 8, :]
            return carry

        lax.fori_loop(0, share // step, body, 0)
        pl.when(has_above)(lambda: line_copy(c, k, place, 0, True).start())
        pl.when(has_below)(lambda: line_copy(c, k, place, 1, True).start())
        side_copy(c, k, place, True).start()
        keep_copy(c, k).start()

    def pass_on(c, k, distance):
        for way, b, here in (
            (0, place - distance, place >= distance),
            (1, place + distance, place + distance < count),
        ):

            @pl.when(here)
            def _(way=way, b=b):
                line_copy(c, k, b, way, False).wait_recv()
                pl.when((has_above, has_below)[way])(
                    lambda: line_copy(c, k, b, way, False).start()
                )
                side_copy(c, k, b, False).start()

    def small_copy(n, target):
        return remote(stages.at[n], came.at[n], small_send.at[n], small_recv.at[n], target)

    def small_sums():
        wide = bias_part.shape[2]
        stages[...] = jnp.zeros_like(stages)
        stages[0, 0:1, :] = jnp.sum(part_ref[0:8, :], axis=0, keepdims=True)
        stages[0, 1:2, :] = jnp.sum(part_ref[8:16, :], axis=0, keepdims=True)
        for s in range(sides):
            stages[0, 2 + s : 3 + s, 0:wide] = jnp.sum(bias_part[s], axis=0, keepdims=True)
        for n, target in enumerate((across, other_core, other_half)):
            copy = small_copy(n, target)
            copy.start()
            copy.wait_recv()
            if n == 0:
                stages[1, 0:2, :] = stages[0, 0:2, :] + came[0, 0:2, :]
                stages[1, 2:3, :] = stages[0, 2:3, :] + came[0, 3:4, :]
            else:
                stages[n + 1] = stages[n] + came[n]

        @pl.when(has_below)
        def _():
            small_copy(3, above).wait_recv()
            stages[3] = stages[3] + came[3]

        pl.when(has_above)(lambda: small_copy(3, above).start())
        stages[4] = stages[3]

        @pl.when(has_above)
        def _():
            small_copy(4, below).wait_recv()
            stages[4] = came[4]

        pl.when(has_below)(lambda: small_copy(4, below).start())
        small_ref[...] = stages[4]
        small_ref[2:3, :] = stages[2, 2:3, :] + came[2, 2:3, :]
        for n, target in enumerate((across, other_core, other_half)):
            small_copy(n, target).wait_send()
        pl.when(has_above)(lambda: small_copy(3, above).wait_send())
        pl.when(has_below)(lambda: small_copy(4, below).wait_send())

    waves = count - 1
    every = max(1, waves // 3)
    works = waves // every

    if count == 4:
        order = ((2, 2, 0), (1, 1, 1), (2, 3, 1))
    else:
        order = tuple((2, distance, distance - 1) for distance in range(1, count))

    def pass_steps(h, live, wave):
        for behind, distance, step in order:
            item = jnp.maximum(h - behind, 0)
            for k in range(2):
                pl.when(
                    live & (wave == step) & (h >= behind) & (lax.rem(item, 2) == k)
                )(lambda: pass_on(item // 2, k, distance))

    def pass_rest():
        for item in range(2 * chunks - 2, 2 * chunks):
            for distance, behind in sorted((step[1], step[0]) for step in order):
                if item + behind >= 2 * chunks:
                    pass_on(item // 2, item % 2, distance)

    def half_steps(h, live, work):
        c = h // 2

        def one(wave, carry):
            pl.when(lax.rem(wave, every) == 0)(lambda: work(wave // every))
            for k in range(2):

                @pl.when(live & (lax.rem(h, 2) == k))
                def _(k=k):
                    more = c + 1 < chunks

                    @pl.when(wave == 0)
                    def _():
                        @pl.when(c > 0)
                        def _():
                            sums_left(c - 1, k)
                            each_first(c - 1, k, lambda copy: copy.wait_send())

                        pl.when(more)(lambda: load_share(c + 1, k).start())
                        pl.when(more & (c > 0))(lambda: load(c + 1, k).start())

                    sums(c, k, wave)

            pass_steps(h, live, wave)
            for k in range(2):

                @pl.when(live & (lax.rem(h, 2) == k) & (wave == waves - 1))
                def _(k=k):
                    more = c + 1 < chunks
                    pl.when(c == 0)(lambda: load(c + 1, k).start())
                    finish(c, k)
                    pl.when(more)(lambda: send_ends(c + 1, k))

            return carry

        lax.fori_loop(0, waves, one, 0)

    tile_halves = -(-sides * (chunks - 1) // works)

    def tiles_scope(*scratch):
        weights = scratch[: 5 * sides]
        scratch = scratch[5 * sides :]
        normed_buf, tile_cot = scratch[:2]
        head_bufs = scratch[2 : 2 + 2 * sides]
        scratch = scratch[2 + 2 * sides :]
        mids, f_buf, g_buf = scratch[: 3 * sides], scratch[3 * sides], scratch[3 * sides + 1]
        f_total, g_total, weight_sem, in_sem, out_sem = scratch[3 * sides + 2 :]

        def weight_copies(s):
            return [
                pltpu.make_async_copy(weight_refs[x], weights[x], weight_sem.at[x])
                for x in range(5 * s, 5 * s + 5)
            ]

        def tile_in(i):
            slot = lax.rem(i, 2)
            at = span(i * chunk_rows, chunk_rows)
            at_side = span(side * rows + i * chunk_rows, chunk_rows)
            pairs = [(normed_ref.at[at, :], normed_buf), (cot_ref.at[at_side, :], tile_cot)]
            pairs += [(ref.at[at, :], buf) for ref, buf in zip(head_refs, head_bufs)]
            return [
                pltpu.make_async_copy(ref, buf.at[slot], in_sem.at[slot, x])
                for x, (ref, buf) in enumerate(pairs)
            ]

        def tile_out(i):
            at = span(i * chunk_rows, chunk_rows)
            pairs = list(zip(mids, mid_refs)) + [(f_buf, f_ref), (g_buf, g_ref)]
            return [
                pltpu.make_async_copy(buf, ref.at[at, :], out_sem.at[x])
                for x, (buf, ref) in enumerate(pairs)
            ]

        def wait_out(i):
            for copy in tile_out(i):
                copy.wait()

        def tile(i, s):
            slot = lax.rem(i, 2)
            if s == 0:
                for copy in tile_in(i):
                    copy.wait()

                @pl.when(i + 1 < chunks)
                def _():
                    for copy in tile_in(i + 1):
                        copy.start()

            @pl.when(i == 0)
            def _():
                for copy in weight_copies(s):
                    copy.wait()

            qkv_w, out_w, gate_w, up_w, down_w = weights[5 * s : 5 * s + 5]
            hidden_buf, gate_buf, up_buf = mids[3 * s : 3 * s + 3]
            normed, cot = normed_buf[slot], tile_cot[slot]
            gate = cols_product(normed, gate_w[...])
            up = cols_product(normed, up_w[...])
            sig = 1.0 / (1.0 + jnp.exp(-gate))
            silu = gate * sig
            hidden = (silu * up).astype(BF16)
            grad_hidden = cols_product(cot, down_w[...])
            if s == 0:
                pl.when(i > 1)(lambda: wait_out(i - 1))
            hidden_buf[...] = hidden
            gate_back = (grad_hidden * up * sig * (1.0 + gate * (1.0 - sig))).astype(BF16)
            up_back = (grad_hidden * silu).astype(BF16)
            gate_buf[...] = gate_back
            up_buf[...] = up_back
            forward = product(hidden, down_w[...])
            forward += product(head_bufs[2 * s][slot], out_w[...])
            backward = product(gate_back, gate_w[...])
            backward += product(up_back, up_w[...])
            qkv_back = head_bufs[2 * s + 1][slot]
            backward += cols_product(qkv_back, qkv_w[...])
            bias_part[s] += (
                qkv_back.astype(F32).reshape(chunk_rows // 8, 8, qkv_back.shape[1]).sum(axis=0)
            )
            if s > 0:
                forward += f_total[...]
                backward += g_total[...]
            if s < sides - 1:
                f_total[...] = forward
                g_total[...] = backward
                return
            f_buf[...] = forward.astype(BF16)
            g_buf[...] = backward.astype(BF16)
            for copy in tile_out(i):
                copy.start()

        def work(turn, n):
            first = turn == 0
            unit = jnp.maximum(works * turn - works, 0) + n
            i = jnp.where(first, 0, 1 + unit // sides)
            part = jnp.where(first, n - works + sides, lax.rem(unit, sides))
            for s in range(sides):
                pl.when((part == s) & (i < chunks))(lambda: tile(i, s))

        for s in range(sides):
            for copy in weight_copies(s):
                copy.start()
        for copy in tile_in(0):
            copy.start()
        for k in range(2):
            load_share(0, k).start()
        part_ref[...] = jnp.zeros_like(part_ref)
        bias_part[...] = jnp.zeros_like(bias_part)
        pl.semaphore_wait(
            barrier, 3 + has_above.astype(jnp.int32) + has_below.astype(jnp.int32)
        )

        def chunk(turn, carry):
            half_steps(
                jnp.maximum(turn, 1) - 1, turn > 0, lambda n: work(turn, n)
            )

            @pl.when(turn == 0)
            def _():
                wait_out(0)
                for k in range(2):
                    load(0, k).start()
                for k in range(2):
                    send_ends(0, k)

            return carry

        lax.fori_loop(0, tile_halves + 1, chunk, 0)
        wait_out(chunks - 1)

    tall = width
    hidden_cols = mid_refs[0].shape[1]
    pl.run_scoped(
        tiles_scope,
        *[pltpu.VMEM(ref.shape, BF16) for ref in weight_refs],
        pltpu.VMEM((2, chunk_rows, width), BF16),
        pltpu.VMEM((2, chunk_rows, width), BF16),
        *[pltpu.VMEM((2, chunk_rows, ref.shape[1]), BF16) for ref in head_refs],
        *[pltpu.VMEM((chunk_rows, hidden_cols), BF16) for _ in mid_refs],
        pltpu.VMEM((chunk_rows, width), BF16),
        pltpu.VMEM((chunk_rows, width), BF16),
        pltpu.VMEM((chunk_rows, width), F32),
        pltpu.VMEM((chunk_rows, width), F32),
        pltpu.SemaphoreType.DMA((5 * sides,)),
        pltpu.SemaphoreType.DMA((2, 2 + 2 * sides)),
        pltpu.SemaphoreType.DMA((3 * sides + 2,)),
    )


    pieces = core_send.shape[2]
    each = 2
    size = tall // pieces

    def grads_scope(*scratch):
        factor_bufs, scratch = scratch[: arrays * sides], scratch[arrays * sides :]
        held, scratch = scratch[: arrays * sides], scratch[arrays * sides :]
        extra, scratch = scratch[: arrays * sides], scratch[arrays * sides :]
        turned, scratch = scratch[: arrays - 1], scratch[arrays - 1 :]
        left_bufs, factor_sem, left_sem = scratch[:2], scratch[2], scratch[3]

        def factor_copy(x):
            return pltpu.make_async_copy(factors[x], factor_bufs[x], factor_sem.at[x])

        def piece(ref, j):
            return ref.at[span(j * size, size), :]

        def piece_of(u):
            owner_core = jnp.where((u // each) % 2 == 0, 1 - core, core)
            owner_half = jnp.where(u < 2 * each, 1 - half, half)
            return (owner_half * 2 + owner_core) * each + lax.rem(u, each)

        def slot_of(u):
            return jnp.where(u < 2 * each, lax.rem(u, each), each + lax.rem(u, each))

        def left_copy(u, which):
            at = span(piece_of(u) * size, size)
            source = (
                normed_ref.at[:, at] if which == 0 else cot_ref.at[span(side * rows, rows), at]
            )
            return pltpu.make_async_copy(
                source, left_bufs[which].at[lax.rem(u, 2)], left_sem.at[which, lax.rem(u, 2)]
            )

        def to_core(a, s, j, slot):
            x = 2 * a + s
            return remote(
                held[x].at[slot], piece(core_land[x], j),
                core_send.at[a, s, j], core_recv.at[a, s, j], other_core,
            )

        def to_far(a, s, i, j):
            x = 2 * a + s
            return remote(
                held[x].at[i], piece(far_land[x], j),
                far_send.at[a, s, j], far_recv.at[a, s, j], other_half,
            )

        def to_over(a, i, j):
            return remote(
                held[2 * a + 1].at[each + i], piece(side_land[a], j),
                over_send.at[a, j], over_recv.at[a, j], across,
            )

        def final_piece(a, j):
            at = span(j * size, size)
            if a == 0:
                return grad_outs[a].at[at, :]
            return grad_outs[a].at[:, at] if a == arrays - 1 else grad_outs[a].at[j]

        def final_source(a, i):
            return turned[a - 1].at[i] if a else held[0].at[each + i]

        def back_copy(a, i, j, way, first):
            target = final_piece(a, j)
            source = final_source(a, i) if first else target
            return remote(
                source, target, back_send.at[a, way, j], back_recv.at[a, j],
                (other_core, other_half)[way],
            )

        def save_copy(a, i, j):
            return pltpu.make_async_copy(
                final_source(a, i), final_piece(a, j), save_sem.at[a, i]
            )

        def their_piece(i):
            return ((1 - half) * 2 + core) * each + i

        def my_piece(i):
            return (half * 2 + core) * each + i

        def add_into(target, slot, source):
            rows_at_once = min(64, size)

            def body(i, carry):
                at = span(i * rows_at_once, rows_at_once)
                target[slot, at, :] = (
                    target[slot, at, :].astype(F32) + source[at, :].astype(F32)
                ).astype(BF16)
                return carry

            lax.fori_loop(0, size // rows_at_once, body, 0)

        def fetch(lands, j, ids, act):
            for n, x in enumerate(ids):
                act(pltpu.make_async_copy(piece(lands[n], j), extra[x], load_sem.at[x]))

        def begin(lands, j, ids):
            fetch(lands, j, ids, lambda copy: copy.start())

        def end(lands, j, ids):
            fetch(lands, j, ids, lambda copy: copy.wait())

        everything = range(2 * arrays)

        def make(u, which):
            @pl.when(u == 0)
            def _():
                for x in everything:
                    if (x // 2 < 3) == (which == 0):
                        factor_copy(x).wait()

            left_copy(u, which).wait()
            pl.when(u + 1 < pieces)(lambda: left_copy(u + 1, which).start())
            slot = slot_of(u)
            left = left_bufs[which][lax.rem(u, 2)].T

            @pl.when((u // each) % 2 == 1)
            def _():
                for x in everything:
                    if (x // 2 < 3) == (which == 0):
                        to_core(x // 2, x % 2, piece_of(u - each), slot).wait_send()

            for x in everything:
                if (x // 2 < 3) == (which == 0):
                    held[x][slot] = product(left, factor_bufs[x][...]).astype(BF16)

            @pl.when((u // each) % 2 == 0)
            def _():
                for x in everything:
                    if (x // 2 < 3) == (which == 0):
                        to_core(x // 2, x % 2, piece_of(u), slot).start()


        def core_begin(j):
            for x in everything:
                to_core(x // 2, x % 2, j, 0).wait_recv()
            begin(core_land, j, everything)

        def core_end(slot, j):
            end(core_land, j, everything)
            for x in everything:
                add_into(held[x], slot, extra[x])

        def far_begin(i):
            core_begin(their_piece(i))

        def far_end(i):
            j = their_piece(i)
            core_end(i, j)
            for x in everything:
                to_far(x // 2, x % 2, i, j).start()

        def over_begin(i):
            core_begin(my_piece(i))

        def over_middle(i):
            j = my_piece(i)
            core_end(each + i, j)
            for x in everything:
                to_far(x // 2, x % 2, i, j).wait_recv()
            begin(far_land, j, everything)

        def over_end(i):
            j = my_piece(i)
            end(far_land, j, everything)
            for a in range(arrays):
                add_into(held[2 * a + 1], each + i, extra[2 * a + 1])
                to_over(a, i, j).start()
            for a in range(arrays):
                add_into(held[2 * a], each + i, extra[2 * a])

        firsts = range(0, 2 * arrays, 2)

        def back_begin(i):
            j = my_piece(i)
            for a in range(arrays):
                to_over(a, i, j).wait_recv()
            begin(side_land, j, firsts)

        def back_end(i):
            j = my_piece(i)
            end(side_land, j, firsts)
            for a in range(arrays):
                if a:
                    total = held[2 * a][each + i].astype(F32) + extra[2 * a][...].astype(F32)
                    turned[a - 1][i] = total.T.astype(BF16)
                else:
                    add_into(held[0], each + i, extra[0])
                back_copy(a, i, j, 1, True).start()
                back_copy(a, i, j, 0, True).start()
                save_copy(a, i, j).start()

        def grads_pass(i):
            j = their_piece(i)
            for a in range(arrays):
                back_copy(a, i, j, 1, False).wait_recv()
                back_copy(a, i, j, 0, False).start()

        def grads_drain():
            for i in range(each):
                mine, theirs = my_piece(i), their_piece(i)
                for a in range(arrays):
                    for s in range(2):
                        to_far(a, s, i, theirs).wait_send()
                    to_over(a, i, mine).wait_send()
                    back_copy(a, i, mine, 1, True).wait_send()
                    back_copy(a, i, mine, 0, True).wait_send()
                    back_copy(a, i, theirs, 0, False).wait_send()
                    save_copy(a, i, mine).wait()
            for u in (*range(each), *range(2 * each, 3 * each)):
                for a in range(arrays):
                    back_copy(a, 0, piece_of(u), 0, False).wait_recv()

        events = {
            (7, 1): (far_begin, 0),
            (7, 2): (far_end, 0),
            (8, 1): (far_begin, 1),
            (8, 2): (far_end, 1),
            (11, 1): (over_begin, 0),
            (11, 2): (over_middle, 0),
            (12, 0): (over_end, 0),
            (12, 1): (over_begin, 1),
            (12, 2): (over_middle, 1),
            (13, 0): (over_end, 1),
            (14, 1): (back_begin, 0),
            (14, 2): (back_end, 0),
        }

        def work(h, n):
            u = h - tile_halves
            for which in range(2):
                pl.when((u < pieces) & (n == which))(lambda: make(u, which))
            for (at, step), (act, i) in events.items():
                pl.when((h == at) & (n == step))(lambda: act(i))

        for x in everything:
            factor_copy(x).start()
        for which in range(2):
            left_copy(0, which).start()

        def chunk(c, carry):
            half_steps(c, c >= 0, lambda n: work(c, n))
            return carry

        lax.fori_loop(tile_halves, 2 * chunks, chunk, 0)
        back_begin(1)
        pass_rest()
        back_end(1)
        small_sums()
        for i in range(each):
            grads_pass(i)
        grads_drain()

    factor_shapes = [ref.shape for ref in factors]
    pl.run_scoped(
        grads_scope,
        *[pltpu.VMEM(shape, BF16) for shape in factor_shapes],
        *[pltpu.VMEM((2 * each, size, shape[1]), BF16) for shape in factor_shapes],
        *[pltpu.VMEM((size, shape[1]), BF16) for shape in factor_shapes],
        *[pltpu.VMEM((each, shape[1], size), BF16) for shape in factor_shapes[2::2]],
        pltpu.VMEM((2, rows, size), BF16),
        pltpu.VMEM((2, rows, size), BF16),
        pltpu.SemaphoreType.DMA((2 * arrays,)),
        pltpu.SemaphoreType.DMA((2, 2)),
    )

    for k in range(2):
        sums_left(chunks - 1, k)
        each_first(chunks - 1, k, lambda copy: copy.wait_send())
        own_left(chunks - 2, k)
        own_left(chunks - 1, k)

    def drain(c, carry):
        for k in range(2):
            for b in range(count):
                pl.when((place > b) & has_above)(
                    lambda: line_copy(c, k, b, 0, False).wait_send()
                )
                pl.when((place < b) & has_below)(
                    lambda: line_copy(c, k, b, 1, False).wait_send()
                )
                pl.when(place != b)(lambda: side_copy(c, k, b, False).wait_send())
                side_copy(c, k, b, False).wait_recv()
        return carry

    lax.fori_loop(0, chunks, drain, 0)


def layer(normed, tokens, cotangent, heads, weights, gain, count, chunks, dp_size):
    row_count, width = tokens.shape
    rows = row_count // 2
    share = rows // chunks // count
    sides, arrays = len(weights), 5
    pieces = 2 * dp_size
    sem = pltpu.SemaphoreType.DMA
    flat_heads = [array for group in heads for array in group]
    flat_weights = [array for group in weights for array in group]
    hidden = weights[0][2].shape[0]
    columns = [heads[0][1].shape[1], hidden, hidden, hidden, heads[0][0].shape[1]]
    whole = jax.ShapeDtypeStruct(tokens.shape, BF16)
    half_sums = [jax.ShapeDtypeStruct((width, n), BF16) for n in columns]
    finals = half_sums[:1] + [
        jax.ShapeDtypeStruct((pieces, n, width // pieces), BF16) for n in columns[1:4]
    ]
    finals.append(jax.ShapeDtypeStruct((columns[4], width), BF16))
    lands = [shape for shape in half_sums for _ in range(sides)]
    anywhere = pl.BlockSpec(memory_space=pl.ANY)
    vmem = pl.BlockSpec(memory_space=pltpu.VMEM)
    own_rows = [jax.ShapeDtypeStruct((rows, width), BF16)] * 2
    own_rows += [jax.ShapeDtypeStruct((rows, hidden), BF16)] * (3 * sides)
    outs = pl.pallas_call(
        functools.partial(layer_kernel, chunks, sides),
        in_specs=[anywhere] * (3 + len(flat_heads) + len(flat_weights)) + [vmem],
        out_specs=[anywhere, anywhere, vmem] + [anywhere] * (6 * arrays + len(own_rows)),
        out_shape=[whole, whole, jax.ShapeDtypeStruct((8, width), F32)]
        + finals + lands + lands + half_sums + own_rows,
        scratch_shapes=[
            pltpu.VMEM((2, 2, count * share, width), BF16),
            pltpu.VMEM((2, 2, 2, count - 1, share, width), BF16),
            pltpu.VMEM((2, 2, share, width), BF16),
            pltpu.VMEM((2, share, width), BF16),
            pltpu.VMEM((2, share, width), BF16),
            sem((2, 2)),
            sem((2, 2)),
            sem((2, 2, 2, count)),
            sem((2, 2, 2, count)),
            sem((chunks, 2, 2, count)),
            sem((chunks, 2, count)),
            sem((chunks, 2, count)),
            sem((chunks, 2, count)),
            sem((chunks, 2)),
            sem((arrays, 2, pieces)),
            sem((arrays, 2, pieces)),
            sem((arrays, 2, pieces)),
            sem((arrays, 2, pieces)),
            sem((arrays, pieces)),
            sem((arrays, pieces)),
            sem((arrays, 2, pieces)),
            sem((arrays, pieces)),
            sem((2 * arrays,)),
            sem((arrays, 2)),
            pltpu.VMEM((16, width), F32),
            pltpu.VMEM((sides, 8, columns[0]), F32),
            pltpu.VMEM((5, 8, width), F32),
            pltpu.VMEM((5, 8, width), F32),
            sem((5,)),
            sem((5,)),
        ],
        compiler_params=pltpu.CompilerParams(
            collective_id=0, has_side_effects=True, vmem_limit_bytes=63 * 2**20
        ),
        cost_estimate=pl.CostEstimate(
            flops=6 * rows * sum(array.size for array in flat_weights),
            bytes_accessed=800 * 2**20,
            transcendentals=0,
        ),
        name="layer",
    )(normed, tokens, cotangent, *flat_heads, *flat_weights, gain)
    out, grad, small = outs[:3]
    grads = [outs[3].astype(F32)]
    for blocks in outs[4:7]:
        grads.append(blocks.transpose(1, 0, 2).reshape(blocks.shape[1], width).astype(F32))
    grads.append(outs[7].astype(F32))
    return out, grad, small[0], small[1], small[2, : columns[0]], grads


def body(
    tokens,
    lengths,
    norm_gain,
    norm_shift,
    qkv_weight,
    qkv_bias,
    out_weight,
    gate_weight,
    up_weight,
    down_weight,
    cotangent,
):
    tensor_size = lax.axis_size("tensor")
    dp_size = lax.axis_size("dp")
    count = tensor_size // 2
    where = lax.axis_index("tensor")
    dp_place = lax.axis_index("dp")
    side = where % 2
    across = [(i, i ^ 1) for i in range(tensor_size)]
    row_count, width = tokens.shape
    rows = row_count // 2
    chunk_count = 8

    def own_part(weight):
        part = weight.shape[0] // dp_size
        return lax.dynamic_slice_in_dim(weight, dp_place * part, part, 0)

    def partner(parts, before, after):
        parts, _ = lax.optimization_barrier((parts, before))
        parts = [lax.ppermute(part, "tensor", across) for part in parts]
        parts, after = lax.optimization_barrier((parts, after))
        return [lax.all_gather(part, "dp", axis=0, tiled=True) for part in parts], after

    head_weights = (qkv_weight, out_weight)
    mid_weights = (gate_weight.T, up_weight.T, down_weight)
    other_bias = lax.ppermute(qkv_bias, "tensor", across)

    length = lax.dynamic_slice_in_dim(lengths, side, 1, 0)
    norm = (norm_gain, norm_shift)
    *own_group, normed = project(side, tokens, cotangent, norm, head_weights, qkv_bias)
    tables = rotary_tables(rows)
    even = (out_weight.shape[0] // HEAD) % 2 == 0
    other_heads, (_, other_bias) = partner(
        [own_part(weight) for weight in head_weights], (), (normed, other_bias)
    )
    mid_parts = [own_part(weight) for weight in mid_weights]
    if even:
        heads = [attention(length, *own_group, *tables)]
        other_mids, _ = partner(mid_parts, normed, heads[0])
        other_group = project(side, normed, cotangent, (), other_heads, other_bias)
        heads.append(attention(length, *other_group, *tables))
    else:
        other_mids, _ = partner(mid_parts, normed, ())
        other_group = project(side, normed, cotangent, (), other_heads, other_bias)
        pairs = zip(own_group, other_group)
        attended, qkv_back = attention(
            length, *[jnp.concatenate(pair, axis=1) for pair in pairs], *tables
        )
        cut, wide = out_weight.shape[0], qkv_weight.shape[1]
        heads = [
            (attended[:, s * cut : (s + 1) * cut], qkv_back[:, s * wide : (s + 1) * wide])
            for s in range(2)
        ]
    weights = ((*head_weights, *mid_weights), (*other_heads, *other_mids))
    layer_out, grad_tokens, gain_part, shift_part, grad_bias, grads = layer(
        normed, tokens, cotangent, heads, weights, norm_gain[None, :], count, chunk_count, dp_size
    )
    grad_qkv, grad_gate, grad_up, grad_down, grad_out = grads
    grad_gate, grad_up = grad_gate.T, grad_up.T
    return (
        layer_out,
        grad_tokens,
        gain_part,
        shift_part,
        grad_qkv,
        grad_bias,
        grad_out,
        grad_gate,
        grad_up,
        grad_down,
    )


def solution(mesh):
    placed = (
        P("dp", None),
        P("dp"),
        P(),
        P(),
        P(None, "tensor"),
        P("tensor"),
        P("tensor", None),
        P(None, "tensor"),
        P(None, "tensor"),
        P("tensor", None),
        P("dp", None),
    )
    return jax.shard_map(
        body,
        mesh=mesh,
        in_specs=placed,
        out_specs=(
            P("dp", None),
            P("dp", None),
            P(),
            P(),
            P(None, "tensor"),
            P("tensor"),
            P("tensor", None),
            P(None, "tensor"),
            P(None, "tensor"),
            P("tensor", None),
        ),
        check_vma=False,
    )
```
